32 devices in a mesh: grp: 2 (over y), bl: 16 (over z, x, core).
Axes of the slice: x: 2, y: 2, z: 4, core: 2. Of those that a mesh axis runs over, the one named last changes fastest.
Arguments:
- measured_correlation: float32 [2, 480, 32, 128], P(None, ('grp', 'bl')), parts along dimension 1, may hold values from -6 to 6
- model_response: bfloat16 [40, 2, 480, 32, 128], P(None, None, ('grp', 'bl')), parts along dimension 2, may hold values from -1 to 1
- validity_mask: int32 [480, 32, 128], P(('grp', 'bl')), parts along dimension 0, may hold values from 0 to 1, as said below
- leading_station_index: int32 [480], P(('grp', 'bl')), parts along dimension 0, may hold values from 0 to 62, as said below
- trailing_station_index: int32 [480], P(('grp', 'bl')), parts along dimension 0, may hold values from 1 to 63, as said below
- gain_real_part: float32 [5120, 128], P(('grp', 'bl')), parts along dimension 0, may hold values from 0.5 to 1.5
- gain_imaginary: float32 [5120, 128], P(('grp', 'bl')), parts along dimension 0, may hold values from -1.5 to 1.5
Outputs:
- gains: float32 [2, 5120, 128], P(None, ('grp', 'bl')), parts along dimension 1
- residual: float32 [2, 480, 32, 128], P(None, ('grp', 'bl')), parts along dimension 1
The draws below stay inside these ranges and needn't reach their ends.
There are 2 independent parts, one for each index of `grp`. The reference program is written for one: setup_inputs(seed, part) draws one part's arguments, and reference() takes and returns one part's arrays. A program takes and returns all parts, laid end to end along the dimension named above; each array names one. Nothing has to cross between parts.
Inputs may be any that keep to these rules, and one draw needn't show every extreme that they name: leading_station_index[b] < trailing_station_index[b]; no pair of stations appears twice; stations 0 and 63 form a baseline. `trailing_station_index`: see leading_station_index. `validity_mask`: whole time samples of a baseline may be flagged, at rates that differ between the baselines of different devices.
All inputs are finite; a program needn't handle non-finite values.
Results may differ from the reference program's by a relative error of at most 0.0003.
Values sent between devices are 32-bit elements; how exact they have to be, the bound alone decides.
No kernel may reach another device: no remote copies, remote signals or barrier semaphores. Data moves between devices by JAX's collectives and lax.ppermute only.
A program may use at most 64 MiB of HBM per device.

```python
import jax
import jax.numpy as jnp
import numpy as np
from jax import lax

STATIONS = 64
SOURCE_COUNT = 40
SPECTRAL_BINS = 128
LOCAL_PAIR_COUNT = 15
EPOCH_COUNT = 32
ITERS = 2
PAIR_COUNT_ALL = 240
UNKNOWNS = 2560
N_BL = 16


def pair_choice(key):
    upper_first, upper_second = np.triu_indices(STATIONS, 1)
    count = upper_first.shape[0]
    device_ranks = jax.random.permutation(key, count).astype(jnp.int32)
    device_ranks = device_ranks.at[STATIONS - 2].set(-1)
    sort_order = jnp.argsort(device_ranks, stable=True)[:PAIR_COUNT_ALL]
    first = jnp.asarray(upper_first, jnp.int32)[sort_order]
    second = jnp.asarray(upper_second, jnp.int32)[sort_order]
    return (first, second)


def draw_leading_station_index(key, part):
    first, second = pair_choice(key)
    return first


def draw_trailing_station_index(key, part):
    first, second = pair_choice(key)
    return second


def draw_validity_mask(key, part):
    key = jax.random.fold_in(key, 7)
    key_rate, block_random_key, cell_random_key = jax.random.split(key, 3)
    holding_processors = PAIR_COUNT_ALL // LOCAL_PAIR_COUNT
    decile_fractions = jax.random.randint(key_rate, (holding_processors,), 0, 7).astype(jnp.int32)
    each_station_pair = jnp.repeat(decile_fractions, LOCAL_PAIR_COUNT)
    block_sample = jax.random.randint(block_random_key, (PAIR_COUNT_ALL, EPOCH_COUNT), 0, 10).astype(jnp.int32)
    block_kept = block_sample >= each_station_pair[:, None]
    cell_sample = jax.random.randint(cell_random_key, (PAIR_COUNT_ALL, EPOCH_COUNT, SPECTRAL_BINS), 0, 8).astype(jnp.int32)
    kept = jnp.logical_and(block_kept[:, :, None], cell_sample != 0)
    return kept.astype(jnp.int32)


def levels(key, shape, cuts, smallest, top_value):
    level, own = 1.0, jax.random.fold_in(key, 6)
    for dim, blocks in cuts:
        heights = jnp.exp(jax.random.uniform(jax.random.fold_in(own, dim), (blocks,), jnp.float32, smallest / len(cuts), top_value / len(cuts)))
        level = level * jnp.repeat(heights, shape[dim] // blocks).reshape([-1 if axis == dim else 1 for axis in range(len(shape))])
    return level


def normal_values(key, shape, spread, most, cuts=(), kind=jnp.bfloat16):
    array = jax.random.normal(key, shape, jnp.float32) * spread
    if len(cuts) > 0:
        array = levels(key, shape, cuts, -0.22, 0.18) * array
    return jnp.clip(array, min=-most, max=most).astype(kind)


def setup_inputs(seed: int = 0, part: int = 0) -> dict:
    streams_of = jax.random.split(jax.random.key(seed), 8)
    part_splits = jax.random.split(jax.random.fold_in(streams_of[7], part), 8)
    measured_correlation = normal_values(part_splits[0], (2, PAIR_COUNT_ALL, EPOCH_COUNT, SPECTRAL_BINS), 1.0, 6.0, ((1, 16),), jnp.float32)
    model_response = normal_values(part_splits[1], (SOURCE_COUNT, 2, PAIR_COUNT_ALL, EPOCH_COUNT, SPECTRAL_BINS), 0.16, 1.0, ((2, 16),))
    validity_mask = draw_validity_mask(jax.random.fold_in(jax.random.fold_in(streams_of[7], part), 71), part)
    leading_station_index = draw_leading_station_index(jax.random.fold_in(jax.random.fold_in(streams_of[7], part), 71), part)
    trailing_station_index = draw_trailing_station_index(jax.random.fold_in(jax.random.fold_in(streams_of[7], part), 71), part)
    gain_real_part = jnp.clip(1.0 + 0.1 * jax.random.normal(part_splits[5], (UNKNOWNS, SPECTRAL_BINS), jnp.float32), 0.5, 1.5)
    gain_imaginary = normal_values(part_splits[6], (UNKNOWNS, SPECTRAL_BINS), 0.3, 1.5, ((0, 16),), jnp.float32)
    return {"measured_correlation": measured_correlation, "model_response": model_response, "validity_mask": validity_mask, "leading_station_index": leading_station_index, "trailing_station_index": trailing_station_index, "gain_real_part": gain_real_part, "gain_imaginary": gain_imaginary}


ridge = 1.0


def block_pass(full_re, full_im, vis_blk, coh_blk, weight, first, second, want_sums):
    ar = jnp.transpose(full_re[first], (1, 0, 2))
    ai = jnp.transpose(full_im[first], (1, 0, 2))
    br = jnp.transpose(full_re[second], (1, 0, 2))
    bi = jnp.transpose(full_im[second], (1, 0, 2))
    mr = coh_blk[:, 0].astype(jnp.float32)
    mi = coh_blk[:, 1].astype(jnp.float32)
    hr = (ar * br + ai * bi)[:, :, None]
    hi = (ai * br - ar * bi)[:, :, None]
    pred_re = hr * mr - hi * mi
    pred_im = hr * mi + hi * mr
    res_re = weight * (vis_blk[0] - jnp.sum(pred_re, 0))
    res_im = weight * (vis_blk[1] - jnp.sum(pred_im, 0))
    residual = jnp.stack([res_re, res_im])
    if not want_sums:
        return residual, None
    x_re = res_re[None] + weight[None] * pred_re
    x_im = res_im[None] + weight[None] * pred_im
    bre = br[:, :, None]
    bim = bi[:, :, None]
    are = ar[:, :, None]
    aim = ai[:, :, None]
    z_re = mr * bre + mi * bim
    z_im = mi * bre - mr * bim
    first_re = jnp.sum(z_re * x_re + z_im * x_im, 2)
    first_im = jnp.sum(z_re * x_im - z_im * x_re, 2)
    u_re = mr * are - mi * aim
    u_im = mr * aim + mi * are
    second_re = jnp.sum(u_re * x_re + u_im * x_im, 2)
    second_im = jnp.sum(u_im * x_re - u_re * x_im, 2)
    power = jnp.sum(weight[None] * (mr * mr + mi * mi), 2)
    den_first = power * (br * br + bi * bi)
    den_second = power * (ar * ar + ai * ai)
    stations = jnp.arange(STATIONS, dtype=jnp.int32)
    onehot_first = (first[:, None] == stations[None, :]).astype(jnp.float32)
    onehot_second = (second[:, None] == stations[None, :]).astype(jnp.float32)
    terms_first = jnp.stack([first_re, first_im, den_first])
    terms_second = jnp.stack([second_re, second_im, den_second])
    sums = jnp.einsum("bs,cdbf->csdf", onehot_first, terms_first, precision=lax.Precision.HIGHEST)
    sums = sums + jnp.einsum("bs,cdbf->csdf", onehot_second, terms_second, precision=lax.Precision.HIGHEST)
    return residual, sums


def update(gre, gim, sums):
    denom = sums[2] + ridge
    return 0.5 * (gre + sums[0] / denom), 0.5 * (gim + sums[1] / denom)


def reference(measured_correlation, model_response, validity_mask, leading_station_index, trailing_station_index, gain_real_part, gain_imaginary):
    measured_pieces = jnp.moveaxis(measured_correlation.reshape(2, N_BL, LOCAL_PAIR_COUNT, EPOCH_COUNT, SPECTRAL_BINS), 1, 0)
    model_pieces = jnp.moveaxis(model_response.reshape(SOURCE_COUNT, 2, N_BL, LOCAL_PAIR_COUNT, EPOCH_COUNT, SPECTRAL_BINS), 2, 0)
    mask_pieces = validity_mask.astype(jnp.float32).reshape(N_BL, LOCAL_PAIR_COUNT, EPOCH_COUNT, SPECTRAL_BINS)
    leading_station_pieces = leading_station_index.reshape(N_BL, LOCAL_PAIR_COUNT)
    trailing_station_pieces = trailing_station_index.reshape(N_BL, LOCAL_PAIR_COUNT)
    gre = gain_real_part.reshape(STATIONS, SOURCE_COUNT, SPECTRAL_BINS)
    gim = gain_imaginary.reshape(STATIONS, SOURCE_COUNT, SPECTRAL_BINS)
    for step in range(ITERS):
        def add_block(total, items):
            vis_blk, coh_blk, weight, first, second = items
            unused, sums = block_pass(gre, gim, vis_blk, coh_blk, weight, first, second, True)
            return total + sums, None
        start = jnp.zeros((3, STATIONS, SOURCE_COUNT, SPECTRAL_BINS), jnp.float32)
        total, unused = lax.scan(add_block, start, (measured_pieces, model_pieces, mask_pieces, leading_station_pieces, trailing_station_pieces))
        gre, gim = update(gre, gim, total)

    def residual_block(items):
        vis_blk, coh_blk, weight, first, second = items
        residual, unused = block_pass(gre, gim, vis_blk, coh_blk, weight, first, second, False)
        return residual
    block_list = lax.map(residual_block, (measured_pieces, model_pieces, mask_pieces, leading_station_pieces, trailing_station_pieces))
    residual = jnp.moveaxis(block_list, 0, 1).reshape(2, PAIR_COUNT_ALL, EPOCH_COUNT, SPECTRAL_BINS)
    gains = jnp.stack([gre.reshape(UNKNOWNS, SPECTRAL_BINS), gim.reshape(UNKNOWNS, SPECTRAL_BINS)])
    return gains, residual
```

```python
import functools

import jax
import jax.numpy as jnp
from jax import lax
from jax.experimental import pallas as pl
from jax.experimental.pallas import tpu as pltpu
from jax.sharding import PartitionSpec as P

STATIONS = 64
SOURCE_COUNT = 40
ITERS = 2
ROWS = 16

ridge = 1.0
F32 = jnp.float32
BF16 = jnp.bfloat16
VMEM_LIMIT = 48 * 1024 * 1024


def swap(x):
    return pltpu.roll(x, x.shape[-1] // 2, axis=x.ndim - 1)


def lower(shape):
    return lax.broadcasted_iota(jnp.int32, shape, len(shape) - 1) < shape[-1] // 2


def cross(a, b):
    lo = lower(a.shape)
    return jnp.where(lo, a, swap(b)), jnp.where(lo, swap(a), b)


def three(x):
    hi = x.astype(BF16)
    rest = x - hi.astype(F32)
    mid = rest.astype(BF16)
    return hi, mid, (rest - mid.astype(F32)).astype(BF16)


def pick(onehot, x, dims):
    return sum(
        lax.dot_general(onehot, part, (dims, ((), ())), preferred_element_type=F32)
        for part in three(x)
    )


def pack_kernel(n, dpc, me_ref, first_ref, second_ref, re_ref, im_ref, *rest):
    outs, halves = rest[:n], rest[n]
    per = re_ref.shape[0] // SOURCE_COUNT
    me = me_ref[0]
    a, b = cross(re_ref[...], im_ref[...])
    halves[0] = a
    halves[1] = b
    base = lax.rem(me, 2) * per
    lane = lax.broadcasted_iota(jnp.int32, (1, dpc * 128), 1)
    sub = lax.broadcasted_iota(jnp.int32, (2 * per, 128), 0)
    count = first_ref.shape[0]
    for o in range(n):
        peer = jnp.bitwise_xor(me, o)
        k, c = lax.div(peer, 2), lax.rem(peer, 2)
        marks = jnp.zeros((1, dpc * 128), F32)
        for r in range(count):
            marks = jnp.where(lane == o * 2 * ROWS + r, (first_ref[r] + 1).astype(F32), marks)
            marks = jnp.where(lane == o * 2 * ROWS + ROWS + r, (second_ref[r] + 1).astype(F32), marks)
        for dd in range(dpc):
            cols = slice(dd * 128, (dd + 1) * 128)
            block = jnp.where(sub == per - base, marks[:, cols], 0.0)
            for s in range(per):
                row = halves[c, pl.ds(s * SOURCE_COUNT + k * dpc + dd, 1), :]
                block = jnp.where(sub == base + s, row, block)
            outs[o][:, cols] = block


def power_kernel(n, dpc, me_ref, model_ref, mask_ref, *rest):
    outs, local, = rest[:n], rest[n]
    b = pl.program_id(0)

    @pl.when(b == 0)
    def _():
        local[...] = jnp.zeros_like(local)

    weight = mask_ref[0].astype(F32)
    for d in range(SOURCE_COUNT):
        mr = model_ref[d, 0, 0].astype(F32)
        mi = model_ref[d, 1, 0].astype(F32)
        local[d, pl.ds(b, 1), :] = jnp.sum(weight * (mr * mr + mi * mi), axis=0, keepdims=True)

    @pl.when(b == pl.num_programs(0) - 1)
    def _():
        me = me_ref[0]
        for o in range(n):
            peer = jnp.bitwise_xor(me, o)
            k, c = lax.div(peer, 2), lax.rem(peer, 2)
            for dd in range(dpc):
                full = local[k * dpc + dd]
                x0, x1 = cross(full[:8], full[8:])
                outs[o][:, dd * 128 : (dd + 1) * 128] = jnp.where(c == 0, x0, x1)


def own_first_kernel(n, dpc, me_ref, *rest):
    ins, (g_ref, onehot_ref), outs = rest[:n], rest[n : n + 2], rest[n + 2 :]
    me = me_ref[0]
    width = dpc * 128
    per = STATIONS // n
    row = lax.broadcasted_iota(jnp.int32, (2 * per, width), 0)
    marks = jnp.zeros((2 * per, width), F32)
    for m in range(n // 2):
        total = jnp.zeros((2 * per, width), F32)
        for o in (2 * m, 2 * m + 1):
            peer = jnp.bitwise_xor(me, o)
            mine = lax.div(row, per) == lax.rem(peer, 2)
            x = ins[o][...]
            total = total + jnp.where(mine, x, 0.0)
            marks = marks + jnp.where(mine, 0.0, x)
        chip = lax.div(jnp.bitwise_xor(me, 2 * m), 2)
        g_ref[pl.ds(pl.multiple_of(chip * 2 * per, 2 * per), 2 * per), :] = total
    marks = jnp.sum(marks, axis=0, keepdims=True)[:, : n * 2 * ROWS]
    station = lax.broadcasted_iota(jnp.int32, (STATIONS, n * 2 * ROWS), 0)
    onehot = jnp.where(station + 1 == marks.astype(jnp.int32), 1.0, 0.0).astype(BF16)
    onehot_ref[...] = onehot
    sel = pick(onehot, g_ref[...], ((0,), (0,)))
    for o in range(n):
        outs[o][...] = sel[o * 2 * ROWS : (o + 1) * 2 * ROWS]


def own_kernel(n, dpc, last, me_ref, g_in, onehot_ref, *rest):
    sums, powers, sels = rest[:n], rest[n : 2 * n], rest[2 * n : 3 * n]
    rest = rest[3 * n :]
    g_out, outs, terms = rest[0], rest[1 : n + 1], rest[n + 1]
    width = dpc * 128
    lo = lower((ROWS, 128))
    lo8 = lower((8, 128))
    sign = jnp.where(lo, -1.0, 1.0)
    for o in range(n):
        for dd in range(dpc):
            cols = slice(dd * 128, (dd + 1) * 128)
            B = sums[o][:, cols]
            W = powers[o][:, cols]
            Wx = swap(W)
            W = jnp.concatenate([jnp.where(lo8, W, Wx), jnp.where(lo8, Wx, W)], 0)
            p = sels[o][:ROWS, cols]
            q = sels[o][ROWS:, cols]
            Bx, px, qx = swap(B), swap(p), swap(q)
            Brr, Bii = jnp.where(lo, B, Bx), jnp.where(lo, Bx, B)
            first = Brr * q + sign * Bii * qx
            second = Brr * p - sign * Bii * px
            q2, p2 = q * q, p * p
            r = o * 2 * ROWS
            terms[r : r + ROWS, cols] = first
            terms[r + ROWS : r + 2 * ROWS, cols] = second
            dcols = slice(width + dd * 128, width + (dd + 1) * 128)
            terms[r : r + ROWS, dcols] = W * (q2 + swap(q2))
            terms[r + ROWS : r + 2 * ROWS, dcols] = W * (p2 + swap(p2))
    onehot = onehot_ref[...]
    total = pick(onehot, terms[...], ((1,), (0,)))
    g = 0.5 * (g_in[...] + total[:, :width] / (total[:, width:] + ridge))
    g_out[...] = g
    sel = pick(onehot, g, ((0,), (0,)))
    for o in range(n):
        outs[o][: 2 * ROWS, :] = sel[o * 2 * ROWS : (o + 1) * 2 * ROWS]
    if last:
        per = STATIONS // n
        line = lax.broadcasted_iota(jnp.int32, (n * 8, STATIONS), 0)
        col = lax.broadcasted_iota(jnp.int32, (n * 8, STATIONS), 1)
        slot, r = lax.div(line, 8), lax.rem(line, 8)
        want = jnp.bitwise_xor(me_ref[0], slot) * per + r
        mine = jnp.where((col == want) & (r < per), 1.0, 0.0).astype(BF16)
        own = pick(mine, g, ((1,), (0,)))
        for o in range(n):
            outs[o][2 * ROWS :, :] = own[o * 8 : (o + 1) * 8]


def unpack_rows(me, ins, m, rows, cols):
    even = lax.rem(me, 2) == 0
    a, b = ins[2 * m][rows, cols], ins[2 * m + 1][rows, cols]
    return cross(jnp.where(even, a, b), jnp.where(even, b, a))


def load_products(n, dpc, me, ins, hre, him):
    for m in range(n // 2):
        k = lax.div(jnp.bitwise_xor(me, 2 * m), 2)
        for dd in range(dpc):
            cols = slice(dd * 128, (dd + 1) * 128)
            pr, pi = unpack_rows(me, ins, m, slice(0, ROWS), cols)
            qr, qi = unpack_rows(me, ins, m, slice(ROWS, 2 * ROWS), cols)
            hre[k * dpc + dd] = pr * qr + pi * qi
            him[k * dpc + dd] = pi * qr - pr * qi


def predict(b, model_ref, vis_ref, mask_ref, hre, him):
    acc_re = vis_ref[0, 0]
    acc_im = vis_ref[1, 0]

    def step(i, acc):
        acc_re, acc_im = acc
        for u in range(8):
            d = i * 8 + u
            mr = model_ref[d, 0, 0].astype(F32)
            mi = model_ref[d, 1, 0].astype(F32)
            hr = hre[d, pl.ds(b, 1), :]
            hi = him[d, pl.ds(b, 1), :]
            acc_re = acc_re - (hr * mr - hi * mi)
            acc_im = acc_im - (hr * mi + hi * mr)
        return acc_re, acc_im

    acc_re, acc_im = lax.fori_loop(0, SOURCE_COUNT // 8, step, (acc_re, acc_im))
    weight = mask_ref[0].astype(F32)
    return weight * acc_re, weight * acc_im


def pass_kernel(n, dpc, me_ref, model_ref, vis_ref, mask_ref, power_ref, *rest):
    ins, outs = rest[:n], rest[n : 2 * n]
    hre, him, cre, cim, halves = rest[2 * n :]
    b = pl.program_id(0)
    me = me_ref[0]

    @pl.when(b == 0)
    def _():
        load_products(n, dpc, me, ins, hre, him)
        cre[...] = jnp.zeros_like(cre)
        cim[...] = jnp.zeros_like(cim)

    res_re, res_im = predict(b, model_ref, vis_ref, mask_ref, hre, him)

    def step(i, carry):
        for u in range(8):
            d = i * 8 + u
            mr = model_ref[d, 0, 0].astype(F32)
            mi = model_ref[d, 1, 0].astype(F32)
            cre[d, pl.ds(b, 1), :] = jnp.sum(mr * res_re + mi * res_im, axis=0, keepdims=True)
            cim[d, pl.ds(b, 1), :] = jnp.sum(mr * res_im - mi * res_re, axis=0, keepdims=True)
        return carry

    lax.fori_loop(0, SOURCE_COUNT // 8, step, 0)

    @pl.when(b == pl.num_programs(0) - 1)
    def _():
        for d in range(SOURCE_COUNT):
            w = power_ref[d]
            x0, x1 = cross(cre[d] + hre[d] * w, cim[d] + him[d] * w)
            halves[0, d] = x0
            halves[1, d] = x1
        for o in range(n):
            peer = jnp.bitwise_xor(me, o)
            k, c = lax.div(peer, 2), lax.rem(peer, 2)
            for dd in range(dpc):
                outs[o][:, dd * 128 : (dd + 1) * 128] = halves[c, k * dpc + dd]


def last_kernel(n, dpc, me_ref, model_ref, vis_ref, mask_ref, *rest):
    ins, (res_ref, gains_ref), (hre, him) = rest[:n], rest[n : n + 2], rest[n + 2 :]
    b = pl.program_id(0)
    me = me_ref[0]

    @pl.when(b == 0)
    def _():
        load_products(n, dpc, me, ins, hre, him)
        per = STATIONS // n
        for m in range(n // 2):
            k = lax.div(jnp.bitwise_xor(me, 2 * m), 2)
            for dd in range(dpc):
                cols = slice(dd * 128, (dd + 1) * 128)
                re, im = unpack_rows(me, ins, m, slice(2 * ROWS, 2 * ROWS + 8), cols)
                for s in range(per):
                    at = s * SOURCE_COUNT + k * dpc + dd
                    gains_ref[0, pl.ds(at, 1), :] = re[s : s + 1]
                    gains_ref[1, pl.ds(at, 1), :] = im[s : s + 1]

    res_re, res_im = predict(b, model_ref, vis_ref, mask_ref, hre, him)
    res_ref[0, 0] = res_re
    res_ref[1, 0] = res_im


SMEM = pl.BlockSpec(memory_space=pltpu.SMEM)


def whole(shape):
    return pl.BlockSpec(shape, lambda *_: (0,) * len(shape))


def spec_like(x):
    return whole(x.shape)


def shape(*dims, dtype=F32):
    return jax.ShapeDtypeStruct(dims, dtype)


def exchange(n, parts):
    done = [parts[0]]
    for o in range(1, n):
        done.append(lax.ppermute(parts[o], "bl", [(i, i ^ o) for i in range(n)]))
    return done


def fast_body(n, vis, model, mask, first, second, gre, gim):
    dpc = SOURCE_COUNT // (n // 2)
    width = dpc * 128
    pairs, times, channels = mask.shape
    me = lax.axis_index("bl").astype(jnp.int32).reshape(1)
    params = pltpu.CompilerParams(vmem_limit_bytes=VMEM_LIMIT)
    plane = (SOURCE_COUNT, ROWS, channels)

    per_model = pl.BlockSpec((SOURCE_COUNT, 2, 1, times, channels), lambda b: (0, 0, b, 0, 0))
    per_vis = pl.BlockSpec((2, 1, times, channels), lambda b: (0, b, 0, 0))
    per_mask = pl.BlockSpec((1, times, channels), lambda b: (b, 0, 0))

    def call(kernel, args, specs, outs, scratch=(), grid=()):
        out_specs = [o[1] if isinstance(o, tuple) else whole(o.shape) for o in outs]
        out_shape = [o[0] if isinstance(o, tuple) else o for o in outs]
        return pl.pallas_call(
            functools.partial(kernel, n, dpc),
            grid=grid,
            in_specs=specs,
            out_specs=out_specs,
            out_shape=out_shape,
            scratch_shapes=list(scratch),
            compiler_params=params,
        )(*args)

    start_rows = 2 * STATIONS // n
    packed = call(
        pack_kernel,
        (me, first, second, gre, gim),
        [SMEM, SMEM, SMEM, spec_like(gre), spec_like(gim)],
        [shape(start_rows, width)] * n,
        [pltpu.VMEM((2,) + gre.shape, F32)],
    )
    packed = exchange(n, packed)
    power = call(
        power_kernel,
        (me, model, mask),
        [SMEM, per_model, per_mask],
        [shape(8, width)] * n + [shape(*plane)],
        grid=(pairs,),
    )
    powers, power = exchange(n, power[:n]), power[n]
    out = call(
        own_first_kernel,
        (me, *packed),
        [SMEM] + [spec_like(x) for x in packed],
        [shape(STATIONS, width), shape(STATIONS, n * 2 * ROWS, dtype=BF16)]
        + [shape(2 * ROWS, width)] * n,
    )
    g, onehot, sels = out[0], out[1], out[2:]
    full = [pltpu.VMEM(plane, F32)] * 2
    for step in range(ITERS):
        got = exchange(n, sels)
        sums = call(
            pass_kernel,
            (me, model, vis, mask, power, *got),
            [SMEM, per_model, per_vis, per_mask, whole(plane)] + [spec_like(x) for x in got],
            [shape(ROWS, width)] * n,
            full * 2 + [pltpu.VMEM((2,) + plane, F32)],
            grid=(pairs,),
        )
        sums = exchange(n, sums)
        last = step == ITERS - 1
        args = (me, g, onehot, *sums, *powers, *sels)
        out = call(
            lambda n, dpc, *refs: own_kernel(n, dpc, last, *refs),
            args,
            [SMEM] + [spec_like(x) for x in args[1:]],
            [shape(STATIONS, width)] + [shape(2 * ROWS + (8 if last else 0), width)] * n,
            [pltpu.VMEM((n * 2 * ROWS, 2 * width), F32)],
        )
        g, sels = out[0], out[1:]
    got = exchange(n, sels)
    residual, gains = call(
        last_kernel,
        (me, model, vis, mask, *got),
        [SMEM, per_model, per_vis, per_mask] + [spec_like(x) for x in got],
        [(shape(*vis.shape), per_vis), shape(2, *gre.shape)],
        full,
        grid=(pairs,),
    )
    return gains, residual


def block_pass(full_re, full_im, vis_blk, coh_blk, weight, first, second, want_sums):
    ar = jnp.transpose(full_re[first], (1, 0, 2))
    ai = jnp.transpose(full_im[first], (1, 0, 2))
    br = jnp.transpose(full_re[second], (1, 0, 2))
    bi = jnp.transpose(full_im[second], (1, 0, 2))
    mr = coh_blk[:, 0].astype(F32)
    mi = coh_blk[:, 1].astype(F32)
    hr = ar * br + ai * bi
    hi = ai * br - ar * bi
    hr_t, hi_t = hr[:, :, None], hi[:, :, None]
    res_re = weight * (vis_blk[0] - jnp.sum(hr_t * mr - hi_t * mi, 0))
    res_im = weight * (vis_blk[1] - jnp.sum(hr_t * mi + hi_t * mr, 0))
    residual = jnp.stack([res_re, res_im])
    if not want_sums:
        return (residual, None)
    power = jnp.sum(weight[None] * (mr * mr + mi * mi), 2)
    sum_re = jnp.sum(mr * res_re + mi * res_im, 2) + hr * power
    sum_im = jnp.sum(mr * res_im - mi * res_re, 2) + hi * power
    terms_first = jnp.stack([br * sum_re - bi * sum_im, br * sum_im + bi * sum_re, power * (br * br + bi * bi)])
    terms_second = jnp.stack([ar * sum_re + ai * sum_im, ai * sum_re - ar * sum_im, power * (ar * ar + ai * ai)])
    stations = jnp.arange(STATIONS, dtype=jnp.int32)
    onehot_first = (first[:, None] == stations[None, :]).astype(F32)
    onehot_second = (second[:, None] == stations[None, :]).astype(F32)
    exact = lax.Precision.HIGHEST
    sums = jnp.einsum("bs,cdbf->csdf", onehot_first, terms_first, precision=exact)
    sums = sums + jnp.einsum("bs,cdbf->csdf", onehot_second, terms_second, precision=exact)
    return (residual, sums)


def plain_body(vis, model, mask, first, second, gre, gim):
    weight = mask.astype(F32)
    rows, channels = gre.shape
    shaped = (STATIONS, SOURCE_COUNT, channels)
    full_re = lax.all_gather(gre, "bl", axis=0, tiled=True).reshape(shaped)
    full_im = lax.all_gather(gim, "bl", axis=0, tiled=True).reshape(shaped)
    for step in range(ITERS):
        unused, sums = block_pass(full_re, full_im, vis, model, weight, first, second, True)
        totals = lax.psum(sums, "bl")
        denom = totals[2] + ridge
        full_re = 0.5 * (full_re + totals[0] / denom)
        full_im = 0.5 * (full_im + totals[1] / denom)
    residual, unused = block_pass(full_re, full_im, vis, model, weight, first, second, False)
    both = jnp.stack([full_re, full_im]).reshape(2, STATIONS * SOURCE_COUNT, channels)
    return lax.dynamic_slice_in_dim(both, lax.axis_index("bl") * rows, rows, 1), residual


def solution(mesh):
    n = mesh.shape["bl"]
    split = n % 2 == 0 and SOURCE_COUNT % (n // 2) == 0 and STATIONS == 4 * n

    def body(vis, model, mask, first, second, gre, gim):
        if split and mask.shape[0] <= ROWS:
            return fast_body(n, vis, model, mask, first, second, gre, gim)
        return plain_body(vis, model, mask, first, second, gre, gim)

    in_specs = (
        P(None, ("grp", "bl"), None, None),
        P(None, None, ("grp", "bl"), None, None),
        P(("grp", "bl"), None, None),
        P(("grp", "bl")),
        P(("grp", "bl")),
        P(("grp", "bl"), None),
        P(("grp", "bl"), None),
    )
    out_specs = (P(None, ("grp", "bl"), None), P(None, ("grp", "bl"), None, None))
    return jax.shard_map(body, mesh=mesh, in_specs=in_specs, out_specs=out_specs, check_vma=False)
```

```python
import functools

import jax
import jax.numpy as jnp
from jax import lax
from jax.experimental import pallas as pl
from jax.experimental.pallas import tpu as pltpu
from jax.sharding import PartitionSpec as P

STATIONS = 64
SOURCE_COUNT = 40
ITERS = 2
ROWS = 16

ridge = 1.0
F32 = jnp.float32
BF16 = jnp.bfloat16
VMEM_LIMIT = 16 * 1024 * 1024


def swap(x):
    return pltpu.roll(x, x.shape[-1] // 2, axis=x.ndim - 1)


def lower(shape):
    return lax.broadcasted_iota(jnp.int32, shape, len(shape) - 1) < shape[-1] // 2


def cross(a, b):
    lo = lower(a.shape)
    return jnp.where(lo, a, swap(b)), jnp.where(lo, swap(a), b)


def three(x):
    hi = x.astype(BF16)
    rest = x - hi.astype(F32)
    mid = rest.astype(BF16)
    return hi, mid, (rest - mid.astype(F32)).astype(BF16)


def pick(onehot, x, dims):
    return sum(
        lax.dot_general(onehot, part, (dims, ((), ())), preferred_element_type=F32)
        for part in three(x)
    )


def pack_kernel(n, dpc, me_ref, first_ref, second_ref, re_ref, im_ref, *rest):
    outs, halves = rest
    per = re_ref.shape[0] // SOURCE_COUNT
    me = me_ref[0]
    a, b = cross(re_ref[...], im_ref[...])
    halves[0] = a
    halves[1] = b
    base = lax.rem(me, 2) * per
    lane = lax.broadcasted_iota(jnp.int32, (1, dpc * 128), 1)
    sub = lax.broadcasted_iota(jnp.int32, (2 * per, 128), 0)
    count = first_ref.shape[0]
    at = me * 2 * ROWS
    marks = jnp.zeros((1, dpc * 128), F32)
    for r in range(count):
        marks = jnp.where(lane == at + r, (first_ref[r] + 1).astype(F32), marks)
        marks = jnp.where(lane == at + ROWS + r, (second_ref[r] + 1).astype(F32), marks)
    for o in range(n):
        k, c = o // 2, o % 2
        for dd in range(dpc):
            cols = slice(dd * 128, (dd + 1) * 128)
            block = jnp.where(sub == per - base, marks[:, cols], 0.0)
            for s in range(per):
                at = s * SOURCE_COUNT + k * dpc + dd
                row = halves[c, at : at + 1, :]
                block = jnp.where(sub == base + s, row, block)
            outs[o, :, cols] = block


def power_kernel(n, dpc, model_ref, mask_ref, out_ref, local):
    local[...] = jnp.zeros_like(local)

    def pair(b, carry):
        weight = mask_ref[b].astype(F32)
        for d in range(SOURCE_COUNT):
            mr = model_ref[d, 0, b].astype(F32)
            mi = model_ref[d, 1, b].astype(F32)
            local[d, pl.ds(b, 1), :] = jnp.sum(weight * (mr * mr + mi * mi), axis=0, keepdims=True)
        return carry

    lax.fori_loop(0, mask_ref.shape[0], pair, 0)
    for k in range(n // 2):
        for dd in range(dpc):
            full = local[k * dpc + dd]
            x0, x1 = cross(full[:8], full[8:])
            out_ref[2 * k, :, dd * 128 : (dd + 1) * 128] = x0
            out_ref[2 * k + 1, :, dd * 128 : (dd + 1) * 128] = x1


def own_first_kernel(n, dpc, ins, g_ref, onehot_ref, outs):
    width = dpc * 128
    per = STATIONS // n
    row = lax.broadcasted_iota(jnp.int32, (2 * per, width), 0)
    marks = jnp.zeros((2 * per, width), F32)
    for m in range(n // 2):
        total = jnp.zeros((2 * per, width), F32)
        for o in (2 * m, 2 * m + 1):
            mine = lax.div(row, per) == o % 2
            x = ins[o]
            total = total + jnp.where(mine, x, 0.0)
            marks = marks + jnp.where(mine, 0.0, x)
        g_ref[m * 2 * per : (m + 1) * 2 * per, :] = total
    marks = jnp.sum(marks, axis=0, keepdims=True)[:, : n * 2 * ROWS]
    station = lax.broadcasted_iota(jnp.int32, (STATIONS, n * 2 * ROWS), 0)
    onehot = jnp.where(station + 1 == marks.astype(jnp.int32), 1.0, 0.0).astype(BF16)
    onehot_ref[...] = onehot
    sel = pick(onehot, g_ref[...], ((0,), (0,)))
    for o in range(n):
        outs[o] = sel[o * 2 * ROWS : (o + 1) * 2 * ROWS]


def own_kernel(n, dpc, last, g_in, onehot_ref, sums, powers, sels, g_out, outs, terms):
    width = dpc * 128
    lo = lower((ROWS, 128))
    lo8 = lower((8, 128))
    sign = jnp.where(lo, -1.0, 1.0)
    for o in range(n):
        for dd in range(dpc):
            cols = slice(dd * 128, (dd + 1) * 128)
            B = sums[o, :, cols]
            W = powers[o, :, cols]
            Wx = swap(W)
            W = jnp.concatenate([jnp.where(lo8, W, Wx), jnp.where(lo8, Wx, W)], 0)
            p = sels[o, :ROWS, cols]
            q = sels[o, ROWS:, cols]
            Bx, px, qx = swap(B), swap(p), swap(q)
            Brr, Bii = jnp.where(lo, B, Bx), jnp.where(lo, Bx, B)
            first = Brr * q + sign * Bii * qx
            second = Brr * p - sign * Bii * px
            q2, p2 = q * q, p * p
            r = o * 2 * ROWS
            terms[r : r + ROWS, cols] = first
            terms[r + ROWS : r + 2 * ROWS, cols] = second
            dcols = slice(width + dd * 128, width + (dd + 1) * 128)
            terms[r : r + ROWS, dcols] = W * (q2 + swap(q2))
            terms[r + ROWS : r + 2 * ROWS, dcols] = W * (p2 + swap(p2))
    onehot = onehot_ref[...]
    total = pick(onehot, terms[...], ((1,), (0,)))
    g = 0.5 * (g_in[...] + total[:, :width] / (total[:, width:] + ridge))
    g_out[...] = g
    sel = pick(onehot, g, ((0,), (0,)))
    for o in range(n):
        outs[o, : 2 * ROWS, :] = sel[o * 2 * ROWS : (o + 1) * 2 * ROWS]
    if last:
        per = STATIONS // n
        line = lax.broadcasted_iota(jnp.int32, (n * 8, STATIONS), 0)
        col = lax.broadcasted_iota(jnp.int32, (n * 8, STATIONS), 1)
        slot, r = lax.div(line, 8), lax.rem(line, 8)
        want = slot * per + r
        mine = jnp.where((col == want) & (r < per), 1.0, 0.0).astype(BF16)
        own = pick(mine, g, ((1,), (0,)))
        for o in range(n):
            outs[o, 2 * ROWS :, :] = own[o * 8 : (o + 1) * 8]


def load_products(n, dpc, ins, hre, him):
    for k in range(n // 2):
        for dd in range(dpc):
            cols = slice(dd * 128, (dd + 1) * 128)
            pr, pi = cross(ins[2 * k, :ROWS, cols], ins[2 * k + 1, :ROWS, cols])
            qr, qi = cross(ins[2 * k, ROWS : 2 * ROWS, cols], ins[2 * k + 1, ROWS : 2 * ROWS, cols])
            hre[k * dpc + dd] = pr * qr + pi * qi
            him[k * dpc + dd] = pi * qr - pr * qi


def predict(b, model_ref, vis_ref, mask_ref, hre, him):
    def step(i, acc):
        acc_re, acc_im = acc
        for u in range(8):
            d = i * 8 + u
            mr = model_ref[d, 0, b].astype(F32)
            mi = model_ref[d, 1, b].astype(F32)
            hr = hre[d, pl.ds(b, 1), :]
            hi = him[d, pl.ds(b, 1), :]
            acc_re = acc_re - (hr * mr - hi * mi)
            acc_im = acc_im - (hr * mi + hi * mr)
        return acc_re, acc_im

    acc = lax.fori_loop(0, SOURCE_COUNT // 8, step, (vis_ref[0, b], vis_ref[1, b]))
    weight = mask_ref[b].astype(F32)
    return weight * acc[0], weight * acc[1]


def pass_kernel(n, dpc, model_ref, vis_ref, mask_ref, power_ref, ins, out_ref, hre, him, cre, cim):
    load_products(n, dpc, ins, hre, him)
    cre[...] = jnp.zeros_like(cre)
    cim[...] = jnp.zeros_like(cim)

    def pair(b, carry):
        res_re, res_im = predict(b, model_ref, vis_ref, mask_ref, hre, him)

        def step(i, carry):
            for u in range(8):
                d = i * 8 + u
                mr = model_ref[d, 0, b].astype(F32)
                mi = model_ref[d, 1, b].astype(F32)
                cre[d, pl.ds(b, 1), :] = jnp.sum(mr * res_re + mi * res_im, axis=0, keepdims=True)
                cim[d, pl.ds(b, 1), :] = jnp.sum(mr * res_im - mi * res_re, axis=0, keepdims=True)
            return carry

        return lax.fori_loop(0, SOURCE_COUNT // 8, step, carry)

    lax.fori_loop(0, mask_ref.shape[0], pair, 0)
    for k in range(n // 2):
        for dd in range(dpc):
            d = k * dpc + dd
            w = power_ref[d]
            x0, x1 = cross(cre[d] + hre[d] * w, cim[d] + him[d] * w)
            out_ref[2 * k, :, dd * 128 : (dd + 1) * 128] = x0
            out_ref[2 * k + 1, :, dd * 128 : (dd + 1) * 128] = x1


def last_kernel(n, dpc, model_ref, vis_ref, mask_ref, ins, res_ref, gains_ref, hre, him):
    load_products(n, dpc, ins, hre, him)
    for k in range(n // 2):
        for dd in range(dpc):
            cols = slice(dd * 128, (dd + 1) * 128)
            re, im = cross(ins[2 * k, 2 * ROWS :, cols], ins[2 * k + 1, 2 * ROWS :, cols])
            for s in range(STATIONS // n):
                at = s * SOURCE_COUNT + k * dpc + dd
                gains_ref[0, at : at + 1, :] = re[s : s + 1]
                gains_ref[1, at : at + 1, :] = im[s : s + 1]

    def pair(b, carry):
        res_re, res_im = predict(b, model_ref, vis_ref, mask_ref, hre, him)
        res_ref[0, b] = res_re
        res_ref[1, b] = res_im
        return carry

    lax.fori_loop(0, mask_ref.shape[0], pair, 0)


SMEM = pl.BlockSpec(memory_space=pltpu.SMEM)
VMEM = pl.BlockSpec(memory_space=pltpu.VMEM)


def shape(*dims, dtype=F32):
    return jax.ShapeDtypeStruct(dims, dtype)


def exchange(x):
    return lax.all_to_all(x, "bl", split_axis=0, concat_axis=0, tiled=True)


def fast_body(n, vis, model, mask, first, second, gre, gim):
    dpc = SOURCE_COUNT // (n // 2)
    width = dpc * 128
    pairs, times, channels = mask.shape
    me = lax.axis_index("bl").astype(jnp.int32).reshape(1)
    params = pltpu.CompilerParams(vmem_limit_bytes=VMEM_LIMIT)
    plane = (SOURCE_COUNT, ROWS, channels)

    def call(kernel, args, outs, scratch=()):
        return pl.pallas_call(
            functools.partial(kernel, n, dpc),
            in_specs=[SMEM if x.ndim == 1 else VMEM for x in args],
            out_specs=[VMEM for o in outs],
            out_shape=outs,
            scratch_shapes=[pltpu.VMEM(x, F32) for x in scratch],
            compiler_params=params,
        )(*args)

    start_rows = 2 * STATIONS // n
    (packed,) = call(
        pack_kernel, (me, first, second, gre, gim), [shape(n, start_rows, width)], [(2,) + gre.shape]
    )
    packed = exchange(packed)
    powers, power = call(power_kernel, (model, mask), [shape(n, 8, width), shape(*plane)])
    powers = exchange(powers)
    g, onehot, sels = call(
        own_first_kernel,
        (packed,),
        [shape(STATIONS, width), shape(STATIONS, n * 2 * ROWS, dtype=BF16), shape(n, 2 * ROWS, width)],
    )
    for step in range(ITERS):
        last = step == ITERS - 1
        got = exchange(sels)
        (sums,) = call(
            pass_kernel, (model, vis, mask, power, got), [shape(n, ROWS, width)], [plane] * 4
        )
        sums = exchange(sums)
        g, sels = call(
            lambda n, dpc, *refs: own_kernel(n, dpc, last, *refs),
            (g, onehot, sums, powers, sels),
            [shape(STATIONS, width), shape(n, 2 * ROWS + (8 if last else 0), width)],
            [(n * 2 * ROWS, 2 * width)],
        )
    got = exchange(sels)
    residual, gains = call(
        last_kernel, (model, vis, mask, got), [shape(*vis.shape), shape(2, *gre.shape)], [plane] * 2
    )
    return gains, residual


def block_pass(full_re, full_im, vis_blk, coh_blk, weight, first, second, want_sums):
    ar = jnp.transpose(full_re[first], (1, 0, 2))
    ai = jnp.transpose(full_im[first], (1, 0, 2))
    br = jnp.transpose(full_re[second], (1, 0, 2))
    bi = jnp.transpose(full_im[second], (1, 0, 2))
    mr = coh_blk[:, 0].astype(F32)
    mi = coh_blk[:, 1].astype(F32)
    hr = ar * br + ai * bi
    hi = ai * br - ar * bi
    hr_t, hi_t = hr[:, :, None], hi[:, :, None]
    res_re = weight * (vis_blk[0] - jnp.sum(hr_t * mr - hi_t * mi, 0))
    res_im = weight * (vis_blk[1] - jnp.sum(hr_t * mi + hi_t * mr, 0))
    residual = jnp.stack([res_re, res_im])
    if not want_sums:
        return (residual, None)
    power = jnp.sum(weight[None] * (mr * mr + mi * mi), 2)
    sum_re = jnp.sum(mr * res_re + mi * res_im, 2) + hr * power
    sum_im = jnp.sum(mr * res_im - mi * res_re, 2) + hi * power
    terms_first = jnp.stack([br * sum_re - bi * sum_im, br * sum_im + bi * sum_re, power * (br * br + bi * bi)])
    terms_second = jnp.stack([ar * sum_re + ai * sum_im, ai * sum_re - ar * sum_im, power * (ar * ar + ai * ai)])
    stations = jnp.arange(STATIONS, dtype=jnp.int32)
    onehot_first = (first[:, None] == stations[None, :]).astype(F32)
    onehot_second = (second[:, None] == stations[None, :]).astype(F32)
    exact = lax.Precision.HIGHEST
    sums = jnp.einsum("bs,cdbf->csdf", onehot_first, terms_first, precision=exact)
    sums = sums + jnp.einsum("bs,cdbf->csdf", onehot_second, terms_second, precision=exact)
    return (residual, sums)


def plain_body(vis, model, mask, first, second, gre, gim):
    weight = mask.astype(F32)
    rows, channels = gre.shape
    shaped = (STATIONS, SOURCE_COUNT, channels)
    full_re = lax.all_gather(gre, "bl", axis=0, tiled=True).reshape(shaped)
    full_im = lax.all_gather(gim, "bl", axis=0, tiled=True).reshape(shaped)
    for step in range(ITERS):
        unused, sums = block_pass(full_re, full_im, vis, model, weight, first, second, True)
        totals = lax.psum(sums, "bl")
        denom = totals[2] + ridge
        full_re = 0.5 * (full_re + totals[0] / denom)
        full_im = 0.5 * (full_im + totals[1] / denom)
    residual, unused = block_pass(full_re, full_im, vis, model, weight, first, second, False)
    both = jnp.stack([full_re, full_im]).reshape(2, STATIONS * SOURCE_COUNT, channels)
    return lax.dynamic_slice_in_dim(both, lax.axis_index("bl") * rows, rows, 1), residual


def solution(mesh):
    n = mesh.shape["bl"]
    split = n % 2 == 0 and SOURCE_COUNT % (n // 2) == 0 and STATIONS == 4 * n

    def body(vis, model, mask, first, second, gre, gim):
        if split and mask.shape[0] <= ROWS:
            return fast_body(n, vis, model, mask, first, second, gre, gim)
        return plain_body(vis, model, mask, first, second, gre, gim)

    in_specs = (
        P(None, ("grp", "bl"), None, None),
        P(None, None, ("grp", "bl"), None, None),
        P(("grp", "bl"), None, None),
        P(("grp", "bl")),
        P(("grp", "bl")),
        P(("grp", "bl"), None),
        P(("grp", "bl"), None),
    )
    out_specs = (P(None, ("grp", "bl"), None), P(None, ("grp", "bl"), None, None))
    return jax.shard_map(body, mesh=mesh, in_specs=in_specs, out_specs=out_specs, check_vma=False)
```

```python
import functools

import jax
import jax.numpy as jnp
from jax import lax
from jax.experimental import pallas as pl
from jax.experimental.pallas import tpu as pltpu
from jax.sharding import PartitionSpec as P

STATIONS = 64
SOURCE_COUNT = 40
ITERS = 2
ROWS = 16

ridge = 1.0
F32 = jnp.float32
BF16 = jnp.bfloat16
VMEM_LIMIT = 16 * 1024 * 1024


def swap(x):
    return pltpu.roll(x, x.shape[-1] // 2, axis=x.ndim - 1)


def lower(shape):
    return lax.broadcasted_iota(jnp.int32, shape, len(shape) - 1) < shape[-1] // 2


def cross(a, b):
    lo = lower(a.shape)
    return jnp.where(lo, a, swap(b)), jnp.where(lo, swap(a), b)


def three(x):
    hi = x.astype(BF16)
    rest = x - hi.astype(F32)
    mid = rest.astype(BF16)
    return hi, mid, (rest - mid.astype(F32)).astype(BF16)


def pick(onehot, x, dims):
    return sum(
        lax.dot_general(onehot, part, (dims, ((), ())), preferred_element_type=F32)
        for part in three(x)
    )


def pack_kernel(n, dpc, first_ref, second_ref, re_ref, im_ref, out_ref):
    rows = re_ref.shape[0]
    out_ref[:rows] = re_ref[...]
    out_ref[rows : 2 * rows] = im_ref[...]
    lane = lax.broadcasted_iota(jnp.int32, (8, 128), 1)
    marks = jnp.zeros((8, 128), F32)
    for r in range(first_ref.shape[0]):
        marks = jnp.where(lane == r, (first_ref[r] + 1).astype(F32), marks)
        marks = jnp.where(lane == ROWS + r, (second_ref[r] + 1).astype(F32), marks)
    out_ref[2 * rows :] = marks


def power_kernel(n, dpc, model_ref, mask_ref, local):
    local[...] = jnp.zeros_like(local)

    def pair(b, carry):
        weight = mask_ref[b].astype(F32)
        for d in range(SOURCE_COUNT):
            mr = model_ref[d, 0, b].astype(F32)
            mi = model_ref[d, 1, b].astype(F32)
            local[d, pl.ds(b, 1), :] = jnp.sum(weight * (mr * mr + mi * mi), axis=0, keepdims=True)
        return carry

    lax.fori_loop(0, mask_ref.shape[0], pair, 0)


def wide(ref):
    return jnp.concatenate([ref[dd] for dd in range(ref.shape[0])], axis=1)


def first_own_kernel(n, dpc, me_ref, *rest):
    ins, (g_ref, onehot_ref, sel_ref, lines) = rest[:n], rest[n:]
    me = me_ref[0]
    k, c = lax.div(me, 2), lax.rem(me, 2)
    per = STATIONS // n
    rows = per * SOURCE_COUNT
    for o in range(n):
        peer = jnp.bitwise_xor(me, o)
        lines[pl.ds(peer, 1), :] = ins[o][2 * rows : 2 * rows + 1, :]
        for s in range(per):
            for dd in range(dpc):
                at = s * SOURCE_COUNT + k * dpc + dd
                x0, x1 = cross(ins[o][pl.ds(at, 1), :], ins[o][pl.ds(rows + at, 1), :])
                g_ref[dd, pl.ds(peer * per + s, 1), :] = jnp.where(c == 0, x0, x1)
    across = 128 // (2 * ROWS)
    station = lax.broadcasted_iota(jnp.int32, (STATIONS, 128), 0)
    for group in range(n // across):
        marks = jnp.zeros((1, 128), F32)
        for i in range(across):
            row = lines[group * across + i : group * across + i + 1, :]
            marks = marks + (pltpu.roll(row, i * 2 * ROWS, axis=1) if i else row)
        hit = station + 1 == marks.astype(jnp.int32)
        onehot_ref[:, group * 128 : (group + 1) * 128] = jnp.where(hit, 1.0, 0.0).astype(BF16)
    sel_ref[...] = pick(onehot_ref[...], wide(g_ref), ((0,), (0,)))


def power_rows(sums, o, cols):
    lo8 = lower((8, 128))
    W = sums[o, ROWS:, cols]
    Wx = swap(W)
    return jnp.concatenate([jnp.where(lo8, W, Wx), jnp.where(lo8, Wx, W)], 0)


def fill_powers(n, dpc, sums, sel_ref, terms, base):
    for o in range(n):
        r = o * 2 * ROWS
        for dd in range(dpc):
            cols = slice(dd * 128, (dd + 1) * 128)
            dcols = slice(base + dd * 128, base + (dd + 1) * 128)
            W = power_rows(sums, o, cols)
            p = sel_ref[r : r + ROWS, cols]
            q = sel_ref[r + ROWS : r + 2 * ROWS, cols]
            p2, q2 = p * p, q * q
            terms[r : r + ROWS, dcols] = W * (q2 + swap(q2))
            terms[r + ROWS : r + 2 * ROWS, dcols] = W * (p2 + swap(p2))


def fill_sums(n, dpc, sums, sel_ref, terms):
    lo = lower((ROWS, 128))
    sign = jnp.where(lo, -1.0, 1.0)
    for o in range(n):
        r = o * 2 * ROWS
        for dd in range(dpc):
            cols = slice(dd * 128, (dd + 1) * 128)
            B = sums[o, :ROWS, cols]
            p = sel_ref[r : r + ROWS, cols]
            q = sel_ref[r + ROWS : r + 2 * ROWS, cols]
            Bx = swap(B)
            Brr, Bii = jnp.where(lo, B, Bx), jnp.where(lo, Bx, B)
            terms[r : r + ROWS, cols] = Brr * q + sign * Bii * swap(q)
            terms[r + ROWS : r + 2 * ROWS, cols] = Brr * p - sign * Bii * swap(p)


def own_kernel(n, dpc, g_in, onehot_ref, sel_ref, sums, g_out, terms):
    width = dpc * 128
    fill_sums(n, dpc, sums, sel_ref, terms)
    fill_powers(n, dpc, sums, sel_ref, terms, width)
    total = pick(onehot_ref[...], terms[...], ((1,), (0,)))
    step = total[:, :width] / (total[:, width:] + ridge)
    for dd in range(dpc):
        g_out[dd] = 0.5 * (g_in[dd] + step[:, dd * 128 : (dd + 1) * 128])


def prepare_kernel(n, dpc, g_ref, onehot_ref, sums, sel_ref, den_ref, terms):
    sel_ref[...] = pick(onehot_ref[...], wide(g_ref), ((0,), (0,)))
    fill_powers(n, dpc, sums, sel_ref, terms, 0)
    den_ref[...] = pick(onehot_ref[...], terms[...], ((1,), (0,))) + ridge


def later_own_kernel(n, dpc, g_in, onehot_ref, sel_ref, den_ref, sums, g_out, terms):
    fill_sums(n, dpc, sums, sel_ref, terms)
    total = pick(onehot_ref[...], terms[...], ((1,), (0,)))
    step = total / den_ref[...]
    for dd in range(dpc):
        g_out[dd] = 0.5 * (g_in[dd] + step[:, dd * 128 : (dd + 1) * 128])


def products_first(n, dpc, me, first_ref, second_ref, ins, hre, him, stack):
    per = STATIONS // n
    rows = per * SOURCE_COUNT
    for o in range(n):
        stack[jnp.bitwise_xor(me, o)] = ins[o][: 2 * rows, :]

    def block(station, part):
        at = lax.rem(station, per) * SOURCE_COUNT + part * rows
        return stack[lax.div(station, per), pl.ds(pl.multiple_of(at, 8), SOURCE_COUNT), :]

    def pair(b, carry):
        p, q = first_ref[b], second_ref[b]
        pr, pi, qr, qi = block(p, 0), block(p, 1), block(q, 0), block(q, 1)
        re, im = pr * qr + pi * qi, pi * qr - pr * qi
        for d in range(SOURCE_COUNT):
            hre[d, pl.ds(b, 1), :] = re[d : d + 1]
            him[d, pl.ds(b, 1), :] = im[d : d + 1]
        return carry

    lax.fori_loop(0, first_ref.shape[0], pair, 0)


def products(n, dpc, me, first_ref, second_ref, ins, hre, him, gp, gq):
    def pair(b, carry):
        p, q = first_ref[b], second_ref[b]
        for o in range(n):
            for dd in range(dpc):
                gp[o * dpc + dd, pl.ds(b, 1), :] = ins[o][dd, pl.ds(p, 1), :]
                gq[o * dpc + dd, pl.ds(b, 1), :] = ins[o][dd, pl.ds(q, 1), :]
        return carry

    lax.fori_loop(0, first_ref.shape[0], pair, 0)
    even = lax.rem(me, 2) == 0
    for m in range(n // 2):
        k = lax.div(jnp.bitwise_xor(me, 2 * m), 2)
        for dd in range(dpc):
            a, b = 2 * m * dpc + dd, (2 * m + 1) * dpc + dd
            pr, pi = cross(jnp.where(even, gp[a], gp[b]), jnp.where(even, gp[b], gp[a]))
            qr, qi = cross(jnp.where(even, gq[a], gq[b]), jnp.where(even, gq[b], gq[a]))
            hre[k * dpc + dd] = pr * qr + pi * qi
            him[k * dpc + dd] = pi * qr - pr * qi


def predict(b, model_ref, vis_ref, mask_ref, hre, him):
    def step(i, acc):
        acc_re, acc_im = acc
        for u in range(8):
            d = i * 8 + u
            mr = model_ref[d, 0, b].astype(F32)
            mi = model_ref[d, 1, b].astype(F32)
            hr = hre[d, pl.ds(b, 1), :]
            hi = him[d, pl.ds(b, 1), :]
            acc_re = acc_re - (hr * mr - hi * mi)
            acc_im = acc_im - (hr * mi + hi * mr)
        return acc_re, acc_im

    acc = lax.fori_loop(0, SOURCE_COUNT // 8, step, (vis_ref[0, b], vis_ref[1, b]))
    weight = mask_ref[b].astype(F32)
    return weight * acc[0], weight * acc[1]


def pass_kernel(n, dpc, start, me_ref, first_ref, second_ref, model_ref, vis_ref, mask_ref, power_ref, *rest):
    ins, (out_ref, hre, him, cre, cim), work = rest[:n], rest[n : n + 5], rest[n + 5 :]
    build = products_first if start else products
    build(n, dpc, me_ref[0], first_ref, second_ref, ins, hre, him, *work)
    cre[...] = jnp.zeros_like(cre)
    cim[...] = jnp.zeros_like(cim)

    def pair(b, carry):
        res_re, res_im = predict(b, model_ref, vis_ref, mask_ref, hre, him)

        def step(i, carry):
            for u in range(8):
                d = i * 8 + u
                mr = model_ref[d, 0, b].astype(F32)
                mi = model_ref[d, 1, b].astype(F32)
                cre[d, pl.ds(b, 1), :] = jnp.sum(mr * res_re + mi * res_im, axis=0, keepdims=True)
                cim[d, pl.ds(b, 1), :] = jnp.sum(mr * res_im - mi * res_re, axis=0, keepdims=True)
            return carry

        return lax.fori_loop(0, SOURCE_COUNT // 8, step, carry)

    lax.fori_loop(0, mask_ref.shape[0], pair, 0)
    pairs = mask_ref.shape[0]
    real = lax.broadcasted_iota(jnp.int32, (ROWS, 128), 0) < pairs
    for k in range(n // 2):
        for dd in range(dpc):
            d = k * dpc + dd
            cols = slice(dd * 128, (dd + 1) * 128)
            w = power_ref[d]
            re = jnp.where(real, cre[d] + hre[d] * w, 0.0)
            im = jnp.where(real, cim[d] + him[d] * w, 0.0)
            out_ref[2 * k, :ROWS, cols], out_ref[2 * k + 1, :ROWS, cols] = cross(re, im)
            if start:
                out_ref[2 * k, ROWS:, cols], out_ref[2 * k + 1, ROWS:, cols] = cross(w[:8], w[8:])


def last_kernel(n, dpc, me_ref, first_ref, second_ref, model_ref, vis_ref, mask_ref, *rest):
    ins, (res_ref, gains_ref, hre, him), work = rest[:n], rest[n : n + 4], rest[n + 4 :]
    me = me_ref[0]
    per = STATIONS // n
    even = lax.rem(me, 2) == 0
    for m in range(n // 2):
        k = lax.div(jnp.bitwise_xor(me, 2 * m), 2)
        for dd in range(dpc):
            for s in range(per):
                a = ins[2 * m][dd, pl.ds(me * per + s, 1), :]
                b = ins[2 * m + 1][dd, pl.ds(me * per + s, 1), :]
                re, im = cross(jnp.where(even, a, b), jnp.where(even, b, a))
                at = s * SOURCE_COUNT + k * dpc + dd
                gains_ref[0, pl.ds(at, 1), :] = re
                gains_ref[1, pl.ds(at, 1), :] = im
    products(n, dpc, me, first_ref, second_ref, ins, hre, him, *work)

    def pair(b, carry):
        res_re, res_im = predict(b, model_ref, vis_ref, mask_ref, hre, him)
        res_ref[0, b] = res_re
        res_ref[1, b] = res_im
        return carry

    lax.fori_loop(0, mask_ref.shape[0], pair, 0)


SMEM = pl.BlockSpec(memory_space=pltpu.SMEM)
VMEM = pl.BlockSpec(memory_space=pltpu.VMEM)


def shape(*dims, dtype=F32):
    return jax.ShapeDtypeStruct(dims, dtype)


def exchange(x):
    return lax.all_to_all(x, "bl", split_axis=0, concat_axis=0, tiled=True)


def gather(n, piece):
    def send(x, o):
        return lax.ppermute(x, "bl", [(i, i ^ o) for i in range(n)])

    got = {0: piece}
    got[4], got[12] = send(piece, 4), send(piece, 12)
    got[2] = send(piece, 2)
    got[8] = send(got[12], 4)
    for o in (4, 12, 8):
        got[o + 2] = send(got[o], 2)
    for o in (0, 2, 4, 12, 6, 14, 8, 10):
        got[o + 1] = send(got[o], 1)
    return [got[o] for o in range(n)]


def fast_body(n, vis, model, mask, first, second, gre, gim):
    dpc = SOURCE_COUNT // (n // 2)
    width = dpc * 128
    pairs, times, channels = mask.shape
    me = lax.axis_index("bl").astype(jnp.int32).reshape(1)
    params = pltpu.CompilerParams(vmem_limit_bytes=VMEM_LIMIT)
    plane = (SOURCE_COUNT, ROWS, channels)
    picked = (n * dpc, ROWS, channels)
    lots = n * 2 * ROWS
    mine = (dpc, STATIONS, channels)

    def call(kernel, args, outs, scratch=()):
        return pl.pallas_call(
            functools.partial(kernel, n, dpc),
            in_specs=[SMEM if x.ndim == 1 else VMEM for x in args],
            out_specs=[VMEM for o in outs],
            out_shape=outs,
            scratch_shapes=[pltpu.VMEM(x, F32) for x in scratch],
            compiler_params=params,
        )(*args)

    (piece,) = call(pack_kernel, (first, second, gre, gim), [shape(2 * gre.shape[0] + 8, channels)])
    got = gather(n, piece)
    (power,) = call(power_kernel, (model, mask), [shape(*plane)])
    g, onehot, sel = call(
        first_own_kernel,
        (me, *got),
        [shape(*mine), shape(STATIONS, lots, dtype=BF16), shape(lots, width)],
        [(n, channels)],
    )
    for step in range(ITERS):
        start = step == 0
        work = [(n, 2 * gre.shape[0], channels)] if start else [picked] * 2
        (sums,) = call(
            lambda n, dpc, *refs: pass_kernel(n, dpc, start, *refs),
            (me, first, second, model, vis, mask, power, *got),
            [shape(n, ROWS + (8 if start else 0), width)],
            [plane] * 4 + work,
        )
        sums = exchange(sums)
        if start:
            powers = sums
            (g,) = call(
                own_kernel, (g, onehot, sel, sums), [shape(*mine)], [(lots, 2 * width)]
            )
        else:
            (g,) = call(
                later_own_kernel, (g, onehot, sel, den, sums), [shape(*mine)], [(lots, width)]
            )
        got = gather(n, g)
        if step < ITERS - 1:
            sel, den = call(
                prepare_kernel,
                (g, onehot, powers),
                [shape(lots, width), shape(STATIONS, width)],
                [(lots, width)],
            )
    residual, gains = call(
        last_kernel,
        (me, first, second, model, vis, mask, *got),
        [shape(*vis.shape), shape(2, *gre.shape)],
        [plane] * 2 + [picked] * 2,
    )
    return gains, residual


def block_pass(full_re, full_im, vis_blk, coh_blk, weight, first, second, want_sums):
    ar = jnp.transpose(full_re[first], (1, 0, 2))
    ai = jnp.transpose(full_im[first], (1, 0, 2))
    br = jnp.transpose(full_re[second], (1, 0, 2))
    bi = jnp.transpose(full_im[second], (1, 0, 2))
    mr = coh_blk[:, 0].astype(F32)
    mi = coh_blk[:, 1].astype(F32)
    hr = ar * br + ai * bi
    hi = ai * br - ar * bi
    hr_t, hi_t = hr[:, :, None], hi[:, :, None]
    res_re = weight * (vis_blk[0] - jnp.sum(hr_t * mr - hi_t * mi, 0))
    res_im = weight * (vis_blk[1] - jnp.sum(hr_t * mi + hi_t * mr, 0))
    residual = jnp.stack([res_re, res_im])
    if not want_sums:
        return (residual, None)
    power = jnp.sum(weight[None] * (mr * mr + mi * mi), 2)
    sum_re = jnp.sum(mr * res_re + mi * res_im, 2) + hr * power
    sum_im = jnp.sum(mr * res_im - mi * res_re, 2) + hi * power
    terms_first = jnp.stack([br * sum_re - bi * sum_im, br * sum_im + bi * sum_re, power * (br * br + bi * bi)])
    terms_second = jnp.stack([ar * sum_re + ai * sum_im, ai * sum_re - ar * sum_im, power * (ar * ar + ai * ai)])
    stations = jnp.arange(STATIONS, dtype=jnp.int32)
    onehot_first = (first[:, None] == stations[None, :]).astype(F32)
    onehot_second = (second[:, None] == stations[None, :]).astype(F32)
    exact = lax.Precision.HIGHEST
    sums = jnp.einsum("bs,cdbf->csdf", onehot_first, terms_first, precision=exact)
    sums = sums + jnp.einsum("bs,cdbf->csdf", onehot_second, terms_second, precision=exact)
    return (residual, sums)


def plain_body(vis, model, mask, first, second, gre, gim):
    weight = mask.astype(F32)
    rows, channels = gre.shape
    shaped = (STATIONS, SOURCE_COUNT, channels)
    full_re = lax.all_gather(gre, "bl", axis=0, tiled=True).reshape(shaped)
    full_im = lax.all_gather(gim, "bl", axis=0, tiled=True).reshape(shaped)
    for step in range(ITERS):
        unused, sums = block_pass(full_re, full_im, vis, model, weight, first, second, True)
        totals = lax.psum(sums, "bl")
        denom = totals[2] + ridge
        full_re = 0.5 * (full_re + totals[0] / denom)
        full_im = 0.5 * (full_im + totals[1] / denom)
    residual, unused = block_pass(full_re, full_im, vis, model, weight, first, second, False)
    both = jnp.stack([full_re, full_im]).reshape(2, STATIONS * SOURCE_COUNT, channels)
    return lax.dynamic_slice_in_dim(both, lax.axis_index("bl") * rows, rows, 1), residual


def solution(mesh):
    n = mesh.shape["bl"]
    split = n == 16

    def body(vis, model, mask, first, second, gre, gim):
        if split and mask.shape[0] <= ROWS:
            return fast_body(n, vis, model, mask, first, second, gre, gim)
        return plain_body(vis, model, mask, first, second, gre, gim)

    in_specs = (
        P(None, ("grp", "bl"), None, None),
        P(None, None, ("grp", "bl"), None, None),
        P(("grp", "bl"), None, None),
        P(("grp", "bl")),
        P(("grp", "bl")),
        P(("grp", "bl"), None),
        P(("grp", "bl"), None),
    )
    out_specs = (P(None, ("grp", "bl"), None), P(None, ("grp", "bl"), None, None))
    return jax.shard_map(body, mesh=mesh, in_specs=in_specs, out_specs=out_specs, check_vma=False)
```

```python
import functools

import jax
import jax.numpy as jnp
from jax import lax
from jax.experimental import pallas as pl
from jax.experimental.pallas import tpu as pltpu
from jax.sharding import PartitionSpec as P

STATIONS = 64
SOURCE_COUNT = 40
ITERS = 2
ROWS = 16

ridge = 1.0
F32 = jnp.float32
BF16 = jnp.bfloat16
VMEM_LIMIT = 24 * 1024 * 1024


def swap(x):
    return pltpu.roll(x, x.shape[-1] // 2, axis=x.ndim - 1)


def lower(shape):
    return lax.broadcasted_iota(jnp.int32, shape, len(shape) - 1) < shape[-1] // 2


def cross(a, b):
    lo = lower(a.shape)
    return jnp.where(lo, a, swap(b)), jnp.where(lo, swap(a), b)


def three(x):
    hi = x.astype(BF16)
    rest = x - hi.astype(F32)
    mid = rest.astype(BF16)
    return hi, mid, (rest - mid.astype(F32)).astype(BF16)


def pick(onehot, x, dims):
    return sum(
        lax.dot_general(onehot, part, (dims, ((), ())), preferred_element_type=F32)
        for part in three(x)
    )


TILE = 8


def pack_kernel(n, dpc, first_ref, second_ref, re_ref, im_ref, out_ref, sems):
    rows = re_ref.shape[0]
    copies = [
        pltpu.make_async_copy(re_ref, out_ref.at[pl.ds(0, rows)], sems.at[0]),
        pltpu.make_async_copy(im_ref, out_ref.at[pl.ds(rows, rows)], sems.at[1]),
    ]
    for copy in copies:
        copy.start()
    lane = lax.broadcasted_iota(jnp.int32, (TILE, 128), 1)
    marks = jnp.zeros((TILE, 128), F32)
    for r in range(first_ref.shape[0]):
        marks = jnp.where(lane == r, (first_ref[r] + 1).astype(F32), marks)
        marks = jnp.where(lane == ROWS + r, (second_ref[r] + 1).astype(F32), marks)
    out_ref[2 * rows :] = marks
    for copy in copies:
        copy.wait()


class Fetch:
    def __init__(self, model, held, sems):
        pairs = held.shape[2]
        parts = 3 if pairs % 3 == 0 else 1
        self.size = pairs // parts
        self.copies = []
        for i in range(parts):
            part = pl.ds(i * self.size, self.size)
            self.copies.append(
                pltpu.make_async_copy(model.at[:, :, part], held.at[:, :, part], sems.at[i])
            )
        for copy in self.copies:
            copy.start()

    def each(self, body):
        for i, copy in enumerate(self.copies):
            copy.wait()
            lax.fori_loop(i * self.size, (i + 1) * self.size, body, 0)


def power_kernel(n, dpc, model_hbm, mask_ref, unused_in, out_ref, unused_out, model_ref, sems):
    fetch = Fetch(model_hbm, model_ref, sems)
    out_ref[...] = jnp.zeros_like(out_ref)

    def pair(b, carry):
        weight = mask_ref[b].astype(F32)
        for d in range(SOURCE_COUNT):
            mr = model_ref[d, 0, b].astype(F32)
            mi = model_ref[d, 1, b].astype(F32)
            row = d // dpc * TILE + d % dpc
            out_ref[b, row : row + 1, :] = jnp.sum(weight * (mr * mr + mi * mi), axis=0, keepdims=True)
        return carry

    fetch.each(pair)


def wide(ref, dpc):
    return jnp.concatenate([ref[pl.ds(dd, STATIONS, stride=dpc), :] for dd in range(dpc)], axis=1)


def put(ref, value, dpc):
    for dd in range(dpc):
        ref[pl.ds(dd, STATIONS, stride=dpc), :] = value[:, dd * 128 : (dd + 1) * 128]
    ref[STATIONS * dpc :, :] = jnp.zeros((TILE, 128), F32)


def first_own_kernel(n, dpc, me_ref, *rest):
    ins, (g_ref, onehot_ref, sel_ref, split, lines) = rest[:n], rest[n:]
    me = me_ref[0]
    k, c = lax.div(me, 2), lax.rem(me, 2)
    per = STATIONS // n
    rows = per * SOURCE_COUNT
    for o in range(n):
        peer = jnp.bitwise_xor(me, o)
        lines[pl.ds(peer, 1), :] = ins[o][2 * rows : 2 * rows + 1, :]
        for s in range(per):
            at = s * SOURCE_COUNT + k * dpc
            x0, x1 = cross(ins[o][pl.ds(at, TILE), :], ins[o][pl.ds(rows + at, TILE), :])
            to = pl.multiple_of((peer * per + s) * TILE, TILE)
            split[pl.ds(to, TILE), :] = jnp.where(c == 0, x0, x1)
    g = jnp.concatenate([split[pl.ds(dd, STATIONS, stride=TILE), :] for dd in range(dpc)], axis=1)
    put(g_ref, g, dpc)
    across = 128 // (2 * ROWS)
    station = lax.broadcasted_iota(jnp.int32, (STATIONS, 128), 0)
    for group in range(n // across):
        marks = jnp.zeros((1, 128), F32)
        for i in range(across):
            row = lines[group * across + i : group * across + i + 1, :]
            marks = marks + (pltpu.roll(row, i * 2 * ROWS, axis=1) if i else row)
        hit = station + 1 == marks.astype(jnp.int32)
        onehot_ref[:, group * 128 : (group + 1) * 128] = jnp.where(hit, 1.0, 0.0).astype(BF16)
    sel_ref[...] = pick(onehot_ref[...], g, ((0,), (0,)))


def fill_powers(n, dpc, sums, sel_ref, terms, base):
    lo = lower((TILE, 128))
    for o in range(n):
        r = o * 2 * ROWS
        for dd in range(dpc):
            cols = slice(dd * 128, (dd + 1) * 128)
            dcols = slice(base + dd * 128, base + (dd + 1) * 128)
            W = sums[o, pl.ds(ROWS * dpc + dd, TILE, stride=dpc), :]
            Wx = swap(W)
            W = jnp.concatenate([jnp.where(lo, W, Wx), jnp.where(lo, Wx, W)], 0)
            p = sel_ref[r : r + ROWS, cols]
            q = sel_ref[r + ROWS : r + 2 * ROWS, cols]
            p2, q2 = p * p, q * q
            terms[r : r + ROWS, dcols] = W * (q2 + swap(q2))
            terms[r + ROWS : r + 2 * ROWS, dcols] = W * (p2 + swap(p2))


def fill_sums(n, dpc, sums, sel_ref, terms):
    lo = lower((ROWS, 128))
    sign = jnp.where(lo, -1.0, 1.0)
    for o in range(n):
        r = o * 2 * ROWS
        for dd in range(dpc):
            cols = slice(dd * 128, (dd + 1) * 128)
            B = sums[o, pl.ds(dd, ROWS, stride=dpc), :]
            p = sel_ref[r : r + ROWS, cols]
            q = sel_ref[r + ROWS : r + 2 * ROWS, cols]
            Bx = swap(B)
            Brr, Bii = jnp.where(lo, B, Bx), sign * jnp.where(lo, Bx, B)
            terms[r : r + ROWS, cols] = Brr * q + Bii * swap(q)
            terms[r + ROWS : r + 2 * ROWS, cols] = Brr * p - Bii * swap(p)


def own_kernel(n, dpc, g_in, onehot_ref, sel_ref, sums, g_out, terms):
    width = dpc * 128
    fill_sums(n, dpc, sums, sel_ref, terms)
    fill_powers(n, dpc, sums, sel_ref, terms, width)
    total = pick(onehot_ref[...], terms[...], ((1,), (0,)))
    put(g_out, 0.5 * (wide(g_in, dpc) + total[:, :width] / (total[:, width:] + ridge)), dpc)


def prepare_kernel(n, dpc, g_ref, onehot_ref, sums, sel_ref, den_ref, terms):
    sel_ref[...] = pick(onehot_ref[...], wide(g_ref, dpc), ((0,), (0,)))
    fill_powers(n, dpc, sums, sel_ref, terms, 0)
    den_ref[...] = pick(onehot_ref[...], terms[...], ((1,), (0,))) + ridge


def later_own_kernel(n, dpc, g_in, onehot_ref, sel_ref, den_ref, sums, g_out, terms):
    fill_sums(n, dpc, sums, sel_ref, terms)
    total = pick(onehot_ref[...], terms[...], ((1,), (0,)))
    put(g_out, 0.5 * (wide(g_in, dpc) + total / den_ref[...]), dpc)


def products_first(n, dpc, me, first_ref, second_ref, ins, hre, him, stack):
    per = STATIONS // n
    rows = per * SOURCE_COUNT
    for o in range(n):
        stack[jnp.bitwise_xor(me, o)] = ins[o][...]

    def pair(b, carry):
        p, q = first_ref[b], second_ref[b]

        def block(station, k, part):
            at = lax.rem(station, per) * SOURCE_COUNT + k * dpc + part * rows
            return stack[lax.div(station, per), pl.ds(at, TILE), :]

        for k in range(n // 2):
            pr, pi, qr, qi = block(p, k, 0), block(p, k, 1), block(q, k, 0), block(q, k, 1)
            hre[b, k * TILE : (k + 1) * TILE, :] = pr * qr + pi * qi
            him[b, k * TILE : (k + 1) * TILE, :] = pi * qr - pr * qi
        return carry

    lax.fori_loop(0, first_ref.shape[0], pair, 0)


def piece_pair(dpc, even, ins, m, station):
    a = ins[2 * m][pl.ds(station * dpc, TILE), :]
    b = ins[2 * m + 1][pl.ds(station * dpc, TILE), :]
    return cross(jnp.where(even, a, b), jnp.where(even, b, a))


def products(n, dpc, me, first_ref, second_ref, ins, hre, him):
    even = lax.rem(me, 2) == 0

    def pair(b, carry):
        p, q = first_ref[b], second_ref[b]
        for m in range(n // 2):
            k = lax.div(jnp.bitwise_xor(me, 2 * m), 2)
            pr, pi = piece_pair(dpc, even, ins, m, p)
            qr, qi = piece_pair(dpc, even, ins, m, q)
            rows = pl.ds(pl.multiple_of(k * TILE, TILE), TILE)
            hre[b, rows, :] = pr * qr + pi * qi
            him[b, rows, :] = pi * qr - pr * qi
        return carry

    lax.fori_loop(0, first_ref.shape[0], pair, 0)


def predict(n, dpc, b, model_ref, vis_ref, mask_ref, hre, him):
    def step(k, acc):
        acc_re, acc_im = acc
        for dd in range(dpc):
            mr = model_ref[k * dpc + dd, 0, b].astype(F32)
            mi = model_ref[k * dpc + dd, 1, b].astype(F32)
            hr = hre[b, pl.ds(k * TILE + dd, 1), :]
            hi = him[b, pl.ds(k * TILE + dd, 1), :]
            acc_re = acc_re - (hr * mr - hi * mi)
            acc_im = acc_im - (hr * mi + hi * mr)
        return acc_re, acc_im

    acc = lax.fori_loop(0, n // 2, step, (vis_ref[0, b], vis_ref[1, b]))
    weight = mask_ref[b].astype(F32)
    return weight * acc[0], weight * acc[1]


def pass_kernel(
    n, dpc, start, me_ref, first_ref, second_ref, model_hbm, vis_ref, mask_ref, power_ref, *rest
):
    ins, (out_ref, model_ref, sems, hre, him, cre, cim), work = rest[:n], rest[n : n + 7], rest[n + 7 :]
    fetch = Fetch(model_hbm, model_ref, sems)
    build = products_first if start else products
    build(n, dpc, me_ref[0], first_ref, second_ref, ins, hre, him, *work)

    def pair(b, carry):
        res_re, res_im = predict(n, dpc, b, model_ref, vis_ref, mask_ref, hre, him)

        def step(k, carry):
            for dd in range(dpc):
                mr = model_ref[k * dpc + dd, 0, b].astype(F32)
                mi = model_ref[k * dpc + dd, 1, b].astype(F32)
                row = pl.ds(k * TILE + dd, 1)
                cre[b, row, :] = jnp.sum(mr * res_re + mi * res_im, axis=0, keepdims=True)
                cim[b, row, :] = jnp.sum(mr * res_im - mi * res_re, axis=0, keepdims=True)
            return carry

        return lax.fori_loop(0, n // 2, step, carry)

    fetch.each(pair)
    pairs = mask_ref.shape[0]
    for k in range(n // 2):
        tile = slice(k * TILE, (k + 1) * TILE)
        for b in range(pairs):
            w = power_ref[b, tile, :]
            x0, x1 = cross(cre[b, tile, :] + hre[b, tile, :] * w, cim[b, tile, :] + him[b, tile, :] * w)
            out_ref[2 * k, b * dpc : (b + 1) * dpc, :] = x0[:dpc]
            out_ref[2 * k + 1, b * dpc : (b + 1) * dpc, :] = x1[:dpc]
        if pairs < ROWS:
            empty = jnp.zeros(((ROWS - pairs) * dpc, 128), F32)
            out_ref[2 * k, pairs * dpc : ROWS * dpc, :] = empty
            out_ref[2 * k + 1, pairs * dpc : ROWS * dpc, :] = empty
        if start:
            for r in range(TILE):
                x0, x1 = cross(power_ref[r, tile, :], power_ref[r + TILE, tile, :])
                to = (ROWS + r) * dpc
                out_ref[2 * k, to : to + dpc, :] = x0[:dpc]
                out_ref[2 * k + 1, to : to + dpc, :] = x1[:dpc]


def last_kernel(n, dpc, me_ref, first_ref, second_ref, model_hbm, vis_ref, mask_ref, *rest):
    ins, (res_ref, gains_ref, model_ref, sems, hre, him) = rest[:n], rest[n:]
    fetch = Fetch(model_hbm, model_ref, sems)
    me = me_ref[0]
    per = STATIONS // n
    even = lax.rem(me, 2) == 0
    for m in range(n // 2):
        k = lax.div(jnp.bitwise_xor(me, 2 * m), 2)
        for s in range(per):
            re, im = piece_pair(dpc, even, ins, m, me * per + s)
            for dd in range(dpc):
                at = s * SOURCE_COUNT + k * dpc + dd
                gains_ref[0, pl.ds(at, 1), :] = re[dd : dd + 1]
                gains_ref[1, pl.ds(at, 1), :] = im[dd : dd + 1]
    products(n, dpc, me, first_ref, second_ref, ins, hre, him)

    def pair(b, carry):
        res_re, res_im = predict(n, dpc, b, model_ref, vis_ref, mask_ref, hre, him)
        res_ref[0, b] = res_re
        res_ref[1, b] = res_im
        return carry

    fetch.each(pair)


SMEM = pl.BlockSpec(memory_space=pltpu.SMEM)
VMEM = pl.BlockSpec(memory_space=pltpu.VMEM)
HBM = pl.BlockSpec(memory_space=pltpu.HBM)


def shape(*dims, dtype=F32):
    return jax.ShapeDtypeStruct(dims, dtype)


def exchange(x):
    return lax.all_to_all(x, "bl", split_axis=0, concat_axis=0, tiled=True)


def gather(n, piece, beside=lambda x: x):
    def send(x, o):
        return lax.ppermute(x, "bl", [(i, i ^ o) for i in range(n)])

    got = {0: piece}
    got[4], got[12] = send(piece, 4), send(piece, 12)
    got[2] = send(piece, 2)
    got[4] = beside(got[4])
    got[8] = send(got[12], 4)
    for o in (4, 12, 8):
        got[o + 2] = send(got[o], 2)
    for o in (0, 2, 4, 12, 6, 14, 8, 10):
        got[o + 1] = send(got[o], 1)
    return [got[o] for o in range(n)]


def fast_body(n, vis, model, mask, first, second, gre, gim):
    model, gre, gim = (pltpu.with_memory_space_constraint(x, pltpu.HBM) for x in (model, gre, gim))
    dpc = SOURCE_COUNT // (n // 2)
    width = dpc * 128
    pairs, times, channels = mask.shape
    me = lax.axis_index("bl").astype(jnp.int32).reshape(1)
    params = pltpu.CompilerParams(vmem_limit_bytes=VMEM_LIMIT)
    plane = (ROWS, n // 2 * TILE, channels)
    lots = n * 2 * ROWS
    mine = (STATIONS * dpc + TILE, channels)
    held = [pltpu.VMEM(model.shape, BF16), pltpu.SemaphoreType.DMA((3,))]

    def call(kernel, args, outs, scratch=(), micros=1, aliases={}):
        def place(x):
            if x is model or x is gre or x is gim:
                return HBM
            return SMEM if x.ndim == 1 else VMEM

        return pl.pallas_call(
            functools.partial(kernel, n, dpc),
            in_specs=[place(x) for x in args],
            out_specs=[VMEM for o in outs],
            out_shape=outs,
            scratch_shapes=[pltpu.VMEM(x, F32) if isinstance(x, tuple) else x for x in scratch],
            compiler_params=params,
            input_output_aliases=aliases,
            cost_estimate=pl.CostEstimate(
                flops=0, bytes_accessed=int(micros * 3.69e6), transcendentals=0
            ),
        )(*args)

    (piece,) = call(
        pack_kernel,
        (first, second, gre, gim),
        [shape(2 * gre.shape[0] + TILE, channels)],
        [pltpu.SemaphoreType.DMA((2,))],
    )
    power = None

    def powers_beside(x):
        nonlocal power
        power, x = call(
            power_kernel, (model, mask, x), [shape(*plane), shape(*x.shape)], held, micros=6, aliases={2: 1}
        )
        return x

    got = gather(n, piece, powers_beside)
    g, onehot, sel = call(
        first_own_kernel,
        (me, *got),
        [shape(*mine), shape(STATIONS, lots, dtype=BF16), shape(lots, width)],
        [(STATIONS * TILE, channels), (n, channels)],
        micros=2,
    )
    for step in range(ITERS):
        start = step == 0
        work = [(n,) + piece.shape] if start else []
        (sums,) = call(
            lambda n, dpc, *refs: pass_kernel(n, dpc, start, *refs),
            (me, first, second, model, vis, mask, power, *got),
            [shape(n, (ROWS + (TILE if start else 0)) * dpc, channels)],
            held + [plane] * 4 + work,
            micros=9,
        )
        sums = exchange(sums)
        if start:
            powers = sums
            (g,) = call(own_kernel, (g, onehot, sel, sums), [shape(*mine)], [(lots, 2 * width)])
        else:
            (g,) = call(later_own_kernel, (g, onehot, sel, den, sums), [shape(*mine)], [(lots, width)])
        got = gather(n, g)
        if step < ITERS - 1:
            sel, den = call(
                prepare_kernel,
                (g, onehot, powers),
                [shape(lots, width), shape(STATIONS, width)],
                [(lots, width)],
                micros=2,
            )
    residual, gains = call(
        last_kernel,
        (me, first, second, model, vis, mask, *got),
        [shape(*vis.shape), shape(2, *gre.shape)],
        held + [plane] * 2,
        micros=6,
    )
    return gains, residual


def block_pass(full_re, full_im, vis_blk, coh_blk, weight, first, second, want_sums):
    ar = jnp.transpose(full_re[first], (1, 0, 2))
    ai = jnp.transpose(full_im[first], (1, 0, 2))
    br = jnp.transpose(full_re[second], (1, 0, 2))
    bi = jnp.transpose(full_im[second], (1, 0, 2))
    mr = coh_blk[:, 0].astype(F32)
    mi = coh_blk[:, 1].astype(F32)
    hr = ar * br + ai * bi
    hi = ai * br - ar * bi
    hr_t, hi_t = hr[:, :, None], hi[:, :, None]
    res_re = weight * (vis_blk[0] - jnp.sum(hr_t * mr - hi_t * mi, 0))
    res_im = weight * (vis_blk[1] - jnp.sum(hr_t * mi + hi_t * mr, 0))
    residual = jnp.stack([res_re, res_im])
    if not want_sums:
        return (residual, None)
    power = jnp.sum(weight[None] * (mr * mr + mi * mi), 2)
    sum_re = jnp.sum(mr * res_re + mi * res_im, 2) + hr * power
    sum_im = jnp.sum(mr * res_im - mi * res_re, 2) + hi * power
    terms_first = jnp.stack([br * sum_re - bi * sum_im, br * sum_im + bi * sum_re, power * (br * br + bi * bi)])
    terms_second = jnp.stack([ar * sum_re + ai * sum_im, ai * sum_re - ar * sum_im, power * (ar * ar + ai * ai)])
    stations = jnp.arange(STATIONS, dtype=jnp.int32)
    onehot_first = (first[:, None] == stations[None, :]).astype(F32)
    onehot_second = (second[:, None] == stations[None, :]).astype(F32)
    exact = lax.Precision.HIGHEST
    sums = jnp.einsum("bs,cdbf->csdf", onehot_first, terms_first, precision=exact)
    sums = sums + jnp.einsum("bs,cdbf->csdf", onehot_second, terms_second, precision=exact)
    return (residual, sums)


def plain_body(vis, model, mask, first, second, gre, gim):
    weight = mask.astype(F32)
    rows, channels = gre.shape
    shaped = (STATIONS, SOURCE_COUNT, channels)
    full_re = lax.all_gather(gre, "bl", axis=0, tiled=True).reshape(shaped)
    full_im = lax.all_gather(gim, "bl", axis=0, tiled=True).reshape(shaped)
    for step in range(ITERS):
        unused, sums = block_pass(full_re, full_im, vis, model, weight, first, second, True)
        totals = lax.psum(sums, "bl")
        denom = totals[2] + ridge
        full_re = 0.5 * (full_re + totals[0] / denom)
        full_im = 0.5 * (full_im + totals[1] / denom)
    residual, unused = block_pass(full_re, full_im, vis, model, weight, first, second, False)
    both = jnp.stack([full_re, full_im]).reshape(2, STATIONS * SOURCE_COUNT, channels)
    return lax.dynamic_slice_in_dim(both, lax.axis_index("bl") * rows, rows, 1), residual


def solution(mesh):
    n = mesh.shape["bl"]
    split = n == 16

    def body(vis, model, mask, first, second, gre, gim):
        if split and mask.shape[0] <= ROWS:
            return fast_body(n, vis, model, mask, first, second, gre, gim)
        return plain_body(vis, model, mask, first, second, gre, gim)

    in_specs = (
        P(None, ("grp", "bl"), None, None),
        P(None, None, ("grp", "bl"), None, None),
        P(("grp", "bl"), None, None),
        P(("grp", "bl")),
        P(("grp", "bl")),
        P(("grp", "bl"), None),
        P(("grp", "bl"), None),
    )
    out_specs = (P(None, ("grp", "bl"), None), P(None, ("grp", "bl"), None, None))
    return jax.shard_map(body, mesh=mesh, in_specs=in_specs, out_specs=out_specs, check_vma=False)
```

```python
import functools

import jax
import jax.numpy as jnp
from jax import lax
from jax.experimental import pallas as pl
from jax.experimental.pallas import tpu as pltpu
from jax.sharding import PartitionSpec as P

STATIONS = 64
SOURCE_COUNT = 40
ITERS = 2
ROWS = 16

ridge = 1.0
F32 = jnp.float32
BF16 = jnp.bfloat16
VMEM_LIMIT = 24 * 1024 * 1024


def swap(x):
    return pltpu.roll(x, x.shape[-1] // 2, axis=x.ndim - 1)


def lower(shape):
    return lax.broadcasted_iota(jnp.int32, shape, len(shape) - 1) < shape[-1] // 2


def cross(a, b):
    lo = lower(a.shape)
    return jnp.where(lo, a, swap(b)), jnp.where(lo, swap(a), b)


def three(x):
    hi = x.astype(BF16)
    rest = x - hi.astype(F32)
    mid = rest.astype(BF16)
    return hi, mid, (rest - mid.astype(F32)).astype(BF16)


def pick(onehot, x, dims):
    return sum(
        lax.dot_general(onehot, part, (dims, ((), ())), preferred_element_type=F32)
        for part in three(x)
    )


TILE = 8


def pack_kernel(n, dpc, first_ref, second_ref, re_ref, im_ref, out_ref, sems):
    rows = re_ref.shape[0]
    copies = [
        pltpu.make_async_copy(re_ref, out_ref.at[pl.ds(0, rows)], sems.at[0]),
        pltpu.make_async_copy(im_ref, out_ref.at[pl.ds(rows, rows)], sems.at[1]),
    ]
    for copy in copies:
        copy.start()
    lane = lax.broadcasted_iota(jnp.int32, (TILE, 128), 1)
    marks = jnp.zeros((TILE, 128), F32)
    for r in range(first_ref.shape[0]):
        marks = jnp.where(lane == r, (first_ref[r] + 1).astype(F32), marks)
        marks = jnp.where(lane == ROWS + r, (second_ref[r] + 1).astype(F32), marks)
    out_ref[2 * rows :] = marks
    for copy in copies:
        copy.wait()


class Fetch:
    def __init__(self, model, held, sems, firsts=(0,)):
        count, pairs = held.shape[0] // len(firsts), held.shape[2]
        parts = 3 if pairs % 3 == 0 else 1
        self.size = pairs // parts
        self.copies = []
        for i in range(parts):
            part = pl.ds(i * self.size, self.size)
            self.copies.append([])
            for j, first in enumerate(firsts):
                self.copies[i].append(
                    pltpu.make_async_copy(
                        model.at[pl.ds(first, count), :, part],
                        held.at[pl.ds(j * count, count), :, part],
                        sems.at[i, j],
                    )
                )
        for copies in self.copies:
            for copy in copies:
                copy.start()

    def each(self, body):
        for i, copies in enumerate(self.copies):
            for copy in copies:
                copy.wait()
            lax.fori_loop(i * self.size, (i + 1) * self.size, body, 0)


def power_kernel(n, dpc, model_hbm, mask_ref, unused_in, out_ref, unused_out, model_ref, sems):
    fetch = Fetch(model_hbm, model_ref, sems)
    out_ref[...] = jnp.zeros_like(out_ref)

    def pair(b, carry):
        weight = mask_ref[b].astype(F32)
        for d in range(SOURCE_COUNT):
            mr = model_ref[d, 0, b].astype(F32)
            mi = model_ref[d, 1, b].astype(F32)
            row = d // dpc * TILE + d % dpc
            out_ref[b, row : row + 1, :] = jnp.sum(weight * (mr * mr + mi * mi), axis=0, keepdims=True)
        return carry

    fetch.each(pair)


def wide(ref, dpc):
    return jnp.concatenate([ref[pl.ds(dd, STATIONS, stride=dpc), :] for dd in range(dpc)], axis=1)


def put(ref, value, dpc):
    for dd in range(dpc):
        ref[pl.ds(dd, STATIONS, stride=dpc), :] = value[:, dd * 128 : (dd + 1) * 128]
    ref[STATIONS * dpc :, :] = jnp.zeros((TILE, 128), F32)


def first_own_kernel(n, dpc, me_ref, *rest):
    ins, (g_ref, onehot_ref, sel_ref, split, lines) = rest[:n], rest[n:]
    me = me_ref[0]
    k, c = lax.div(me, 2), lax.rem(me, 2)
    per = STATIONS // n
    rows = per * SOURCE_COUNT
    for o in range(n):
        peer = jnp.bitwise_xor(me, o)
        lines[pl.ds(peer, 1), :] = ins[o][2 * rows : 2 * rows + 1, :]
        for s in range(per):
            at = s * SOURCE_COUNT + k * dpc
            x0, x1 = cross(ins[o][pl.ds(at, TILE), :], ins[o][pl.ds(rows + at, TILE), :])
            to = pl.multiple_of((peer * per + s) * TILE, TILE)
            split[pl.ds(to, TILE), :] = jnp.where(c == 0, x0, x1)
    g = jnp.concatenate([split[pl.ds(dd, STATIONS, stride=TILE), :] for dd in range(dpc)], axis=1)
    put(g_ref, g, dpc)
    across = 128 // (2 * ROWS)
    station = lax.broadcasted_iota(jnp.int32, (STATIONS, 128), 0)
    for group in range(n // across):
        marks = jnp.zeros((1, 128), F32)
        for i in range(across):
            row = lines[group * across + i : group * across + i + 1, :]
            marks = marks + (pltpu.roll(row, i * 2 * ROWS, axis=1) if i else row)
        hit = station + 1 == marks.astype(jnp.int32)
        onehot_ref[:, group * 128 : (group + 1) * 128] = jnp.where(hit, 1.0, 0.0).astype(BF16)
    sel_ref[...] = pick(onehot_ref[...], g, ((0,), (0,)))


def fill_powers(n, dpc, sums, sel_ref, terms, base):
    lo = lower((TILE, 128))
    for o in range(n):
        r = o * 2 * ROWS
        for dd in range(dpc):
            cols = slice(dd * 128, (dd + 1) * 128)
            dcols = slice(base + dd * 128, base + (dd + 1) * 128)
            W = sums[o, pl.ds(ROWS * dpc + dd, TILE, stride=dpc), :]
            Wx = swap(W)
            W = jnp.concatenate([jnp.where(lo, W, Wx), jnp.where(lo, Wx, W)], 0)
            p = sel_ref[r : r + ROWS, cols]
            q = sel_ref[r + ROWS : r + 2 * ROWS, cols]
            p2, q2 = p * p, q * q
            terms[r : r + ROWS, dcols] = W * (q2 + swap(q2))
            terms[r + ROWS : r + 2 * ROWS, dcols] = W * (p2 + swap(p2))


def fill_sums(n, dpc, sums, sel_ref, terms):
    lo = lower((ROWS, 128))
    sign = jnp.where(lo, -1.0, 1.0)
    for o in range(n):
        r = o * 2 * ROWS
        for dd in range(dpc):
            cols = slice(dd * 128, (dd + 1) * 128)
            B = sums[o, pl.ds(dd, ROWS, stride=dpc), :]
            p = sel_ref[r : r + ROWS, cols]
            q = sel_ref[r + ROWS : r + 2 * ROWS, cols]
            Bx = swap(B)
            Brr, Bii = jnp.where(lo, B, Bx), sign * jnp.where(lo, Bx, B)
            terms[r : r + ROWS, cols] = Brr * q + Bii * swap(q)
            terms[r + ROWS : r + 2 * ROWS, cols] = Brr * p - Bii * swap(p)


def own_kernel(n, dpc, g_in, onehot_ref, sel_ref, sums, g_out, terms):
    width = dpc * 128
    fill_sums(n, dpc, sums, sel_ref, terms)
    fill_powers(n, dpc, sums, sel_ref, terms, width)
    total = pick(onehot_ref[...], terms[...], ((1,), (0,)))
    put(g_out, 0.5 * (wide(g_in, dpc) + total[:, :width] / (total[:, width:] + ridge)), dpc)


def prepare_kernel(n, dpc, g_ref, onehot_ref, sums, sel_ref, den_ref, terms):
    sel_ref[...] = pick(onehot_ref[...], wide(g_ref, dpc), ((0,), (0,)))
    fill_powers(n, dpc, sums, sel_ref, terms, 0)
    den_ref[...] = pick(onehot_ref[...], terms[...], ((1,), (0,))) + ridge


def later_own_kernel(n, dpc, g_in, onehot_ref, sel_ref, den_ref, sums, g_out, terms):
    fill_sums(n, dpc, sums, sel_ref, terms)
    total = pick(onehot_ref[...], terms[...], ((1,), (0,)))
    put(g_out, 0.5 * (wide(g_in, dpc) + total / den_ref[...]), dpc)


def products_first(n, dpc, me, first_ref, second_ref, ins, hre, him, stack):
    per = STATIONS // n
    rows = per * SOURCE_COUNT
    for o in range(n):
        stack[jnp.bitwise_xor(me, o)] = ins[o][...]

    def pair(b, carry):
        p, q = first_ref[b], second_ref[b]

        def block(station, k, part):
            at = lax.rem(station, per) * SOURCE_COUNT + k * dpc + part * rows
            return stack[lax.div(station, per), pl.ds(at, TILE), :]

        for k in range(n // 2):
            pr, pi, qr, qi = block(p, k, 0), block(p, k, 1), block(q, k, 0), block(q, k, 1)
            hre[b, k * TILE : (k + 1) * TILE, :] = pr * qr + pi * qi
            him[b, k * TILE : (k + 1) * TILE, :] = pi * qr - pr * qi
        return carry

    lax.fori_loop(0, first_ref.shape[0], pair, 0)


def piece_pair(dpc, even, ins, m, station):
    a = ins[2 * m][pl.ds(station * dpc, TILE), :]
    b = ins[2 * m + 1][pl.ds(station * dpc, TILE), :]
    return cross(jnp.where(even, a, b), jnp.where(even, b, a))


def products(dpc, me, first_ref, second_ref, ins, hre, him):
    even = lax.rem(me, 2) == 0

    def pair(b, carry):
        p, q = first_ref[b], second_ref[b]
        for m in range(len(ins) // 2):
            pr, pi = piece_pair(dpc, even, ins, m, p)
            qr, qi = piece_pair(dpc, even, ins, m, q)
            hre[b, m * TILE : (m + 1) * TILE, :] = pr * qr + pi * qi
            him[b, m * TILE : (m + 1) * TILE, :] = pi * qr - pr * qi
        return carry

    lax.fori_loop(0, first_ref.shape[0], pair, 0)


def predict(dpc, b, acc, chips, model_ref, hre, him):
    acc_re, acc_im = acc
    for m, k in enumerate(chips):
        for dd in range(dpc):
            mr = model_ref[k * dpc + dd, 0, b].astype(F32)
            mi = model_ref[k * dpc + dd, 1, b].astype(F32)
            row = m * TILE + dd
            hr = hre[b, row : row + 1, :]
            hi = him[b, row : row + 1, :]
            acc_re = acc_re - (hr * mr - hi * mi)
            acc_im = acc_im - (hr * mi + hi * mr)
    return acc_re, acc_im


def weighted(b, acc, mask_ref):
    weight = mask_ref[b].astype(F32)
    return weight * acc[0], weight * acc[1]


def correlate(dpc, b, res, chips, model_ref, cre, cim):
    res_re, res_im = res
    for m, k in enumerate(chips):
        for dd in range(dpc):
            mr = model_ref[k * dpc + dd, 0, b].astype(F32)
            mi = model_ref[k * dpc + dd, 1, b].astype(F32)
            row = m * TILE + dd
            cre[b, row : row + 1, :] = jnp.sum(mr * res_re + mi * res_im, axis=0, keepdims=True)
            cim[b, row : row + 1, :] = jnp.sum(mr * res_im - mi * res_re, axis=0, keepdims=True)


def write_sums(dpc, pairs, chips, cre, cim, tiles, power_ref, out_ref, start):
    for m, k in enumerate(chips):
        tile = slice(m * TILE, (m + 1) * TILE)
        strong = pl.ds(k * TILE, TILE)
        for b in range(pairs):
            hr, hi = tiles(b, m)
            w = power_ref[b, strong, :]
            x0, x1 = cross(cre[b, tile, :] + hr * w, cim[b, tile, :] + hi * w)
            out_ref[2 * k, b * dpc : (b + 1) * dpc, :] = x0[:dpc]
            out_ref[2 * k + 1, b * dpc : (b + 1) * dpc, :] = x1[:dpc]
        if pairs < ROWS:
            empty = jnp.zeros(((ROWS - pairs) * dpc, 128), F32)
            out_ref[2 * k, pairs * dpc : ROWS * dpc, :] = empty
            out_ref[2 * k + 1, pairs * dpc : ROWS * dpc, :] = empty
        if start:
            for r in range(TILE):
                x0, x1 = cross(power_ref[r, strong, :], power_ref[r + TILE, strong, :])
                to = (ROWS + r) * dpc
                out_ref[2 * k, to : to + dpc, :] = x0[:dpc]
                out_ref[2 * k + 1, to : to + dpc, :] = x1[:dpc]


def first_pass_kernel(
    n, dpc, me_ref, first_ref, second_ref, model_hbm, vis_ref, mask_ref, power_ref, *rest
):
    ins, (out_ref, model_ref, sems, hre, him, cre, cim, stack) = rest[:n], rest[n:]
    fetch = Fetch(model_hbm, model_ref, sems)
    products_first(n, dpc, me_ref[0], first_ref, second_ref, ins, hre, him, stack)
    chips = range(n // 2)

    def pair(b, carry):
        acc = predict(dpc, b, (vis_ref[0, b], vis_ref[1, b]), chips, model_ref, hre, him)
        correlate(dpc, b, weighted(b, acc, mask_ref), chips, model_ref, cre, cim)
        return carry

    fetch.each(pair)

    def tiles(b, m):
        tile = slice(m * TILE, (m + 1) * TILE)
        return hre[b, tile, :], him[b, tile, :]

    write_sums(dpc, mask_ref.shape[0], chips, cre, cim, tiles, power_ref, out_ref, True)


NEAR, FAR = (0, 1, 2, 6), (3, 4, 5, 7)


def chips_of(me, pairs):
    return [jnp.bitwise_xor(lax.div(me, 2), m) for m in pairs]


def early_kernel(n, dpc, me_ref, first_ref, second_ref, model_hbm, vis_ref, unused_in, *rest):
    ins, (acc_ref, hre, him, unused_out, model_ref, sems) = rest[: 2 * len(NEAR)], rest[2 * len(NEAR) :]
    me = me_ref[0]
    fetch = Fetch(model_hbm, model_ref, sems, [k * dpc for k in chips_of(me, NEAR)])
    products(dpc, me, first_ref, second_ref, ins, hre, him)

    def pair(b, carry):
        acc = vis_ref[0, b], vis_ref[1, b]
        acc_ref[0, b], acc_ref[1, b] = predict(dpc, b, acc, range(len(NEAR)), model_ref, hre, him)
        return carry

    fetch.each(pair)


def later_pass_kernel(
    n, dpc, me_ref, first_ref, second_ref, model_hbm, mask_ref, power_ref, acc_ref, near_re, near_im, *rest
):
    ins, (out_ref, model_ref, sems, hre, him, cre, cim) = rest[: 2 * len(FAR)], rest[2 * len(FAR) :]
    fetch = Fetch(model_hbm, model_ref, sems)
    me = me_ref[0]
    products(dpc, me, first_ref, second_ref, ins, hre, him)
    far = chips_of(me, FAR)
    chips = chips_of(me, NEAR) + far

    def pair(b, carry):
        acc = predict(dpc, b, (acc_ref[0, b], acc_ref[1, b]), far, model_ref, hre, him)
        correlate(dpc, b, weighted(b, acc, mask_ref), chips, model_ref, cre, cim)
        return carry

    fetch.each(pair)

    def tiles(b, m):
        re, im = (near_re, near_im) if m < len(NEAR) else (hre, him)
        m = m % len(NEAR)
        tile = slice(m * TILE, (m + 1) * TILE)
        return re[b, tile, :], im[b, tile, :]

    write_sums(dpc, mask_ref.shape[0], chips, cre, cim, tiles, power_ref, out_ref, False)


def last_kernel(n, dpc, me_ref, first_ref, second_ref, model_hbm, mask_ref, acc_ref, *rest):
    ins, (res_ref, gains_ref, model_ref, sems, hre, him) = rest[:n], rest[n:]
    me = me_ref[0]
    fetch = Fetch(model_hbm, model_ref, sems, [k * dpc for k in chips_of(me, FAR)])
    products(dpc, me, first_ref, second_ref, ins[: 2 * len(FAR)], hre, him)
    per = STATIONS // n
    even = lax.rem(me, 2) == 0
    for m, k in enumerate(chips_of(me, FAR + NEAR)):
        for s in range(per):
            re, im = piece_pair(dpc, even, ins, m, me * per + s)
            for dd in range(dpc):
                at = s * SOURCE_COUNT + k * dpc + dd
                gains_ref[0, pl.ds(at, 1), :] = re[dd : dd + 1]
                gains_ref[1, pl.ds(at, 1), :] = im[dd : dd + 1]

    def pair(b, carry):
        acc = acc_ref[0, b], acc_ref[1, b]
        acc = predict(dpc, b, acc, range(len(FAR)), model_ref, hre, him)
        res_ref[0, b], res_ref[1, b] = weighted(b, acc, mask_ref)
        return carry

    fetch.each(pair)


SMEM = pl.BlockSpec(memory_space=pltpu.SMEM)
VMEM = pl.BlockSpec(memory_space=pltpu.VMEM)
HBM = pl.BlockSpec(memory_space=pltpu.HBM)


def shape(*dims, dtype=F32):
    return jax.ShapeDtypeStruct(dims, dtype)


def exchange(x):
    return lax.all_to_all(x, "bl", split_axis=0, concat_axis=0, tiled=True)


def gather(n, piece, beside):
    def send(x, o):
        return lax.ppermute(x, "bl", [(i, i ^ o) for i in range(n)])

    got = {0: piece}
    got[4], got[12] = send(piece, 4), send(piece, 12)
    got[2] = send(piece, 2)
    got[6] = send(got[4], 2)
    got[8] = send(got[12], 4)
    got[14], got[10] = send(got[12], 2), send(got[8], 2)
    for o in (0, 2, 4, 12):
        got[o + 1] = send(got[o], 1)
    got[6] = beside(got[6], got)
    for o in (6, 14, 8, 10):
        got[o + 1] = send(got[o], 1)
    return [got[o] for o in range(n)]


def fast_body(n, vis, model, mask, first, second, gre, gim):
    model, gre, gim = (pltpu.with_memory_space_constraint(x, pltpu.HBM) for x in (model, gre, gim))
    dpc = SOURCE_COUNT // (n // 2)
    width = dpc * 128
    pairs, times, channels = mask.shape
    me = lax.axis_index("bl").astype(jnp.int32).reshape(1)
    params = pltpu.CompilerParams(vmem_limit_bytes=VMEM_LIMIT)
    plane = (ROWS, n // 2 * TILE, channels)
    half = (ROWS, n // 4 * TILE, channels)
    lots = n * 2 * ROWS
    mine = (STATIONS * dpc + TILE, channels)
    sems = pltpu.SemaphoreType.DMA((3, n // 4))
    held = [pltpu.VMEM(model.shape, BF16), sems]
    held_half = [pltpu.VMEM((SOURCE_COUNT // 2,) + model.shape[1:], BF16), sems]

    def call(kernel, args, outs, scratch=(), micros=1, aliases={}):
        def place(x):
            if x is model or x is gre or x is gim:
                return HBM
            return SMEM if x.ndim == 1 else VMEM

        return pl.pallas_call(
            functools.partial(kernel, n, dpc),
            in_specs=[place(x) for x in args],
            out_specs=[VMEM for o in outs],
            out_shape=outs,
            scratch_shapes=[pltpu.VMEM(x, F32) if isinstance(x, tuple) else x for x in scratch],
            compiler_params=params,
            input_output_aliases=aliases,
            cost_estimate=pl.CostEstimate(
                flops=0, bytes_accessed=int(micros * 3.69e6), transcendentals=0
            ),
        )(*args)

    (piece,) = call(
        pack_kernel,
        (first, second, gre, gim),
        [shape(2 * gre.shape[0] + TILE, channels)],
        [pltpu.SemaphoreType.DMA((2,))],
    )
    power = None

    def powers_beside(x, got):
        nonlocal power
        power, x = call(
            power_kernel, (model, mask, x), [shape(*plane), shape(*x.shape)], held, micros=20, aliases={2: 1}
        )
        return x

    got = gather(n, piece, powers_beside)
    g, onehot, sel = call(
        first_own_kernel,
        (me, *got),
        [shape(*mine), shape(STATIONS, lots, dtype=BF16), shape(lots, width)],
        [(STATIONS * TILE, channels), (n, channels)],
        micros=2,
    )
    (sums,) = call(
        first_pass_kernel,
        (me, first, second, model, vis, mask, power, *got),
        [shape(n, (ROWS + TILE) * dpc, channels)],
        held + [plane] * 4 + [(n,) + piece.shape],
        micros=9,
    )
    powers = exchange(sums)
    (g,) = call(own_kernel, (g, onehot, sel, powers), [shape(*mine)], [(lots, 2 * width)])

    def slots(got, pairs):
        return [got[2 * m + c] for m in pairs for c in (0, 1)]

    def gather_near(g):
        near = None

        def beside(x, got):
            nonlocal near
            args = (me, first, second, model, vis, x, *slots(got, NEAR))
            outs = [shape(*vis.shape), shape(*half), shape(*half), shape(*x.shape)]
            *near, x = call(early_kernel, args, outs, held_half, micros=20, aliases={5: 3})
            return x

        got = gather(n, g, beside)
        return near, slots(got, NEAR), slots(got, FAR)

    for step in range(1, ITERS):
        near, _, far_slots = gather_near(g)
        sel, den = call(
            prepare_kernel,
            (g, onehot, powers),
            [shape(lots, width), shape(STATIONS, width)],
            [(lots, width)],
            micros=2,
        )
        (sums,) = call(
            later_pass_kernel,
            (me, first, second, model, mask, power, *near, *far_slots),
            [shape(n, ROWS * dpc, channels)],
            held + [half] * 2 + [plane] * 2,
            micros=7,
        )
        sums = exchange(sums)
        (g,) = call(later_own_kernel, (g, onehot, sel, den, sums), [shape(*mine)], [(lots, width)])
    near, near_slots, far_slots = gather_near(g)
    residual, gains = call(
        last_kernel,
        (me, first, second, model, mask, near[0], *far_slots, *near_slots),
        [shape(*vis.shape), shape(2, *gre.shape)],
        held_half + [half] * 2,
        micros=4,
    )
    return gains, residual


def block_pass(full_re, full_im, vis_blk, coh_blk, weight, first, second, want_sums):
    ar = jnp.transpose(full_re[first], (1, 0, 2))
    ai = jnp.transpose(full_im[first], (1, 0, 2))
    br = jnp.transpose(full_re[second], (1, 0, 2))
    bi = jnp.transpose(full_im[second], (1, 0, 2))
    mr = coh_blk[:, 0].astype(F32)
    mi = coh_blk[:, 1].astype(F32)
    hr = ar * br + ai * bi
    hi = ai * br - ar * bi
    hr_t, hi_t = hr[:, :, None], hi[:, :, None]
    res_re = weight * (vis_blk[0] - jnp.sum(hr_t * mr - hi_t * mi, 0))
    res_im = weight * (vis_blk[1] - jnp.sum(hr_t * mi + hi_t * mr, 0))
    residual = jnp.stack([res_re, res_im])
    if not want_sums:
        return (residual, None)
    power = jnp.sum(weight[None] * (mr * mr + mi * mi), 2)
    sum_re = jnp.sum(mr * res_re + mi * res_im, 2) + hr * power
    sum_im = jnp.sum(mr * res_im - mi * res_re, 2) + hi * power
    terms_first = jnp.stack([br * sum_re - bi * sum_im, br * sum_im + bi * sum_re, power * (br * br + bi * bi)])
    terms_second = jnp.stack([ar * sum_re + ai * sum_im, ai * sum_re - ar * sum_im, power * (ar * ar + ai * ai)])
    stations = jnp.arange(STATIONS, dtype=jnp.int32)
    onehot_first = (first[:, None] == stations[None, :]).astype(F32)
    onehot_second = (second[:, None] == stations[None, :]).astype(F32)
    exact = lax.Precision.HIGHEST
    sums = jnp.einsum("bs,cdbf->csdf", onehot_first, terms_first, precision=exact)
    sums = sums + jnp.einsum("bs,cdbf->csdf", onehot_second, terms_second, precision=exact)
    return (residual, sums)


def plain_body(vis, model, mask, first, second, gre, gim):
    weight = mask.astype(F32)
    rows, channels = gre.shape
    shaped = (STATIONS, SOURCE_COUNT, channels)
    full_re = lax.all_gather(gre, "bl", axis=0, tiled=True).reshape(shaped)
    full_im = lax.all_gather(gim, "bl", axis=0, tiled=True).reshape(shaped)
    for step in range(ITERS):
        unused, sums = block_pass(full_re, full_im, vis, model, weight, first, second, True)
        totals = lax.psum(sums, "bl")
        denom = totals[2] + ridge
        full_re = 0.5 * (full_re + totals[0] / denom)
        full_im = 0.5 * (full_im + totals[1] / denom)
    residual, unused = block_pass(full_re, full_im, vis, model, weight, first, second, False)
    both = jnp.stack([full_re, full_im]).reshape(2, STATIONS * SOURCE_COUNT, channels)
    return lax.dynamic_slice_in_dim(both, lax.axis_index("bl") * rows, rows, 1), residual


def solution(mesh):
    n = mesh.shape["bl"]
    split = n == 16

    def body(vis, model, mask, first, second, gre, gim):
        if split and mask.shape[0] <= ROWS:
            return fast_body(n, vis, model, mask, first, second, gre, gim)
        return plain_body(vis, model, mask, first, second, gre, gim)

    in_specs = (
        P(None, ("grp", "bl"), None, None),
        P(None, None, ("grp", "bl"), None, None),
        P(("grp", "bl"), None, None),
        P(("grp", "bl")),
        P(("grp", "bl")),
        P(("grp", "bl"), None),
        P(("grp", "bl"), None),
    )
    out_specs = (P(None, ("grp", "bl"), None), P(None, ("grp", "bl"), None, None))
    return jax.shard_map(body, mesh=mesh, in_specs=in_specs, out_specs=out_specs, check_vma=False)
```

```python
import functools

import jax
import jax.numpy as jnp
from jax import lax
from jax.experimental import pallas as pl
from jax.experimental.pallas import tpu as pltpu
from jax.sharding import PartitionSpec as P

STATIONS = 64
SOURCE_COUNT = 40
ITERS = 2
ROWS = 16

ridge = 1.0
F32 = jnp.float32
BF16 = jnp.bfloat16
VMEM_LIMIT = 24 * 1024 * 1024


def swap(x):
    return pltpu.roll(x, x.shape[-1] // 2, axis=x.ndim - 1)


def lower(shape):
    return lax.broadcasted_iota(jnp.int32, shape, len(shape) - 1) < shape[-1] // 2


def cross(a, b):
    lo = lower(a.shape)
    return jnp.where(lo, a, swap(b)), jnp.where(lo, swap(a), b)


def three(x):
    hi = x.astype(BF16)
    rest = x - hi.astype(F32)
    mid = rest.astype(BF16)
    return hi, mid, (rest - mid.astype(F32)).astype(BF16)


def pick(onehot, x, dims):
    return sum(
        lax.dot_general(onehot, part, (dims, ((), ())), preferred_element_type=F32)
        for part in three(x)
    )


TILE = 8
PARTS = (1, 3, 7, ROWS)


def pack_kernel(n, dpc, first_ref, second_ref, re_ref, im_ref, out_ref, sems):
    rows = re_ref.shape[0]
    copies = [
        pltpu.make_async_copy(re_ref, out_ref.at[pl.ds(0, rows)], sems.at[0]),
        pltpu.make_async_copy(im_ref, out_ref.at[pl.ds(rows, rows)], sems.at[1]),
    ]
    for copy in copies:
        copy.start()
    lane = lax.broadcasted_iota(jnp.int32, (TILE, 128), 1)
    marks = jnp.zeros((TILE, 128), F32)
    for r in range(first_ref.shape[0]):
        marks = jnp.where(lane == r, (first_ref[r] + 1).astype(F32), marks)
        marks = jnp.where(lane == ROWS + r, (second_ref[r] + 1).astype(F32), marks)
    out_ref[2 * rows :] = marks
    for copy in copies:
        copy.wait()


class Fetch:
    def __init__(self, model, held, sems, firsts=(0,)):
        count, pairs = held.shape[0] // len(firsts), held.shape[2]
        self.copies = []
        self.ends = [0] + [min(end, pairs) for end in PARTS]
        for i in range(len(PARTS)):
            part = pl.ds(self.ends[i], self.ends[i + 1] - self.ends[i])
            self.copies.append([])
            for j, first in enumerate(firsts):
                self.copies[i].append(
                    pltpu.make_async_copy(
                        model.at[pl.ds(first, count), :, part],
                        held.at[pl.ds(j * count, count), :, part],
                        sems.at[i, j],
                    )
                )
        for copies in self.copies:
            for copy in copies:
                copy.start()

    def each(self, body):
        for i, copies in enumerate(self.copies):
            for copy in copies:
                copy.wait()
            lax.fori_loop(self.ends[i], self.ends[i + 1], body, 0)


def power_kernel(n, dpc, model_hbm, mask_ref, unused_in, out_ref, unused_out, model_ref, sems):
    fetch = Fetch(model_hbm, model_ref, sems)
    out_ref[...] = jnp.zeros_like(out_ref)

    def pair(b, carry):
        weight = mask_ref[b].astype(F32)
        for d in range(SOURCE_COUNT):
            mr = model_ref[d, 0, b].astype(F32)
            mi = model_ref[d, 1, b].astype(F32)
            row = pl.ds(b * dpc + d % dpc, 1)
            out_ref[d // dpc, row, :] = jnp.sum(weight * (mr * mr + mi * mi), axis=0, keepdims=True)
        return carry

    fetch.each(pair)


def wide(ref, dpc):
    return jnp.concatenate([ref[pl.ds(dd, STATIONS, stride=dpc), :] for dd in range(dpc)], axis=1)


def put(ref, value, dpc):
    for dd in range(dpc):
        ref[pl.ds(dd, STATIONS, stride=dpc), :] = value[:, dd * 128 : (dd + 1) * 128]
    ref[STATIONS * dpc :, :] = jnp.zeros((TILE, 128), F32)


def first_own_kernel(n, dpc, me_ref, *rest):
    ins, (g_ref, onehot_ref, sel_ref, split, lines) = rest[:n], rest[n:]
    me = me_ref[0]
    k, c = lax.div(me, 2), lax.rem(me, 2)
    per = STATIONS // n
    rows = per * SOURCE_COUNT
    for o in range(n):
        peer = jnp.bitwise_xor(me, o)
        lines[pl.ds(peer, 1), :] = ins[o][2 * rows : 2 * rows + 1, :]
        for s in range(per):
            at = s * SOURCE_COUNT + k * dpc
            x0, x1 = cross(ins[o][pl.ds(at, TILE), :], ins[o][pl.ds(rows + at, TILE), :])
            to = pl.multiple_of((peer * per + s) * TILE, TILE)
            split[pl.ds(to, TILE), :] = jnp.where(c == 0, x0, x1)
    g = jnp.concatenate([split[pl.ds(dd, STATIONS, stride=TILE), :] for dd in range(dpc)], axis=1)
    put(g_ref, g, dpc)
    across = 128 // (2 * ROWS)
    station = lax.broadcasted_iota(jnp.int32, (STATIONS, 128), 0)
    for group in range(n // across):
        marks = jnp.zeros((1, 128), F32)
        for i in range(across):
            row = lines[group * across + i : group * across + i + 1, :]
            marks = marks + (pltpu.roll(row, i * 2 * ROWS, axis=1) if i else row)
        hit = station + 1 == marks.astype(jnp.int32)
        onehot_ref[:, group * 128 : (group + 1) * 128] = jnp.where(hit, 1.0, 0.0).astype(BF16)
    sel_ref[...] = pick(onehot_ref[...], g, ((0,), (0,)))


def fill_powers(n, dpc, sums, sel_ref, terms, base):
    lo = lower((TILE, 128))
    for o in range(n):
        r = o * 2 * ROWS
        for dd in range(dpc):
            cols = slice(dd * 128, (dd + 1) * 128)
            dcols = slice(base + dd * 128, base + (dd + 1) * 128)
            W = sums[o, pl.ds(ROWS * dpc + dd, TILE, stride=dpc), :]
            Wx = swap(W)
            W = jnp.concatenate([jnp.where(lo, W, Wx), jnp.where(lo, Wx, W)], 0)
            p = sel_ref[r : r + ROWS, cols]
            q = sel_ref[r + ROWS : r + 2 * ROWS, cols]
            p2, q2 = p * p, q * q
            terms[r : r + ROWS, dcols] = W * (q2 + swap(q2))
            terms[r + ROWS : r + 2 * ROWS, dcols] = W * (p2 + swap(p2))


def fill_sums(n, dpc, sums, sel_ref, terms):
    lo = lower((ROWS, 128))
    sign = jnp.where(lo, -1.0, 1.0)
    for o in range(n):
        r = o * 2 * ROWS
        for dd in range(dpc):
            cols = slice(dd * 128, (dd + 1) * 128)
            B = sums[o, pl.ds(dd, ROWS, stride=dpc), :]
            p = sel_ref[r : r + ROWS, cols]
            q = sel_ref[r + ROWS : r + 2 * ROWS, cols]
            Bx = swap(B)
            Brr, Bii = jnp.where(lo, B, Bx), sign * jnp.where(lo, Bx, B)
            terms[r : r + ROWS, cols] = Brr * q + Bii * swap(q)
            terms[r + ROWS : r + 2 * ROWS, cols] = Brr * p - Bii * swap(p)


def own_kernel(n, dpc, g_in, onehot_ref, sel_ref, sums, g_out, terms):
    width = dpc * 128
    fill_sums(n, dpc, sums, sel_ref, terms)
    fill_powers(n, dpc, sums, sel_ref, terms, width)
    total = pick(onehot_ref[...], terms[...], ((1,), (0,)))
    put(g_out, 0.5 * (wide(g_in, dpc) + total[:, :width] / (total[:, width:] + ridge)), dpc)


def prepare_kernel(n, dpc, g_ref, onehot_ref, sums, sel_ref, den_ref, terms):
    sel_ref[...] = pick(onehot_ref[...], wide(g_ref, dpc), ((0,), (0,)))
    fill_powers(n, dpc, sums, sel_ref, terms, 0)
    den_ref[...] = pick(onehot_ref[...], terms[...], ((1,), (0,))) + ridge


def later_own_kernel(n, dpc, g_in, onehot_ref, sel_ref, den_ref, sums, g_out, terms):
    fill_sums(n, dpc, sums, sel_ref, terms)
    total = pick(onehot_ref[...], terms[...], ((1,), (0,)))
    put(g_out, 0.5 * (wide(g_in, dpc) + total / den_ref[...]), dpc)


def clear(dpc, pairs, *refs):
    for ref in refs:
        chips, rows, _ = ref.shape
        for m in range(chips):
            ref[m, pairs * dpc :, :] = jnp.zeros((rows - pairs * dpc, 128), F32)


def products_first(n, dpc, me, first_ref, second_ref, ins, hre, him, stack):
    per = STATIONS // n
    rows = per * SOURCE_COUNT
    for o in range(n):
        stack[jnp.bitwise_xor(me, o)] = ins[o][...]

    def pair(b, carry):
        p, q = first_ref[b], second_ref[b]

        def block(station, k, part):
            at = lax.rem(station, per) * SOURCE_COUNT + k * dpc + part * rows
            return stack[lax.div(station, per), pl.ds(at, TILE), :]

        for k in range(n // 2):
            pr, pi, qr, qi = block(p, k, 0), block(p, k, 1), block(q, k, 0), block(q, k, 1)
            hre[k, pl.ds(b * dpc, TILE), :] = pr * qr + pi * qi
            him[k, pl.ds(b * dpc, TILE), :] = pi * qr - pr * qi
        return carry

    lax.fori_loop(0, first_ref.shape[0], pair, 0)
    clear(dpc, first_ref.shape[0], hre, him)


def piece_pair(dpc, even, ins, m, station):
    a = ins[2 * m][pl.ds(station * dpc, TILE), :]
    b = ins[2 * m + 1][pl.ds(station * dpc, TILE), :]
    return cross(jnp.where(even, a, b), jnp.where(even, b, a))


def products(dpc, me, first_ref, second_ref, ins, hre, him):
    even = lax.rem(me, 2) == 0

    def pair(b, carry):
        p, q = first_ref[b], second_ref[b]
        for m in range(len(ins) // 2):
            pr, pi = piece_pair(dpc, even, ins, m, p)
            qr, qi = piece_pair(dpc, even, ins, m, q)
            hre[m, pl.ds(b * dpc, TILE), :] = pr * qr + pi * qi
            him[m, pl.ds(b * dpc, TILE), :] = pi * qr - pr * qi
        return carry

    lax.fori_loop(0, first_ref.shape[0], pair, 0)
    clear(dpc, first_ref.shape[0], hre, him)


def predict(dpc, b, acc, chips, model_ref, hre, him):
    acc_re, acc_im = acc
    for m, k in enumerate(chips):
        for dd in range(dpc):
            mr = model_ref[k * dpc + dd, 0, b].astype(F32)
            mi = model_ref[k * dpc + dd, 1, b].astype(F32)
            row = pl.ds(b * dpc + dd, 1)
            hr, hi = hre[m, row, :], him[m, row, :]
            acc_re = acc_re - (hr * mr - hi * mi)
            acc_im = acc_im - (hr * mi + hi * mr)
    return acc_re, acc_im


def weighted(b, acc, mask_ref):
    weight = mask_ref[b].astype(F32)
    return weight * acc[0], weight * acc[1]


def correlate(dpc, b, res, chips, model_ref, cre, cim):
    res_re, res_im = res
    for m, k in enumerate(chips):
        for dd in range(dpc):
            mr = model_ref[k * dpc + dd, 0, b].astype(F32)
            mi = model_ref[k * dpc + dd, 1, b].astype(F32)
            row = pl.ds(b * dpc + dd, 1)
            cre[m, row, :] = jnp.sum(mr * res_re + mi * res_im, axis=0, keepdims=True)
            cim[m, row, :] = jnp.sum(mr * res_im - mi * res_re, axis=0, keepdims=True)


def write_sums(dpc, chips, cre, cim, tiles, power_ref, out_ref, start):
    for m, k in enumerate(chips):
        re, im, at = tiles(m)
        for t in range(ROWS * dpc // TILE):
            rows = slice(t * TILE, (t + 1) * TILE)
            w = power_ref[k, rows, :]
            x0, x1 = cross(cre[m, rows, :] + re[at, rows, :] * w, cim[m, rows, :] + im[at, rows, :] * w)
            out_ref[2 * k, rows, :] = x0
            out_ref[2 * k + 1, rows, :] = x1
        if start:
            for t in range(dpc):
                x0, x1 = cross(
                    power_ref[k, t * TILE : (t + 1) * TILE, :],
                    power_ref[k, (t + dpc) * TILE : (t + dpc + 1) * TILE, :],
                )
                rows = slice(ROWS * dpc + t * TILE, ROWS * dpc + (t + 1) * TILE)
                out_ref[2 * k, rows, :] = x0
                out_ref[2 * k + 1, rows, :] = x1


def first_pass_kernel(
    n, dpc, me_ref, first_ref, second_ref, model_hbm, vis_ref, mask_ref, power_ref, *rest
):
    ins, (out_ref, model_ref, sems, hre, him, cre, cim, stack) = rest[:n], rest[n:]
    fetch = Fetch(model_hbm, model_ref, sems)
    products_first(n, dpc, me_ref[0], first_ref, second_ref, ins, hre, him, stack)
    chips = range(n // 2)

    def pair(b, carry):
        acc = predict(dpc, b, (vis_ref[0, b], vis_ref[1, b]), chips, model_ref, hre, him)
        correlate(dpc, b, weighted(b, acc, mask_ref), chips, model_ref, cre, cim)
        return carry

    fetch.each(pair)

    clear(dpc, mask_ref.shape[0], cre, cim)
    write_sums(dpc, chips, cre, cim, lambda m: (hre, him, m), power_ref, out_ref, True)


NEAR, FAR = (0, 1, 2, 6), (3, 4, 5, 7)


def chips_of(me, pairs):
    return [jnp.bitwise_xor(lax.div(me, 2), m) for m in pairs]


def early_kernel(n, dpc, me_ref, first_ref, second_ref, model_hbm, vis_ref, unused_in, *rest):
    ins, (acc_ref, hre, him, unused_out, model_ref, sems) = rest[: 2 * len(NEAR)], rest[2 * len(NEAR) :]
    me = me_ref[0]
    fetch = Fetch(model_hbm, model_ref, sems, [k * dpc for k in chips_of(me, NEAR)])
    products(dpc, me, first_ref, second_ref, ins, hre, him)

    def pair(b, carry):
        acc = vis_ref[0, b], vis_ref[1, b]
        acc_ref[0, b], acc_ref[1, b] = predict(dpc, b, acc, range(len(NEAR)), model_ref, hre, him)
        return carry

    fetch.each(pair)


def later_pass_kernel(
    n, dpc, me_ref, first_ref, second_ref, model_hbm, mask_ref, power_ref, acc_ref, near_re, near_im, *rest
):
    ins, (out_ref, model_ref, sems, hre, him, cre, cim) = rest[: 2 * len(FAR)], rest[2 * len(FAR) :]
    fetch = Fetch(model_hbm, model_ref, sems)
    me = me_ref[0]
    products(dpc, me, first_ref, second_ref, ins, hre, him)
    far = chips_of(me, FAR)
    chips = chips_of(me, NEAR) + far

    def pair(b, carry):
        acc = predict(dpc, b, (acc_ref[0, b], acc_ref[1, b]), far, model_ref, hre, him)
        correlate(dpc, b, weighted(b, acc, mask_ref), chips, model_ref, cre, cim)
        return carry

    fetch.each(pair)

    def tiles(m):
        return (near_re, near_im, m) if m < len(NEAR) else (hre, him, m - len(NEAR))

    clear(dpc, mask_ref.shape[0], cre, cim)
    write_sums(dpc, chips, cre, cim, tiles, power_ref, out_ref, False)


def last_kernel(n, dpc, me_ref, first_ref, second_ref, model_hbm, mask_ref, acc_ref, *rest):
    ins, (res_ref, gains_ref, model_ref, sems, hre, him) = rest[:n], rest[n:]
    me = me_ref[0]
    fetch = Fetch(model_hbm, model_ref, sems, [k * dpc for k in chips_of(me, FAR)])
    products(dpc, me, first_ref, second_ref, ins[: 2 * len(FAR)], hre, him)
    per = STATIONS // n
    even = lax.rem(me, 2) == 0
    for m, k in enumerate(chips_of(me, FAR + NEAR)):
        for s in range(per):
            re, im = piece_pair(dpc, even, ins, m, me * per + s)
            for dd in range(dpc):
                at = s * SOURCE_COUNT + k * dpc + dd
                gains_ref[0, pl.ds(at, 1), :] = re[dd : dd + 1]
                gains_ref[1, pl.ds(at, 1), :] = im[dd : dd + 1]

    def pair(b, carry):
        acc = acc_ref[0, b], acc_ref[1, b]
        acc = predict(dpc, b, acc, range(len(FAR)), model_ref, hre, him)
        res_ref[0, b], res_ref[1, b] = weighted(b, acc, mask_ref)
        return carry

    fetch.each(pair)


SMEM = pl.BlockSpec(memory_space=pltpu.SMEM)
VMEM = pl.BlockSpec(memory_space=pltpu.VMEM)
HBM = pl.BlockSpec(memory_space=pltpu.HBM)


def shape(*dims, dtype=F32):
    return jax.ShapeDtypeStruct(dims, dtype)


def exchange(x):
    return lax.all_to_all(x, "bl", split_axis=0, concat_axis=0, tiled=True)


def gather(n, piece, beside, at):
    def send(x, o):
        return lax.ppermute(x, "bl", [(i, i ^ o) for i in range(n)])

    got = {0: piece}
    got[4], got[12] = send(piece, 4), send(piece, 12)
    got[2] = send(piece, 2)
    got[6] = send(got[4], 2)
    got[8] = send(got[12], 4)
    got[14], got[10] = send(got[12], 2), send(got[8], 2)
    for o in (0, 2, 4, 12, 6, 14, 8, 10):
        if o == at:
            got[o] = beside(got[o], got)
        got[o + 1] = send(got[o], 1)
    return [got[o] for o in range(n)]


def fast_body(n, vis, model, mask, first, second, gre, gim):
    model, gre, gim = (pltpu.with_memory_space_constraint(x, pltpu.HBM) for x in (model, gre, gim))
    dpc = SOURCE_COUNT // (n // 2)
    width = dpc * 128
    pairs, times, channels = mask.shape
    me = lax.axis_index("bl").astype(jnp.int32).reshape(1)
    params = pltpu.CompilerParams(vmem_limit_bytes=VMEM_LIMIT)
    plane = (n // 2, ROWS * dpc + TILE, channels)
    half = (n // 4, ROWS * dpc + TILE, channels)
    lots = n * 2 * ROWS
    mine = (STATIONS * dpc + TILE, channels)
    sems = pltpu.SemaphoreType.DMA((len(PARTS), n // 4))
    held = [pltpu.VMEM(model.shape, BF16), sems]
    held_half = [pltpu.VMEM((SOURCE_COUNT // 2,) + model.shape[1:], BF16), sems]

    def call(kernel, args, outs, scratch=(), micros=1, aliases={}):
        def place(x):
            if x is model or x is gre or x is gim:
                return HBM
            return SMEM if x.ndim == 1 else VMEM

        return pl.pallas_call(
            functools.partial(kernel, n, dpc),
            in_specs=[place(x) for x in args],
            out_specs=[VMEM for o in outs],
            out_shape=outs,
            scratch_shapes=[pltpu.VMEM(x, F32) if isinstance(x, tuple) else x for x in scratch],
            compiler_params=params,
            input_output_aliases=aliases,
            cost_estimate=pl.CostEstimate(
                flops=0, bytes_accessed=int(micros * 3.69e6), transcendentals=0
            ),
        )(*args)

    (piece,) = call(
        pack_kernel,
        (first, second, gre, gim),
        [shape(2 * gre.shape[0] + TILE, channels)],
        [pltpu.SemaphoreType.DMA((2,))],
    )
    power = None

    def powers_beside(x, got):
        nonlocal power
        power, x = call(
            power_kernel, (model, mask, x), [shape(*plane), shape(*x.shape)], held, micros=20, aliases={2: 1}
        )
        return x

    got = gather(n, piece, powers_beside, 14)
    g, onehot, sel = call(
        first_own_kernel,
        (me, *got),
        [shape(*mine), shape(STATIONS, lots, dtype=BF16), shape(lots, width)],
        [(STATIONS * TILE, channels), (n, channels)],
        micros=2,
    )
    (sums,) = call(
        first_pass_kernel,
        (me, first, second, model, vis, mask, power, *got),
        [shape(n, (ROWS + TILE) * dpc, channels)],
        held + [plane] * 4 + [(n,) + piece.shape],
        micros=9,
    )
    powers = exchange(sums)
    (g,) = call(
        own_kernel,
        (g, onehot, sel, powers),
        [shape(*mine)],
        [(lots, 2 * width)],
    )

    def slots(got, pairs):
        return [got[2 * m + c] for m in pairs for c in (0, 1)]

    def gather_near(g):
        near = None

        def beside(x, got):
            nonlocal near
            args = (me, first, second, model, vis, x, *slots(got, NEAR))
            outs = [shape(*vis.shape), shape(*half), shape(*half), shape(*x.shape)]
            *near, x = call(early_kernel, args, outs, held_half, micros=20, aliases={5: 3})
            return x

        got = gather(n, g, beside, 14)
        return near, slots(got, NEAR), slots(got, FAR)

    for step in range(1, ITERS):
        near, _, far_slots = gather_near(g)
        sel, den = call(
            prepare_kernel,
            (g, onehot, powers),
            [shape(lots, width), shape(STATIONS, width)],
            [(lots, width)],
            micros=2,
        )
        (sums,) = call(
            later_pass_kernel,
            (me, first, second, model, mask, power, *near, *far_slots),
            [shape(n, ROWS * dpc, channels)],
            held + [half] * 2 + [plane] * 2,
            micros=7,
        )
        sums = exchange(sums)
        (g,) = call(
            later_own_kernel,
            (g, onehot, sel, den, sums),
            [shape(*mine)],
            [(lots, width)],
        )
    near, near_slots, far_slots = gather_near(g)
    residual, gains = call(
        last_kernel,
        (me, first, second, model, mask, near[0], *far_slots, *near_slots),
        [shape(*vis.shape), shape(2, *gre.shape)],
        held_half + [half] * 2,
        micros=4,
    )
    return gains, residual


def block_pass(full_re, full_im, vis_blk, coh_blk, weight, first, second, want_sums):
    ar = jnp.transpose(full_re[first], (1, 0, 2))
    ai = jnp.transpose(full_im[first], (1, 0, 2))
    br = jnp.transpose(full_re[second], (1, 0, 2))
    bi = jnp.transpose(full_im[second], (1, 0, 2))
    mr = coh_blk[:, 0].astype(F32)
    mi = coh_blk[:, 1].astype(F32)
    hr = ar * br + ai * bi
    hi = ai * br - ar * bi
    hr_t, hi_t = hr[:, :, None], hi[:, :, None]
    res_re = weight * (vis_blk[0] - jnp.sum(hr_t * mr - hi_t * mi, 0))
    res_im = weight * (vis_blk[1] - jnp.sum(hr_t * mi + hi_t * mr, 0))
    residual = jnp.stack([res_re, res_im])
    if not want_sums:
        return (residual, None)
    power = jnp.sum(weight[None] * (mr * mr + mi * mi), 2)
    sum_re = jnp.sum(mr * res_re + mi * res_im, 2) + hr * power
    sum_im = jnp.sum(mr * res_im - mi * res_re, 2) + hi * power
    terms_first = jnp.stack([br * sum_re - bi * sum_im, br * sum_im + bi * sum_re, power * (br * br + bi * bi)])
    terms_second = jnp.stack([ar * sum_re + ai * sum_im, ai * sum_re - ar * sum_im, power * (ar * ar + ai * ai)])
    stations = jnp.arange(STATIONS, dtype=jnp.int32)
    onehot_first = (first[:, None] == stations[None, :]).astype(F32)
    onehot_second = (second[:, None] == stations[None, :]).astype(F32)
    exact = lax.Precision.HIGHEST
    sums = jnp.einsum("bs,cdbf->csdf", onehot_first, terms_first, precision=exact)
    sums = sums + jnp.einsum("bs,cdbf->csdf", onehot_second, terms_second, precision=exact)
    return (residual, sums)


def plain_body(vis, model, mask, first, second, gre, gim):
    weight = mask.astype(F32)
    rows, channels = gre.shape
    shaped = (STATIONS, SOURCE_COUNT, channels)
    full_re = lax.all_gather(gre, "bl", axis=0, tiled=True).reshape(shaped)
    full_im = lax.all_gather(gim, "bl", axis=0, tiled=True).reshape(shaped)
    for step in range(ITERS):
        unused, sums = block_pass(full_re, full_im, vis, model, weight, first, second, True)
        totals = lax.psum(sums, "bl")
        denom = totals[2] + ridge
        full_re = 0.5 * (full_re + totals[0] / denom)
        full_im = 0.5 * (full_im + totals[1] / denom)
    residual, unused = block_pass(full_re, full_im, vis, model, weight, first, second, False)
    both = jnp.stack([full_re, full_im]).reshape(2, STATIONS * SOURCE_COUNT, channels)
    return lax.dynamic_slice_in_dim(both, lax.axis_index("bl") * rows, rows, 1), residual


def solution(mesh):
    n = mesh.shape["bl"]
    split = n == 16

    def body(vis, model, mask, first, second, gre, gim):
        if split and mask.shape[0] <= ROWS:
            return fast_body(n, vis, model, mask, first, second, gre, gim)
        return plain_body(vis, model, mask, first, second, gre, gim)

    in_specs = (
        P(None, ("grp", "bl"), None, None),
        P(None, None, ("grp", "bl"), None, None),
        P(("grp", "bl"), None, None),
        P(("grp", "bl")),
        P(("grp", "bl")),
        P(("grp", "bl"), None),
        P(("grp", "bl"), None),
    )
    out_specs = (P(None, ("grp", "bl"), None), P(None, ("grp", "bl"), None, None))
    return jax.shard_map(body, mesh=mesh, in_specs=in_specs, out_specs=out_specs, check_vma=False)
```

```python
import functools

import jax
import jax.numpy as jnp
from jax import lax
from jax.experimental import pallas as pl
from jax.experimental.pallas import tpu as pltpu
from jax.sharding import PartitionSpec as P

STATIONS = 64
SOURCE_COUNT = 40
ITERS = 2
ROWS = 16

ridge = 1.0
F32 = jnp.float32
BF16 = jnp.bfloat16
VMEM_LIMIT = 24 * 1024 * 1024


def swap(x):
    return pltpu.roll(x, x.shape[-1] // 2, axis=x.ndim - 1)


def lower(shape):
    return lax.broadcasted_iota(jnp.int32, shape, len(shape) - 1) < shape[-1] // 2


def cross(a, b):
    lo = lower(a.shape)
    return jnp.where(lo, a, swap(b)), jnp.where(lo, swap(a), b)


def three(x):
    hi = x.astype(BF16)
    rest = x - hi.astype(F32)
    mid = rest.astype(BF16)
    return hi, mid, (rest - mid.astype(F32)).astype(BF16)


def pick(onehot, x, dims):
    return sum(
        lax.dot_general(onehot, part, (dims, ((), ())), preferred_element_type=F32)
        for part in three(x)
    )


TILE = 8
PARTS = (1, 3, 7, ROWS)


def pack_kernel(n, dpc, first_ref, second_ref, re_ref, im_ref, out_ref, sems):
    rows = re_ref.shape[0]
    copies = [
        pltpu.make_async_copy(re_ref, out_ref.at[pl.ds(0, rows)], sems.at[0]),
        pltpu.make_async_copy(im_ref, out_ref.at[pl.ds(rows, rows)], sems.at[1]),
    ]
    for copy in copies:
        copy.start()
    lane = lax.broadcasted_iota(jnp.int32, (TILE, 128), 1)
    marks = jnp.zeros((TILE, 128), F32)
    for r in range(first_ref.shape[0]):
        marks = jnp.where(lane == r, (first_ref[r] + 1).astype(F32), marks)
        marks = jnp.where(lane == ROWS + r, (second_ref[r] + 1).astype(F32), marks)
    out_ref[2 * rows :] = marks
    for copy in copies:
        copy.wait()


class Fetch:
    def __init__(self, model, held, sems, firsts=(0,)):
        count, pairs = held.shape[0] // len(firsts), held.shape[2]
        self.copies = []
        self.ends = [0] + [min(end, pairs) for end in PARTS]
        for i in range(len(PARTS)):
            part = pl.ds(self.ends[i], self.ends[i + 1] - self.ends[i])
            self.copies.append([])
            for j, first in enumerate(firsts):
                self.copies[i].append(
                    pltpu.make_async_copy(
                        model.at[pl.ds(first, count), :, part],
                        held.at[pl.ds(j * count, count), :, part],
                        sems.at[i, j],
                    )
                )
        for copies in self.copies:
            for copy in copies:
                copy.start()

    def each(self, body):
        for i, copies in enumerate(self.copies):
            for copy in copies:
                copy.wait()
            lax.fori_loop(self.ends[i], self.ends[i + 1], body, 0)


def power_kernel(n, dpc, model_hbm, mask_ref, unused_in, out_ref, unused_out, model_ref, sems):
    fetch = Fetch(model_hbm, model_ref, sems)
    out_ref[...] = jnp.zeros_like(out_ref)

    def pair(b, carry):
        weight = mask_ref[b].astype(F32)
        for d in range(SOURCE_COUNT):
            mr = model_ref[d, 0, b].astype(F32)
            mi = model_ref[d, 1, b].astype(F32)
            row = pl.ds(b * dpc + d % dpc, 1)
            out_ref[d // dpc, row, :] = jnp.sum(weight * (mr * mr + mi * mi), axis=0, keepdims=True)
        return carry

    fetch.each(pair)


def wide(ref, dpc):
    return jnp.concatenate([ref[pl.ds(dd, STATIONS, stride=dpc), :] for dd in range(dpc)], axis=1)


def put(ref, value, dpc):
    for dd in range(dpc):
        ref[pl.ds(dd, STATIONS, stride=dpc), :] = value[:, dd * 128 : (dd + 1) * 128]
    ref[STATIONS * dpc :, :] = jnp.zeros((TILE, 128), F32)


def first_own_kernel(n, dpc, me_ref, *rest):
    ins, (g_ref, onehot_ref, split, lines) = rest[:n], rest[n:]
    me = me_ref[0]
    k, c = lax.div(me, 2), lax.rem(me, 2)
    per = STATIONS // n
    rows = per * SOURCE_COUNT
    for o in range(n):
        peer = jnp.bitwise_xor(me, o)
        lines[pl.ds(peer, 1), :] = ins[o][2 * rows : 2 * rows + 1, :]
        for s in range(per):
            at = s * SOURCE_COUNT + k * dpc
            x0, x1 = cross(ins[o][pl.ds(at, TILE), :], ins[o][pl.ds(rows + at, TILE), :])
            to = pl.multiple_of((peer * per + s) * TILE, TILE)
            split[pl.ds(to, TILE), :] = jnp.where(c == 0, x0, x1)
    g = jnp.concatenate([split[pl.ds(dd, STATIONS, stride=TILE), :] for dd in range(dpc)], axis=1)
    put(g_ref, g, dpc)
    across = 128 // (2 * ROWS)
    station = lax.broadcasted_iota(jnp.int32, (STATIONS, 128), 0)
    for group in range(n // across):
        marks = jnp.zeros((1, 128), F32)
        for i in range(across):
            row = lines[group * across + i : group * across + i + 1, :]
            marks = marks + (pltpu.roll(row, i * 2 * ROWS, axis=1) if i else row)
        hit = station + 1 == marks.astype(jnp.int32)
        onehot_ref[:, group * 128 : (group + 1) * 128] = jnp.where(hit, 1.0, 0.0).astype(BF16)


def fill_powers(n, dpc, sums, sel_ref, terms, base):
    lo = lower((TILE, 128))
    for o in range(n):
        r = o * 2 * ROWS
        for dd in range(dpc):
            cols = slice(dd * 128, (dd + 1) * 128)
            dcols = slice(base + dd * 128, base + (dd + 1) * 128)
            W = sums[o, pl.ds(ROWS * dpc + dd, TILE, stride=dpc), :]
            Wx = swap(W)
            W = jnp.concatenate([jnp.where(lo, W, Wx), jnp.where(lo, Wx, W)], 0)
            p = sel_ref[r : r + ROWS, cols]
            q = sel_ref[r + ROWS : r + 2 * ROWS, cols]
            p2, q2 = p * p, q * q
            terms[r : r + ROWS, dcols] = W * (q2 + swap(q2))
            terms[r + ROWS : r + 2 * ROWS, dcols] = W * (p2 + swap(p2))


def fill_sums(n, dpc, sums, sel_ref, terms):
    lo = lower((ROWS, 128))
    sign = jnp.where(lo, -1.0, 1.0)
    for o in range(n):
        r = o * 2 * ROWS
        for dd in range(dpc):
            cols = slice(dd * 128, (dd + 1) * 128)
            B = sums[o, pl.ds(dd, ROWS, stride=dpc), :]
            p = sel_ref[r : r + ROWS, cols]
            q = sel_ref[r + ROWS : r + 2 * ROWS, cols]
            Bx = swap(B)
            Brr, Bii = jnp.where(lo, B, Bx), sign * jnp.where(lo, Bx, B)
            terms[r : r + ROWS, cols] = Brr * q + Bii * swap(q)
            terms[r + ROWS : r + 2 * ROWS, cols] = Brr * p - Bii * swap(p)


def own_kernel(n, dpc, g_in, onehot_ref, sums, g_out, terms, sel_ref):
    width = dpc * 128
    sel_ref[...] = pick(onehot_ref[...], wide(g_in, dpc), ((0,), (0,)))
    fill_sums(n, dpc, sums, sel_ref, terms)
    fill_powers(n, dpc, sums, sel_ref, terms, width)
    total = pick(onehot_ref[...], terms[...], ((1,), (0,)))
    put(g_out, 0.5 * (wide(g_in, dpc) + total[:, :width] / (total[:, width:] + ridge)), dpc)


def prepare_kernel(n, dpc, g_ref, onehot_ref, sums, den_ref, terms, sel_ref):
    sel_ref[...] = pick(onehot_ref[...], wide(g_ref, dpc), ((0,), (0,)))
    fill_powers(n, dpc, sums, sel_ref, terms, 0)
    den_ref[...] = pick(onehot_ref[...], terms[...], ((1,), (0,))) + ridge


def later_own_kernel(n, dpc, g_in, onehot_ref, den_ref, sums, g_out, terms, sel_ref):
    sel_ref[...] = pick(onehot_ref[...], wide(g_in, dpc), ((0,), (0,)))
    fill_sums(n, dpc, sums, sel_ref, terms)
    total = pick(onehot_ref[...], terms[...], ((1,), (0,)))
    put(g_out, 0.5 * (wide(g_in, dpc) + total / den_ref[...]), dpc)


def clear(dpc, pairs, *refs):
    for ref in refs:
        chips, rows, _ = ref.shape
        for m in range(chips):
            ref[m, pairs * dpc :, :] = jnp.zeros((rows - pairs * dpc, 128), F32)


def products_first(n, dpc, me, first_ref, second_ref, ins, hre, him, stack):
    per = STATIONS // n
    rows = per * SOURCE_COUNT
    for o in range(n):
        stack[jnp.bitwise_xor(me, o)] = ins[o][...]

    def pair(b, carry):
        p, q = first_ref[b], second_ref[b]

        def block(station, k, part):
            at = lax.rem(station, per) * SOURCE_COUNT + k * dpc + part * rows
            return stack[lax.div(station, per), pl.ds(at, TILE), :]

        for k in range(n // 2):
            pr, pi, qr, qi = block(p, k, 0), block(p, k, 1), block(q, k, 0), block(q, k, 1)
            hre[k, pl.ds(b * dpc, TILE), :] = pr * qr + pi * qi
            him[k, pl.ds(b * dpc, TILE), :] = pi * qr - pr * qi
        return carry

    lax.fori_loop(0, first_ref.shape[0], pair, 0)
    clear(dpc, first_ref.shape[0], hre, him)


def piece_pair(dpc, even, ins, m, station):
    a = ins[2 * m][pl.ds(station * dpc, TILE), :]
    b = ins[2 * m + 1][pl.ds(station * dpc, TILE), :]
    return cross(jnp.where(even, a, b), jnp.where(even, b, a))


def products(dpc, me, first_ref, second_ref, ins, hre, him):
    even = lax.rem(me, 2) == 0

    def pair(b, carry):
        p, q = first_ref[b], second_ref[b]
        for m in range(len(ins) // 2):
            pr, pi = piece_pair(dpc, even, ins, m, p)
            qr, qi = piece_pair(dpc, even, ins, m, q)
            hre[m, pl.ds(b * dpc, TILE), :] = pr * qr + pi * qi
            him[m, pl.ds(b * dpc, TILE), :] = pi * qr - pr * qi
        return carry

    lax.fori_loop(0, first_ref.shape[0], pair, 0)
    clear(dpc, first_ref.shape[0], hre, him)


def predict(dpc, b, acc, chips, model_ref, hre, him):
    acc_re, acc_im = acc
    for m, k in enumerate(chips):
        for dd in range(dpc):
            mr = model_ref[k * dpc + dd, 0, b].astype(F32)
            mi = model_ref[k * dpc + dd, 1, b].astype(F32)
            row = pl.ds(b * dpc + dd, 1)
            hr, hi = hre[m, row, :], him[m, row, :]
            acc_re = acc_re - (hr * mr - hi * mi)
            acc_im = acc_im - (hr * mi + hi * mr)
    return acc_re, acc_im


def weighted(b, acc, mask_ref):
    weight = mask_ref[b].astype(F32)
    return weight * acc[0], weight * acc[1]


def fold(a, b, step):
    if a is None:
        return None
    if b is None:
        return a + pltpu.roll(a, step, axis=0)
    mine = (lax.broadcasted_iota(jnp.int32, a.shape, 0) & step) == 0
    return jnp.where(mine, a, b) + pltpu.roll(jnp.where(mine, b, a), step, axis=0)


def row_sums(values):
    values = list(values) + [None] * (TILE - len(values))
    step = 1
    while step < TILE:
        values = [fold(a, b, step) for a, b in zip(values[::2], values[1::2])]
        step *= 2
    return values[0]


def tile_sum(x):
    total = x[:TILE]
    for t in range(1, x.shape[0] // TILE):
        total = total + x[t * TILE : (t + 1) * TILE]
    return total


def correlate(dpc, b, res, chips, model_ref, cre, cim):
    res_re, res_im = res
    for m, k in enumerate(chips):
        re, im = [], []
        for dd in range(dpc):
            mr = model_ref[k * dpc + dd, 0, b].astype(F32)
            mi = model_ref[k * dpc + dd, 1, b].astype(F32)
            re.append(tile_sum(mr * res_re + mi * res_im))
            im.append(tile_sum(mr * res_im - mi * res_re))
        cre[m, pl.ds(b * dpc, TILE), :] = row_sums(re)
        cim[m, pl.ds(b * dpc, TILE), :] = row_sums(im)


def write_sums(dpc, chips, cre, cim, tiles, power_ref, out_ref, start):
    for m, k in enumerate(chips):
        re, im, at = tiles(m)
        for t in range(ROWS * dpc // TILE):
            rows = slice(t * TILE, (t + 1) * TILE)
            w = power_ref[k, rows, :]
            x0, x1 = cross(cre[m, rows, :] + re[at, rows, :] * w, cim[m, rows, :] + im[at, rows, :] * w)
            out_ref[2 * k, rows, :] = x0
            out_ref[2 * k + 1, rows, :] = x1
        if start:
            for t in range(dpc):
                x0, x1 = cross(
                    power_ref[k, t * TILE : (t + 1) * TILE, :],
                    power_ref[k, (t + dpc) * TILE : (t + dpc + 1) * TILE, :],
                )
                rows = slice(ROWS * dpc + t * TILE, ROWS * dpc + (t + 1) * TILE)
                out_ref[2 * k, rows, :] = x0
                out_ref[2 * k + 1, rows, :] = x1


def first_pass_kernel(
    n, dpc, me_ref, first_ref, second_ref, model_hbm, vis_ref, mask_ref, power_ref, *rest
):
    ins, (out_ref, model_ref, sems, hre, him, cre, cim, stack) = rest[:n], rest[n:]
    fetch = Fetch(model_hbm, model_ref, sems)
    products_first(n, dpc, me_ref[0], first_ref, second_ref, ins, hre, him, stack)
    chips = range(n // 2)

    def pair(b, carry):
        acc = predict(dpc, b, (vis_ref[0, b], vis_ref[1, b]), chips, model_ref, hre, him)
        correlate(dpc, b, weighted(b, acc, mask_ref), chips, model_ref, cre, cim)
        return carry

    fetch.each(pair)

    clear(dpc, mask_ref.shape[0], cre, cim)
    write_sums(dpc, chips, cre, cim, lambda m: (hre, him, m), power_ref, out_ref, True)


OWN, NEAR, FAR = (0,), (1, 2, 6), (3, 4, 5, 7)


def chips_of(me, pairs):
    return [jnp.bitwise_xor(lax.div(me, 2), m) for m in pairs]


def early_kernel(n, dpc, pairs, me_ref, first_ref, second_ref, model_hbm, acc_in, handed, *rest):
    ins, (acc_ref, hre, him, handed_out, model_ref, sems) = rest[: 2 * len(pairs)], rest[2 * len(pairs) :]
    me = me_ref[0]
    fetch = Fetch(model_hbm, model_ref, sems, [k * dpc for k in chips_of(me, pairs)])
    handed_out[...] = handed[...]
    products(dpc, me, first_ref, second_ref, ins, hre, him)

    def pair(b, carry):
        acc = acc_in[0, b], acc_in[1, b]
        acc_ref[0, b], acc_ref[1, b] = predict(dpc, b, acc, range(len(pairs)), model_ref, hre, him)
        return carry

    fetch.each(pair)


def later_pass_kernel(
    n,
    dpc,
    me_ref,
    first_ref,
    second_ref,
    model_hbm,
    mask_ref,
    power_ref,
    acc_ref,
    own_re,
    own_im,
    near_re,
    near_im,
    *rest,
):
    ins, (out_ref, model_ref, sems, hre, him, cre, cim) = rest[: 2 * len(FAR)], rest[2 * len(FAR) :]
    fetch = Fetch(model_hbm, model_ref, sems)
    me = me_ref[0]
    products(dpc, me, first_ref, second_ref, ins, hre, him)
    far = chips_of(me, FAR)
    chips = chips_of(me, OWN + NEAR) + far

    def pair(b, carry):
        acc = predict(dpc, b, (acc_ref[0, b], acc_ref[1, b]), far, model_ref, hre, him)
        correlate(dpc, b, weighted(b, acc, mask_ref), chips, model_ref, cre, cim)
        return carry

    fetch.each(pair)

    def tiles(m):
        for re, im, pairs in ((own_re, own_im, OWN), (near_re, near_im, NEAR), (hre, him, FAR)):
            if m < len(pairs):
                return re, im, m
            m -= len(pairs)

    clear(dpc, mask_ref.shape[0], cre, cim)
    write_sums(dpc, chips, cre, cim, tiles, power_ref, out_ref, False)


def last_kernel(n, dpc, me_ref, first_ref, second_ref, model_hbm, mask_ref, acc_ref, *rest):
    ins, (res_ref, gains_ref, model_ref, sems, hre, him) = rest[:n], rest[n:]
    me = me_ref[0]
    fetch = Fetch(model_hbm, model_ref, sems, [k * dpc for k in chips_of(me, FAR)])
    products(dpc, me, first_ref, second_ref, ins[: 2 * len(FAR)], hre, him)
    per = STATIONS // n
    even = lax.rem(me, 2) == 0
    for m, k in enumerate(chips_of(me, FAR + NEAR + OWN)):
        for s in range(per):
            re, im = piece_pair(dpc, even, ins, m, me * per + s)
            for dd in range(dpc):
                at = s * SOURCE_COUNT + k * dpc + dd
                gains_ref[0, pl.ds(at, 1), :] = re[dd : dd + 1]
                gains_ref[1, pl.ds(at, 1), :] = im[dd : dd + 1]

    def pair(b, carry):
        acc = acc_ref[0, b], acc_ref[1, b]
        acc = predict(dpc, b, acc, range(len(FAR)), model_ref, hre, him)
        res_ref[0, b], res_ref[1, b] = weighted(b, acc, mask_ref)
        return carry

    fetch.each(pair)


SMEM = pl.BlockSpec(memory_space=pltpu.SMEM)
VMEM = pl.BlockSpec(memory_space=pltpu.VMEM)
HBM = pl.BlockSpec(memory_space=pltpu.HBM)


def shape(*dims, dtype=F32):
    return jax.ShapeDtypeStruct(dims, dtype)


def exchange(x):
    return lax.all_to_all(x, "bl", split_axis=0, concat_axis=0, tiled=True)


def gather(n, piece, beside, early=None):
    def send(x, o):
        return lax.ppermute(x, "bl", [(i, i ^ o) for i in range(n)])

    got = {0: piece}
    got[12], got[2], got[4], got[1] = (send(piece, o) for o in (12, 2, 4, 1))
    got[8] = send(early(piece, got), 8) if early else send(got[12], 4)
    got[6], got[14], got[10] = send(got[4], 2), send(got[12], 2), send(got[8], 2)
    for o in (2, 4, 12, 6, 14, 8, 10):
        if o == 6:
            got[o] = beside(got[o], got)
        got[o + 1] = send(got[o], 1)
    return [got[o] for o in range(n)]


def fast_body(n, vis, model, mask, first, second, gre, gim):
    model, gre, gim = (pltpu.with_memory_space_constraint(x, pltpu.HBM) for x in (model, gre, gim))
    dpc = SOURCE_COUNT // (n // 2)
    width = dpc * 128
    pairs, times, channels = mask.shape
    me = lax.axis_index("bl").astype(jnp.int32).reshape(1)
    params = pltpu.CompilerParams(vmem_limit_bytes=VMEM_LIMIT)
    plane = (n // 2, ROWS * dpc + TILE, channels)
    half = (len(FAR), ROWS * dpc + TILE, channels)
    lots = n * 2 * ROWS
    mine = (STATIONS * dpc + TILE, channels)
    sems = pltpu.SemaphoreType.DMA((len(PARTS), n // 4))
    held = [pltpu.VMEM(model.shape, BF16), sems]
    held_half = [pltpu.VMEM((SOURCE_COUNT // 2,) + model.shape[1:], BF16), sems]

    def call(kernel, args, outs, scratch=(), micros=1, aliases={}):
        def place(x):
            if x is model or x is gre or x is gim:
                return HBM
            return SMEM if x.ndim == 1 else VMEM

        return pl.pallas_call(
            functools.partial(kernel, n, dpc),
            in_specs=[place(x) for x in args],
            out_specs=[VMEM for o in outs],
            out_shape=outs,
            scratch_shapes=[pltpu.VMEM(x, F32) if isinstance(x, tuple) else x for x in scratch],
            compiler_params=params,
            input_output_aliases=aliases,
            cost_estimate=pl.CostEstimate(
                flops=0, bytes_accessed=int(micros * 3.69e6), transcendentals=0
            ),
        )(*args)

    (piece,) = call(
        pack_kernel,
        (first, second, gre, gim),
        [shape(2 * gre.shape[0] + TILE, channels)],
        [pltpu.SemaphoreType.DMA((2,))],
    )
    power = None

    def powers_beside(x, got):
        nonlocal power
        power, x = call(
            power_kernel, (model, mask, x), [shape(*plane), shape(*x.shape)], held, micros=20, aliases={2: 1}
        )
        return x

    got = gather(n, piece, powers_beside)
    g, onehot = call(
        first_own_kernel,
        (me, *got),
        [shape(*mine), shape(STATIONS, lots, dtype=BF16)],
        [(STATIONS * TILE, channels), (n, channels)],
        micros=2,
    )
    (sums,) = call(
        first_pass_kernel,
        (me, first, second, model, vis, mask, power, *got),
        [shape(n, (ROWS + TILE) * dpc, channels)],
        held + [plane] * 4 + [(n,) + piece.shape],
        micros=9,
    )
    powers = exchange(sums)
    (g,) = call(
        own_kernel,
        (g, onehot, powers),
        [shape(*mine)],
        [(lots, 2 * width), (lots, width)],
    )

    def slots(got, pairs):
        return [got[2 * m + c] for m in pairs for c in (0, 1)]

    def gather_near(g):
        acc, products = vis, []

        def work(pairs):
            def beside(x, got):
                nonlocal acc
                args = (me, first, second, model, acc, x, *slots(got, pairs))
                size = (len(pairs),) + plane[1:]
                outs = [shape(*vis.shape), shape(*size), shape(*size), shape(*x.shape)]
                part = pltpu.VMEM((len(pairs) * dpc,) + model.shape[1:], BF16)
                kernel = lambda n, dpc, *refs: early_kernel(n, dpc, pairs, *refs)
                acc, re, im, x = call(kernel, args, outs, [part, sems])
                products.extend([re, im])
                return x

            return beside

        got = gather(n, g, work(NEAR), work(OWN))
        return acc, products, slots(got, FAR + NEAR + OWN)

    for step in range(1, ITERS):
        acc, products, got = gather_near(g)
        (den,) = call(
            prepare_kernel,
            (g, onehot, powers),
            [shape(STATIONS, width)],
            [(lots, width)] * 2,
            micros=2,
        )
        (sums,) = call(
            later_pass_kernel,
            (me, first, second, model, mask, power, acc, *products, *got[: 2 * len(FAR)]),
            [shape(n, ROWS * dpc, channels)],
            held + [half] * 2 + [plane] * 2,
            micros=7,
        )
        sums = exchange(sums)
        (g,) = call(
            later_own_kernel,
            (g, onehot, den, sums),
            [shape(*mine)],
            [(lots, width)] * 2,
        )
    acc, products, got = gather_near(g)
    residual, gains = call(
        last_kernel,
        (me, first, second, model, mask, acc, *got),
        [shape(*vis.shape), shape(2, *gre.shape)],
        held_half + [half] * 2,
        micros=4,
    )
    return gains, residual


def block_pass(full_re, full_im, vis_blk, coh_blk, weight, first, second, want_sums):
    ar = jnp.transpose(full_re[first], (1, 0, 2))
    ai = jnp.transpose(full_im[first], (1, 0, 2))
    br = jnp.transpose(full_re[second], (1, 0, 2))
    bi = jnp.transpose(full_im[second], (1, 0, 2))
    mr = coh_blk[:, 0].astype(F32)
    mi = coh_blk[:, 1].astype(F32)
    hr = ar * br + ai * bi
    hi = ai * br - ar * bi
    hr_t, hi_t = hr[:, :, None], hi[:, :, None]
    res_re = weight * (vis_blk[0] - jnp.sum(hr_t * mr - hi_t * mi, 0))
    res_im = weight * (vis_blk[1] - jnp.sum(hr_t * mi + hi_t * mr, 0))
    residual = jnp.stack([res_re, res_im])
    if not want_sums:
        return (residual, None)
    power = jnp.sum(weight[None] * (mr * mr + mi * mi), 2)
    sum_re = jnp.sum(mr * res_re + mi * res_im, 2) + hr * power
    sum_im = jnp.sum(mr * res_im - mi * res_re, 2) + hi * power
    terms_first = jnp.stack([br * sum_re - bi * sum_im, br * sum_im + bi * sum_re, power * (br * br + bi * bi)])
    terms_second = jnp.stack([ar * sum_re + ai * sum_im, ai * sum_re - ar * sum_im, power * (ar * ar + ai * ai)])
    stations = jnp.arange(STATIONS, dtype=jnp.int32)
    onehot_first = (first[:, None] == stations[None, :]).astype(F32)
    onehot_second = (second[:, None] == stations[None, :]).astype(F32)
    exact = lax.Precision.HIGHEST
    sums = jnp.einsum("bs,cdbf->csdf", onehot_first, terms_first, precision=exact)
    sums = sums + jnp.einsum("bs,cdbf->csdf", onehot_second, terms_second, precision=exact)
    return (residual, sums)


def plain_body(vis, model, mask, first, second, gre, gim):
    weight = mask.astype(F32)
    rows, channels = gre.shape
    shaped = (STATIONS, SOURCE_COUNT, channels)
    full_re = lax.all_gather(gre, "bl", axis=0, tiled=True).reshape(shaped)
    full_im = lax.all_gather(gim, "bl", axis=0, tiled=True).reshape(shaped)
    for step in range(ITERS):
        unused, sums = block_pass(full_re, full_im, vis, model, weight, first, second, True)
        totals = lax.psum(sums, "bl")
        denom = totals[2] + ridge
        full_re = 0.5 * (full_re + totals[0] / denom)
        full_im = 0.5 * (full_im + totals[1] / denom)
    residual, unused = block_pass(full_re, full_im, vis, model, weight, first, second, False)
    both = jnp.stack([full_re, full_im]).reshape(2, STATIONS * SOURCE_COUNT, channels)
    return lax.dynamic_slice_in_dim(both, lax.axis_index("bl") * rows, rows, 1), residual


def solution(mesh):
    n = mesh.shape["bl"]
    split = n == 16

    def body(vis, model, mask, first, second, gre, gim):
        if split and mask.shape[0] <= ROWS:
            return fast_body(n, vis, model, mask, first, second, gre, gim)
        return plain_body(vis, model, mask, first, second, gre, gim)

    in_specs = (
        P(None, ("grp", "bl"), None, None),
        P(None, None, ("grp", "bl"), None, None),
        P(("grp", "bl"), None, None),
        P(("grp", "bl")),
        P(("grp", "bl")),
        P(("grp", "bl"), None),
        P(("grp", "bl"), None),
    )
    out_specs = (P(None, ("grp", "bl"), None), P(None, ("grp", "bl"), None, None))
    return jax.shard_map(body, mesh=mesh, in_specs=in_specs, out_specs=out_specs, check_vma=False)
```

```python
import functools

import jax
import jax.numpy as jnp
from jax import lax
from jax.experimental import pallas as pl
from jax.experimental.pallas import tpu as pltpu
from jax.sharding import PartitionSpec as P

STATIONS = 64
SOURCE_COUNT = 40
ITERS = 2
ROWS = 16

ridge = 1.0
F32 = jnp.float32
BF16 = jnp.bfloat16
VMEM_LIMIT = 24 * 1024 * 1024


def swap(x):
    return pltpu.roll(x, x.shape[-1] // 2, axis=x.ndim - 1)


def lower(shape):
    return lax.broadcasted_iota(jnp.int32, shape, len(shape) - 1) < shape[-1] // 2


def cross(a, b):
    lo = lower(a.shape)
    return jnp.where(lo, a, swap(b)), jnp.where(lo, swap(a), b)


def halves_of(x):
    hi = x.astype(BF16)
    return hi, (x - hi.astype(F32)).astype(BF16)


def pick(onehot, x, dims):
    return sum(
        lax.dot_general(onehot, part, (dims, ((), ())), preferred_element_type=F32)
        for part in halves_of(x)
    )


TILE = 8
PARTS = (1, 3, 7, ROWS)


def pack_kernel(n, dpc, first_ref, second_ref, re_ref, im_ref, out_ref, sems):
    rows = re_ref.shape[0]
    copies = [
        pltpu.make_async_copy(re_ref, out_ref.at[pl.ds(0, rows)], sems.at[0]),
        pltpu.make_async_copy(im_ref, out_ref.at[pl.ds(rows, rows)], sems.at[1]),
    ]
    for copy in copies:
        copy.start()
    lane = lax.broadcasted_iota(jnp.int32, (TILE, 128), 1)
    marks = jnp.zeros((TILE, 128), F32)
    for r in range(first_ref.shape[0]):
        marks = jnp.where(lane == r, (first_ref[r] + 1).astype(F32), marks)
        marks = jnp.where(lane == ROWS + r, (second_ref[r] + 1).astype(F32), marks)
    out_ref[2 * rows :] = marks
    for copy in copies:
        copy.wait()


class Fetch:
    def __init__(self, model, held, sems, firsts=(0,)):
        count, pairs = held.shape[0] // len(firsts), held.shape[2]
        self.copies = []
        self.ends = [0] + [min(end, pairs) for end in PARTS]
        for i in range(len(PARTS)):
            part = pl.ds(self.ends[i], self.ends[i + 1] - self.ends[i])
            self.copies.append([])
            for j, first in enumerate(firsts):
                self.copies[i].append(
                    pltpu.make_async_copy(
                        model.at[pl.ds(first, count), :, part],
                        held.at[pl.ds(j * count, count), :, part],
                        sems.at[i, j],
                    )
                )
        for copies in self.copies:
            for copy in copies:
                copy.start()

    def each(self, body):
        for i, copies in enumerate(self.copies):
            for copy in copies:
                copy.wait()
            lax.fori_loop(self.ends[i], self.ends[i + 1], body, 0)


def power_kernel(n, dpc, model_hbm, mask_ref, unused_in, out_ref, unused_out, model_ref, sems):
    fetch = Fetch(model_hbm, model_ref, sems)
    out_ref[...] = jnp.zeros_like(out_ref)

    def pair(b, carry):
        weight = mask_ref[b].astype(F32)
        for d in range(SOURCE_COUNT):
            mr = model_ref[d, 0, b].astype(F32)
            mi = model_ref[d, 1, b].astype(F32)
            row = pl.ds(b * dpc + d % dpc, 1)
            out_ref[d // dpc, row, :] = jnp.sum(weight * (mr * mr + mi * mi), axis=0, keepdims=True)
        return carry

    fetch.each(pair)


def wide(ref, dpc):
    return jnp.concatenate([ref[pl.ds(dd, STATIONS, stride=dpc), :] for dd in range(dpc)], axis=1)


def put(ref, value, dpc):
    for dd in range(dpc):
        ref[pl.ds(dd, STATIONS, stride=dpc), :] = value[:, dd * 128 : (dd + 1) * 128]
    ref[STATIONS * dpc :, :] = jnp.zeros((TILE, 128), F32)


def first_own_kernel(n, dpc, me_ref, *rest):
    ins, (g_ref, onehot_ref, split, lines) = rest[:n], rest[n:]
    me = me_ref[0]
    k, c = lax.div(me, 2), lax.rem(me, 2)
    per = STATIONS // n
    rows = per * SOURCE_COUNT
    for o in range(n):
        peer = jnp.bitwise_xor(me, o)
        lines[pl.ds(peer, 1), :] = ins[o][2 * rows : 2 * rows + 1, :]
        for s in range(per):
            at = s * SOURCE_COUNT + k * dpc
            x0, x1 = cross(ins[o][pl.ds(at, TILE), :], ins[o][pl.ds(rows + at, TILE), :])
            to = pl.multiple_of((peer * per + s) * TILE, TILE)
            split[pl.ds(to, TILE), :] = jnp.where(c == 0, x0, x1)
    g = jnp.concatenate([split[pl.ds(dd, STATIONS, stride=TILE), :] for dd in range(dpc)], axis=1)
    put(g_ref, g, dpc)
    across = 128 // (2 * ROWS)
    station = lax.broadcasted_iota(jnp.int32, (STATIONS, 128), 0)
    for group in range(n // across):
        marks = jnp.zeros((1, 128), F32)
        for i in range(across):
            row = lines[group * across + i : group * across + i + 1, :]
            marks = marks + (pltpu.roll(row, i * 2 * ROWS, axis=1) if i else row)
        hit = station + 1 == marks.astype(jnp.int32)
        onehot_ref[:, group * 128 : (group + 1) * 128] = jnp.where(hit, 1.0, 0.0).astype(BF16)


def fill_powers(n, dpc, sums, sel_ref, terms, base):
    lo = lower((TILE, 128))
    for o in range(n):
        r = o * 2 * ROWS
        for dd in range(dpc):
            cols = slice(dd * 128, (dd + 1) * 128)
            dcols = slice(base + dd * 128, base + (dd + 1) * 128)
            W = sums[o, pl.ds(ROWS * dpc + dd, TILE, stride=dpc), :]
            Wx = swap(W)
            W = jnp.concatenate([jnp.where(lo, W, Wx), jnp.where(lo, Wx, W)], 0)
            p = sel_ref[r : r + ROWS, cols]
            q = sel_ref[r + ROWS : r + 2 * ROWS, cols]
            p2, q2 = p * p, q * q
            terms[r : r + ROWS, dcols] = W * (q2 + swap(q2))
            terms[r + ROWS : r + 2 * ROWS, dcols] = W * (p2 + swap(p2))


def fill_sums(n, dpc, sums, sel_ref, terms):
    lo = lower((ROWS, 128))
    sign = jnp.where(lo, -1.0, 1.0)
    for o in range(n):
        r = o * 2 * ROWS
        for dd in range(dpc):
            cols = slice(dd * 128, (dd + 1) * 128)
            B = sums[o, pl.ds(dd, ROWS, stride=dpc), :]
            p = sel_ref[r : r + ROWS, cols]
            q = sel_ref[r + ROWS : r + 2 * ROWS, cols]
            Bx = swap(B)
            Brr, Bii = jnp.where(lo, B, Bx), sign * jnp.where(lo, Bx, B)
            terms[r : r + ROWS, cols] = Brr * q + Bii * swap(q)
            terms[r + ROWS : r + 2 * ROWS, cols] = Brr * p - Bii * swap(p)


def own_kernel(n, dpc, g_in, onehot_ref, sums, g_out, terms, sel_ref):
    width = dpc * 128
    sel_ref[...] = pick(onehot_ref[...], wide(g_in, dpc), ((0,), (0,)))
    fill_sums(n, dpc, sums, sel_ref, terms)
    fill_powers(n, dpc, sums, sel_ref, terms, width)
    total = pick(onehot_ref[...], terms[...], ((1,), (0,)))
    put(g_out, 0.5 * (wide(g_in, dpc) + total[:, :width] / (total[:, width:] + ridge)), dpc)


def prepare_kernel(n, dpc, g_ref, onehot_ref, sums, den_ref, terms, sel_ref):
    sel_ref[...] = pick(onehot_ref[...], wide(g_ref, dpc), ((0,), (0,)))
    fill_powers(n, dpc, sums, sel_ref, terms, 0)
    den_ref[...] = pick(onehot_ref[...], terms[...], ((1,), (0,))) + ridge


def later_own_kernel(n, dpc, g_in, onehot_ref, den_ref, sums, g_out, terms, sel_ref):
    sel_ref[...] = pick(onehot_ref[...], wide(g_in, dpc), ((0,), (0,)))
    fill_sums(n, dpc, sums, sel_ref, terms)
    total = pick(onehot_ref[...], terms[...], ((1,), (0,)))
    put(g_out, 0.5 * (wide(g_in, dpc) + total / den_ref[...]), dpc)


def clear(dpc, pairs, *refs):
    for ref in refs:
        chips, rows, _ = ref.shape
        for m in range(chips):
            ref[m, pairs * dpc :, :] = jnp.zeros((rows - pairs * dpc, 128), F32)


def products_first(n, dpc, me, first_ref, second_ref, ins, hre, him, stack):
    per = STATIONS // n
    rows = per * SOURCE_COUNT
    for o in range(n):
        stack[jnp.bitwise_xor(me, o)] = ins[o][...]

    def pair(b, carry):
        p, q = first_ref[b], second_ref[b]

        def block(station, k, part):
            at = lax.rem(station, per) * SOURCE_COUNT + k * dpc + part * rows
            return stack[lax.div(station, per), pl.ds(at, TILE), :]

        for k in range(n // 2):
            pr, pi, qr, qi = block(p, k, 0), block(p, k, 1), block(q, k, 0), block(q, k, 1)
            hre[k, pl.ds(b * dpc, TILE), :] = pr * qr + pi * qi
            him[k, pl.ds(b * dpc, TILE), :] = pi * qr - pr * qi
        return carry

    lax.fori_loop(0, first_ref.shape[0], pair, 0)
    clear(dpc, first_ref.shape[0], hre, him)


def piece_pair(dpc, even, ins, m, station):
    a = ins[2 * m][pl.ds(station * dpc, TILE), :]
    b = ins[2 * m + 1][pl.ds(station * dpc, TILE), :]
    return cross(jnp.where(even, a, b), jnp.where(even, b, a))


def products(dpc, me, first_ref, second_ref, ins, hre, him):
    even = lax.rem(me, 2) == 0

    def pair(b, carry):
        p, q = first_ref[b], second_ref[b]
        for m in range(len(ins) // 2):
            pr, pi = piece_pair(dpc, even, ins, m, p)
            qr, qi = piece_pair(dpc, even, ins, m, q)
            hre[m, pl.ds(b * dpc, TILE), :] = pr * qr + pi * qi
            him[m, pl.ds(b * dpc, TILE), :] = pi * qr - pr * qi
        return carry

    lax.fori_loop(0, first_ref.shape[0], pair, 0)
    clear(dpc, first_ref.shape[0], hre, him)


def predict(dpc, b, acc, chips, model_ref, hre, him):
    tiles = [slice(t, t + TILE) for t in range(0, acc[0].shape[0], TILE)]
    acc_re, acc_im = ([x[t] for t in tiles] for x in acc)
    for m, k in enumerate(chips):
        for dd in range(dpc):
            mr = model_ref[k * dpc + dd, 0, b].astype(F32)
            mi = model_ref[k * dpc + dd, 1, b].astype(F32)
            row = pl.ds(b * dpc + dd, TILE, stride=0)
            hr, hi = hre[m, row, :], him[m, row, :]
            for i, t in enumerate(tiles):
                acc_re[i] = acc_re[i] - (hr * mr[t] - hi * mi[t])
                acc_im[i] = acc_im[i] - (hr * mi[t] + hi * mr[t])
    return jnp.concatenate(acc_re, 0), jnp.concatenate(acc_im, 0)


def weighted(b, acc, mask_ref):
    weight = mask_ref[b].astype(F32)
    return weight * acc[0], weight * acc[1]


def fold(a, b, step):
    if a is None:
        return None
    if b is None:
        return a + pltpu.roll(a, step, axis=0)
    mine = (lax.broadcasted_iota(jnp.int32, a.shape, 0) & step) == 0
    return jnp.where(mine, a, b) + pltpu.roll(jnp.where(mine, b, a), step, axis=0)


def row_sums(values):
    values = list(values) + [None] * (TILE - len(values))
    step = 1
    while step < TILE:
        values = [fold(a, b, step) for a, b in zip(values[::2], values[1::2])]
        step *= 2
    return values[0]


def tile_sum(x):
    total = x[:TILE]
    for t in range(1, x.shape[0] // TILE):
        total = total + x[t * TILE : (t + 1) * TILE]
    return total


def correlate(dpc, b, res, chips, model_ref, cre, cim):
    res_re, res_im = res
    for m, k in enumerate(chips):
        re, im = [], []
        for dd in range(dpc):
            mr = model_ref[k * dpc + dd, 0, b].astype(F32)
            mi = model_ref[k * dpc + dd, 1, b].astype(F32)
            re.append(tile_sum(mr * res_re + mi * res_im))
            im.append(tile_sum(mr * res_im - mi * res_re))
        cre[m, pl.ds(b * dpc, TILE), :] = row_sums(re)
        cim[m, pl.ds(b * dpc, TILE), :] = row_sums(im)


def write_sums(dpc, chips, cre, cim, tiles, power_ref, out_ref, start):
    for m, k in enumerate(chips):
        re, im, at = tiles(m)
        for t in range(ROWS * dpc // TILE):
            rows = slice(t * TILE, (t + 1) * TILE)
            w = power_ref[k, rows, :]
            x0, x1 = cross(cre[m, rows, :] + re[at, rows, :] * w, cim[m, rows, :] + im[at, rows, :] * w)
            out_ref[2 * k, rows, :] = x0
            out_ref[2 * k + 1, rows, :] = x1
        if start:
            for t in range(dpc):
                x0, x1 = cross(
                    power_ref[k, t * TILE : (t + 1) * TILE, :],
                    power_ref[k, (t + dpc) * TILE : (t + dpc + 1) * TILE, :],
                )
                rows = slice(ROWS * dpc + t * TILE, ROWS * dpc + (t + 1) * TILE)
                out_ref[2 * k, rows, :] = x0
                out_ref[2 * k + 1, rows, :] = x1


def first_pass_kernel(
    n, dpc, me_ref, first_ref, second_ref, model_hbm, vis_ref, mask_ref, power_ref, *rest
):
    ins, (out_ref, model_ref, sems, hre, him, cre, cim, stack) = rest[:n], rest[n:]
    fetch = Fetch(model_hbm, model_ref, sems)
    products_first(n, dpc, me_ref[0], first_ref, second_ref, ins, hre, him, stack)
    chips = range(n // 2)

    def pair(b, carry):
        acc = predict(dpc, b, (vis_ref[0, b], vis_ref[1, b]), chips, model_ref, hre, him)
        correlate(dpc, b, weighted(b, acc, mask_ref), chips, model_ref, cre, cim)
        return carry

    fetch.each(pair)

    clear(dpc, mask_ref.shape[0], cre, cim)
    write_sums(dpc, chips, cre, cim, lambda m: (hre, him, m), power_ref, out_ref, True)


NEAR, FAR = (0, 1, 2, 6), (3, 4, 5, 7)


def chips_of(me, pairs):
    return [jnp.bitwise_xor(lax.div(me, 2), m) for m in pairs]


def early_kernel(n, dpc, me_ref, first_ref, second_ref, model_hbm, vis_ref, unused_in, *rest):
    ins, (acc_ref, hre, him, unused_out, model_ref, sems) = rest[: 2 * len(NEAR)], rest[2 * len(NEAR) :]
    me = me_ref[0]
    fetch = Fetch(model_hbm, model_ref, sems, [k * dpc for k in chips_of(me, NEAR)])
    products(dpc, me, first_ref, second_ref, ins, hre, him)

    def pair(b, carry):
        acc = vis_ref[0, b], vis_ref[1, b]
        acc_ref[0, b], acc_ref[1, b] = predict(dpc, b, acc, range(len(NEAR)), model_ref, hre, him)
        return carry

    fetch.each(pair)


def later_pass_kernel(
    n,
    dpc,
    me_ref,
    first_ref,
    second_ref,
    model_hbm,
    mask_ref,
    power_ref,
    acc_ref,
    near_re,
    near_im,
    *rest,
):
    ins, (out_ref, model_ref, sems, hre, him, cre, cim) = rest[: 2 * len(FAR)], rest[2 * len(FAR) :]
    fetch = Fetch(model_hbm, model_ref, sems)
    me = me_ref[0]
    products(dpc, me, first_ref, second_ref, ins, hre, him)
    far = chips_of(me, FAR)
    chips = chips_of(me, NEAR) + far

    def pair(b, carry):
        acc = predict(dpc, b, (acc_ref[0, b], acc_ref[1, b]), far, model_ref, hre, him)
        correlate(dpc, b, weighted(b, acc, mask_ref), chips, model_ref, cre, cim)
        return carry

    fetch.each(pair)

    def tiles(m):
        for re, im, pairs in ((near_re, near_im, NEAR), (hre, him, FAR)):
            if m < len(pairs):
                return re, im, m
            m -= len(pairs)

    clear(dpc, mask_ref.shape[0], cre, cim)
    write_sums(dpc, chips, cre, cim, tiles, power_ref, out_ref, False)


def last_kernel(n, dpc, me_ref, first_ref, second_ref, model_hbm, mask_ref, acc_ref, *rest):
    ins, (res_ref, gains_ref, model_ref, sems, hre, him) = rest[:n], rest[n:]
    me = me_ref[0]
    fetch = Fetch(model_hbm, model_ref, sems, [k * dpc for k in chips_of(me, FAR)])
    products(dpc, me, first_ref, second_ref, ins[: 2 * len(FAR)], hre, him)
    per = STATIONS // n
    even = lax.rem(me, 2) == 0
    for m, k in enumerate(chips_of(me, FAR + NEAR)):
        for s in range(per):
            re, im = piece_pair(dpc, even, ins, m, me * per + s)
            for dd in range(dpc):
                at = s * SOURCE_COUNT + k * dpc + dd
                gains_ref[0, pl.ds(at, 1), :] = re[dd : dd + 1]
                gains_ref[1, pl.ds(at, 1), :] = im[dd : dd + 1]

    def pair(b, carry):
        acc = acc_ref[0, b], acc_ref[1, b]
        acc = predict(dpc, b, acc, range(len(FAR)), model_ref, hre, him)
        res_ref[0, b], res_ref[1, b] = weighted(b, acc, mask_ref)
        return carry

    fetch.each(pair)


SMEM = pl.BlockSpec(memory_space=pltpu.SMEM)
VMEM = pl.BlockSpec(memory_space=pltpu.VMEM)
HBM = pl.BlockSpec(memory_space=pltpu.HBM)


def shape(*dims, dtype=F32):
    return jax.ShapeDtypeStruct(dims, dtype)


def exchange(x):
    return lax.all_to_all(x, "bl", split_axis=0, concat_axis=0, tiled=True)


def gather(n, piece, beside):
    def send(x, o):
        return lax.ppermute(x, "bl", [(i, i ^ o) for i in range(n)])

    got = {0: piece}
    got[12], got[2], got[4], got[1] = (send(piece, o) for o in (12, 2, 4, 1))
    got[8] = send(got[12], 4)
    got[6], got[14], got[10] = send(got[4], 2), send(got[12], 2), send(got[8], 2)
    for o in (2, 4, 12, 6, 14, 8, 10):
        if o == 6:
            got[o] = beside(got[o], got)
        got[o + 1] = send(got[o], 1)
    return [got[o] for o in range(n)]


def fast_body(n, vis, model, mask, first, second, gre, gim):
    model, gre, gim = (pltpu.with_memory_space_constraint(x, pltpu.HBM) for x in (model, gre, gim))
    dpc = SOURCE_COUNT // (n // 2)
    width = dpc * 128
    pairs, times, channels = mask.shape
    me = lax.axis_index("bl").astype(jnp.int32).reshape(1)
    params = pltpu.CompilerParams(vmem_limit_bytes=VMEM_LIMIT)
    plane = (n // 2, ROWS * dpc + TILE, channels)
    half = (len(FAR), ROWS * dpc + TILE, channels)
    lots = n * 2 * ROWS
    mine = (STATIONS * dpc + TILE, channels)
    sems = pltpu.SemaphoreType.DMA((len(PARTS), n // 4))
    held = [pltpu.VMEM(model.shape, BF16), sems]
    held_half = [pltpu.VMEM((SOURCE_COUNT // 2,) + model.shape[1:], BF16), sems]

    def call(kernel, args, outs, scratch=(), micros=1, aliases={}):
        def place(x):
            if x is model or x is gre or x is gim:
                return HBM
            return SMEM if x.ndim == 1 else VMEM

        return pl.pallas_call(
            functools.partial(kernel, n, dpc),
            in_specs=[place(x) for x in args],
            out_specs=[VMEM for o in outs],
            out_shape=outs,
            scratch_shapes=[pltpu.VMEM(x, F32) if isinstance(x, tuple) else x for x in scratch],
            compiler_params=params,
            input_output_aliases=aliases,
            cost_estimate=pl.CostEstimate(
                flops=0, bytes_accessed=int(micros * 3.69e6), transcendentals=0
            ),
        )(*args)

    (piece,) = call(
        pack_kernel,
        (first, second, gre, gim),
        [shape(2 * gre.shape[0] + TILE, channels)],
        [pltpu.SemaphoreType.DMA((2,))],
    )
    power = None

    def powers_beside(x, got):
        nonlocal power
        power, x = call(
            power_kernel, (model, mask, x), [shape(*plane), shape(*x.shape)], held, micros=20, aliases={2: 1}
        )
        return x

    got = gather(n, piece, powers_beside)
    g, onehot = call(
        first_own_kernel,
        (me, *got),
        [shape(*mine), shape(STATIONS, lots, dtype=BF16)],
        [(STATIONS * TILE, channels), (n, channels)],
        micros=2,
    )
    (sums,) = call(
        first_pass_kernel,
        (me, first, second, model, vis, mask, power, *got),
        [shape(n, (ROWS + TILE) * dpc, channels)],
        held + [plane] * 4 + [(n,) + piece.shape],
        micros=9,
    )
    powers = exchange(sums)
    (g,) = call(
        own_kernel,
        (g, onehot, powers),
        [shape(*mine)],
        [(lots, 2 * width), (lots, width)],
    )

    def slots(got, pairs):
        return [got[2 * m + c] for m in pairs for c in (0, 1)]

    def gather_near(g):
        near = None

        def beside(x, got):
            nonlocal near
            args = (me, first, second, model, vis, x, *slots(got, NEAR))
            outs = [shape(*vis.shape), shape(*half), shape(*half), shape(*x.shape)]
            *near, x = call(early_kernel, args, outs, held_half, aliases={5: 3})
            return x

        got = gather(n, g, beside)
        return near, slots(got, FAR + NEAR)

    for step in range(1, ITERS):
        near, got = gather_near(g)
        (den,) = call(
            prepare_kernel,
            (g, onehot, powers),
            [shape(STATIONS, width)],
            [(lots, width)] * 2,
            micros=2,
        )
        (sums,) = call(
            later_pass_kernel,
            (me, first, second, model, mask, power, *near, *got[: 2 * len(FAR)]),
            [shape(n, ROWS * dpc, channels)],
            held + [half] * 2 + [plane] * 2,
            micros=7,
        )
        sums = exchange(sums)
        (g,) = call(
            later_own_kernel,
            (g, onehot, den, sums),
            [shape(*mine)],
            [(lots, width)] * 2,
        )
    near, got = gather_near(g)
    residual, gains = call(
        last_kernel,
        (me, first, second, model, mask, near[0], *got),
        [shape(*vis.shape), shape(2, *gre.shape)],
        held_half + [half] * 2,
        micros=4,
    )
    return gains, residual


def block_pass(full_re, full_im, vis_blk, coh_blk, weight, first, second, want_sums):
    ar = jnp.transpose(full_re[first], (1, 0, 2))
    ai = jnp.transpose(full_im[first], (1, 0, 2))
    br = jnp.transpose(full_re[second], (1, 0, 2))
    bi = jnp.transpose(full_im[second], (1, 0, 2))
    mr = coh_blk[:, 0].astype(F32)
    mi = coh_blk[:, 1].astype(F32)
    hr = ar * br + ai * bi
    hi = ai * br - ar * bi
    hr_t, hi_t = hr[:, :, None], hi[:, :, None]
    res_re = weight * (vis_blk[0] - jnp.sum(hr_t * mr - hi_t * mi, 0))
    res_im = weight * (vis_blk[1] - jnp.sum(hr_t * mi + hi_t * mr, 0))
    residual = jnp.stack([res_re, res_im])
    if not want_sums:
        return (residual, None)
    power = jnp.sum(weight[None] * (mr * mr + mi * mi), 2)
    sum_re = jnp.sum(mr * res_re + mi * res_im, 2) + hr * power
    sum_im = jnp.sum(mr * res_im - mi * res_re, 2) + hi * power
    terms_first = jnp.stack([br * sum_re - bi * sum_im, br * sum_im + bi * sum_re, power * (br * br + bi * bi)])
    terms_second = jnp.stack([ar * sum_re + ai * sum_im, ai * sum_re - ar * sum_im, power * (ar * ar + ai * ai)])
    stations = jnp.arange(STATIONS, dtype=jnp.int32)
    onehot_first = (first[:, None] == stations[None, :]).astype(F32)
    onehot_second = (second[:, None] == stations[None, :]).astype(F32)
    exact = lax.Precision.HIGHEST
    sums = jnp.einsum("bs,cdbf->csdf", onehot_first, terms_first, precision=exact)
    sums = sums + jnp.einsum("bs,cdbf->csdf", onehot_second, terms_second, precision=exact)
    return (residual, sums)


def plain_body(vis, model, mask, first, second, gre, gim):
    weight = mask.astype(F32)
    rows, channels = gre.shape
    shaped = (STATIONS, SOURCE_COUNT, channels)
    full_re = lax.all_gather(gre, "bl", axis=0, tiled=True).reshape(shaped)
    full_im = lax.all_gather(gim, "bl", axis=0, tiled=True).reshape(shaped)
    for step in range(ITERS):
        unused, sums = block_pass(full_re, full_im, vis, model, weight, first, second, True)
        totals = lax.psum(sums, "bl")
        denom = totals[2] + ridge
        full_re = 0.5 * (full_re + totals[0] / denom)
        full_im = 0.5 * (full_im + totals[1] / denom)
    residual, unused = block_pass(full_re, full_im, vis, model, weight, first, second, False)
    both = jnp.stack([full_re, full_im]).reshape(2, STATIONS * SOURCE_COUNT, channels)
    return lax.dynamic_slice_in_dim(both, lax.axis_index("bl") * rows, rows, 1), residual


def solution(mesh):
    n = mesh.shape["bl"]
    split = n == 16

    def body(vis, model, mask, first, second, gre, gim):
        if split and mask.shape[0] <= ROWS:
            return fast_body(n, vis, model, mask, first, second, gre, gim)
        return plain_body(vis, model, mask, first, second, gre, gim)

    in_specs = (
        P(None, ("grp", "bl"), None, None),
        P(None, None, ("grp", "bl"), None, None),
        P(("grp", "bl"), None, None),
        P(("grp", "bl")),
        P(("grp", "bl")),
        P(("grp", "bl"), None),
        P(("grp", "bl"), None),
    )
    out_specs = (P(None, ("grp", "bl"), None), P(None, ("grp", "bl"), None, None))
    return jax.shard_map(body, mesh=mesh, in_specs=in_specs, out_specs=out_specs, check_vma=False)
```

```python
import functools

import jax
import jax.numpy as jnp
from jax import lax
from jax.experimental import pallas as pl
from jax.experimental.pallas import tpu as pltpu
from jax.sharding import PartitionSpec as P

STATIONS = 64
SOURCE_COUNT = 40
ITERS = 2
ROWS = 16

ridge = 1.0
F32 = jnp.float32
BF16 = jnp.bfloat16
VMEM_LIMIT = 16 * 1024 * 1024


def swap(x):
    return pltpu.roll(x, x.shape[-1] // 2, axis=x.ndim - 1)


def lower(shape):
    return lax.broadcasted_iota(jnp.int32, shape, len(shape) - 1) < shape[-1] // 2


def cross(a, b):
    lo = lower(a.shape)
    return jnp.where(lo, a, swap(b)), jnp.where(lo, swap(a), b)


def halves_of(x):
    hi = x.astype(BF16)
    return hi, (x - hi.astype(F32)).astype(BF16)


def pick(onehot, x, dims):
    return sum(
        lax.dot_general(onehot, part, (dims, ((), ())), preferred_element_type=F32)
        for part in halves_of(x)
    )


TILE = 8
PARTS = (1, 2, 4, 6, 8, 10, 12, ROWS)


def pack_kernel(n, dpc, first_ref, second_ref, re_ref, im_ref, out_ref, sems):
    rows = re_ref.shape[0]
    copies = [
        pltpu.make_async_copy(re_ref, out_ref.at[pl.ds(0, rows)], sems.at[0]),
        pltpu.make_async_copy(im_ref, out_ref.at[pl.ds(rows, rows)], sems.at[1]),
    ]
    for copy in copies:
        copy.start()
    lane = lax.broadcasted_iota(jnp.int32, (TILE, 128), 1)
    marks = jnp.zeros((TILE, 128), F32)
    for r in range(first_ref.shape[0]):
        marks = jnp.where(lane == r, (first_ref[r] + 1).astype(F32), marks)
        marks = jnp.where(lane == ROWS + r, (second_ref[r] + 1).astype(F32), marks)
    out_ref[2 * rows :] = marks
    for copy in copies:
        copy.wait()


class Fetch:
    def __init__(self, model, held, sems):
        pairs = held.shape[2]
        self.ends = [0] + [min(end, pairs) for end in PARTS]
        self.copies = []
        for i in range(len(PARTS)):
            part = pl.ds(self.ends[i], self.ends[i + 1] - self.ends[i])
            self.copies.append(
                pltpu.make_async_copy(model.at[:, :, part], held.at[:, :, part], sems.at[i])
            )
        for copy in self.copies:
            copy.start()

    def each(self, body):
        for i, copy in enumerate(self.copies):
            copy.wait()
            lax.fori_loop(self.ends[i], self.ends[i + 1], body, 0)


def power_kernel(n, dpc, model_hbm, mask_ref, unused_in, out_ref, unused_out, model_ref, sems):
    fetch = Fetch(model_hbm, model_ref, sems)
    out_ref[...] = jnp.zeros_like(out_ref)

    def pair(b, carry):
        weight = mask_ref[b].astype(F32)
        for d in range(SOURCE_COUNT):
            mr = model_ref[d, 0, b].astype(F32)
            mi = model_ref[d, 1, b].astype(F32)
            row = pl.ds(b * dpc + d % dpc, 1)
            out_ref[d // dpc, row, :] = jnp.sum(weight * (mr * mr + mi * mi), axis=0, keepdims=True)
        return carry

    fetch.each(pair)


def wide(ref, dpc):
    return jnp.concatenate([ref[pl.ds(dd, STATIONS, stride=dpc), :] for dd in range(dpc)], axis=1)


def put(ref, value, dpc):
    for dd in range(dpc):
        ref[pl.ds(dd, STATIONS, stride=dpc), :] = value[:, dd * 128 : (dd + 1) * 128]
    ref[STATIONS * dpc :, :] = jnp.zeros((TILE, 128), F32)


def first_own_kernel(n, dpc, me_ref, *rest):
    ins, (g_ref, onehot_ref, split, lines) = rest[:n], rest[n:]
    me = me_ref[0]
    k, c = lax.div(me, 2), lax.rem(me, 2)
    per = STATIONS // n
    rows = per * SOURCE_COUNT
    for o in range(n):
        peer = jnp.bitwise_xor(me, o)
        lines[pl.ds(peer, 1), :] = ins[o][2 * rows : 2 * rows + 1, :]
        for s in range(per):
            at = s * SOURCE_COUNT + k * dpc
            x0, x1 = cross(ins[o][pl.ds(at, TILE), :], ins[o][pl.ds(rows + at, TILE), :])
            to = pl.multiple_of((peer * per + s) * TILE, TILE)
            split[pl.ds(to, TILE), :] = jnp.where(c == 0, x0, x1)
    g = jnp.concatenate([split[pl.ds(dd, STATIONS, stride=TILE), :] for dd in range(dpc)], axis=1)
    put(g_ref, g, dpc)
    across = 128 // (2 * ROWS)
    station = lax.broadcasted_iota(jnp.int32, (STATIONS, 128), 0)
    for group in range(n // across):
        marks = jnp.zeros((1, 128), F32)
        for i in range(across):
            row = lines[group * across + i : group * across + i + 1, :]
            marks = marks + (pltpu.roll(row, i * 2 * ROWS, axis=1) if i else row)
        hit = station + 1 == marks.astype(jnp.int32)
        onehot_ref[:, group * 128 : (group + 1) * 128] = jnp.where(hit, 1.0, 0.0).astype(BF16)


def fill_powers(n, dpc, sums, sel_ref, terms, base):
    lo = lower((TILE, 128))
    for o in range(n):
        r = o * 2 * ROWS
        for dd in range(dpc):
            cols = slice(dd * 128, (dd + 1) * 128)
            dcols = slice(base + dd * 128, base + (dd + 1) * 128)
            W = sums[o, pl.ds(ROWS * dpc + dd, TILE, stride=dpc), :]
            Wx = swap(W)
            W = jnp.concatenate([jnp.where(lo, W, Wx), jnp.where(lo, Wx, W)], 0)
            p = sel_ref[r : r + ROWS, cols]
            q = sel_ref[r + ROWS : r + 2 * ROWS, cols]
            p2, q2 = p * p, q * q
            terms[r : r + ROWS, dcols] = W * (q2 + swap(q2))
            terms[r + ROWS : r + 2 * ROWS, dcols] = W * (p2 + swap(p2))


def fill_sums(n, dpc, sums, sel_ref, terms):
    lo = lower((ROWS, 128))
    sign = jnp.where(lo, -1.0, 1.0)
    for o in range(n):
        r = o * 2 * ROWS
        for dd in range(dpc):
            cols = slice(dd * 128, (dd + 1) * 128)
            B = sums[o, pl.ds(dd, ROWS, stride=dpc), :]
            p = sel_ref[r : r + ROWS, cols]
            q = sel_ref[r + ROWS : r + 2 * ROWS, cols]
            Bx = swap(B)
            Brr, Bii = jnp.where(lo, B, Bx), sign * jnp.where(lo, Bx, B)
            terms[r : r + ROWS, cols] = Brr * q + Bii * swap(q)
            terms[r + ROWS : r + 2 * ROWS, cols] = Brr * p - Bii * swap(p)


def own_kernel(n, dpc, g_in, onehot_ref, sums, g_out, terms, sel_ref):
    width = dpc * 128
    sel_ref[...] = pick(onehot_ref[...], wide(g_in, dpc), ((0,), (0,)))
    fill_sums(n, dpc, sums, sel_ref, terms)
    fill_powers(n, dpc, sums, sel_ref, terms, width)
    total = pick(onehot_ref[...], terms[...], ((1,), (0,)))
    put(g_out, 0.5 * (wide(g_in, dpc) + total[:, :width] / (total[:, width:] + ridge)), dpc)


def prepare_kernel(n, dpc, g_ref, onehot_ref, sums, den_ref, terms, sel_ref):
    sel_ref[...] = pick(onehot_ref[...], wide(g_ref, dpc), ((0,), (0,)))
    fill_powers(n, dpc, sums, sel_ref, terms, 0)
    den_ref[...] = pick(onehot_ref[...], terms[...], ((1,), (0,))) + ridge


def later_own_kernel(n, dpc, g_in, onehot_ref, den_ref, sums, g_out, terms, sel_ref):
    sel_ref[...] = pick(onehot_ref[...], wide(g_in, dpc), ((0,), (0,)))
    fill_sums(n, dpc, sums, sel_ref, terms)
    total = pick(onehot_ref[...], terms[...], ((1,), (0,)))
    put(g_out, 0.5 * (wide(g_in, dpc) + total / den_ref[...]), dpc)


def clear(dpc, pairs, *refs):
    for ref in refs:
        chips, rows, _ = ref.shape
        for m in range(chips):
            ref[m, pairs * dpc :, :] = jnp.zeros((rows - pairs * dpc, 128), F32)


def products_first(n, dpc, me, first_ref, second_ref, ins, hre, him, stack):
    per = STATIONS // n
    rows = per * SOURCE_COUNT
    for o in range(n):
        stack[jnp.bitwise_xor(me, o)] = ins[o][...]

    def pair(b, carry):
        p, q = first_ref[b], second_ref[b]

        def block(station, k, part):
            at = lax.rem(station, per) * SOURCE_COUNT + k * dpc + part * rows
            return stack[lax.div(station, per), pl.ds(at, TILE), :]

        for k in range(n // 2):
            pr, pi, qr, qi = block(p, k, 0), block(p, k, 1), block(q, k, 0), block(q, k, 1)
            hre[k, pl.ds(b * dpc, TILE), :] = pr * qr + pi * qi
            him[k, pl.ds(b * dpc, TILE), :] = pi * qr - pr * qi
        return carry

    lax.fori_loop(0, first_ref.shape[0], pair, 0)
    clear(dpc, first_ref.shape[0], hre, him)


def piece_pair(dpc, even, ins, m, station):
    a = ins[2 * m][pl.ds(station * dpc, TILE), :]
    b = ins[2 * m + 1][pl.ds(station * dpc, TILE), :]
    return cross(jnp.where(even, a, b), jnp.where(even, b, a))


def products(dpc, me, first_ref, second_ref, ins, hre, him):
    even = lax.rem(me, 2) == 0

    def pair(b, carry):
        p, q = first_ref[b], second_ref[b]
        for m in range(len(ins) // 2):
            pr, pi = piece_pair(dpc, even, ins, m, p)
            qr, qi = piece_pair(dpc, even, ins, m, q)
            hre[m, pl.ds(b * dpc, TILE), :] = pr * qr + pi * qi
            him[m, pl.ds(b * dpc, TILE), :] = pi * qr - pr * qi
        return carry

    lax.fori_loop(0, first_ref.shape[0], pair, 0)
    clear(dpc, first_ref.shape[0], hre, him)


def predict(dpc, b, acc, chips, model_ref, hre, him):
    tiles = [slice(t, t + TILE) for t in range(0, acc[0].shape[0], TILE)]
    acc_re, acc_im = ([x[t] for t in tiles] for x in acc)
    for m, k in enumerate(chips):
        for dd in range(dpc):
            mr = model_ref[k * dpc + dd, 0, b].astype(F32)
            mi = model_ref[k * dpc + dd, 1, b].astype(F32)
            row = pl.ds(b * dpc + dd, TILE, stride=0)
            hr, hi = hre[m, row, :], him[m, row, :]
            for i, t in enumerate(tiles):
                acc_re[i] = acc_re[i] - (hr * mr[t] - hi * mi[t])
                acc_im[i] = acc_im[i] - (hr * mi[t] + hi * mr[t])
    return jnp.concatenate(acc_re, 0), jnp.concatenate(acc_im, 0)


def weighted(b, acc, mask_ref):
    weight = mask_ref[b].astype(F32)
    return weight * acc[0], weight * acc[1]


def fold(a, b, step):
    if a is None:
        return None
    if b is None:
        return a + pltpu.roll(a, step, axis=0)
    mine = (lax.broadcasted_iota(jnp.int32, a.shape, 0) & step) == 0
    return jnp.where(mine, a, b) + pltpu.roll(jnp.where(mine, b, a), step, axis=0)


def row_sums(values):
    values = list(values) + [None] * (TILE - len(values))
    step = 1
    while step < TILE:
        values = [fold(a, b, step) for a, b in zip(values[::2], values[1::2])]
        step *= 2
    return values[0]


def tile_sum(x):
    total = x[:TILE]
    for t in range(1, x.shape[0] // TILE):
        total = total + x[t * TILE : (t + 1) * TILE]
    return total


def correlate(dpc, b, res, chips, model_ref, cre, cim):
    res_re, res_im = res
    for m, k in enumerate(chips):
        re, im = [], []
        for dd in range(dpc):
            mr = model_ref[k * dpc + dd, 0, b].astype(F32)
            mi = model_ref[k * dpc + dd, 1, b].astype(F32)
            re.append(tile_sum(mr * res_re + mi * res_im))
            im.append(tile_sum(mr * res_im - mi * res_re))
        cre[m, pl.ds(b * dpc, TILE), :] = row_sums(re)
        cim[m, pl.ds(b * dpc, TILE), :] = row_sums(im)


def write_sums(dpc, chips, cre, cim, tiles, power_ref, out_ref, start):
    for m, k in enumerate(chips):
        re, im, at = tiles(m)
        for t in range(ROWS * dpc // TILE):
            rows = slice(t * TILE, (t + 1) * TILE)
            w = power_ref[k, rows, :]
            x0, x1 = cross(cre[m, rows, :] + re[at, rows, :] * w, cim[m, rows, :] + im[at, rows, :] * w)
            out_ref[2 * k, rows, :] = x0
            out_ref[2 * k + 1, rows, :] = x1
        if start:
            for t in range(dpc):
                x0, x1 = cross(
                    power_ref[k, t * TILE : (t + 1) * TILE, :],
                    power_ref[k, (t + dpc) * TILE : (t + dpc + 1) * TILE, :],
                )
                rows = slice(ROWS * dpc + t * TILE, ROWS * dpc + (t + 1) * TILE)
                out_ref[2 * k, rows, :] = x0
                out_ref[2 * k + 1, rows, :] = x1


def first_pass_kernel(
    n, dpc, me_ref, first_ref, second_ref, model_ref, vis_ref, mask_ref, power_ref, *rest
):
    ins, (out_ref, hre, him, cre, cim, stack) = rest[:n], rest[n:]
    products_first(n, dpc, me_ref[0], first_ref, second_ref, ins, hre, him, stack)
    chips = range(n // 2)

    def pair(b, carry):
        acc = predict(dpc, b, (vis_ref[0, b], vis_ref[1, b]), chips, model_ref, hre, him)
        correlate(dpc, b, weighted(b, acc, mask_ref), chips, model_ref, cre, cim)
        return carry

    lax.fori_loop(0, mask_ref.shape[0], pair, 0)

    clear(dpc, mask_ref.shape[0], cre, cim)
    write_sums(dpc, chips, cre, cim, lambda m: (hre, him, m), power_ref, out_ref, True)


NEAR, FAR = (0, 1, 2, 6), (3, 4, 5, 7)


def chips_of(me, pairs):
    return [jnp.bitwise_xor(lax.div(me, 2), m) for m in pairs]


def early_kernel(n, dpc, me_ref, first_ref, second_ref, model_ref, vis_ref, unused_in, *rest):
    ins, (acc_ref, hre, him, unused_out) = rest[: 2 * len(NEAR)], rest[2 * len(NEAR) :]
    me = me_ref[0]
    chips = chips_of(me, NEAR)
    products(dpc, me, first_ref, second_ref, ins, hre, him)

    def pair(b, carry):
        acc = vis_ref[0, b], vis_ref[1, b]
        acc_ref[0, b], acc_ref[1, b] = predict(dpc, b, acc, chips, model_ref, hre, him)
        return carry

    lax.fori_loop(0, vis_ref.shape[1], pair, 0)


def later_pass_kernel(
    n,
    dpc,
    me_ref,
    first_ref,
    second_ref,
    model_ref,
    mask_ref,
    power_ref,
    acc_ref,
    near_re,
    near_im,
    *rest,
):
    ins, (out_ref, hre, him, cre, cim) = rest[: 2 * len(FAR)], rest[2 * len(FAR) :]
    me = me_ref[0]
    products(dpc, me, first_ref, second_ref, ins, hre, him)
    far = chips_of(me, FAR)
    chips = chips_of(me, NEAR) + far

    def pair(b, carry):
        acc = predict(dpc, b, (acc_ref[0, b], acc_ref[1, b]), far, model_ref, hre, him)
        correlate(dpc, b, weighted(b, acc, mask_ref), chips, model_ref, cre, cim)
        return carry

    lax.fori_loop(0, mask_ref.shape[0], pair, 0)

    def tiles(m):
        for re, im, pairs in ((near_re, near_im, NEAR), (hre, him, FAR)):
            if m < len(pairs):
                return re, im, m
            m -= len(pairs)

    clear(dpc, mask_ref.shape[0], cre, cim)
    write_sums(dpc, chips, cre, cim, tiles, power_ref, out_ref, False)


def last_kernel(n, dpc, me_ref, first_ref, second_ref, model_ref, mask_ref, acc_ref, *rest):
    ins, (res_ref, gains_ref, hre, him) = rest[:n], rest[n:]
    me = me_ref[0]
    far = chips_of(me, FAR)
    products(dpc, me, first_ref, second_ref, ins[: 2 * len(FAR)], hre, him)
    per = STATIONS // n
    even = lax.rem(me, 2) == 0
    for m, k in enumerate(chips_of(me, FAR + NEAR)):
        for s in range(per):
            re, im = piece_pair(dpc, even, ins, m, me * per + s)
            for dd in range(dpc):
                at = s * SOURCE_COUNT + k * dpc + dd
                gains_ref[0, pl.ds(at, 1), :] = re[dd : dd + 1]
                gains_ref[1, pl.ds(at, 1), :] = im[dd : dd + 1]

    def pair(b, carry):
        acc = acc_ref[0, b], acc_ref[1, b]
        acc = predict(dpc, b, acc, far, model_ref, hre, him)
        res_ref[0, b], res_ref[1, b] = weighted(b, acc, mask_ref)
        return carry

    lax.fori_loop(0, mask_ref.shape[0], pair, 0)


SMEM = pl.BlockSpec(memory_space=pltpu.SMEM)
VMEM = pl.BlockSpec(memory_space=pltpu.VMEM)
HBM = pl.BlockSpec(memory_space=pltpu.HBM)


def shape(*dims, dtype=F32):
    return jax.ShapeDtypeStruct(dims, dtype)


def exchange(x):
    return lax.all_to_all(x, "bl", split_axis=0, concat_axis=0, tiled=True)


def gather(n, piece, beside):
    def send(x, o):
        return lax.ppermute(x, "bl", [(i, i ^ o) for i in range(n)])

    got = {0: piece}
    got[12], got[2], got[4], got[1] = (send(piece, o) for o in (12, 2, 4, 1))
    got[8] = send(got[12], 4)
    got[6], got[14], got[10] = send(got[4], 2), send(got[12], 2), send(got[8], 2)
    for o in (2, 4, 12, 6, 14, 8, 10):
        if o == 6:
            got[o] = beside(got[o], got)
        got[o + 1] = send(got[o], 1)
    return [got[o] for o in range(n)]


def fast_body(n, vis, model, mask, first, second, gre, gim):
    model, gre, gim = (pltpu.with_memory_space_constraint(x, pltpu.HBM) for x in (model, gre, gim))
    dpc = SOURCE_COUNT // (n // 2)
    width = dpc * 128
    pairs, times, channels = mask.shape
    me = lax.axis_index("bl").astype(jnp.int32).reshape(1)
    params = pltpu.CompilerParams(vmem_limit_bytes=VMEM_LIMIT)
    plane = (n // 2, ROWS * dpc + TILE, channels)
    half = (len(FAR), ROWS * dpc + TILE, channels)
    lots = n * 2 * ROWS
    mine = (STATIONS * dpc + TILE, channels)
    sems = pltpu.SemaphoreType.DMA((len(PARTS),))

    def call(kernel, args, outs, scratch=(), micros=1, aliases={}):
        def place(x):
            if x is model or x is gre or x is gim:
                return HBM
            return SMEM if x.ndim == 1 else VMEM

        return pl.pallas_call(
            functools.partial(kernel, n, dpc),
            in_specs=[place(x) for x in args],
            out_specs=[VMEM for o in outs],
            out_shape=outs,
            scratch_shapes=[pltpu.VMEM(x, F32) if isinstance(x, tuple) else x for x in scratch],
            compiler_params=params,
            input_output_aliases=aliases,
            cost_estimate=pl.CostEstimate(
                flops=0, bytes_accessed=int(micros * 3.69e6), transcendentals=0
            ),
        )(*args)

    (piece,) = call(
        pack_kernel,
        (first, second, gre, gim),
        [shape(2 * gre.shape[0] + TILE, channels)],
        [pltpu.SemaphoreType.DMA((2,))],
    )
    power = held = None

    def powers_beside(x, got):
        nonlocal power, held
        outs = [shape(*plane), shape(*x.shape), pltpu.VMEM(model.shape, BF16)]
        power, x, held = call(power_kernel, (model, mask, x), outs, [sems], aliases={2: 1})
        return x

    got = gather(n, piece, powers_beside)
    g, onehot = call(
        first_own_kernel,
        (me, *got),
        [shape(*mine), shape(STATIONS, lots, dtype=BF16)],
        [(STATIONS * TILE, channels), (n, channels)],
        micros=2,
    )
    (sums,) = call(
        first_pass_kernel,
        (me, first, second, held, vis, mask, power, *got),
        [shape(n, (ROWS + TILE) * dpc, channels)],
        [plane] * 4 + [(n,) + piece.shape],
        micros=9,
    )
    powers = exchange(sums)
    (g,) = call(
        own_kernel,
        (g, onehot, powers),
        [shape(*mine)],
        [(lots, 2 * width), (lots, width)],
    )

    def slots(got, pairs):
        return [got[2 * m + c] for m in pairs for c in (0, 1)]

    def gather_near(g):
        near = None

        def beside(x, got):
            nonlocal near
            args = (me, first, second, held, vis, x, *slots(got, NEAR))
            outs = [shape(*vis.shape), shape(*half), shape(*half), shape(*x.shape)]
            *near, x = call(early_kernel, args, outs, aliases={5: 3})
            return x

        got = gather(n, g, beside)
        return near, slots(got, FAR + NEAR)

    for step in range(1, ITERS):
        near, got = gather_near(g)
        (den,) = call(
            prepare_kernel,
            (g, onehot, powers),
            [shape(STATIONS, width)],
            [(lots, width)] * 2,
            micros=2,
        )
        (sums,) = call(
            later_pass_kernel,
            (me, first, second, held, mask, power, *near, *got[: 2 * len(FAR)]),
            [shape(n, ROWS * dpc, channels)],
            [half] * 2 + [plane] * 2,
            micros=7,
        )
        sums = exchange(sums)
        (g,) = call(
            later_own_kernel,
            (g, onehot, den, sums),
            [shape(*mine)],
            [(lots, width)] * 2,
        )
    near, got = gather_near(g)
    residual, gains = call(
        last_kernel,
        (me, first, second, held, mask, near[0], *got),
        [shape(*vis.shape), shape(2, *gre.shape)],
        [half] * 2,
        micros=4,
    )
    return gains, residual


def block_pass(full_re, full_im, vis_blk, coh_blk, weight, first, second, want_sums):
    ar = jnp.transpose(full_re[first], (1, 0, 2))
    ai = jnp.transpose(full_im[first], (1, 0, 2))
    br = jnp.transpose(full_re[second], (1, 0, 2))
    bi = jnp.transpose(full_im[second], (1, 0, 2))
    mr = coh_blk[:, 0].astype(F32)
    mi = coh_blk[:, 1].astype(F32)
    hr = ar * br + ai * bi
    hi = ai * br - ar * bi
    hr_t, hi_t = hr[:, :, None], hi[:, :, None]
    res_re = weight * (vis_blk[0] - jnp.sum(hr_t * mr - hi_t * mi, 0))
    res_im = weight * (vis_blk[1] - jnp.sum(hr_t * mi + hi_t * mr, 0))
    residual = jnp.stack([res_re, res_im])
    if not want_sums:
        return (residual, None)
    power = jnp.sum(weight[None] * (mr * mr + mi * mi), 2)
    sum_re = jnp.sum(mr * res_re + mi * res_im, 2) + hr * power
    sum_im = jnp.sum(mr * res_im - mi * res_re, 2) + hi * power
    terms_first = jnp.stack([br * sum_re - bi * sum_im, br * sum_im + bi * sum_re, power * (br * br + bi * bi)])
    terms_second = jnp.stack([ar * sum_re + ai * sum_im, ai * sum_re - ar * sum_im, power * (ar * ar + ai * ai)])
    stations = jnp.arange(STATIONS, dtype=jnp.int32)
    onehot_first = (first[:, None] == stations[None, :]).astype(F32)
    onehot_second = (second[:, None] == stations[None, :]).astype(F32)
    exact = lax.Precision.HIGHEST
    sums = jnp.einsum("bs,cdbf->csdf", onehot_first, terms_first, precision=exact)
    sums = sums + jnp.einsum("bs,cdbf->csdf", onehot_second, terms_second, precision=exact)
    return (residual, sums)


def plain_body(vis, model, mask, first, second, gre, gim):
    weight = mask.astype(F32)
    rows, channels = gre.shape
    shaped = (STATIONS, SOURCE_COUNT, channels)
    full_re = lax.all_gather(gre, "bl", axis=0, tiled=True).reshape(shaped)
    full_im = lax.all_gather(gim, "bl", axis=0, tiled=True).reshape(shaped)
    for step in range(ITERS):
        unused, sums = block_pass(full_re, full_im, vis, model, weight, first, second, True)
        totals = lax.psum(sums, "bl")
        denom = totals[2] + ridge
        full_re = 0.5 * (full_re + totals[0] / denom)
        full_im = 0.5 * (full_im + totals[1] / denom)
    residual, unused = block_pass(full_re, full_im, vis, model, weight, first, second, False)
    both = jnp.stack([full_re, full_im]).reshape(2, STATIONS * SOURCE_COUNT, channels)
    return lax.dynamic_slice_in_dim(both, lax.axis_index("bl") * rows, rows, 1), residual


def solution(mesh):
    n = mesh.shape["bl"]
    split = n == 16

    def body(vis, model, mask, first, second, gre, gim):
        if split and mask.shape[0] <= ROWS:
            return fast_body(n, vis, model, mask, first, second, gre, gim)
        return plain_body(vis, model, mask, first, second, gre, gim)

    in_specs = (
        P(None, ("grp", "bl"), None, None),
        P(None, None, ("grp", "bl"), None, None),
        P(("grp", "bl"), None, None),
        P(("grp", "bl")),
        P(("grp", "bl")),
        P(("grp", "bl"), None),
        P(("grp", "bl"), None),
    )
    out_specs = (P(None, ("grp", "bl"), None), P(None, ("grp", "bl"), None, None))
    return jax.shard_map(body, mesh=mesh, in_specs=in_specs, out_specs=out_specs, check_vma=False)
```

```python
import functools

import jax
import jax.numpy as jnp
from jax import lax
from jax.experimental import pallas as pl
from jax.experimental.pallas import tpu as pltpu
from jax.sharding import PartitionSpec as P

STATIONS = 64
SOURCE_COUNT = 40
ITERS = 2
ROWS = 16

ridge = 1.0
F32 = jnp.float32
BF16 = jnp.bfloat16
VMEM_LIMIT = 24 * 1024 * 1024


def swap(x):
    return pltpu.roll(x, x.shape[-1] // 2, axis=x.ndim - 1)


def lower(shape):
    return lax.broadcasted_iota(jnp.int32, shape, len(shape) - 1) < shape[-1] // 2


def cross(a, b):
    lo = lower(a.shape)
    return jnp.where(lo, a, swap(b)), jnp.where(lo, swap(a), b)


def halves_of(x):
    hi = x.astype(BF16)
    return hi, (x - hi.astype(F32)).astype(BF16)


def pick(onehot, x, dims):
    return sum(
        lax.dot_general(onehot, part, (dims, ((), ())), preferred_element_type=F32)
        for part in halves_of(x)
    )


TILE = 8


def pack_kernel(n, dpc, first_hbm, second_hbm, re_hbm, im_hbm, out_ref, first_ref, second_ref, sems):
    rows = re_hbm.shape[0]
    copies = [
        pltpu.make_async_copy(first_hbm, first_ref, sems.at[0]),
        pltpu.make_async_copy(second_hbm, second_ref, sems.at[1]),
        pltpu.make_async_copy(re_hbm, out_ref.at[pl.ds(0, rows)], sems.at[2]),
        pltpu.make_async_copy(im_hbm, out_ref.at[pl.ds(rows, rows)], sems.at[3]),
    ]
    for copy in copies:
        copy.start()
    out_ref[2 * rows :] = jnp.zeros((TILE, 128), F32)
    for copy in copies:
        copy.wait()
    pairs = first_ref.shape[1]
    out_ref[2 * rows : 2 * rows + 1, :pairs] = (first_ref[...] + 1).astype(F32)
    out_ref[2 * rows : 2 * rows + 1, ROWS : ROWS + pairs] = (second_ref[...] + 1).astype(F32)


class Fetch:
    def __init__(self, model, held, sems, firsts=(0,)):
        self.model, self.held, self.sems, self.firsts = model, held, sems, firsts
        self.pairs = held.shape[2]
        self.size = 3 if self.pairs % 3 == 0 else 1
        for i in range(self.pairs // self.size):
            for copy in self.part(i):
                copy.start()

    def part(self, i):
        count = self.held.shape[0] // len(self.firsts)
        pairs = pl.ds(i * self.size, self.size)
        return [
            pltpu.make_async_copy(
                self.model.at[pl.ds(first, count), :, pairs],
                self.held.at[pl.ds(j * count, count), :, pairs],
                self.sems.at[i, j],
            )
            for j, first in enumerate(self.firsts)
        ]

    def each(self, body):
        def part(i, carry):
            for copy in self.part(i):
                copy.wait()
            for u in range(self.size):
                body(i * self.size + u)
            return carry

        lax.fori_loop(0, self.pairs // self.size, part, 0)


def power_kernel(n, dpc, model_hbm, mask_ref, unused_in, out_ref, unused_out, model_ref, sems):
    fetch = Fetch(model_hbm, model_ref, sems)
    out_ref[...] = jnp.zeros_like(out_ref)

    def pair(b):
        weight = mask_ref[b].astype(F32)
        for d in range(SOURCE_COUNT):
            mr = model_ref[d, 0, b].astype(F32)
            mi = model_ref[d, 1, b].astype(F32)
            row = pl.ds(b * dpc + d % dpc, 1)
            out_ref[d // dpc, row, :] = jnp.sum(weight * (mr * mr + mi * mi), axis=0, keepdims=True)

    fetch.each(pair)


def wide(ref, dpc):
    return jnp.concatenate([ref[pl.ds(dd, STATIONS, stride=dpc), :] for dd in range(dpc)], axis=1)


def put(ref, value, dpc):
    for dd in range(dpc):
        ref[pl.ds(dd, STATIONS, stride=dpc), :] = value[:, dd * 128 : (dd + 1) * 128]
    ref[STATIONS * dpc :, :] = jnp.zeros((TILE, 128), F32)


def first_own_kernel(n, dpc, *rest):
    ins, (g_ref, onehot_ref, split, lines) = rest[:n], rest[n:]
    me = lax.axis_index("bl")
    k, c = lax.div(me, 2), lax.rem(me, 2)
    per = STATIONS // n
    rows = per * SOURCE_COUNT
    for o in range(n):
        peer = jnp.bitwise_xor(me, o)
        lines[pl.ds(peer, 1), :] = ins[o][2 * rows : 2 * rows + 1, :]
        for s in range(per):
            at = s * SOURCE_COUNT + k * dpc
            x0, x1 = cross(ins[o][pl.ds(at, TILE), :], ins[o][pl.ds(rows + at, TILE), :])
            to = pl.multiple_of((peer * per + s) * TILE, TILE)
            split[pl.ds(to, TILE), :] = jnp.where(c == 0, x0, x1)
    g = jnp.concatenate([split[pl.ds(dd, STATIONS, stride=TILE), :] for dd in range(dpc)], axis=1)
    put(g_ref, g, dpc)
    across = 128 // (2 * ROWS)
    station = lax.broadcasted_iota(jnp.int32, (STATIONS, 128), 0)
    for group in range(n // across):
        marks = jnp.zeros((1, 128), F32)
        for i in range(across):
            row = lines[group * across + i : group * across + i + 1, :]
            marks = marks + (pltpu.roll(row, i * 2 * ROWS, axis=1) if i else row)
        hit = station + 1 == marks.astype(jnp.int32)
        onehot_ref[:, group * 128 : (group + 1) * 128] = jnp.where(hit, 1.0, 0.0).astype(BF16)


def fill_powers(n, dpc, sums, sel_ref, terms, base):
    lo = lower((TILE, 128))
    for o in range(n):
        r = o * 2 * ROWS
        for dd in range(dpc):
            cols = slice(dd * 128, (dd + 1) * 128)
            dcols = slice(base + dd * 128, base + (dd + 1) * 128)
            W = sums[o, pl.ds(ROWS * dpc + dd, TILE, stride=dpc), :]
            Wx = swap(W)
            W = jnp.concatenate([jnp.where(lo, W, Wx), jnp.where(lo, Wx, W)], 0)
            p = sel_ref[r : r + ROWS, cols]
            q = sel_ref[r + ROWS : r + 2 * ROWS, cols]
            p2, q2 = p * p, q * q
            terms[r : r + ROWS, dcols] = W * (q2 + swap(q2))
            terms[r + ROWS : r + 2 * ROWS, dcols] = W * (p2 + swap(p2))


def fill_sums(n, dpc, sums, sel_ref, terms):
    lo = lower((ROWS, 128))
    sign = jnp.where(lo, -1.0, 1.0)
    for o in range(n):
        r = o * 2 * ROWS
        for dd in range(dpc):
            cols = slice(dd * 128, (dd + 1) * 128)
            B = sums[o, pl.ds(dd, ROWS, stride=dpc), :]
            p = sel_ref[r : r + ROWS, cols]
            q = sel_ref[r + ROWS : r + 2 * ROWS, cols]
            Bx = swap(B)
            Brr, Bii = jnp.where(lo, B, Bx), sign * jnp.where(lo, Bx, B)
            terms[r : r + ROWS, cols] = Brr * q + Bii * swap(q)
            terms[r + ROWS : r + 2 * ROWS, cols] = Brr * p - Bii * swap(p)


def own_kernel(n, dpc, g_in, onehot_ref, sums, g_out, terms, sel_ref):
    width = dpc * 128
    sel_ref[...] = pick(onehot_ref[...], wide(g_in, dpc), ((0,), (0,)))
    fill_sums(n, dpc, sums, sel_ref, terms)
    fill_powers(n, dpc, sums, sel_ref, terms, width)
    total = pick(onehot_ref[...], terms[...], ((1,), (0,)))
    put(g_out, 0.5 * (wide(g_in, dpc) + total[:, :width] / (total[:, width:] + ridge)), dpc)


def prepare_kernel(n, dpc, g_ref, onehot_ref, sums, den_ref, terms, sel_ref):
    sel_ref[...] = pick(onehot_ref[...], wide(g_ref, dpc), ((0,), (0,)))
    fill_powers(n, dpc, sums, sel_ref, terms, 0)
    den_ref[...] = pick(onehot_ref[...], terms[...], ((1,), (0,))) + ridge


def later_own_kernel(n, dpc, g_in, onehot_ref, den_ref, sums, g_out, terms, sel_ref):
    sel_ref[...] = pick(onehot_ref[...], wide(g_in, dpc), ((0,), (0,)))
    fill_sums(n, dpc, sums, sel_ref, terms)
    total = pick(onehot_ref[...], terms[...], ((1,), (0,)))
    put(g_out, 0.5 * (wide(g_in, dpc) + total / den_ref[...]), dpc)


def clear(dpc, pairs, *refs):
    for ref in refs:
        chips, rows, _ = ref.shape
        for m in range(chips):
            ref[m, pairs * dpc :, :] = jnp.zeros((rows - pairs * dpc, 128), F32)


def products_first(n, dpc, me, pairs, ends_ref, ins, hre, him, stack):
    per = STATIONS // n
    rows = per * SOURCE_COUNT
    for o in range(n):
        stack[jnp.bitwise_xor(me, o)] = ins[o][...]

    def pair(b, carry):
        p, q = ends_ref[b], ends_ref[pairs + b]

        def block(station, k, part):
            at = lax.rem(station, per) * SOURCE_COUNT + k * dpc + part * rows
            return stack[lax.div(station, per), pl.ds(at, TILE), :]

        for k in range(n // 2):
            pr, pi, qr, qi = block(p, k, 0), block(p, k, 1), block(q, k, 0), block(q, k, 1)
            hre[k, pl.ds(b * dpc, TILE), :] = pr * qr + pi * qi
            him[k, pl.ds(b * dpc, TILE), :] = pi * qr - pr * qi
        return carry

    lax.fori_loop(0, pairs, pair, 0, unroll=5 if pairs % 5 == 0 else 1)
    clear(dpc, pairs, hre, him)


def piece_pair(dpc, even, ins, m, station):
    a = ins[2 * m][pl.ds(station * dpc, TILE), :]
    b = ins[2 * m + 1][pl.ds(station * dpc, TILE), :]
    return cross(jnp.where(even, a, b), jnp.where(even, b, a))


def products(dpc, me, pairs, ends_ref, ins, hre, him):
    even = lax.rem(me, 2) == 0

    def pair(b, carry):
        p, q = ends_ref[b], ends_ref[pairs + b]
        for m in range(len(ins) // 2):
            pr, pi = piece_pair(dpc, even, ins, m, p)
            qr, qi = piece_pair(dpc, even, ins, m, q)
            hre[m, pl.ds(b * dpc, TILE), :] = pr * qr + pi * qi
            him[m, pl.ds(b * dpc, TILE), :] = pi * qr - pr * qi
        return carry

    lax.fori_loop(0, pairs, pair, 0, unroll=5 if pairs % 5 == 0 else 1)
    clear(dpc, pairs, hre, him)


def predict(dpc, b, acc, chips, model_ref, hre, him):
    tiles = [slice(t, t + TILE) for t in range(0, acc[0].shape[0], TILE)]
    acc_re, acc_im = ([x[t] for t in tiles] for x in acc)
    for m, k in enumerate(chips):
        for dd in range(dpc):
            mr = model_ref[k * dpc + dd, 0, b].astype(F32)
            mi = model_ref[k * dpc + dd, 1, b].astype(F32)
            row = pl.ds(b * dpc + dd, TILE, stride=0)
            hr, hi = hre[m, row, :], him[m, row, :]
            for i, t in enumerate(tiles):
                acc_re[i] = acc_re[i] - (hr * mr[t] - hi * mi[t])
                acc_im[i] = acc_im[i] - (hr * mi[t] + hi * mr[t])
    return jnp.concatenate(acc_re, 0), jnp.concatenate(acc_im, 0)


def weighted(b, acc, mask_ref):
    weight = mask_ref[b].astype(F32)
    return weight * acc[0], weight * acc[1]


def fold(a, b, step):
    if a is None:
        return None
    if b is None:
        return a + pltpu.roll(a, step, axis=0)
    mine = (lax.broadcasted_iota(jnp.int32, a.shape, 0) & step) == 0
    return jnp.where(mine, a, b) + pltpu.roll(jnp.where(mine, b, a), step, axis=0)


def row_sums(values):
    values = list(values) + [None] * (TILE - len(values))
    step = 1
    while step < TILE:
        values = [fold(a, b, step) for a, b in zip(values[::2], values[1::2])]
        step *= 2
    return values[0]


def tile_sum(x):
    total = x[:TILE]
    for t in range(1, x.shape[0] // TILE):
        total = total + x[t * TILE : (t + 1) * TILE]
    return total


def correlate(dpc, b, res, chips, model_ref, cre, cim):
    res_re, res_im = res
    for m, k in enumerate(chips):
        re, im = [], []
        for dd in range(dpc):
            mr = model_ref[k * dpc + dd, 0, b].astype(F32)
            mi = model_ref[k * dpc + dd, 1, b].astype(F32)
            re.append(tile_sum(mr * res_re + mi * res_im))
            im.append(tile_sum(mr * res_im - mi * res_re))
        cre[m, pl.ds(b * dpc, TILE), :] = row_sums(re)
        cim[m, pl.ds(b * dpc, TILE), :] = row_sums(im)


def write_sums(dpc, chips, cre, cim, tiles, power_ref, out_ref, start):
    for m, k in enumerate(chips):
        re, im, at = tiles(m)
        for t in range(ROWS * dpc // TILE):
            rows = slice(t * TILE, (t + 1) * TILE)
            w = power_ref[k, rows, :]
            x0, x1 = cross(cre[m, rows, :] + re[at, rows, :] * w, cim[m, rows, :] + im[at, rows, :] * w)
            out_ref[2 * k, rows, :] = x0
            out_ref[2 * k + 1, rows, :] = x1
        if start:
            for t in range(dpc):
                x0, x1 = cross(
                    power_ref[k, t * TILE : (t + 1) * TILE, :],
                    power_ref[k, (t + dpc) * TILE : (t + dpc + 1) * TILE, :],
                )
                rows = slice(ROWS * dpc + t * TILE, ROWS * dpc + (t + 1) * TILE)
                out_ref[2 * k, rows, :] = x0
                out_ref[2 * k + 1, rows, :] = x1


def first_pass_kernel(n, dpc, ends_ref, model_hbm, vis_ref, mask_ref, power_ref, *rest):
    ins, (out_ref, model_ref, sems, hre, him, cre, cim, stack) = rest[:n], rest[n:]
    fetch = Fetch(model_hbm, model_ref, sems)
    products_first(n, dpc, lax.axis_index("bl"), mask_ref.shape[0], ends_ref, ins, hre, him, stack)
    chips = range(n // 2)

    def pair(b):
        acc = predict(dpc, b, (vis_ref[0, b], vis_ref[1, b]), chips, model_ref, hre, him)
        correlate(dpc, b, weighted(b, acc, mask_ref), chips, model_ref, cre, cim)

    fetch.each(pair)

    clear(dpc, mask_ref.shape[0], cre, cim)
    write_sums(dpc, chips, cre, cim, lambda m: (hre, him, m), power_ref, out_ref, True)


NEAR, FAR = (0, 1, 2, 6), (3, 4, 5, 7)


def chips_of(me, pairs):
    return [jnp.bitwise_xor(lax.div(me, 2), m) for m in pairs]


def early_kernel(n, dpc, ends_ref, model_hbm, vis_ref, unused_in, *rest):
    ins, (acc_ref, hre, him, unused_out, model_ref, sems) = rest[: 2 * len(NEAR)], rest[2 * len(NEAR) :]
    me = lax.axis_index("bl")
    fetch = Fetch(model_hbm, model_ref, sems, [k * dpc for k in chips_of(me, NEAR)])
    products(dpc, me, model_hbm.shape[2], ends_ref, ins, hre, him)

    def pair(b):
        acc = vis_ref[0, b], vis_ref[1, b]
        acc_ref[0, b], acc_ref[1, b] = predict(dpc, b, acc, range(len(NEAR)), model_ref, hre, him)

    fetch.each(pair)


def later_pass_kernel(
    n,
    dpc,
    ends_ref,
    model_hbm,
    mask_ref,
    power_ref,
    acc_ref,
    near_re,
    near_im,
    *rest,
):
    ins, (out_ref, model_ref, sems, hre, him, cre, cim) = rest[: 2 * len(FAR)], rest[2 * len(FAR) :]
    fetch = Fetch(model_hbm, model_ref, sems)
    me = lax.axis_index("bl")
    products(dpc, me, model_hbm.shape[2], ends_ref, ins, hre, him)
    far = chips_of(me, FAR)
    chips = chips_of(me, NEAR) + far

    def pair(b):
        acc = predict(dpc, b, (acc_ref[0, b], acc_ref[1, b]), far, model_ref, hre, him)
        correlate(dpc, b, weighted(b, acc, mask_ref), chips, model_ref, cre, cim)

    fetch.each(pair)

    def tiles(m):
        for re, im, pairs in ((near_re, near_im, NEAR), (hre, him, FAR)):
            if m < len(pairs):
                return re, im, m
            m -= len(pairs)

    clear(dpc, mask_ref.shape[0], cre, cim)
    write_sums(dpc, chips, cre, cim, tiles, power_ref, out_ref, False)


def last_kernel(n, dpc, ends_ref, model_hbm, mask_ref, acc_ref, *rest):
    ins, (res_ref, gains_ref, model_ref, sems, hre, him) = rest[:n], rest[n:]
    me = lax.axis_index("bl")
    fetch = Fetch(model_hbm, model_ref, sems, [k * dpc for k in chips_of(me, FAR)])
    products(dpc, me, model_hbm.shape[2], ends_ref, ins[: 2 * len(FAR)], hre, him)
    per = STATIONS // n
    even = lax.rem(me, 2) == 0
    for m, k in enumerate(chips_of(me, FAR + NEAR)):
        for s in range(per):
            re, im = piece_pair(dpc, even, ins, m, me * per + s)
            for dd in range(dpc):
                at = s * SOURCE_COUNT + k * dpc + dd
                gains_ref[0, pl.ds(at, 1), :] = re[dd : dd + 1]
                gains_ref[1, pl.ds(at, 1), :] = im[dd : dd + 1]

    def pair(b):
        acc = acc_ref[0, b], acc_ref[1, b]
        acc = predict(dpc, b, acc, range(len(FAR)), model_ref, hre, him)
        res_ref[0, b], res_ref[1, b] = weighted(b, acc, mask_ref)

    fetch.each(pair)


SMEM = pl.BlockSpec(memory_space=pltpu.SMEM)
VMEM = pl.BlockSpec(memory_space=pltpu.VMEM)
HBM = pl.BlockSpec(memory_space=pltpu.HBM)


def shape(*dims, dtype=F32):
    return jax.ShapeDtypeStruct(dims, dtype)


def exchange(x):
    return lax.all_to_all(x, "bl", split_axis=0, concat_axis=0, tiled=True)


def gather(n, piece, beside):
    def send(x, o):
        return lax.ppermute(x, "bl", [(i, i ^ o) for i in range(n)])

    got = {0: piece}
    got[12], got[2], got[4], got[1] = (send(piece, o) for o in (12, 2, 4, 1))
    got[8] = send(got[12], 4)
    got[6], got[14], got[10] = send(got[4], 2), send(got[12], 2), send(got[8], 2)
    for o in (2, 4, 12, 6, 14, 8, 10):
        if o == 6:
            got[o] = beside(got[o], got)
        got[o + 1] = send(got[o], 1)
    return [got[o] for o in range(n)]


def fast_body(n, vis, model, mask, first, second, gre, gim):
    ends = jnp.concatenate([first, second])
    starts = (first.reshape(1, -1), second.reshape(1, -1), gre, gim)
    model, *starts = (pltpu.with_memory_space_constraint(x, pltpu.HBM) for x in (model, *starts))
    dpc = SOURCE_COUNT // (n // 2)
    width = dpc * 128
    pairs, times, channels = mask.shape
    params = pltpu.CompilerParams(vmem_limit_bytes=VMEM_LIMIT)
    plane = (n // 2, ROWS * dpc + TILE, channels)
    half = (len(FAR), ROWS * dpc + TILE, channels)
    lots = n * 2 * ROWS
    mine = (STATIONS * dpc + TILE, channels)
    sems = pltpu.SemaphoreType.DMA((pairs, n // 4))
    held = [pltpu.VMEM(model.shape, BF16), sems]
    held_half = [pltpu.VMEM((SOURCE_COUNT // 2,) + model.shape[1:], BF16), sems]

    def call(kernel, args, outs, scratch=(), micros=1, aliases={}):
        def place(x):
            if x is model or any(x is y for y in starts):
                return HBM
            return SMEM if x.ndim == 1 else VMEM

        return pl.pallas_call(
            functools.partial(kernel, n, dpc),
            in_specs=[place(x) for x in args],
            out_specs=[VMEM for o in outs],
            out_shape=outs,
            scratch_shapes=[pltpu.VMEM(x, F32) if isinstance(x, tuple) else x for x in scratch],
            compiler_params=params,
            input_output_aliases=aliases,
            cost_estimate=pl.CostEstimate(
                flops=0, bytes_accessed=int(micros * 3.69e6), transcendentals=0
            ),
        )(*args)

    (piece,) = call(
        pack_kernel,
        starts,
        [shape(2 * gre.shape[0] + TILE, channels)],
        [pltpu.VMEM((1, pairs), jnp.int32)] * 2 + [pltpu.SemaphoreType.DMA((4,))],
    )
    power = None

    def powers_beside(x, got):
        nonlocal power
        power, x = call(
            power_kernel, (model, mask, x), [shape(*plane), shape(*x.shape)], held, micros=20, aliases={2: 1}
        )
        return x

    got = gather(n, piece, powers_beside)
    g, onehot = call(
        first_own_kernel,
        got,
        [shape(*mine), shape(STATIONS, lots, dtype=BF16)],
        [(STATIONS * TILE, channels), (n, channels)],
        micros=2,
    )
    (sums,) = call(
        first_pass_kernel,
        (ends, model, vis, mask, power, *got),
        [shape(n, (ROWS + TILE) * dpc, channels)],
        held + [plane] * 4 + [(n,) + piece.shape],
        micros=9,
    )
    powers = exchange(sums)
    (g,) = call(
        own_kernel,
        (g, onehot, powers),
        [shape(*mine)],
        [(lots, 2 * width), (lots, width)],
    )

    def slots(got, pairs):
        return [got[2 * m + c] for m in pairs for c in (0, 1)]

    def gather_near(g):
        near = None

        def beside(x, got):
            nonlocal near
            args = (ends, model, vis, x, *slots(got, NEAR))
            outs = [shape(*vis.shape), shape(*half), shape(*half), shape(*x.shape)]
            *near, x = call(early_kernel, args, outs, held_half, aliases={3: 3})
            return x

        got = gather(n, g, beside)
        return near, slots(got, FAR + NEAR)

    for step in range(1, ITERS):
        near, got = gather_near(g)
        (den,) = call(
            prepare_kernel,
            (g, onehot, powers),
            [shape(STATIONS, width)],
            [(lots, width)] * 2,
            micros=2,
        )
        (sums,) = call(
            later_pass_kernel,
            (ends, model, mask, power, *near, *got[: 2 * len(FAR)]),
            [shape(n, ROWS * dpc, channels)],
            held + [half] * 2 + [plane] * 2,
            micros=7,
        )
        sums = exchange(sums)
        (g,) = call(
            later_own_kernel,
            (g, onehot, den, sums),
            [shape(*mine)],
            [(lots, width)] * 2,
        )
    near, got = gather_near(g)
    residual, gains = call(
        last_kernel,
        (ends, model, mask, near[0], *got),
        [shape(*vis.shape), shape(2, *gre.shape)],
        held_half + [half] * 2,
        micros=4,
    )
    return gains, residual


def block_pass(full_re, full_im, vis_blk, coh_blk, weight, first, second, want_sums):
    ar = jnp.transpose(full_re[first], (1, 0, 2))
    ai = jnp.transpose(full_im[first], (1, 0, 2))
    br = jnp.transpose(full_re[second], (1, 0, 2))
    bi = jnp.transpose(full_im[second], (1, 0, 2))
    mr = coh_blk[:, 0].astype(F32)
    mi = coh_blk[:, 1].astype(F32)
    hr = ar * br + ai * bi
    hi = ai * br - ar * bi
    hr_t, hi_t = hr[:, :, None], hi[:, :, None]
    res_re = weight * (vis_blk[0] - jnp.sum(hr_t * mr - hi_t * mi, 0))
    res_im = weight * (vis_blk[1] - jnp.sum(hr_t * mi + hi_t * mr, 0))
    residual = jnp.stack([res_re, res_im])
    if not want_sums:
        return (residual, None)
    power = jnp.sum(weight[None] * (mr * mr + mi * mi), 2)
    sum_re = jnp.sum(mr * res_re + mi * res_im, 2) + hr * power
    sum_im = jnp.sum(mr * res_im - mi * res_re, 2) + hi * power
    terms_first = jnp.stack([br * sum_re - bi * sum_im, br * sum_im + bi * sum_re, power * (br * br + bi * bi)])
    terms_second = jnp.stack([ar * sum_re + ai * sum_im, ai * sum_re - ar * sum_im, power * (ar * ar + ai * ai)])
    stations = jnp.arange(STATIONS, dtype=jnp.int32)
    onehot_first = (first[:, None] == stations[None, :]).astype(F32)
    onehot_second = (second[:, None] == stations[None, :]).astype(F32)
    exact = lax.Precision.HIGHEST
    sums = jnp.einsum("bs,cdbf->csdf", onehot_first, terms_first, precision=exact)
    sums = sums + jnp.einsum("bs,cdbf->csdf", onehot_second, terms_second, precision=exact)
    return (residual, sums)


def plain_body(vis, model, mask, first, second, gre, gim):
    weight = mask.astype(F32)
    rows, channels = gre.shape
    shaped = (STATIONS, SOURCE_COUNT, channels)
    full_re = lax.all_gather(gre, "bl", axis=0, tiled=True).reshape(shaped)
    full_im = lax.all_gather(gim, "bl", axis=0, tiled=True).reshape(shaped)
    for step in range(ITERS):
        unused, sums = block_pass(full_re, full_im, vis, model, weight, first, second, True)
        totals = lax.psum(sums, "bl")
        denom = totals[2] + ridge
        full_re = 0.5 * (full_re + totals[0] / denom)
        full_im = 0.5 * (full_im + totals[1] / denom)
    residual, unused = block_pass(full_re, full_im, vis, model, weight, first, second, False)
    both = jnp.stack([full_re, full_im]).reshape(2, STATIONS * SOURCE_COUNT, channels)
    return lax.dynamic_slice_in_dim(both, lax.axis_index("bl") * rows, rows, 1), residual


def solution(mesh):
    n = mesh.shape["bl"]
    split = n == 16

    def body(vis, model, mask, first, second, gre, gim):
        if split and mask.shape[0] <= ROWS:
            return fast_body(n, vis, model, mask, first, second, gre, gim)
        return plain_body(vis, model, mask, first, second, gre, gim)

    in_specs = (
        P(None, ("grp", "bl"), None, None),
        P(None, None, ("grp", "bl"), None, None),
        P(("grp", "bl"), None, None),
        P(("grp", "bl")),
        P(("grp", "bl")),
        P(("grp", "bl"), None),
        P(("grp", "bl"), None),
    )
    out_specs = (P(None, ("grp", "bl"), None), P(None, ("grp", "bl"), None, None))
    return jax.shard_map(body, mesh=mesh, in_specs=in_specs, out_specs=out_specs, check_vma=False)
```

```python
import functools

import jax
import jax.numpy as jnp
from jax import lax
from jax.experimental import pallas as pl
from jax.experimental.pallas import tpu as pltpu
from jax.sharding import PartitionSpec as P

STATIONS = 64
SOURCE_COUNT = 40
ITERS = 2
ROWS = 16

ridge = 1.0
F32 = jnp.float32
BF16 = jnp.bfloat16
VMEM_LIMIT = 24 * 1024 * 1024


def swap(x):
    return pltpu.roll(x, x.shape[-1] // 2, axis=x.ndim - 1)


def lower(shape):
    return lax.broadcasted_iota(jnp.int32, shape, len(shape) - 1) < shape[-1] // 2


def cross(a, b):
    lo = lower(a.shape)
    return jnp.where(lo, a, swap(b)), jnp.where(lo, swap(a), b)


def halves_of(x):
    hi = x.astype(BF16)
    return hi, (x - hi.astype(F32)).astype(BF16)


def pick(onehot, x, dims):
    return sum(
        lax.dot_general(onehot, part, (dims, ((), ())), preferred_element_type=F32)
        for part in halves_of(x)
    )


TILE = 8
TRIP = 2


def pack_kernel(n, dpc, first_hbm, second_hbm, re_hbm, im_hbm, out_ref, first_ref, second_ref, sems):
    rows = re_hbm.shape[0]
    copies = [
        pltpu.make_async_copy(first_hbm, first_ref, sems.at[0]),
        pltpu.make_async_copy(second_hbm, second_ref, sems.at[1]),
        pltpu.make_async_copy(re_hbm, out_ref.at[pl.ds(0, rows)], sems.at[2]),
        pltpu.make_async_copy(im_hbm, out_ref.at[pl.ds(rows, rows)], sems.at[3]),
    ]
    for copy in copies:
        copy.start()
    out_ref[2 * rows :] = jnp.zeros((TILE, 128), F32)
    for copy in copies:
        copy.wait()
    pairs = first_ref.shape[1]
    out_ref[2 * rows : 2 * rows + 1, :pairs] = (first_ref[...] + 1).astype(F32)
    out_ref[2 * rows : 2 * rows + 1, ROWS : ROWS + pairs] = (second_ref[...] + 1).astype(F32)


class Fetch:
    def __init__(self, model, held, sems, firsts=(0,)):
        self.model, self.held, self.sems, self.firsts = model, held, sems, firsts
        self.pairs = held.shape[2]
        self.size = 3 if self.pairs % 3 == 0 else 1
        for i in range(self.pairs // self.size):
            for copy in self.part(i):
                copy.start()

    def part(self, i):
        count = self.held.shape[0] // len(self.firsts)
        pairs = pl.ds(i * self.size, self.size)
        return [
            pltpu.make_async_copy(
                self.model.at[pl.ds(first, count), :, pairs],
                self.held.at[pl.ds(j * count, count), :, pairs],
                self.sems.at[i, j],
            )
            for j, first in enumerate(self.firsts)
        ]

    def each(self, body):
        def part(i, carry):
            for copy in self.part(i):
                copy.wait()
            def one(u, carry):
                body(i * self.size + u)
                return carry

            return lax.fori_loop(0, self.size, one, carry)

        lax.fori_loop(0, self.pairs // self.size, part, 0)


def power_kernel(n, dpc, model_hbm, mask_ref, unused_in, out_ref, unused_out, model_ref, sems):
    fetch = Fetch(model_hbm, model_ref, sems)
    out_ref[...] = jnp.zeros_like(out_ref)

    def pair(b):
        weight = mask_ref[b].astype(F32)
        for d in range(SOURCE_COUNT):
            mr = model_ref[d, 0, b].astype(F32)
            mi = model_ref[d, 1, b].astype(F32)
            row = pl.ds(b * dpc + d % dpc, 1)
            out_ref[d // dpc, row, :] = jnp.sum(weight * (mr * mr + mi * mi), axis=0, keepdims=True)

    fetch.each(pair)


def wide(ref, dpc):
    return jnp.concatenate([ref[pl.ds(dd, STATIONS, stride=dpc), :] for dd in range(dpc)], axis=1)


def put(ref, value, dpc):
    for dd in range(dpc):
        ref[pl.ds(dd, STATIONS, stride=dpc), :] = value[:, dd * 128 : (dd + 1) * 128]
    ref[STATIONS * dpc :, :] = jnp.zeros((TILE, 128), F32)


def first_own(n, dpc, me, ins, g_ref, onehot_ref, split, lines):
    k, c = lax.div(me, 2), lax.rem(me, 2)
    per = STATIONS // n
    rows = per * SOURCE_COUNT
    for o in range(n):
        peer = jnp.bitwise_xor(me, o)
        lines[pl.ds(peer, 1), :] = ins[o][2 * rows : 2 * rows + 1, :]
        for s in range(per):
            at = s * SOURCE_COUNT + k * dpc
            x0, x1 = cross(ins[o][pl.ds(at, TILE), :], ins[o][pl.ds(rows + at, TILE), :])
            to = pl.multiple_of((peer * per + s) * TILE, TILE)
            split[pl.ds(to, TILE), :] = jnp.where(c == 0, x0, x1)
    g = jnp.concatenate([split[pl.ds(dd, STATIONS, stride=TILE), :] for dd in range(dpc)], axis=1)
    put(g_ref, g, dpc)
    across = 128 // (2 * ROWS)
    station = lax.broadcasted_iota(jnp.int32, (STATIONS, 128), 0)
    for group in range(n // across):
        marks = jnp.zeros((1, 128), F32)
        for i in range(across):
            row = lines[group * across + i : group * across + i + 1, :]
            marks = marks + (pltpu.roll(row, i * 2 * ROWS, axis=1) if i else row)
        hit = station + 1 == marks.astype(jnp.int32)
        onehot_ref[:, group * 128 : (group + 1) * 128] = jnp.where(hit, 1.0, 0.0).astype(BF16)


def fill_powers(n, dpc, sums, sel_ref, terms, base):
    lo = lower((TILE, 128))
    for o in range(n):
        r = o * 2 * ROWS
        for dd in range(dpc):
            cols = slice(dd * 128, (dd + 1) * 128)
            dcols = slice(base + dd * 128, base + (dd + 1) * 128)
            W = sums[o, pl.ds(ROWS * dpc + dd, TILE, stride=dpc), :]
            Wx = swap(W)
            W = jnp.concatenate([jnp.where(lo, W, Wx), jnp.where(lo, Wx, W)], 0)
            p = sel_ref[r : r + ROWS, cols]
            q = sel_ref[r + ROWS : r + 2 * ROWS, cols]
            p2, q2 = p * p, q * q
            terms[r : r + ROWS, dcols] = W * (q2 + swap(q2))
            terms[r + ROWS : r + 2 * ROWS, dcols] = W * (p2 + swap(p2))


def fill_sums(n, dpc, sums, sel_ref, terms):
    lo = lower((ROWS, 128))
    sign = jnp.where(lo, -1.0, 1.0)
    for o in range(n):
        r = o * 2 * ROWS
        for dd in range(dpc):
            cols = slice(dd * 128, (dd + 1) * 128)
            B = sums[o, pl.ds(dd, ROWS, stride=dpc), :]
            p = sel_ref[r : r + ROWS, cols]
            q = sel_ref[r + ROWS : r + 2 * ROWS, cols]
            Bx = swap(B)
            Brr, Bii = jnp.where(lo, B, Bx), sign * jnp.where(lo, Bx, B)
            terms[r : r + ROWS, cols] = Brr * q + Bii * swap(q)
            terms[r + ROWS : r + 2 * ROWS, cols] = Brr * p - Bii * swap(p)


def own_kernel(n, dpc, g_in, onehot_ref, sums, g_out, terms, sel_ref):
    width = dpc * 128
    sel_ref[...] = pick(onehot_ref[...], wide(g_in, dpc), ((0,), (0,)))
    fill_sums(n, dpc, sums, sel_ref, terms)
    fill_powers(n, dpc, sums, sel_ref, terms, width)
    total = pick(onehot_ref[...], terms[...], ((1,), (0,)))
    put(g_out, 0.5 * (wide(g_in, dpc) + total[:, :width] / (total[:, width:] + ridge)), dpc)


def prepare_kernel(n, dpc, g_ref, onehot_ref, sums, den_ref, terms, sel_ref):
    sel_ref[...] = pick(onehot_ref[...], wide(g_ref, dpc), ((0,), (0,)))
    fill_powers(n, dpc, sums, sel_ref, terms, 0)
    den_ref[...] = pick(onehot_ref[...], terms[...], ((1,), (0,))) + ridge


def later_own_kernel(n, dpc, g_in, onehot_ref, den_ref, sums, g_out, terms, sel_ref):
    sel_ref[...] = pick(onehot_ref[...], wide(g_in, dpc), ((0,), (0,)))
    fill_sums(n, dpc, sums, sel_ref, terms)
    total = pick(onehot_ref[...], terms[...], ((1,), (0,)))
    put(g_out, 0.5 * (wide(g_in, dpc) + total / den_ref[...]), dpc)


def clear(dpc, pairs, *refs):
    for ref in refs:
        chips, rows, _ = ref.shape
        for m in range(chips):
            ref[m, pairs * dpc :, :] = jnp.zeros((rows - pairs * dpc, 128), F32)


def products_first(n, dpc, me, pairs, ends_ref, ins, hre, him, stack):
    per = STATIONS // n
    rows = per * SOURCE_COUNT
    for o in range(n):
        stack[jnp.bitwise_xor(me, o)] = ins[o][...]

    def pair(b, carry):
        p, q = ends_ref[b], ends_ref[pairs + b]

        def block(station, k, part):
            at = lax.rem(station, per) * SOURCE_COUNT + k * dpc + part * rows
            return stack[lax.div(station, per), pl.ds(at, TILE), :]

        for k in range(n // 2):
            pr, pi, qr, qi = block(p, k, 0), block(p, k, 1), block(q, k, 0), block(q, k, 1)
            hre[k, pl.ds(b * dpc, TILE), :] = pr * qr + pi * qi
            him[k, pl.ds(b * dpc, TILE), :] = pi * qr - pr * qi
        return carry

    lax.fori_loop(0, pairs, pair, 0, unroll=5 if pairs % 5 == 0 else 1)
    clear(dpc, pairs, hre, him)


def piece_pair(dpc, even, ins, m, station):
    a = ins[2 * m][pl.ds(station * dpc, TILE), :]
    b = ins[2 * m + 1][pl.ds(station * dpc, TILE), :]
    return cross(jnp.where(even, a, b), jnp.where(even, b, a))


def products(dpc, me, pairs, ends_ref, ins, hre, him):
    even = lax.rem(me, 2) == 0

    def pair(b, carry):
        p, q = ends_ref[b], ends_ref[pairs + b]
        for m in range(len(ins) // 2):
            pr, pi = piece_pair(dpc, even, ins, m, p)
            qr, qi = piece_pair(dpc, even, ins, m, q)
            hre[m, pl.ds(b * dpc, TILE), :] = pr * qr + pi * qi
            him[m, pl.ds(b * dpc, TILE), :] = pi * qr - pr * qi
        return carry

    lax.fori_loop(0, pairs, pair, 0, unroll=5 if pairs % 5 == 0 else 1)
    clear(dpc, pairs, hre, him)


def predict(dpc, b, acc, first, chips, model_ref, hre, him):
    def trip(i, acc):
        tiles = [slice(t, t + TILE) for t in range(0, acc[0].shape[0], TILE)]
        acc_re, acc_im = ([x[t] for t in tiles] for x in acc)
        for u in range(TRIP * dpc):
            d = first + i * TRIP * dpc + u
            mr = model_ref[d, 0, b].astype(F32)
            mi = model_ref[d, 1, b].astype(F32)
            m, row = i * TRIP + u // dpc, pl.ds(b * dpc + u % dpc, TILE, stride=0)
            hr, hi = hre[m, row, :], him[m, row, :]
            for j, t in enumerate(tiles):
                acc_re[j] = acc_re[j] - (hr * mr[t] - hi * mi[t])
                acc_im[j] = acc_im[j] - (hr * mi[t] + hi * mr[t])
        return jnp.concatenate(acc_re, 0), jnp.concatenate(acc_im, 0)

    return lax.fori_loop(0, chips // TRIP, trip, acc)


def weighted(b, acc, mask_ref):
    weight = mask_ref[b].astype(F32)
    return weight * acc[0], weight * acc[1]


def fold(a, b, step):
    if a is None:
        return None
    if b is None:
        return a + pltpu.roll(a, step, axis=0)
    mine = (lax.broadcasted_iota(jnp.int32, a.shape, 0) & step) == 0
    return jnp.where(mine, a, b) + pltpu.roll(jnp.where(mine, b, a), step, axis=0)


def row_sums(values):
    values = list(values) + [None] * (TILE - len(values))
    step = 1
    while step < TILE:
        values = [fold(a, b, step) for a, b in zip(values[::2], values[1::2])]
        step *= 2
    return values[0]


def tile_sum(x):
    total = x[:TILE]
    for t in range(1, x.shape[0] // TILE):
        total = total + x[t * TILE : (t + 1) * TILE]
    return total


def correlate(dpc, b, res, chips, model_ref, cre, cim):
    res_re, res_im = res

    def trip(i, carry):
        for v in range(TRIP):
            re, im = [], []
            for dd in range(dpc):
                d = (i * TRIP + v) * dpc + dd
                mr = model_ref[d, 0, b].astype(F32)
                mi = model_ref[d, 1, b].astype(F32)
                re.append(tile_sum(mr * res_re + mi * res_im))
                im.append(tile_sum(mr * res_im - mi * res_re))
            rows = pl.ds(b * dpc, TILE)
            cre[i * TRIP + v, rows, :] = row_sums(re)
            cim[i * TRIP + v, rows, :] = row_sums(im)
        return carry

    lax.fori_loop(0, chips // TRIP, trip, 0)


def write_sums(dpc, chips, cre, cim, tiles, power_ref, out_ref, start):
    for m, k in enumerate(chips):
        re, im, at = tiles(m)
        for t in range(ROWS * dpc // TILE):
            rows = slice(t * TILE, (t + 1) * TILE)
            w = power_ref[k, rows, :]
            x0, x1 = cross(cre[m, rows, :] + re[at, rows, :] * w, cim[m, rows, :] + im[at, rows, :] * w)
            out_ref[2 * k, rows, :] = x0
            out_ref[2 * k + 1, rows, :] = x1
        if start:
            for t in range(dpc):
                x0, x1 = cross(
                    power_ref[k, t * TILE : (t + 1) * TILE, :],
                    power_ref[k, (t + dpc) * TILE : (t + dpc + 1) * TILE, :],
                )
                rows = slice(ROWS * dpc + t * TILE, ROWS * dpc + (t + 1) * TILE)
                out_ref[2 * k, rows, :] = x0
                out_ref[2 * k + 1, rows, :] = x1


def first_pass_kernel(n, dpc, ends_ref, model_hbm, vis_ref, mask_ref, power_ref, *rest):
    ins, (out_ref, g_ref, onehot_ref, model_ref, sems, hre, him, cre, cim, stack, split, lines) = rest[:n], rest[n:]
    fetch = Fetch(model_hbm, model_ref, sems)
    me = lax.axis_index("bl")
    pairs, chips = mask_ref.shape[0], n // 2
    products_first(n, dpc, me, pairs, ends_ref, ins, hre, him, stack)
    first_own(n, dpc, me, ins, g_ref, onehot_ref, split, lines)

    def pair(b):
        acc = predict(dpc, b, (vis_ref[0, b], vis_ref[1, b]), 0, chips, model_ref, hre, him)
        correlate(dpc, b, weighted(b, acc, mask_ref), chips, model_ref, cre, cim)

    fetch.each(pair)
    clear(dpc, pairs, cre, cim)
    write_sums(dpc, range(chips), cre, cim, lambda m: (hre, him, m), power_ref, out_ref, True)


NEAR, FAR = (0, 1, 2, 6), (3, 4, 5, 7)


def chips_of(me, pairs):
    return [jnp.bitwise_xor(lax.div(me, 2), m) for m in pairs]


def early_kernel(n, dpc, ends_ref, model_hbm, vis_ref, unused_in, *rest):
    ins, (acc_ref, hre, him, unused_out, model_ref, sems) = rest[: 2 * len(NEAR)], rest[2 * len(NEAR) :]
    me = lax.axis_index("bl")
    fetch = Fetch(model_hbm, model_ref, sems, [k * dpc for k in chips_of(me, NEAR)])
    products(dpc, me, model_hbm.shape[2], ends_ref, ins, hre, him)

    def pair(b):
        acc = vis_ref[0, b], vis_ref[1, b]
        acc_ref[0, b], acc_ref[1, b] = predict(dpc, b, acc, 0, len(NEAR), model_ref, hre, him)

    fetch.each(pair)


def later_pass_kernel(
    n,
    dpc,
    ends_ref,
    model_hbm,
    mask_ref,
    power_ref,
    acc_ref,
    near_re,
    near_im,
    *rest,
):
    ins, (out_ref, model_ref, sems, hre, him, cre, cim) = rest[: 2 * len(FAR)], rest[2 * len(FAR) :]
    me = lax.axis_index("bl")
    chips = chips_of(me, NEAR + FAR)
    fetch = Fetch(model_hbm, model_ref, sems, [k * dpc for k in chips])
    products(dpc, me, model_hbm.shape[2], ends_ref, ins, hre, him)

    def pair(b):
        acc = predict(dpc, b, (acc_ref[0, b], acc_ref[1, b]), len(NEAR) * dpc, len(FAR), model_ref, hre, him)
        correlate(dpc, b, weighted(b, acc, mask_ref), len(chips), model_ref, cre, cim)

    fetch.each(pair)

    def tiles(m):
        for re, im, pairs in ((near_re, near_im, NEAR), (hre, him, FAR)):
            if m < len(pairs):
                return re, im, m
            m -= len(pairs)

    clear(dpc, mask_ref.shape[0], cre, cim)
    write_sums(dpc, chips, cre, cim, tiles, power_ref, out_ref, False)


def last_kernel(n, dpc, ends_ref, model_hbm, mask_ref, acc_ref, *rest):
    ins, (res_ref, gains_ref, model_ref, sems, hre, him) = rest[:n], rest[n:]
    me = lax.axis_index("bl")
    fetch = Fetch(model_hbm, model_ref, sems, [k * dpc for k in chips_of(me, FAR)])
    products(dpc, me, model_hbm.shape[2], ends_ref, ins[: 2 * len(FAR)], hre, him)
    per = STATIONS // n
    even = lax.rem(me, 2) == 0
    for m, k in enumerate(chips_of(me, FAR + NEAR)):
        for s in range(per):
            re, im = piece_pair(dpc, even, ins, m, me * per + s)
            for dd in range(dpc):
                at = s * SOURCE_COUNT + k * dpc + dd
                gains_ref[0, pl.ds(at, 1), :] = re[dd : dd + 1]
                gains_ref[1, pl.ds(at, 1), :] = im[dd : dd + 1]

    def pair(b):
        acc = acc_ref[0, b], acc_ref[1, b]
        acc = predict(dpc, b, acc, 0, len(FAR), model_ref, hre, him)
        res_ref[0, b], res_ref[1, b] = weighted(b, acc, mask_ref)

    fetch.each(pair)


SMEM = pl.BlockSpec(memory_space=pltpu.SMEM)
VMEM = pl.BlockSpec(memory_space=pltpu.VMEM)
HBM = pl.BlockSpec(memory_space=pltpu.HBM)


def shape(*dims, dtype=F32):
    return jax.ShapeDtypeStruct(dims, dtype)


def exchange(x):
    return lax.all_to_all(x, "bl", split_axis=0, concat_axis=0, tiled=True)


def gather(n, piece, beside):
    def send(x, o):
        return lax.ppermute(x, "bl", [(i, i ^ o) for i in range(n)])

    got = {0: piece}
    got[12], got[2], got[4], got[1] = (send(piece, o) for o in (12, 2, 4, 1))
    got[8] = send(got[12], 4)
    got[6], got[14], got[10] = send(got[4], 2), send(got[12], 2), send(got[8], 2)
    for o in (2, 4, 12, 6, 14, 8, 10):
        if o == 6:
            got[o] = beside(got[o], got)
        got[o + 1] = send(got[o], 1)
    return [got[o] for o in range(n)]


def fast_body(n, vis, model, mask, first, second, gre, gim):
    ends = jnp.concatenate([first, second])
    starts = (first.reshape(1, -1), second.reshape(1, -1), gre, gim)
    model, *starts = (pltpu.with_memory_space_constraint(x, pltpu.HBM) for x in (model, *starts))
    dpc = SOURCE_COUNT // (n // 2)
    width = dpc * 128
    pairs, times, channels = mask.shape
    params = pltpu.CompilerParams(vmem_limit_bytes=VMEM_LIMIT)
    plane = (n // 2, ROWS * dpc + TILE, channels)
    half = (len(FAR), ROWS * dpc + TILE, channels)
    lots = n * 2 * ROWS
    mine = (STATIONS * dpc + TILE, channels)
    sems = pltpu.SemaphoreType.DMA((pairs, n // 2))
    held = [pltpu.VMEM(model.shape, BF16), sems]
    held_half = [pltpu.VMEM((SOURCE_COUNT // 2,) + model.shape[1:], BF16), sems]

    def call(kernel, args, outs, scratch=(), micros=1, aliases={}):
        def place(x):
            if x is model or any(x is y for y in starts):
                return HBM
            return SMEM if x.ndim == 1 else VMEM

        return pl.pallas_call(
            functools.partial(kernel, n, dpc),
            in_specs=[place(x) for x in args],
            out_specs=[VMEM for o in outs],
            out_shape=outs,
            scratch_shapes=[pltpu.VMEM(x, F32) if isinstance(x, tuple) else x for x in scratch],
            compiler_params=params,
            input_output_aliases=aliases,
            cost_estimate=pl.CostEstimate(
                flops=0, bytes_accessed=int(micros * 3.69e6), transcendentals=0
            ),
        )(*args)

    (piece,) = call(
        pack_kernel,
        starts,
        [shape(2 * gre.shape[0] + TILE, channels)],
        [pltpu.VMEM((1, pairs), jnp.int32)] * 2 + [pltpu.SemaphoreType.DMA((4,))],
    )
    power = None

    def powers_beside(x, got):
        nonlocal power
        power, x = call(
            power_kernel, (model, mask, x), [shape(*plane), shape(*x.shape)], held, micros=20, aliases={2: 1}
        )
        return x

    got = gather(n, piece, powers_beside)
    sums, g, onehot = call(
        first_pass_kernel,
        (ends, model, vis, mask, power, *got),
        [
            shape(n, (ROWS + TILE) * dpc, channels),
            shape(*mine),
            shape(STATIONS, lots, dtype=BF16),
        ],
        held + [plane] * 4 + [(n,) + piece.shape, (STATIONS * TILE, channels), (n, channels)],
        micros=9,
    )
    powers = exchange(sums)
    (g,) = call(
        own_kernel,
        (g, onehot, powers),
        [shape(*mine)],
        [(lots, 2 * width), (lots, width)],
    )

    def slots(got, pairs):
        return [got[2 * m + c] for m in pairs for c in (0, 1)]

    def gather_near(g):
        near = None

        def beside(x, got):
            nonlocal near
            args = (ends, model, vis, x, *slots(got, NEAR))
            outs = [shape(*vis.shape), shape(*half), shape(*half), shape(*x.shape)]
            *near, x = call(early_kernel, args, outs, held_half, aliases={3: 3})
            return x

        got = gather(n, g, beside)
        return near, slots(got, FAR + NEAR)

    for step in range(1, ITERS):
        near, got = gather_near(g)
        (den,) = call(
            prepare_kernel,
            (g, onehot, powers),
            [shape(STATIONS, width)],
            [(lots, width)] * 2,
            micros=2,
        )
        (sums,) = call(
            later_pass_kernel,
            (ends, model, mask, power, *near, *got[: 2 * len(FAR)]),
            [shape(n, ROWS * dpc, channels)],
            held + [half] * 2 + [plane] * 2,
            micros=7,
        )
        sums = exchange(sums)
        (g,) = call(
            later_own_kernel,
            (g, onehot, den, sums),
            [shape(*mine)],
            [(lots, width)] * 2,
        )
    near, got = gather_near(g)
    residual, gains = call(
        last_kernel,
        (ends, model, mask, near[0], *got),
        [shape(*vis.shape), shape(2, *gre.shape)],
        held_half + [half] * 2,
        micros=4,
    )
    return gains, residual


def block_pass(full_re, full_im, vis_blk, coh_blk, weight, first, second, want_sums):
    ar = jnp.transpose(full_re[first], (1, 0, 2))
    ai = jnp.transpose(full_im[first], (1, 0, 2))
    br = jnp.transpose(full_re[second], (1, 0, 2))
    bi = jnp.transpose(full_im[second], (1, 0, 2))
    mr = coh_blk[:, 0].astype(F32)
    mi = coh_blk[:, 1].astype(F32)
    hr = ar * br + ai * bi
    hi = ai * br - ar * bi
    hr_t, hi_t = hr[:, :, None], hi[:, :, None]
    res_re = weight * (vis_blk[0] - jnp.sum(hr_t * mr - hi_t * mi, 0))
    res_im = weight * (vis_blk[1] - jnp.sum(hr_t * mi + hi_t * mr, 0))
    residual = jnp.stack([res_re, res_im])
    if not want_sums:
        return (residual, None)
    power = jnp.sum(weight[None] * (mr * mr + mi * mi), 2)
    sum_re = jnp.sum(mr * res_re + mi * res_im, 2) + hr * power
    sum_im = jnp.sum(mr * res_im - mi * res_re, 2) + hi * power
    terms_first = jnp.stack([br * sum_re - bi * sum_im, br * sum_im + bi * sum_re, power * (br * br + bi * bi)])
    terms_second = jnp.stack([ar * sum_re + ai * sum_im, ai * sum_re - ar * sum_im, power * (ar * ar + ai * ai)])
    stations = jnp.arange(STATIONS, dtype=jnp.int32)
    onehot_first = (first[:, None] == stations[None, :]).astype(F32)
    onehot_second = (second[:, None] == stations[None, :]).astype(F32)
    exact = lax.Precision.HIGHEST
    sums = jnp.einsum("bs,cdbf->csdf", onehot_first, terms_first, precision=exact)
    sums = sums + jnp.einsum("bs,cdbf->csdf", onehot_second, terms_second, precision=exact)
    return (residual, sums)


def plain_body(vis, model, mask, first, second, gre, gim):
    weight = mask.astype(F32)
    rows, channels = gre.shape
    shaped = (STATIONS, SOURCE_COUNT, channels)
    full_re = lax.all_gather(gre, "bl", axis=0, tiled=True).reshape(shaped)
    full_im = lax.all_gather(gim, "bl", axis=0, tiled=True).reshape(shaped)
    for step in range(ITERS):
        unused, sums = block_pass(full_re, full_im, vis, model, weight, first, second, True)
        totals = lax.psum(sums, "bl")
        denom = totals[2] + ridge
        full_re = 0.5 * (full_re + totals[0] / denom)
        full_im = 0.5 * (full_im + totals[1] / denom)
    residual, unused = block_pass(full_re, full_im, vis, model, weight, first, second, False)
    both = jnp.stack([full_re, full_im]).reshape(2, STATIONS * SOURCE_COUNT, channels)
    return lax.dynamic_slice_in_dim(both, lax.axis_index("bl") * rows, rows, 1), residual


def solution(mesh):
    n = mesh.shape["bl"]
    split = n == 16

    def body(vis, model, mask, first, second, gre, gim):
        if split and mask.shape[0] <= ROWS:
            return fast_body(n, vis, model, mask, first, second, gre, gim)
        return plain_body(vis, model, mask, first, second, gre, gim)

    in_specs = (
        P(None, ("grp", "bl"), None, None),
        P(None, None, ("grp", "bl"), None, None),
        P(("grp", "bl"), None, None),
        P(("grp", "bl")),
        P(("grp", "bl")),
        P(("grp", "bl"), None),
        P(("grp", "bl"), None),
    )
    out_specs = (P(None, ("grp", "bl"), None), P(None, ("grp", "bl"), None, None))
    return jax.shard_map(body, mesh=mesh, in_specs=in_specs, out_specs=out_specs, check_vma=False)
```

```python
import functools

import jax
import jax.numpy as jnp
from jax import lax
from jax.experimental import pallas as pl
from jax.experimental.pallas import tpu as pltpu
from jax.sharding import PartitionSpec as P

STATIONS = 64
SOURCE_COUNT = 40
ITERS = 2
ROWS = 16

ridge = 1.0
F32 = jnp.float32
BF16 = jnp.bfloat16
VMEM_LIMIT = 24 * 1024 * 1024


def swap(x):
    return pltpu.roll(x, x.shape[-1] // 2, axis=x.ndim - 1)


def lower(shape):
    return lax.broadcasted_iota(jnp.int32, shape, len(shape) - 1) < shape[-1] // 2


def cross(a, b):
    lo = lower(a.shape)
    return jnp.where(lo, a, swap(b)), jnp.where(lo, swap(a), b)


def halves_of(x):
    hi = x.astype(BF16)
    return hi, (x - hi.astype(F32)).astype(BF16)


def pick(onehot, x, dims):
    return sum(
        lax.dot_general(onehot, part, (dims, ((), ())), preferred_element_type=F32)
        for part in halves_of(x)
    )


TILE = 8


def pack_kernel(n, dpc, first_hbm, second_hbm, re_hbm, im_hbm, out_ref, first_ref, second_ref, sems):
    rows = re_hbm.shape[0]
    copies = [
        pltpu.make_async_copy(first_hbm, first_ref, sems.at[0]),
        pltpu.make_async_copy(second_hbm, second_ref, sems.at[1]),
        pltpu.make_async_copy(re_hbm, out_ref.at[pl.ds(0, rows)], sems.at[2]),
        pltpu.make_async_copy(im_hbm, out_ref.at[pl.ds(rows, rows)], sems.at[3]),
    ]
    for copy in copies:
        copy.start()
    out_ref[2 * rows :] = jnp.zeros((TILE, 128), F32)
    for copy in copies:
        copy.wait()
    pairs = first_ref.shape[1]
    out_ref[2 * rows : 2 * rows + 1, :pairs] = (first_ref[...] + 1).astype(F32)
    out_ref[2 * rows : 2 * rows + 1, ROWS : ROWS + pairs] = (second_ref[...] + 1).astype(F32)


class Fetch:
    def __init__(self, model, held, sems, firsts=(0,)):
        self.model, self.held, self.sems, self.firsts = model, held, sems, firsts
        self.pairs = held.shape[2]
        self.size = 3 if self.pairs % 3 == 0 else 1
        for i in range(self.pairs // self.size):
            for copy in self.part(i):
                copy.start()

    def part(self, i):
        count = self.held.shape[0] // len(self.firsts)
        pairs = pl.ds(i * self.size, self.size)
        return [
            pltpu.make_async_copy(
                self.model.at[pl.ds(first, count), :, pairs],
                self.held.at[pl.ds(j * count, count), :, pairs],
                self.sems.at[i, j],
            )
            for j, first in enumerate(self.firsts)
        ]

    def each(self, body, after=lambda i: None):
        def part(i, carry):
            for copy in self.part(i):
                copy.wait()
            def one(u, carry):
                body(i * self.size + u)
                return carry

            carry = lax.fori_loop(0, self.size, one, carry)
            after(i)
            return carry

        lax.fori_loop(0, self.pairs // self.size, part, 0)


def power_kernel(n, dpc, ends_in, model_hbm, mask_ref, unused_in, ends_ref, out_ref, unused_out, model_ref, sems):
    fetch = Fetch(model_hbm, model_ref, sems)
    for i in range(ends_in.shape[0]):
        ends_ref[i] = ends_in[i]
    out_ref[...] = jnp.zeros_like(out_ref)

    def pair(b):
        weight = mask_ref[b].astype(F32)
        for d in range(SOURCE_COUNT):
            mr = model_ref[d, 0, b].astype(F32)
            mi = model_ref[d, 1, b].astype(F32)
            row = pl.ds(b * dpc + d % dpc, 1)
            out_ref[d // dpc, row, :] = jnp.sum(weight * (mr * mr + mi * mi), axis=0, keepdims=True)

    fetch.each(pair)


def wide(ref, dpc):
    return jnp.concatenate([ref[pl.ds(dd, STATIONS, stride=dpc), :] for dd in range(dpc)], axis=1)


def put(ref, value, dpc):
    for dd in range(dpc):
        ref[pl.ds(dd, STATIONS, stride=dpc), :] = value[:, dd * 128 : (dd + 1) * 128]
    ref[STATIONS * dpc :, :] = jnp.zeros((TILE, 128), F32)


def first_own(n, dpc, me, ins, g_ref, onehot_ref, split, lines):
    k, c = lax.div(me, 2), lax.rem(me, 2)
    per = STATIONS // n
    rows = per * SOURCE_COUNT
    for o in range(n):
        peer = jnp.bitwise_xor(me, o)
        lines[pl.ds(peer, 1), :] = ins[o][2 * rows : 2 * rows + 1, :]
        for s in range(per):
            at = s * SOURCE_COUNT + k * dpc
            x0, x1 = cross(ins[o][pl.ds(at, TILE), :], ins[o][pl.ds(rows + at, TILE), :])
            to = pl.multiple_of((peer * per + s) * TILE, TILE)
            split[pl.ds(to, TILE), :] = jnp.where(c == 0, x0, x1)
    g = jnp.concatenate([split[pl.ds(dd, STATIONS, stride=TILE), :] for dd in range(dpc)], axis=1)
    put(g_ref, g, dpc)
    across = 128 // (2 * ROWS)
    station = lax.broadcasted_iota(jnp.int32, (STATIONS, 128), 0)
    for group in range(n // across):
        marks = jnp.zeros((1, 128), F32)
        for i in range(across):
            row = lines[group * across + i : group * across + i + 1, :]
            marks = marks + (pltpu.roll(row, i * 2 * ROWS, axis=1) if i else row)
        hit = station + 1 == marks.astype(jnp.int32)
        onehot_ref[:, group * 128 : (group + 1) * 128] = jnp.where(hit, 1.0, 0.0).astype(BF16)


def fill_powers(n, dpc, sums, sel_ref, terms, base):
    lo = lower((TILE, 128))
    for o in range(n):
        r = o * 2 * ROWS
        for dd in range(dpc):
            cols = slice(dd * 128, (dd + 1) * 128)
            dcols = slice(base + dd * 128, base + (dd + 1) * 128)
            W = sums[o, pl.ds(ROWS * dpc + dd, TILE, stride=dpc), :]
            Wx = swap(W)
            W = jnp.concatenate([jnp.where(lo, W, Wx), jnp.where(lo, Wx, W)], 0)
            p = sel_ref[r : r + ROWS, cols]
            q = sel_ref[r + ROWS : r + 2 * ROWS, cols]
            p2, q2 = p * p, q * q
            terms[r : r + ROWS, dcols] = W * (q2 + swap(q2))
            terms[r + ROWS : r + 2 * ROWS, dcols] = W * (p2 + swap(p2))


def fill_sums(n, dpc, sums, sel_ref, terms):
    lo = lower((ROWS, 128))
    sign = jnp.where(lo, -1.0, 1.0)
    for o in range(n):
        r = o * 2 * ROWS
        for dd in range(dpc):
            cols = slice(dd * 128, (dd + 1) * 128)
            B = sums[o, pl.ds(dd, ROWS, stride=dpc), :]
            p = sel_ref[r : r + ROWS, cols]
            q = sel_ref[r + ROWS : r + 2 * ROWS, cols]
            Bx = swap(B)
            Brr, Bii = jnp.where(lo, B, Bx), sign * jnp.where(lo, Bx, B)
            terms[r : r + ROWS, cols] = Brr * q + Bii * swap(q)
            terms[r + ROWS : r + 2 * ROWS, cols] = Brr * p - Bii * swap(p)


def own_kernel(n, dpc, g_in, onehot_ref, sums, g_out, terms, sel_ref):
    width = dpc * 128
    sel_ref[...] = pick(onehot_ref[...], wide(g_in, dpc), ((0,), (0,)))
    fill_sums(n, dpc, sums, sel_ref, terms)
    fill_powers(n, dpc, sums, sel_ref, terms, width)
    total = pick(onehot_ref[...], terms[...], ((1,), (0,)))
    put(g_out, 0.5 * (wide(g_in, dpc) + total[:, :width] / (total[:, width:] + ridge)), dpc)


def prepare_kernel(n, dpc, g_ref, onehot_ref, sums, den_ref, terms, sel_ref):
    sel_ref[...] = pick(onehot_ref[...], wide(g_ref, dpc), ((0,), (0,)))
    fill_powers(n, dpc, sums, sel_ref, terms, 0)
    den_ref[...] = pick(onehot_ref[...], terms[...], ((1,), (0,))) + ridge


def later_own_kernel(n, dpc, g_in, onehot_ref, den_ref, sums, g_out, terms, sel_ref):
    sel_ref[...] = pick(onehot_ref[...], wide(g_in, dpc), ((0,), (0,)))
    fill_sums(n, dpc, sums, sel_ref, terms)
    total = pick(onehot_ref[...], terms[...], ((1,), (0,)))
    put(g_out, 0.5 * (wide(g_in, dpc) + total / den_ref[...]), dpc)


def clear(dpc, pairs, *refs):
    for ref in refs:
        chips, rows, _ = ref.shape
        for m in range(chips):
            ref[m, pairs * dpc :, :] = jnp.zeros((rows - pairs * dpc, 128), F32)


def products_first(n, dpc, me, pairs, ends_ref, ins, hre, him, stack):
    per = STATIONS // n
    rows = per * SOURCE_COUNT
    for o in range(n):
        stack[jnp.bitwise_xor(me, o)] = ins[o][...]

    def pair(b, carry):
        p, q = ends_ref[b], ends_ref[pairs + b]

        def block(station, k, part):
            at = lax.rem(station, per) * SOURCE_COUNT + k * dpc + part * rows
            return stack[lax.div(station, per), pl.ds(at, TILE), :]

        for k in range(n // 2):
            pr, pi, qr, qi = block(p, k, 0), block(p, k, 1), block(q, k, 0), block(q, k, 1)
            hre[k, pl.ds(b * dpc, TILE), :] = pr * qr + pi * qi
            him[k, pl.ds(b * dpc, TILE), :] = pi * qr - pr * qi
        return carry

    lax.fori_loop(0, pairs, pair, 0, unroll=5 if pairs % 5 == 0 else 1)
    clear(dpc, pairs, hre, him)


def piece_pair(dpc, even, ins, m, station):
    a = ins[2 * m][pl.ds(station * dpc, TILE), :]
    b = ins[2 * m + 1][pl.ds(station * dpc, TILE), :]
    return cross(jnp.where(even, a, b), jnp.where(even, b, a))


def products(dpc, me, pairs, ends_ref, ins, hre, him):
    even = lax.rem(me, 2) == 0

    def pair(b, carry):
        p, q = ends_ref[b], ends_ref[pairs + b]
        for m in range(len(ins) // 2):
            pr, pi = piece_pair(dpc, even, ins, m, p)
            qr, qi = piece_pair(dpc, even, ins, m, q)
            hre[m, pl.ds(b * dpc, TILE), :] = pr * qr + pi * qi
            him[m, pl.ds(b * dpc, TILE), :] = pi * qr - pr * qi
        return carry

    lax.fori_loop(0, pairs, pair, 0, unroll=5 if pairs % 5 == 0 else 1)
    clear(dpc, pairs, hre, him)


def predict(dpc, b, acc, first, chips, model_ref, hre, him):
    tiles = [slice(t, t + TILE) for t in range(0, acc[0].shape[0], TILE)]
    acc_re, acc_im = ([x[t] for t in tiles] for x in acc)
    for m in range(chips):
        for dd in range(dpc):
            d = first + m * dpc + dd
            mr = model_ref[d, 0, b].astype(F32)
            mi = model_ref[d, 1, b].astype(F32)
            row = pl.ds(b * dpc + dd, TILE, stride=0)
            hr, hi = hre[m, row, :], him[m, row, :]
            for j, t in enumerate(tiles):
                acc_re[j] = acc_re[j] - (hr * mr[t] - hi * mi[t])
                acc_im[j] = acc_im[j] - (hr * mi[t] + hi * mr[t])
    return jnp.concatenate(acc_re, 0), jnp.concatenate(acc_im, 0)


def weighted(b, acc, mask_ref):
    weight = mask_ref[b].astype(F32)
    return weight * acc[0], weight * acc[1]


def fold(a, b, step):
    if a is None:
        return None
    if b is None:
        return a + pltpu.roll(a, step, axis=0)
    mine = (lax.broadcasted_iota(jnp.int32, a.shape, 0) & step) == 0
    return jnp.where(mine, a, b) + pltpu.roll(jnp.where(mine, b, a), step, axis=0)


def row_sums(values):
    values = list(values) + [None] * (TILE - len(values))
    step = 1
    while step < TILE:
        values = [fold(a, b, step) for a, b in zip(values[::2], values[1::2])]
        step *= 2
    return values[0]


def tile_sum(x):
    total = x[:TILE]
    for t in range(1, x.shape[0] // TILE):
        total = total + x[t * TILE : (t + 1) * TILE]
    return total


def correlate(dpc, b, res, chips, model_ref, cre, cim):
    res_re, res_im = res
    for m in range(chips):
        re, im = [], []
        for dd in range(dpc):
            mr = model_ref[m * dpc + dd, 0, b].astype(F32)
            mi = model_ref[m * dpc + dd, 1, b].astype(F32)
            re.append(tile_sum(mr * res_re + mi * res_im))
            im.append(tile_sum(mr * res_im - mi * res_re))
        cre[m, pl.ds(b * dpc, TILE), :] = row_sums(re)
        cim[m, pl.ds(b * dpc, TILE), :] = row_sums(im)


def write_sums(dpc, chips, cre, cim, tiles, power_ref, out_ref, out_hbm, sems, start):
    copies = []
    for m, k in enumerate(chips):
        re, im, at = tiles(m)
        for t in range(ROWS * dpc // TILE):
            rows = slice(t * TILE, (t + 1) * TILE)
            w = power_ref[k, rows, :]
            x0, x1 = cross(cre[m, rows, :] + re[at, rows, :] * w, cim[m, rows, :] + im[at, rows, :] * w)
            out_ref[2 * m, rows, :] = x0
            out_ref[2 * m + 1, rows, :] = x1
        if start:
            for t in range(dpc):
                x0, x1 = cross(
                    power_ref[k, t * TILE : (t + 1) * TILE, :],
                    power_ref[k, (t + dpc) * TILE : (t + dpc + 1) * TILE, :],
                )
                rows = slice(ROWS * dpc + t * TILE, ROWS * dpc + (t + 1) * TILE)
                out_ref[2 * m, rows, :] = x0
                out_ref[2 * m + 1, rows, :] = x1
        copies.append(
            pltpu.make_async_copy(out_ref.at[pl.ds(2 * m, 2)], out_hbm.at[pl.ds(2 * k, 2)], sems.at[m])
        )
        copies[-1].start()
    for copy in copies:
        copy.wait()


def first_pass_kernel(n, dpc, ends_ref, model_hbm, vis_ref, mask_ref, power_ref, *rest):
    ins, rest = rest[:n], rest[n:]
    out_hbm, g_ref, onehot_ref, out_ref, out_sems, model_ref, sems, hre, him, cre, cim, stack, split, lines = rest
    fetch = Fetch(model_hbm, model_ref, sems)
    me = lax.axis_index("bl")
    pairs, chips = mask_ref.shape[0], n // 2
    products_first(n, dpc, me, pairs, ends_ref, ins, hre, him, stack)
    first_own(n, dpc, me, ins, g_ref, onehot_ref, split, lines)

    def pair(b):
        acc = predict(dpc, b, (vis_ref[0, b], vis_ref[1, b]), 0, chips, model_ref, hre, him)
        correlate(dpc, b, weighted(b, acc, mask_ref), chips, model_ref, cre, cim)

    fetch.each(pair)
    clear(dpc, pairs, cre, cim)
    write_sums(dpc, range(chips), cre, cim, lambda m: (hre, him, m), power_ref, out_ref, out_hbm, out_sems, True)


NEAR, FAR = (0, 1, 2, 6), (3, 4, 5, 7)


def chips_of(me, pairs):
    return [jnp.bitwise_xor(lax.div(me, 2), m) for m in pairs]


def early_kernel(n, dpc, ends_ref, model_hbm, vis_ref, unused_in, *rest):
    ins, (acc_ref, hre, him, unused_out, model_ref, sems) = rest[: 2 * len(NEAR)], rest[2 * len(NEAR) :]
    me = lax.axis_index("bl")
    fetch = Fetch(model_hbm, model_ref, sems, [k * dpc for k in chips_of(me, NEAR)])
    products(dpc, me, model_hbm.shape[2], ends_ref, ins, hre, him)

    def pair(b):
        acc = vis_ref[0, b], vis_ref[1, b]
        acc_ref[0, b], acc_ref[1, b] = predict(dpc, b, acc, 0, len(NEAR), model_ref, hre, him)

    fetch.each(pair)


def later_pass_kernel(
    n,
    dpc,
    ends_ref,
    model_hbm,
    mask_ref,
    power_ref,
    acc_ref,
    near_re,
    near_im,
    *rest,
):
    ins, rest = rest[: 2 * len(FAR)], rest[2 * len(FAR) :]
    out_hbm, out_ref, out_sems, model_ref, sems, hre, him, cre, cim = rest
    me = lax.axis_index("bl")
    chips = chips_of(me, NEAR + FAR)
    fetch = Fetch(model_hbm, model_ref, sems, [k * dpc for k in chips])
    products(dpc, me, model_hbm.shape[2], ends_ref, ins, hre, him)

    def pair(b):
        acc = predict(dpc, b, (acc_ref[0, b], acc_ref[1, b]), len(NEAR) * dpc, len(FAR), model_ref, hre, him)
        correlate(dpc, b, weighted(b, acc, mask_ref), len(chips), model_ref, cre, cim)

    fetch.each(pair)

    def tiles(m):
        for re, im, pairs in ((near_re, near_im, NEAR), (hre, him, FAR)):
            if m < len(pairs):
                return re, im, m
            m -= len(pairs)

    clear(dpc, mask_ref.shape[0], cre, cim)
    write_sums(dpc, chips, cre, cim, tiles, power_ref, out_ref, out_hbm, out_sems, False)


def last_kernel(n, dpc, ends_ref, model_hbm, mask_ref, acc_ref, *rest):
    ins, (res_hbm, gains_ref, res_ref, res_sems, model_ref, sems, hre, him) = rest[:n], rest[n:]
    me = lax.axis_index("bl")
    fetch = Fetch(model_hbm, model_ref, sems, [k * dpc for k in chips_of(me, FAR)])
    products(dpc, me, model_hbm.shape[2], ends_ref, ins[: 2 * len(FAR)], hre, him)
    per = STATIONS // n
    even = lax.rem(me, 2) == 0
    for m, k in enumerate(chips_of(me, FAR + NEAR)):
        for s in range(per):
            re, im = piece_pair(dpc, even, ins, m, me * per + s)
            for dd in range(dpc):
                at = s * SOURCE_COUNT + k * dpc + dd
                gains_ref[0, pl.ds(at, 1), :] = re[dd : dd + 1]
                gains_ref[1, pl.ds(at, 1), :] = im[dd : dd + 1]

    def pair(b):
        acc = acc_ref[0, b], acc_ref[1, b]
        acc = predict(dpc, b, acc, 0, len(FAR), model_ref, hre, him)
        res_ref[0, b], res_ref[1, b] = weighted(b, acc, mask_ref)

    def leave(i):
        part = pl.ds(i * fetch.size, fetch.size)
        return pltpu.make_async_copy(res_ref.at[:, part], res_hbm.at[:, part], res_sems.at[i])

    fetch.each(pair, lambda i: leave(i).start())
    for i in range(mask_ref.shape[0] // fetch.size):
        leave(i).wait()


SMEM = pl.BlockSpec(memory_space=pltpu.SMEM)
VMEM = pl.BlockSpec(memory_space=pltpu.VMEM)
HBM = pl.BlockSpec(memory_space=pltpu.HBM)
ANY = pl.BlockSpec(memory_space=pl.ANY)


def shape(*dims, dtype=F32):
    return jax.ShapeDtypeStruct(dims, dtype)


def exchange(x):
    return lax.all_to_all(x, "bl", split_axis=0, concat_axis=0, tiled=True)


def gather(n, piece, beside):
    def send(x, o):
        return lax.ppermute(x, "bl", [(i, i ^ o) for i in range(n)])

    got = {0: piece}
    got[12], got[2], got[4], got[1] = (send(piece, o) for o in (12, 2, 4, 1))
    got[8] = send(got[12], 4)
    got[6], got[14], got[10] = send(got[4], 2), send(got[12], 2), send(got[8], 2)
    for o in (2, 4, 12, 6, 14, 8, 10):
        if o == 6:
            got[o] = beside(got[o], got)
        got[o + 1] = send(got[o], 1)
    return [got[o] for o in range(n)]


def fast_body(n, vis, model, mask, first, second, gre, gim):
    ends = jnp.concatenate([first, second])
    starts = (first.reshape(1, -1), second.reshape(1, -1), gre, gim)
    model, *starts = (pltpu.with_memory_space_constraint(x, pltpu.HBM) for x in (model, *starts))
    dpc = SOURCE_COUNT // (n // 2)
    width = dpc * 128
    pairs, times, channels = mask.shape
    params = pltpu.CompilerParams(vmem_limit_bytes=VMEM_LIMIT)
    plane = (n // 2, ROWS * dpc + TILE, channels)
    half = (len(FAR), ROWS * dpc + TILE, channels)
    lots = n * 2 * ROWS
    mine = (STATIONS * dpc + TILE, channels)
    sems = pltpu.SemaphoreType.DMA((pairs, n // 2))
    few = pltpu.SemaphoreType.DMA((n // 2,))
    held = [pltpu.VMEM(model.shape, BF16), sems]
    held_half = [pltpu.VMEM((SOURCE_COUNT // 2,) + model.shape[1:], BF16), sems]

    def call(kernel, args, outs, scratch=(), micros=1, aliases={}, away=()):
        def place(x):
            if x is model or any(x is y for y in starts):
                return HBM
            return SMEM if x.ndim == 1 else VMEM

        return pl.pallas_call(
            functools.partial(kernel, n, dpc),
            in_specs=[place(x) for x in args],
            out_specs=[ANY if i in away else SMEM if o.dtype == jnp.int32 else VMEM for i, o in enumerate(outs)],
            out_shape=outs,
            scratch_shapes=[pltpu.VMEM(x, F32) if isinstance(x, tuple) else x for x in scratch],
            compiler_params=params,
            input_output_aliases=aliases,
            cost_estimate=pl.CostEstimate(
                flops=0, bytes_accessed=int(micros * 3.69e6), transcendentals=0
            ),
        )(*args)

    (piece,) = call(
        pack_kernel,
        starts,
        [shape(2 * gre.shape[0] + TILE, channels)],
        [pltpu.VMEM((1, pairs), jnp.int32)] * 2 + [pltpu.SemaphoreType.DMA((4,))],
    )
    power = None

    def powers_beside(x, got):
        nonlocal power, ends
        outs = [pltpu.SMEM(ends.shape, jnp.int32), shape(*plane), shape(*x.shape)]
        ends, power, x = call(power_kernel, (ends, model, mask, x), outs, held, micros=20, aliases={3: 2})
        return x

    got = gather(n, piece, powers_beside)
    sums, g, onehot = call(
        first_pass_kernel,
        (ends, model, vis, mask, power, *got),
        [
            shape(n, (ROWS + TILE) * dpc, channels),
            shape(*mine),
            shape(STATIONS, lots, dtype=BF16),
        ],
        [(n, (ROWS + TILE) * dpc, channels), few]
        + held
        + [plane] * 4
        + [(n,) + piece.shape, (STATIONS * TILE, channels), (n, channels)],
        micros=9,
        away=(0,),
    )
    powers = exchange(sums)
    (g,) = call(
        own_kernel,
        (g, onehot, powers),
        [shape(*mine)],
        [(lots, 2 * width), (lots, width)],
    )

    def slots(got, pairs):
        return [got[2 * m + c] for m in pairs for c in (0, 1)]

    def gather_near(g):
        near = None

        def beside(x, got):
            nonlocal near
            args = (ends, model, vis, x, *slots(got, NEAR))
            outs = [shape(*vis.shape), shape(*half), shape(*half), shape(*x.shape)]
            *near, x = call(early_kernel, args, outs, held_half, aliases={3: 3})
            return x

        got = gather(n, g, beside)
        return near, slots(got, FAR + NEAR)

    for step in range(1, ITERS):
        near, got = gather_near(g)
        (den,) = call(
            prepare_kernel,
            (g, onehot, powers),
            [shape(STATIONS, width)],
            [(lots, width)] * 2,
            micros=2,
        )
        (sums,) = call(
            later_pass_kernel,
            (ends, model, mask, power, *near, *got[: 2 * len(FAR)]),
            [shape(n, ROWS * dpc, channels)],
            [(n, ROWS * dpc, channels), few] + held + [half] * 2 + [plane] * 2,
            micros=7,
            away=(0,),
        )
        sums = exchange(sums)
        (g,) = call(
            later_own_kernel,
            (g, onehot, den, sums),
            [shape(*mine)],
            [(lots, width)] * 2,
        )
    near, got = gather_near(g)
    residual, gains = call(
        last_kernel,
        (ends, model, mask, near[0], *got),
        [shape(*vis.shape), shape(2, *gre.shape)],
        [vis.shape, pltpu.SemaphoreType.DMA((pairs,))] + held_half + [half] * 2,
        micros=4,
        away=(0,),
    )
    return gains, residual


def block_pass(full_re, full_im, vis_blk, coh_blk, weight, first, second, want_sums):
    ar = jnp.transpose(full_re[first], (1, 0, 2))
    ai = jnp.transpose(full_im[first], (1, 0, 2))
    br = jnp.transpose(full_re[second], (1, 0, 2))
    bi = jnp.transpose(full_im[second], (1, 0, 2))
    mr = coh_blk[:, 0].astype(F32)
    mi = coh_blk[:, 1].astype(F32)
    hr = ar * br + ai * bi
    hi = ai * br - ar * bi
    hr_t, hi_t = hr[:, :, None], hi[:, :, None]
    res_re = weight * (vis_blk[0] - jnp.sum(hr_t * mr - hi_t * mi, 0))
    res_im = weight * (vis_blk[1] - jnp.sum(hr_t * mi + hi_t * mr, 0))
    residual = jnp.stack([res_re, res_im])
    if not want_sums:
        return (residual, None)
    power = jnp.sum(weight[None] * (mr * mr + mi * mi), 2)
    sum_re = jnp.sum(mr * res_re + mi * res_im, 2) + hr * power
    sum_im = jnp.sum(mr * res_im - mi * res_re, 2) + hi * power
    terms_first = jnp.stack([br * sum_re - bi * sum_im, br * sum_im + bi * sum_re, power * (br * br + bi * bi)])
    terms_second = jnp.stack([ar * sum_re + ai * sum_im, ai * sum_re - ar * sum_im, power * (ar * ar + ai * ai)])
    stations = jnp.arange(STATIONS, dtype=jnp.int32)
    onehot_first = (first[:, None] == stations[None, :]).astype(F32)
    onehot_second = (second[:, None] == stations[None, :]).astype(F32)
    exact = lax.Precision.HIGHEST
    sums = jnp.einsum("bs,cdbf->csdf", onehot_first, terms_first, precision=exact)
    sums = sums + jnp.einsum("bs,cdbf->csdf", onehot_second, terms_second, precision=exact)
    return (residual, sums)


def plain_body(vis, model, mask, first, second, gre, gim):
    weight = mask.astype(F32)
    rows, channels = gre.shape
    shaped = (STATIONS, SOURCE_COUNT, channels)
    full_re = lax.all_gather(gre, "bl", axis=0, tiled=True).reshape(shaped)
    full_im = lax.all_gather(gim, "bl", axis=0, tiled=True).reshape(shaped)
    for step in range(ITERS):
        unused, sums = block_pass(full_re, full_im, vis, model, weight, first, second, True)
        totals = lax.psum(sums, "bl")
        denom = totals[2] + ridge
        full_re = 0.5 * (full_re + totals[0] / denom)
        full_im = 0.5 * (full_im + totals[1] / denom)
    residual, unused = block_pass(full_re, full_im, vis, model, weight, first, second, False)
    both = jnp.stack([full_re, full_im]).reshape(2, STATIONS * SOURCE_COUNT, channels)
    return lax.dynamic_slice_in_dim(both, lax.axis_index("bl") * rows, rows, 1), residual


def solution(mesh):
    n = mesh.shape["bl"]
    split = n == 16

    def body(vis, model, mask, first, second, gre, gim):
        if split and mask.shape[0] <= ROWS:
            return fast_body(n, vis, model, mask, first, second, gre, gim)
        return plain_body(vis, model, mask, first, second, gre, gim)

    in_specs = (
        P(None, ("grp", "bl"), None, None),
        P(None, None, ("grp", "bl"), None, None),
        P(("grp", "bl"), None, None),
        P(("grp", "bl")),
        P(("grp", "bl")),
        P(("grp", "bl"), None),
        P(("grp", "bl"), None),
    )
    out_specs = (P(None, ("grp", "bl"), None), P(None, ("grp", "bl"), None, None))
    return jax.shard_map(body, mesh=mesh, in_specs=in_specs, out_specs=out_specs, check_vma=False)
```

```python
import functools

import jax
import jax.numpy as jnp
from jax import lax
from jax.experimental import pallas as pl
from jax.experimental.pallas import tpu as pltpu
from jax.sharding import PartitionSpec as P

STATIONS = 64
SOURCE_COUNT = 40
ITERS = 2
ROWS = 16

ridge = 1.0
F32 = jnp.float32
BF16 = jnp.bfloat16
VMEM_LIMIT = 24 * 1024 * 1024


def swap(x):
    return pltpu.roll(x, x.shape[-1] // 2, axis=x.ndim - 1)


def lower(shape):
    return lax.broadcasted_iota(jnp.int32, shape, len(shape) - 1) < shape[-1] // 2


def cross(a, b):
    lo = lower(a.shape)
    return jnp.where(lo, a, swap(b)), jnp.where(lo, swap(a), b)


def halves_of(x):
    hi = x.astype(BF16)
    return hi, (x - hi.astype(F32)).astype(BF16)


def pick(onehot, x, dims):
    return sum(
        lax.dot_general(onehot, part, (dims, ((), ())), preferred_element_type=F32)
        for part in halves_of(x)
    )


TILE = 8
PARTS = (1, 3, 7, ROWS)


def pack_kernel(n, dpc, first_ref, second_ref, re_ref, im_ref, out_ref, sems):
    rows = re_ref.shape[0]
    copies = [
        pltpu.make_async_copy(re_ref, out_ref.at[pl.ds(0, rows)], sems.at[0]),
        pltpu.make_async_copy(im_ref, out_ref.at[pl.ds(rows, rows)], sems.at[1]),
    ]
    for copy in copies:
        copy.start()
    lane = lax.broadcasted_iota(jnp.int32, (TILE, 128), 1)
    marks = jnp.zeros((TILE, 128), F32)
    for r in range(first_ref.shape[0]):
        marks = jnp.where(lane == r, (first_ref[r] + 1).astype(F32), marks)
        marks = jnp.where(lane == ROWS + r, (second_ref[r] + 1).astype(F32), marks)
    out_ref[2 * rows :] = marks
    for copy in copies:
        copy.wait()


class Fetch:
    def __init__(self, model, held, sems, firsts=(0,)):
        count, pairs = held.shape[0] // len(firsts), held.shape[2]
        self.copies = []
        self.ends = [0] + [min(end, pairs) for end in PARTS]
        for i in range(len(PARTS)):
            part = pl.ds(self.ends[i], self.ends[i + 1] - self.ends[i])
            self.copies.append([])
            for j, first in enumerate(firsts):
                self.copies[i].append(
                    pltpu.make_async_copy(
                        model.at[pl.ds(first, count), :, part],
                        held.at[pl.ds(j * count, count), :, part],
                        sems.at[i, j],
                    )
                )
        for copies in self.copies:
            for copy in copies:
                copy.start()

    def each(self, body):
        for i, copies in enumerate(self.copies):
            for copy in copies:
                copy.wait()
            lax.fori_loop(self.ends[i], self.ends[i + 1], body, 0)


def power_kernel(n, dpc, model_hbm, mask_ref, unused_in, out_ref, unused_out, model_ref, sems):
    fetch = Fetch(model_hbm, model_ref, sems)
    out_ref[...] = jnp.zeros_like(out_ref)

    def pair(b, carry):
        weight = mask_ref[b].astype(F32)
        for d in range(SOURCE_COUNT):
            mr = model_ref[d, 0, b].astype(F32)
            mi = model_ref[d, 1, b].astype(F32)
            row = pl.ds(b * dpc + d % dpc, 1)
            out_ref[d // dpc, row, :] = jnp.sum(weight * (mr * mr + mi * mi), axis=0, keepdims=True)
        return carry

    fetch.each(pair)


def wide(ref, dpc):
    return jnp.concatenate([ref[pl.ds(dd, STATIONS, stride=dpc), :] for dd in range(dpc)], axis=1)


def put(ref, value, dpc):
    for dd in range(dpc):
        ref[pl.ds(dd, STATIONS, stride=dpc), :] = value[:, dd * 128 : (dd + 1) * 128]
    ref[STATIONS * dpc :, :] = jnp.zeros((TILE, 128), F32)


def first_own_kernel(n, dpc, me_ref, *rest):
    ins, (g_ref, onehot_ref, split, lines) = rest[:n], rest[n:]
    me = me_ref[0]
    k, c = lax.div(me, 2), lax.rem(me, 2)
    per = STATIONS // n
    rows = per * SOURCE_COUNT
    for o in range(n):
        peer = jnp.bitwise_xor(me, o)
        lines[pl.ds(peer, 1), :] = ins[o][2 * rows : 2 * rows + 1, :]
        done = []
        for s in range(per):
            at = s * SOURCE_COUNT + k * dpc
            x0, x1 = cross(ins[o][pl.ds(at, TILE), :], ins[o][pl.ds(rows + at, TILE), :])
            done.append(jnp.where(c == 0, x0, x1))
        for s in range(per):
            to = pl.multiple_of((peer * per + s) * TILE, TILE)
            split[pl.ds(to, TILE), :] = done[s]
    g = jnp.concatenate([split[pl.ds(dd, STATIONS, stride=TILE), :] for dd in range(dpc)], axis=1)
    put(g_ref, g, dpc)
    across = 128 // (2 * ROWS)
    station = lax.broadcasted_iota(jnp.int32, (STATIONS, 128), 0)
    for group in range(n // across):
        marks = jnp.zeros((1, 128), F32)
        for i in range(across):
            row = lines[group * across + i : group * across + i + 1, :]
            marks = marks + (pltpu.roll(row, i * 2 * ROWS, axis=1) if i else row)
        hit = station + 1 == marks.astype(jnp.int32)
        onehot_ref[:, group * 128 : (group + 1) * 128] = jnp.where(hit, 1.0, 0.0).astype(BF16)


def fill_powers(n, dpc, sums, sel_ref, terms, base):
    lo = lower((TILE, 128))
    for o in range(n):
        r = o * 2 * ROWS
        for dd in range(dpc):
            cols = slice(dd * 128, (dd + 1) * 128)
            dcols = slice(base + dd * 128, base + (dd + 1) * 128)
            W = sums[o, pl.ds(ROWS * dpc + dd, TILE, stride=dpc), :]
            Wx = swap(W)
            W = jnp.concatenate([jnp.where(lo, W, Wx), jnp.where(lo, Wx, W)], 0)
            p = sel_ref[r : r + ROWS, cols]
            q = sel_ref[r + ROWS : r + 2 * ROWS, cols]
            p2, q2 = p * p, q * q
            terms[r : r + ROWS, dcols] = W * (q2 + swap(q2))
            terms[r + ROWS : r + 2 * ROWS, dcols] = W * (p2 + swap(p2))


def fill_sums(n, dpc, sums, sel_ref, terms):
    lo = lower((ROWS, 128))
    sign = jnp.where(lo, -1.0, 1.0)
    for o in range(n):
        r = o * 2 * ROWS
        for dd in range(dpc):
            cols = slice(dd * 128, (dd + 1) * 128)
            B = sums[o, pl.ds(dd, ROWS, stride=dpc), :]
            p = sel_ref[r : r + ROWS, cols]
            q = sel_ref[r + ROWS : r + 2 * ROWS, cols]
            Bx = swap(B)
            Brr, Bii = jnp.where(lo, B, Bx), sign * jnp.where(lo, Bx, B)
            terms[r : r + ROWS, cols] = Brr * q + Bii * swap(q)
            terms[r + ROWS : r + 2 * ROWS, cols] = Brr * p - Bii * swap(p)


def own_kernel(n, dpc, g_in, onehot_ref, sums, g_out, terms, sel_ref):
    width = dpc * 128
    sel_ref[...] = pick(onehot_ref[...], wide(g_in, dpc), ((0,), (0,)))
    fill_sums(n, dpc, sums, sel_ref, terms)
    fill_powers(n, dpc, sums, sel_ref, terms, width)
    total = pick(onehot_ref[...], terms[...], ((1,), (0,)))
    put(g_out, 0.5 * (wide(g_in, dpc) + total[:, :width] / (total[:, width:] + ridge)), dpc)


def prepare_kernel(n, dpc, g_ref, onehot_ref, sums, den_ref, terms, sel_ref):
    sel_ref[...] = pick(onehot_ref[...], wide(g_ref, dpc), ((0,), (0,)))
    fill_powers(n, dpc, sums, sel_ref, terms, 0)
    den_ref[...] = pick(onehot_ref[...], terms[...], ((1,), (0,))) + ridge


def later_own_kernel(n, dpc, g_in, onehot_ref, den_ref, sums, g_out, terms, sel_ref):
    sel_ref[...] = pick(onehot_ref[...], wide(g_in, dpc), ((0,), (0,)))
    fill_sums(n, dpc, sums, sel_ref, terms)
    total = pick(onehot_ref[...], terms[...], ((1,), (0,)))
    put(g_out, 0.5 * (wide(g_in, dpc) + total / den_ref[...]), dpc)


def clear(dpc, pairs, *refs):
    for ref in refs:
        chips, rows, _ = ref.shape
        for m in range(chips):
            ref[m, pairs * dpc :, :] = jnp.zeros((rows - pairs * dpc, 128), F32)


def products_first(n, dpc, me, first_ref, second_ref, ins, hre, him, stack):
    per = STATIONS // n
    rows = per * SOURCE_COUNT
    for o in range(n):
        stack[jnp.bitwise_xor(me, o)] = ins[o][...]

    def block(station, k, part):
        at = lax.rem(station, per) * SOURCE_COUNT + k * dpc + part * rows
        return stack[lax.div(station, per), pl.ds(at, TILE), :]

    def one(b, k):
        p, q = first_ref[b], second_ref[b]
        return block(p, k, 0), block(p, k, 1), block(q, k, 0), block(q, k, 1)

    assemble(dpc, first_ref.shape[0], range(n // 2), one, hre, him)


def assemble(dpc, pairs, chips, one, hre, him):
    size = 3 if pairs % 3 == 0 else 1

    def group(i, carry):
        done = []
        for u in range(size):
            for m in chips:
                pr, pi, qr, qi = one(i * size + u, m)
                done.append((u, m, pr * qr + pi * qi, pi * qr - pr * qi))
        for u, m, re, im in done:
            rows = pl.ds((i * size + u) * dpc, TILE)
            hre[m, rows, :] = re
            him[m, rows, :] = im
        return carry

    lax.fori_loop(0, pairs // size, group, 0)
    clear(dpc, pairs, hre, him)


def piece_pair(dpc, even, ins, m, station):
    a = ins[2 * m][pl.ds(station * dpc, TILE), :]
    b = ins[2 * m + 1][pl.ds(station * dpc, TILE), :]
    return cross(jnp.where(even, a, b), jnp.where(even, b, a))


def products(dpc, me, first_ref, second_ref, ins, hre, him):
    even = lax.rem(me, 2) == 0

    def one(b, m):
        return *piece_pair(dpc, even, ins, m, first_ref[b]), *piece_pair(dpc, even, ins, m, second_ref[b])

    assemble(dpc, first_ref.shape[0], range(len(ins) // 2), one, hre, him)


def predict(dpc, b, acc, chips, model_ref, hre, him):
    tiles = [slice(t, t + TILE) for t in range(0, acc[0].shape[0], TILE)]
    acc_re, acc_im = ([x[t] for t in tiles] for x in acc)
    for m, k in enumerate(chips):
        for dd in range(dpc):
            mr = model_ref[k * dpc + dd, 0, b].astype(F32)
            mi = model_ref[k * dpc + dd, 1, b].astype(F32)
            row = pl.ds(b * dpc + dd, TILE, stride=0)
            hr, hi = hre[m, row, :], him[m, row, :]
            for i, t in enumerate(tiles):
                acc_re[i] = acc_re[i] - (hr * mr[t] - hi * mi[t])
                acc_im[i] = acc_im[i] - (hr * mi[t] + hi * mr[t])
    return jnp.concatenate(acc_re, 0), jnp.concatenate(acc_im, 0)


def weighted(b, acc, mask_ref):
    weight = mask_ref[b].astype(F32)
    return weight * acc[0], weight * acc[1]


def fold(a, b, step):
    if a is None:
        return None
    if b is None:
        return a + pltpu.roll(a, step, axis=0)
    mine = (lax.broadcasted_iota(jnp.int32, a.shape, 0) & step) == 0
    return jnp.where(mine, a, b) + pltpu.roll(jnp.where(mine, b, a), step, axis=0)


def row_sums(values):
    values = list(values) + [None] * (TILE - len(values))
    step = 1
    while step < TILE:
        values = [fold(a, b, step) for a, b in zip(values[::2], values[1::2])]
        step *= 2
    return values[0]


def tile_sum(x):
    total = x[:TILE]
    for t in range(1, x.shape[0] // TILE):
        total = total + x[t * TILE : (t + 1) * TILE]
    return total


def correlate(dpc, b, res, chips, model_ref, cre, cim):
    res_re, res_im = res
    done = []
    for m, k in enumerate(chips):
        re, im = [], []
        for dd in range(dpc):
            mr = model_ref[k * dpc + dd, 0, b].astype(F32)
            mi = model_ref[k * dpc + dd, 1, b].astype(F32)
            re.append(tile_sum(mr * res_re + mi * res_im))
            im.append(tile_sum(mr * res_im - mi * res_re))
        done.append((m, row_sums(re), row_sums(im)))
    for m, re, im in done:
        cre[m, pl.ds(b * dpc, TILE), :] = re
        cim[m, pl.ds(b * dpc, TILE), :] = im


def write_sums(dpc, chips, cre, cim, tiles, power_ref, out_ref, start):
    for m, k in enumerate(chips):
        re, im, at = tiles(m)
        done = []
        for t in range(ROWS * dpc // TILE):
            rows = slice(t * TILE, (t + 1) * TILE)
            w = power_ref[k, rows, :]
            done.append(cross(cre[m, rows, :] + re[at, rows, :] * w, cim[m, rows, :] + im[at, rows, :] * w))
        if start:
            for t in range(dpc):
                low, high = (slice(u * TILE, (u + 1) * TILE) for u in (t, t + dpc))
                done.append(cross(power_ref[k, low, :], power_ref[k, high, :]))
        for t, (x0, x1) in enumerate(done):
            rows = slice(t * TILE, (t + 1) * TILE)
            out_ref[2 * k, rows, :] = x0
            out_ref[2 * k + 1, rows, :] = x1


def first_pass_kernel(
    n, dpc, me_ref, first_ref, second_ref, model_hbm, vis_ref, mask_ref, power_ref, *rest
):
    ins, (out_ref, model_ref, sems, hre, him, cre, cim, stack) = rest[:n], rest[n:]
    fetch = Fetch(model_hbm, model_ref, sems)
    products_first(n, dpc, me_ref[0], first_ref, second_ref, ins, hre, him, stack)
    chips = range(n // 2)

    def pair(b, carry):
        acc = predict(dpc, b, (vis_ref[0, b], vis_ref[1, b]), chips, model_ref, hre, him)
        correlate(dpc, b, weighted(b, acc, mask_ref), chips, model_ref, cre, cim)
        return carry

    fetch.each(pair)

    clear(dpc, mask_ref.shape[0], cre, cim)
    write_sums(dpc, chips, cre, cim, lambda m: (hre, him, m), power_ref, out_ref, True)


NEAR, FAR = (0, 1, 2, 6), (3, 4, 5, 7)


def chips_of(me, pairs):
    return [jnp.bitwise_xor(lax.div(me, 2), m) for m in pairs]


def early_kernel(n, dpc, me_ref, first_ref, second_ref, model_hbm, vis_ref, unused_in, *rest):
    ins, (acc_ref, hre, him, unused_out, model_ref, sems) = rest[: 2 * len(NEAR)], rest[2 * len(NEAR) :]
    me = me_ref[0]
    fetch = Fetch(model_hbm, model_ref, sems, [k * dpc for k in chips_of(me, NEAR)])
    products(dpc, me, first_ref, second_ref, ins, hre, him)

    def pair(b, carry):
        acc = vis_ref[0, b], vis_ref[1, b]
        acc_ref[0, b], acc_ref[1, b] = predict(dpc, b, acc, range(len(NEAR)), model_ref, hre, him)
        return carry

    fetch.each(pair)


def later_pass_kernel(
    n,
    dpc,
    me_ref,
    first_ref,
    second_ref,
    model_hbm,
    mask_ref,
    power_ref,
    acc_ref,
    near_re,
    near_im,
    *rest,
):
    ins, (out_ref, model_ref, sems, hre, him, cre, cim) = rest[: 2 * len(FAR)], rest[2 * len(FAR) :]
    fetch = Fetch(model_hbm, model_ref, sems)
    me = me_ref[0]
    products(dpc, me, first_ref, second_ref, ins, hre, him)
    far = chips_of(me, FAR)
    chips = chips_of(me, NEAR) + far

    def pair(b, carry):
        acc = predict(dpc, b, (acc_ref[0, b], acc_ref[1, b]), far, model_ref, hre, him)
        correlate(dpc, b, weighted(b, acc, mask_ref), chips, model_ref, cre, cim)
        return carry

    fetch.each(pair)

    def tiles(m):
        for re, im, pairs in ((near_re, near_im, NEAR), (hre, him, FAR)):
            if m < len(pairs):
                return re, im, m
            m -= len(pairs)

    clear(dpc, mask_ref.shape[0], cre, cim)
    write_sums(dpc, chips, cre, cim, tiles, power_ref, out_ref, False)


def last_kernel(n, dpc, me_ref, first_ref, second_ref, model_hbm, mask_ref, acc_ref, *rest):
    ins, (res_ref, gains_ref, model_ref, sems, hre, him) = rest[:n], rest[n:]
    me = me_ref[0]
    fetch = Fetch(model_hbm, model_ref, sems, [k * dpc for k in chips_of(me, FAR)])
    products(dpc, me, first_ref, second_ref, ins[: 2 * len(FAR)], hre, him)
    per = STATIONS // n
    even = lax.rem(me, 2) == 0
    for m, k in enumerate(chips_of(me, FAR + NEAR)):
        done = [piece_pair(dpc, even, ins, m, me * per + s) for s in range(per)]
        for s, parts in enumerate(done):
            for dd in range(dpc):
                at = s * SOURCE_COUNT + k * dpc + dd
                gains_ref[0, pl.ds(at, 1), :] = parts[0][dd : dd + 1]
                gains_ref[1, pl.ds(at, 1), :] = parts[1][dd : dd + 1]

    def pair(b, carry):
        acc = acc_ref[0, b], acc_ref[1, b]
        acc = predict(dpc, b, acc, range(len(FAR)), model_ref, hre, him)
        res_ref[0, b], res_ref[1, b] = weighted(b, acc, mask_ref)
        return carry

    fetch.each(pair)


SMEM = pl.BlockSpec(memory_space=pltpu.SMEM)
VMEM = pl.BlockSpec(memory_space=pltpu.VMEM)
HBM = pl.BlockSpec(memory_space=pltpu.HBM)


def shape(*dims, dtype=F32):
    return jax.ShapeDtypeStruct(dims, dtype)


def exchange(x):
    return lax.all_to_all(x, "bl", split_axis=0, concat_axis=0, tiled=True)


def gather(n, piece, beside):
    def send(x, o):
        return lax.ppermute(x, "bl", [(i, i ^ o) for i in range(n)])

    got = {0: piece}
    got[12], got[2], got[4], got[1] = (send(piece, o) for o in (12, 2, 4, 1))
    got[8] = send(got[12], 4)
    got[6], got[14], got[10] = send(got[4], 2), send(got[12], 2), send(got[8], 2)
    for o in (2, 4, 12, 6, 14, 8, 10):
        if o == 6:
            got[o] = beside(got[o], got)
        got[o + 1] = send(got[o], 1)
    return [got[o] for o in range(n)]


def fast_body(n, vis, model, mask, first, second, gre, gim):
    model, gre, gim = (pltpu.with_memory_space_constraint(x, pltpu.HBM) for x in (model, gre, gim))
    dpc = SOURCE_COUNT // (n // 2)
    width = dpc * 128
    pairs, times, channels = mask.shape
    me = lax.axis_index("bl").astype(jnp.int32).reshape(1)
    params = pltpu.CompilerParams(vmem_limit_bytes=VMEM_LIMIT)
    plane = (n // 2, ROWS * dpc + TILE, channels)
    half = (len(FAR), ROWS * dpc + TILE, channels)
    lots = n * 2 * ROWS
    mine = (STATIONS * dpc + TILE, channels)
    sems = pltpu.SemaphoreType.DMA((len(PARTS), n // 4))
    held = [pltpu.VMEM(model.shape, BF16), sems]
    held_half = [pltpu.VMEM((SOURCE_COUNT // 2,) + model.shape[1:], BF16), sems]

    def call(kernel, args, outs, scratch=(), micros=1, aliases={}):
        def place(x):
            if x is model or x is gre or x is gim:
                return HBM
            return SMEM if x.ndim == 1 else VMEM

        return pl.pallas_call(
            functools.partial(kernel, n, dpc),
            in_specs=[place(x) for x in args],
            out_specs=[VMEM for o in outs],
            out_shape=outs,
            scratch_shapes=[pltpu.VMEM(x, F32) if isinstance(x, tuple) else x for x in scratch],
            compiler_params=params,
            input_output_aliases=aliases,
            cost_estimate=pl.CostEstimate(
                flops=0, bytes_accessed=int(micros * 3.69e6), transcendentals=0
            ),
        )(*args)

    (piece,) = call(
        pack_kernel,
        (first, second, gre, gim),
        [shape(2 * gre.shape[0] + TILE, channels)],
        [pltpu.SemaphoreType.DMA((2,))],
    )
    power = None

    def powers_beside(x, got):
        nonlocal power
        power, x = call(
            power_kernel, (model, mask, x), [shape(*plane), shape(*x.shape)], held, micros=20, aliases={2: 1}
        )
        return x

    got = gather(n, piece, powers_beside)
    g, onehot = call(
        first_own_kernel,
        (me, *got),
        [shape(*mine), shape(STATIONS, lots, dtype=BF16)],
        [(STATIONS * TILE, channels), (n, channels)],
        micros=2,
    )
    (sums,) = call(
        first_pass_kernel,
        (me, first, second, model, vis, mask, power, *got),
        [shape(n, (ROWS + TILE) * dpc, channels)],
        held + [plane] * 4 + [(n,) + piece.shape],
        micros=9,
    )
    powers = exchange(sums)
    (g,) = call(
        own_kernel,
        (g, onehot, powers),
        [shape(*mine)],
        [(lots, 2 * width), (lots, width)],
    )

    def slots(got, pairs):
        return [got[2 * m + c] for m in pairs for c in (0, 1)]

    def gather_near(g):
        near = None

        def beside(x, got):
            nonlocal near
            args = (me, first, second, model, vis, x, *slots(got, NEAR))
            outs = [shape(*vis.shape), shape(*half), shape(*half), shape(*x.shape)]
            *near, x = call(early_kernel, args, outs, held_half, aliases={5: 3})
            return x

        got = gather(n, g, beside)
        return near, slots(got, FAR + NEAR)

    for step in range(1, ITERS):
        near, got = gather_near(g)
        (den,) = call(
            prepare_kernel,
            (g, onehot, powers),
            [shape(STATIONS, width)],
            [(lots, width)] * 2,
            micros=2,
        )
        (sums,) = call(
            later_pass_kernel,
            (me, first, second, model, mask, power, *near, *got[: 2 * len(FAR)]),
            [shape(n, ROWS * dpc, channels)],
            held + [half] * 2 + [plane] * 2,
            micros=7,
        )
        sums = exchange(sums)
        (g,) = call(
            later_own_kernel,
            (g, onehot, den, sums),
            [shape(*mine)],
            [(lots, width)] * 2,
        )
    near, got = gather_near(g)
    residual, gains = call(
        last_kernel,
        (me, first, second, model, mask, near[0], *got),
        [shape(*vis.shape), shape(2, *gre.shape)],
        held_half + [half] * 2,
        micros=4,
    )
    return gains, residual


def block_pass(full_re, full_im, vis_blk, coh_blk, weight, first, second, want_sums):
    ar = jnp.transpose(full_re[first], (1, 0, 2))
    ai = jnp.transpose(full_im[first], (1, 0, 2))
    br = jnp.transpose(full_re[second], (1, 0, 2))
    bi = jnp.transpose(full_im[second], (1, 0, 2))
    mr = coh_blk[:, 0].astype(F32)
    mi = coh_blk[:, 1].astype(F32)
    hr = ar * br + ai * bi
    hi = ai * br - ar * bi
    hr_t, hi_t = hr[:, :, None], hi[:, :, None]
    res_re = weight * (vis_blk[0] - jnp.sum(hr_t * mr - hi_t * mi, 0))
    res_im = weight * (vis_blk[1] - jnp.sum(hr_t * mi + hi_t * mr, 0))
    residual = jnp.stack([res_re, res_im])
    if not want_sums:
        return (residual, None)
    power = jnp.sum(weight[None] * (mr * mr + mi * mi), 2)
    sum_re = jnp.sum(mr * res_re + mi * res_im, 2) + hr * power
    sum_im = jnp.sum(mr * res_im - mi * res_re, 2) + hi * power
    terms_first = jnp.stack([br * sum_re - bi * sum_im, br * sum_im + bi * sum_re, power * (br * br + bi * bi)])
    terms_second = jnp.stack([ar * sum_re + ai * sum_im, ai * sum_re - ar * sum_im, power * (ar * ar + ai * ai)])
    stations = jnp.arange(STATIONS, dtype=jnp.int32)
    onehot_first = (first[:, None] == stations[None, :]).astype(F32)
    onehot_second = (second[:, None] == stations[None, :]).astype(F32)
    exact = lax.Precision.HIGHEST
    sums = jnp.einsum("bs,cdbf->csdf", onehot_first, terms_first, precision=exact)
    sums = sums + jnp.einsum("bs,cdbf->csdf", onehot_second, terms_second, precision=exact)
    return (residual, sums)


def plain_body(vis, model, mask, first, second, gre, gim):
    weight = mask.astype(F32)
    rows, channels = gre.shape
    shaped = (STATIONS, SOURCE_COUNT, channels)
    full_re = lax.all_gather(gre, "bl", axis=0, tiled=True).reshape(shaped)
    full_im = lax.all_gather(gim, "bl", axis=0, tiled=True).reshape(shaped)
    for step in range(ITERS):
        unused, sums = block_pass(full_re, full_im, vis, model, weight, first, second, True)
        totals = lax.psum(sums, "bl")
        denom = totals[2] + ridge
        full_re = 0.5 * (full_re + totals[0] / denom)
        full_im = 0.5 * (full_im + totals[1] / denom)
    residual, unused = block_pass(full_re, full_im, vis, model, weight, first, second, False)
    both = jnp.stack([full_re, full_im]).reshape(2, STATIONS * SOURCE_COUNT, channels)
    return lax.dynamic_slice_in_dim(both, lax.axis_index("bl") * rows, rows, 1), residual


def solution(mesh):
    n = mesh.shape["bl"]
    split = n == 16

    def body(vis, model, mask, first, second, gre, gim):
        if split and mask.shape[0] <= ROWS:
            return fast_body(n, vis, model, mask, first, second, gre, gim)
        return plain_body(vis, model, mask, first, second, gre, gim)

    in_specs = (
        P(None, ("grp", "bl"), None, None),
        P(None, None, ("grp", "bl"), None, None),
        P(("grp", "bl"), None, None),
        P(("grp", "bl")),
        P(("grp", "bl")),
        P(("grp", "bl"), None),
        P(("grp", "bl"), None),
    )
    out_specs = (P(None, ("grp", "bl"), None), P(None, ("grp", "bl"), None, None))
    return jax.shard_map(body, mesh=mesh, in_specs=in_specs, out_specs=out_specs, check_vma=False)
```

```python
import functools

import jax
import jax.numpy as jnp
from jax import lax
from jax.experimental import pallas as pl
from jax.experimental.pallas import tpu as pltpu
from jax.sharding import PartitionSpec as P

STATIONS = 64
SOURCE_COUNT = 40
ITERS = 2
ROWS = 16

ridge = 1.0
F32 = jnp.float32
BF16 = jnp.bfloat16
VMEM_LIMIT = 24 * 1024 * 1024


def swap(x):
    return pltpu.roll(x, x.shape[-1] // 2, axis=x.ndim - 1)


def lower(shape):
    return lax.broadcasted_iota(jnp.int32, shape, len(shape) - 1) < shape[-1] // 2


def cross(a, b):
    lo = lower(a.shape)
    return jnp.where(lo, a, swap(b)), jnp.where(lo, swap(a), b)


def halves_of(x):
    hi = x.astype(BF16)
    return hi, (x - hi.astype(F32)).astype(BF16)


def pick(onehot, x, dims):
    return sum(
        lax.dot_general(onehot, part, (dims, ((), ())), preferred_element_type=F32)
        for part in halves_of(x)
    )


TILE = 8
PARTS = (1, 3, 7, ROWS)


def pack_kernel(n, dpc, first_hbm, second_hbm, re_hbm, im_hbm, out_ref, first_ref, second_ref, sems):
    rows = re_hbm.shape[0]
    copies = [
        pltpu.make_async_copy(first_hbm, first_ref, sems.at[0]),
        pltpu.make_async_copy(second_hbm, second_ref, sems.at[1]),
        pltpu.make_async_copy(re_hbm, out_ref.at[pl.ds(0, rows)], sems.at[2]),
        pltpu.make_async_copy(im_hbm, out_ref.at[pl.ds(rows, rows)], sems.at[3]),
    ]
    for copy in copies:
        copy.start()
    out_ref[2 * rows :] = jnp.zeros((TILE, 128), F32)
    for copy in copies:
        copy.wait()
    pairs = first_ref.shape[1]
    out_ref[2 * rows : 2 * rows + 1, :pairs] = (first_ref[...] + 1).astype(F32)
    out_ref[2 * rows : 2 * rows + 1, ROWS : ROWS + pairs] = (second_ref[...] + 1).astype(F32)


class Fetch:
    def __init__(self, model, held, sems, firsts=(0,)):
        count, pairs = held.shape[0] // len(firsts), held.shape[2]
        self.copies = []
        self.ends = [0] + [min(end, pairs) for end in PARTS]
        for i in range(len(PARTS)):
            part = pl.ds(self.ends[i], self.ends[i + 1] - self.ends[i])
            self.copies.append([])
            for j, first in enumerate(firsts):
                self.copies[i].append(
                    pltpu.make_async_copy(
                        model.at[pl.ds(first, count), :, part],
                        held.at[pl.ds(j * count, count), :, part],
                        sems.at[i, j],
                    )
                )
        for copies in self.copies:
            for copy in copies:
                copy.start()

    def each(self, body):
        for i, copies in enumerate(self.copies):
            for copy in copies:
                copy.wait()
            lax.fori_loop(self.ends[i], self.ends[i + 1], body, 0)


def power_kernel(n, dpc, model_hbm, mask_ref, unused_in, out_ref, unused_out, model_ref, sems):
    fetch = Fetch(model_hbm, model_ref, sems)
    out_ref[...] = jnp.zeros_like(out_ref)

    def pair(b, carry):
        weight = mask_ref[b].astype(F32)
        for d in range(model_ref.shape[0]):
            mr = model_ref[d, 0, b].astype(F32)
            mi = model_ref[d, 1, b].astype(F32)
            row = pl.ds(b * dpc + d % dpc, 1)
            out_ref[d // dpc, row, :] = jnp.sum(weight * (mr * mr + mi * mi), axis=0, keepdims=True)
        return carry

    fetch.each(pair)


def wide(ref, dpc):
    return jnp.concatenate([ref[pl.ds(dd, STATIONS, stride=dpc), :] for dd in range(dpc)], axis=1)


def put(ref, value, dpc):
    for dd in range(dpc):
        ref[pl.ds(dd, STATIONS, stride=dpc), :] = value[:, dd * 128 : (dd + 1) * 128]
    ref[STATIONS * dpc :, :] = jnp.zeros((TILE, 128), F32)


def first_own_kernel(n, dpc, me_ref, *rest):
    ins, (g_ref, onehot_ref, split, lines) = rest[:n], rest[n:]
    me = me_ref[0]
    k, c = lax.div(me, 2), lax.rem(me, 2)
    per = STATIONS // n
    rows = per * SOURCE_COUNT
    for o in range(n):
        peer = jnp.bitwise_xor(me, o)
        lines[pl.ds(peer, 1), :] = ins[o][2 * rows : 2 * rows + 1, :]
        done = []
        for s in range(per):
            at = s * SOURCE_COUNT + k * dpc
            x0, x1 = cross(ins[o][pl.ds(at, TILE), :], ins[o][pl.ds(rows + at, TILE), :])
            done.append(jnp.where(c == 0, x0, x1))
        for s in range(per):
            to = pl.multiple_of((peer * per + s) * TILE, TILE)
            split[pl.ds(to, TILE), :] = done[s]
    g = jnp.concatenate([split[pl.ds(dd, STATIONS, stride=TILE), :] for dd in range(dpc)], axis=1)
    put(g_ref, g, dpc)
    across = 128 // (2 * ROWS)
    station = lax.broadcasted_iota(jnp.int32, (STATIONS, 128), 0)
    for group in range(n // across):
        marks = jnp.zeros((1, 128), F32)
        for i in range(across):
            row = lines[group * across + i : group * across + i + 1, :]
            marks = marks + (pltpu.roll(row, i * 2 * ROWS, axis=1) if i else row)
        hit = station + 1 == marks.astype(jnp.int32)
        onehot_ref[:, group * 128 : (group + 1) * 128] = jnp.where(hit, 1.0, 0.0).astype(BF16)


def fill_powers(n, dpc, sums, sel_ref, terms, base):
    lo = lower((TILE, 128))
    for o in range(n):
        r = o * 2 * ROWS
        for dd in range(dpc):
            cols = slice(dd * 128, (dd + 1) * 128)
            dcols = slice(base + dd * 128, base + (dd + 1) * 128)
            W = sums[o, pl.ds(ROWS * dpc + dd, TILE, stride=dpc), :]
            Wx = swap(W)
            W = jnp.concatenate([jnp.where(lo, W, Wx), jnp.where(lo, Wx, W)], 0)
            p = sel_ref[r : r + ROWS, cols]
            q = sel_ref[r + ROWS : r + 2 * ROWS, cols]
            p2, q2 = p * p, q * q
            terms[r : r + ROWS, dcols] = W * (q2 + swap(q2))
            terms[r + ROWS : r + 2 * ROWS, dcols] = W * (p2 + swap(p2))


def fill_sums(n, dpc, sums, sel_ref, terms):
    lo = lower((ROWS, 128))
    sign = jnp.where(lo, -1.0, 1.0)
    for o in range(n):
        r = o * 2 * ROWS
        for dd in range(dpc):
            cols = slice(dd * 128, (dd + 1) * 128)
            B = sums[o, pl.ds(dd, ROWS, stride=dpc), :]
            p = sel_ref[r : r + ROWS, cols]
            q = sel_ref[r + ROWS : r + 2 * ROWS, cols]
            Bx = swap(B)
            Brr, Bii = jnp.where(lo, B, Bx), sign * jnp.where(lo, Bx, B)
            terms[r : r + ROWS, cols] = Brr * q + Bii * swap(q)
            terms[r + ROWS : r + 2 * ROWS, cols] = Brr * p - Bii * swap(p)


def own_kernel(n, dpc, g_in, onehot_ref, sums, g_out, terms, sel_ref):
    width = dpc * 128
    sel_ref[...] = pick(onehot_ref[...], wide(g_in, dpc), ((0,), (0,)))
    fill_sums(n, dpc, sums, sel_ref, terms)
    fill_powers(n, dpc, sums, sel_ref, terms, width)
    total = pick(onehot_ref[...], terms[...], ((1,), (0,)))
    put(g_out, 0.5 * (wide(g_in, dpc) + total[:, :width] / (total[:, width:] + ridge)), dpc)


def prepare_kernel(n, dpc, g_ref, onehot_ref, sums, den_ref, terms, sel_ref):
    sel_ref[...] = pick(onehot_ref[...], wide(g_ref, dpc), ((0,), (0,)))
    fill_powers(n, dpc, sums, sel_ref, terms, 0)
    den_ref[...] = pick(onehot_ref[...], terms[...], ((1,), (0,))) + ridge


def later_own_kernel(n, dpc, g_in, onehot_ref, den_ref, sums, g_out, terms, sel_ref):
    sel_ref[...] = pick(onehot_ref[...], wide(g_in, dpc), ((0,), (0,)))
    fill_sums(n, dpc, sums, sel_ref, terms)
    total = pick(onehot_ref[...], terms[...], ((1,), (0,)))
    put(g_out, 0.5 * (wide(g_in, dpc) + total / den_ref[...]), dpc)


def clear(dpc, pairs, *refs):
    for ref in refs:
        chips, rows, _ = ref.shape
        for m in range(chips):
            ref[m, pairs * dpc :, :] = jnp.zeros((rows - pairs * dpc, 128), F32)


def products_first(n, dpc, me, first_ref, second_ref, ins, hre, him, stack):
    per = STATIONS // n
    rows = per * SOURCE_COUNT
    for o in range(n):
        stack[jnp.bitwise_xor(me, o)] = ins[o][...]

    def block(station, k, part):
        at = lax.rem(station, per) * SOURCE_COUNT + k * dpc + part * rows
        return stack[lax.div(station, per), pl.ds(at, TILE), :]

    def one(b, k):
        p, q = first_ref[b], second_ref[b]
        return block(p, k, 0), block(p, k, 1), block(q, k, 0), block(q, k, 1)

    assemble(dpc, first_ref.shape[0], range(n // 2), one, hre, him)


def assemble(dpc, pairs, chips, one, hre, him):
    size = 3 if pairs % 3 == 0 else 1

    def group(i, carry):
        done = []
        for u in range(size):
            for m in chips:
                pr, pi, qr, qi = one(i * size + u, m)
                done.append((u, m, pr * qr + pi * qi, pi * qr - pr * qi))
        for u, m, re, im in done:
            rows = pl.ds((i * size + u) * dpc, TILE)
            hre[m, rows, :] = re
            him[m, rows, :] = im
        return carry

    lax.fori_loop(0, pairs // size, group, 0)
    clear(dpc, pairs, hre, him)


def piece_pair(dpc, even, ins, m, station):
    a = ins[2 * m][pl.ds(station * dpc, TILE), :]
    b = ins[2 * m + 1][pl.ds(station * dpc, TILE), :]
    return cross(jnp.where(even, a, b), jnp.where(even, b, a))


def products(dpc, me, first_ref, second_ref, ins, hre, him):
    even = lax.rem(me, 2) == 0

    def one(b, m):
        return *piece_pair(dpc, even, ins, m, first_ref[b]), *piece_pair(dpc, even, ins, m, second_ref[b])

    assemble(dpc, first_ref.shape[0], range(len(ins) // 2), one, hre, him)


def predict(dpc, b, acc, chips, model_ref, hre, him):
    tiles = [slice(t, t + TILE) for t in range(0, acc[0].shape[0], TILE)]
    acc_re, acc_im = ([x[t] for t in tiles] for x in acc)
    for m, k in enumerate(chips):
        for dd in range(dpc):
            mr = model_ref[k * dpc + dd, 0, b].astype(F32)
            mi = model_ref[k * dpc + dd, 1, b].astype(F32)
            row = pl.ds(b * dpc + dd, TILE, stride=0)
            hr, hi = hre[m, row, :], him[m, row, :]
            for i, t in enumerate(tiles):
                acc_re[i] = acc_re[i] - (hr * mr[t] - hi * mi[t])
                acc_im[i] = acc_im[i] - (hr * mi[t] + hi * mr[t])
    return jnp.concatenate(acc_re, 0), jnp.concatenate(acc_im, 0)


def weighted(b, acc, mask_ref):
    weight = mask_ref[b].astype(F32)
    return weight * acc[0], weight * acc[1]


def fold(a, b, step):
    if a is None:
        return None
    if b is None:
        return a + pltpu.roll(a, step, axis=0)
    mine = (lax.broadcasted_iota(jnp.int32, a.shape, 0) & step) == 0
    return jnp.where(mine, a, b) + pltpu.roll(jnp.where(mine, b, a), step, axis=0)


def row_sums(values):
    values = list(values) + [None] * (TILE - len(values))
    step = 1
    while step < TILE:
        values = [fold(a, b, step) for a, b in zip(values[::2], values[1::2])]
        step *= 2
    return values[0]


def tile_sum(x):
    total = x[:TILE]
    for t in range(1, x.shape[0] // TILE):
        total = total + x[t * TILE : (t + 1) * TILE]
    return total


def correlate(dpc, b, res, chips, model_ref, cre, cim, weight=None, power_ref=None):
    res_re, res_im = res
    done = []
    for m, k in enumerate(chips):
        re, im, power = [], [], []
        for dd in range(dpc):
            mr = model_ref[k * dpc + dd, 0, b].astype(F32)
            mi = model_ref[k * dpc + dd, 1, b].astype(F32)
            re.append(tile_sum(mr * res_re + mi * res_im))
            im.append(tile_sum(mr * res_im - mi * res_re))
            if weight is not None and m >= len(chips) // 2:
                power.append(tile_sum(weight * (mr * mr + mi * mi)))
        done.append((m, row_sums(re), row_sums(im), row_sums(power) if power else None))
    for m, re, im, power in done:
        cre[m, pl.ds(b * dpc, TILE), :] = re
        cim[m, pl.ds(b * dpc, TILE), :] = im
        if power is not None:
            power_ref[m, pl.ds(b * dpc, TILE), :] = power


def write_sums(dpc, chips, cre, cim, tiles, power_ref, out_ref, start):
    for m, k in enumerate(chips):
        re, im, at = tiles(m)
        done = []
        for t in range(ROWS * dpc // TILE):
            rows = slice(t * TILE, (t + 1) * TILE)
            w = power_ref[k, rows, :]
            done.append(cross(cre[m, rows, :] + re[at, rows, :] * w, cim[m, rows, :] + im[at, rows, :] * w))
        if start:
            for t in range(dpc):
                low, high = (slice(u * TILE, (u + 1) * TILE) for u in (t, t + dpc))
                done.append(cross(power_ref[k, low, :], power_ref[k, high, :]))
        for t, (x0, x1) in enumerate(done):
            rows = slice(t * TILE, (t + 1) * TILE)
            out_ref[2 * k, rows, :] = x0
            out_ref[2 * k + 1, rows, :] = x1


def first_pass_kernel(
    n, dpc, me_ref, first_ref, second_ref, model_hbm, vis_ref, mask_ref, power_in, *rest
):
    ins, (out_ref, power_ref, model_ref, sems, hre, him, cre, cim, stack) = rest[:n], rest[n:]
    fetch = Fetch(model_hbm, model_ref, sems)
    products_first(n, dpc, me_ref[0], first_ref, second_ref, ins, hre, him, stack)
    chips = range(n // 2)
    power_ref[: n // 4] = power_in[...]

    def pair(b, carry):
        acc = predict(dpc, b, (vis_ref[0, b], vis_ref[1, b]), chips, model_ref, hre, him)
        weight = mask_ref[b].astype(F32)
        correlate(dpc, b, weighted(b, acc, mask_ref), chips, model_ref, cre, cim, weight, power_ref)
        return carry

    fetch.each(pair)
    clear(dpc, mask_ref.shape[0], cre, cim, power_ref)
    write_sums(dpc, chips, cre, cim, lambda m: (hre, him, m), power_ref, out_ref, True)


NEAR, FAR = (0, 1, 2, 6), (3, 4, 5, 7)


def chips_of(me, pairs):
    return [jnp.bitwise_xor(lax.div(me, 2), m) for m in pairs]


def early_kernel(n, dpc, me_ref, first_ref, second_ref, model_hbm, vis_ref, unused_in, *rest):
    ins, (acc_ref, hre, him, unused_out, model_ref, sems) = rest[: 2 * len(NEAR)], rest[2 * len(NEAR) :]
    me = me_ref[0]
    fetch = Fetch(model_hbm, model_ref, sems, [k * dpc for k in chips_of(me, NEAR)])
    products(dpc, me, first_ref, second_ref, ins, hre, him)

    def pair(b, carry):
        acc = vis_ref[0, b], vis_ref[1, b]
        acc_ref[0, b], acc_ref[1, b] = predict(dpc, b, acc, range(len(NEAR)), model_ref, hre, him)
        return carry

    fetch.each(pair)


def later_pass_kernel(
    n,
    dpc,
    me_ref,
    first_ref,
    second_ref,
    model_hbm,
    mask_ref,
    power_ref,
    acc_ref,
    near_re,
    near_im,
    *rest,
):
    ins, (out_ref, model_ref, sems, hre, him, cre, cim) = rest[: 2 * len(FAR)], rest[2 * len(FAR) :]
    fetch = Fetch(model_hbm, model_ref, sems)
    me = me_ref[0]
    products(dpc, me, first_ref, second_ref, ins, hre, him)
    far = chips_of(me, FAR)
    chips = chips_of(me, NEAR) + far

    def pair(b, carry):
        acc = predict(dpc, b, (acc_ref[0, b], acc_ref[1, b]), far, model_ref, hre, him)
        correlate(dpc, b, weighted(b, acc, mask_ref), chips, model_ref, cre, cim)
        return carry

    fetch.each(pair)

    def tiles(m):
        for re, im, pairs in ((near_re, near_im, NEAR), (hre, him, FAR)):
            if m < len(pairs):
                return re, im, m
            m -= len(pairs)

    clear(dpc, mask_ref.shape[0], cre, cim)
    write_sums(dpc, chips, cre, cim, tiles, power_ref, out_ref, False)


def last_kernel(n, dpc, me_ref, first_ref, second_ref, model_hbm, mask_ref, acc_ref, *rest):
    ins, (res_ref, gains_ref, model_ref, sems, hre, him) = rest[:n], rest[n:]
    me = me_ref[0]
    fetch = Fetch(model_hbm, model_ref, sems, [k * dpc for k in chips_of(me, FAR)])
    products(dpc, me, first_ref, second_ref, ins[: 2 * len(FAR)], hre, him)
    per = STATIONS // n
    even = lax.rem(me, 2) == 0
    for m, k in enumerate(chips_of(me, FAR + NEAR)):
        done = [piece_pair(dpc, even, ins, m, me * per + s) for s in range(per)]
        for s, parts in enumerate(done):
            for dd in range(dpc):
                at = s * SOURCE_COUNT + k * dpc + dd
                gains_ref[0, pl.ds(at, 1), :] = parts[0][dd : dd + 1]
                gains_ref[1, pl.ds(at, 1), :] = parts[1][dd : dd + 1]

    def pair(b, carry):
        acc = acc_ref[0, b], acc_ref[1, b]
        acc = predict(dpc, b, acc, range(len(FAR)), model_ref, hre, him)
        res_ref[0, b], res_ref[1, b] = weighted(b, acc, mask_ref)
        return carry

    fetch.each(pair)


SMEM = pl.BlockSpec(memory_space=pltpu.SMEM)
VMEM = pl.BlockSpec(memory_space=pltpu.VMEM)
HBM = pl.BlockSpec(memory_space=pltpu.HBM)


def shape(*dims, dtype=F32):
    return jax.ShapeDtypeStruct(dims, dtype)


def exchange(x):
    return lax.all_to_all(x, "bl", split_axis=0, concat_axis=0, tiled=True)


def gather(n, piece, beside):
    def send(x, o):
        return lax.ppermute(x, "bl", [(i, i ^ o) for i in range(n)])

    got = {0: piece}
    got[12], got[2], got[4], got[1] = (send(piece, o) for o in (12, 2, 4, 1))
    got[8] = send(got[12], 4)
    got[6], got[14], got[10] = send(got[4], 2), send(got[12], 2), send(got[8], 2)
    for o in (2, 4, 12, 6, 14, 8, 10):
        if o == 6:
            got[o] = beside(got[o], got)
        got[o + 1] = send(got[o], 1)
    return [got[o] for o in range(n)]


def fast_body(n, vis, model, mask, first, second, gre, gim):
    starts = (first.reshape(1, -1), second.reshape(1, -1), gre, gim)
    model, *starts = (pltpu.with_memory_space_constraint(x, pltpu.HBM) for x in (model, *starts))
    dpc = SOURCE_COUNT // (n // 2)
    width = dpc * 128
    pairs, times, channels = mask.shape
    me = lax.axis_index("bl").astype(jnp.int32).reshape(1)
    params = pltpu.CompilerParams(vmem_limit_bytes=VMEM_LIMIT)
    plane = (n // 2, ROWS * dpc + TILE, channels)
    half = (len(FAR), ROWS * dpc + TILE, channels)
    lots = n * 2 * ROWS
    mine = (STATIONS * dpc + TILE, channels)
    sems = pltpu.SemaphoreType.DMA((len(PARTS), n // 4))
    held = [pltpu.VMEM(model.shape, BF16), sems]
    held_half = [pltpu.VMEM((SOURCE_COUNT // 2,) + model.shape[1:], BF16), sems]

    def call(kernel, args, outs, scratch=(), micros=1, aliases={}):
        def place(x):
            if x is model or any(x is y for y in starts):
                return HBM
            return SMEM if x.ndim == 1 else VMEM

        return pl.pallas_call(
            functools.partial(kernel, n, dpc),
            in_specs=[place(x) for x in args],
            out_specs=[VMEM for o in outs],
            out_shape=outs,
            scratch_shapes=[pltpu.VMEM(x, F32) if isinstance(x, tuple) else x for x in scratch],
            compiler_params=params,
            input_output_aliases=aliases,
            cost_estimate=pl.CostEstimate(
                flops=0, bytes_accessed=int(micros * 3.69e6), transcendentals=0
            ),
        )(*args)

    (piece,) = call(
        pack_kernel,
        starts,
        [shape(2 * gre.shape[0] + TILE, channels)],
        [pltpu.VMEM((1, pairs), jnp.int32)] * 2 + [pltpu.SemaphoreType.DMA((4,))],
    )
    power = None

    def powers_beside(x, got):
        nonlocal power
        outs = [shape(*half), shape(*x.shape)]
        power, x = call(power_kernel, (model, mask, x), outs, held_half, micros=20, aliases={2: 1})
        return x

    got = gather(n, piece, powers_beside)
    g, onehot = call(
        first_own_kernel,
        (me, *got),
        [shape(*mine), shape(STATIONS, lots, dtype=BF16)],
        [(STATIONS * TILE, channels), (n, channels)],
        micros=2,
    )
    sums, power = call(
        first_pass_kernel,
        (me, first, second, model, vis, mask, power, *got),
        [shape(n, (ROWS + TILE) * dpc, channels), shape(*plane)],
        held + [plane] * 4 + [(n,) + piece.shape],
        micros=9,
    )
    powers = exchange(sums)
    (g,) = call(
        own_kernel,
        (g, onehot, powers),
        [shape(*mine)],
        [(lots, 2 * width), (lots, width)],
    )

    def slots(got, pairs):
        return [got[2 * m + c] for m in pairs for c in (0, 1)]

    def gather_near(g):
        near = None

        def beside(x, got):
            nonlocal near
            args = (me, first, second, model, vis, x, *slots(got, NEAR))
            outs = [shape(*vis.shape), shape(*half), shape(*half), shape(*x.shape)]
            *near, x = call(early_kernel, args, outs, held_half, aliases={5: 3})
            return x

        got = gather(n, g, beside)
        return near, slots(got, FAR + NEAR)

    for step in range(1, ITERS):
        near, got = gather_near(g)
        (den,) = call(
            prepare_kernel,
            (g, onehot, powers),
            [shape(STATIONS, width)],
            [(lots, width)] * 2,
            micros=2,
        )
        (sums,) = call(
            later_pass_kernel,
            (me, first, second, model, mask, power, *near, *got[: 2 * len(FAR)]),
            [shape(n, ROWS * dpc, channels)],
            held + [half] * 2 + [plane] * 2,
            micros=7,
        )
        sums = exchange(sums)
        (g,) = call(
            later_own_kernel,
            (g, onehot, den, sums),
            [shape(*mine)],
            [(lots, width)] * 2,
        )
    near, got = gather_near(g)
    residual, gains = call(
        last_kernel,
        (me, first, second, model, mask, near[0], *got),
        [shape(*vis.shape), shape(2, *gre.shape)],
        held_half + [half] * 2,
        micros=4,
    )
    return gains, residual


def block_pass(full_re, full_im, vis_blk, coh_blk, weight, first, second, want_sums):
    ar = jnp.transpose(full_re[first], (1, 0, 2))
    ai = jnp.transpose(full_im[first], (1, 0, 2))
    br = jnp.transpose(full_re[second], (1, 0, 2))
    bi = jnp.transpose(full_im[second], (1, 0, 2))
    mr = coh_blk[:, 0].astype(F32)
    mi = coh_blk[:, 1].astype(F32)
    hr = ar * br + ai * bi
    hi = ai * br - ar * bi
    hr_t, hi_t = hr[:, :, None], hi[:, :, None]
    res_re = weight * (vis_blk[0] - jnp.sum(hr_t * mr - hi_t * mi, 0))
    res_im = weight * (vis_blk[1] - jnp.sum(hr_t * mi + hi_t * mr, 0))
    residual = jnp.stack([res_re, res_im])
    if not want_sums:
        return (residual, None)
    power = jnp.sum(weight[None] * (mr * mr + mi * mi), 2)
    sum_re = jnp.sum(mr * res_re + mi * res_im, 2) + hr * power
    sum_im = jnp.sum(mr * res_im - mi * res_re, 2) + hi * power
    terms_first = jnp.stack([br * sum_re - bi * sum_im, br * sum_im + bi * sum_re, power * (br * br + bi * bi)])
    terms_second = jnp.stack([ar * sum_re + ai * sum_im, ai * sum_re - ar * sum_im, power * (ar * ar + ai * ai)])
    stations = jnp.arange(STATIONS, dtype=jnp.int32)
    onehot_first = (first[:, None] == stations[None, :]).astype(F32)
    onehot_second = (second[:, None] == stations[None, :]).astype(F32)
    exact = lax.Precision.HIGHEST
    sums = jnp.einsum("bs,cdbf->csdf", onehot_first, terms_first, precision=exact)
    sums = sums + jnp.einsum("bs,cdbf->csdf", onehot_second, terms_second, precision=exact)
    return (residual, sums)


def plain_body(vis, model, mask, first, second, gre, gim):
    weight = mask.astype(F32)
    rows, channels = gre.shape
    shaped = (STATIONS, SOURCE_COUNT, channels)
    full_re = lax.all_gather(gre, "bl", axis=0, tiled=True).reshape(shaped)
    full_im = lax.all_gather(gim, "bl", axis=0, tiled=True).reshape(shaped)
    for step in range(ITERS):
        unused, sums = block_pass(full_re, full_im, vis, model, weight, first, second, True)
        totals = lax.psum(sums, "bl")
        denom = totals[2] + ridge
        full_re = 0.5 * (full_re + totals[0] / denom)
        full_im = 0.5 * (full_im + totals[1] / denom)
    residual, unused = block_pass(full_re, full_im, vis, model, weight, first, second, False)
    both = jnp.stack([full_re, full_im]).reshape(2, STATIONS * SOURCE_COUNT, channels)
    return lax.dynamic_slice_in_dim(both, lax.axis_index("bl") * rows, rows, 1), residual


def solution(mesh):
    n = mesh.shape["bl"]
    split = n == 16

    def body(vis, model, mask, first, second, gre, gim):
        if split and mask.shape[0] <= ROWS:
            return fast_body(n, vis, model, mask, first, second, gre, gim)
        return plain_body(vis, model, mask, first, second, gre, gim)

    in_specs = (
        P(None, ("grp", "bl"), None, None),
        P(None, None, ("grp", "bl"), None, None),
        P(("grp", "bl"), None, None),
        P(("grp", "bl")),
        P(("grp", "bl")),
        P(("grp", "bl"), None),
        P(("grp", "bl"), None),
    )
    out_specs = (P(None, ("grp", "bl"), None), P(None, ("grp", "bl"), None, None))
    return jax.shard_map(body, mesh=mesh, in_specs=in_specs, out_specs=out_specs, check_vma=False)
```

```python
import functools

import jax
import jax.numpy as jnp
from jax import lax
from jax.experimental import pallas as pl
from jax.experimental.pallas import tpu as pltpu
from jax.sharding import PartitionSpec as P

STATIONS = 64
SOURCE_COUNT = 40
ITERS = 2
ROWS = 16

ridge = 1.0
F32 = jnp.float32
BF16 = jnp.bfloat16
VMEM_LIMIT = 24 * 1024 * 1024


def swap(x):
    return pltpu.roll(x, x.shape[-1] // 2, axis=x.ndim - 1)


def lower(shape):
    return lax.broadcasted_iota(jnp.int32, shape, len(shape) - 1) < shape[-1] // 2


def cross(a, b):
    lo = lower(a.shape)
    return jnp.where(lo, a, swap(b)), jnp.where(lo, swap(a), b)


def halves_of(x):
    hi = x.astype(BF16)
    return hi, (x - hi.astype(F32)).astype(BF16)


def pick(onehot, x, dims):
    return sum(
        lax.dot_general(onehot, part, (dims, ((), ())), preferred_element_type=F32)
        for part in halves_of(x)
    )


TILE = 8
PARTS = (1, 3, 7, ROWS)


def pack_kernel(n, dpc, first_hbm, second_hbm, re_hbm, im_hbm, out_ref, first_ref, second_ref, sems):
    rows = re_hbm.shape[0]
    copies = [
        pltpu.make_async_copy(first_hbm, first_ref, sems.at[0]),
        pltpu.make_async_copy(second_hbm, second_ref, sems.at[1]),
        pltpu.make_async_copy(re_hbm, out_ref.at[pl.ds(0, rows)], sems.at[2]),
        pltpu.make_async_copy(im_hbm, out_ref.at[pl.ds(rows, rows)], sems.at[3]),
    ]
    for copy in copies:
        copy.start()
    out_ref[2 * rows :] = jnp.zeros((TILE, 128), F32)
    for copy in copies:
        copy.wait()
    pairs = first_ref.shape[1]
    out_ref[2 * rows : 2 * rows + 1, :pairs] = (first_ref[...] + 1).astype(F32)
    out_ref[2 * rows : 2 * rows + 1, ROWS : ROWS + pairs] = (second_ref[...] + 1).astype(F32)


class Fetch:
    def __init__(self, model, held, sems, firsts=(0,)):
        count, pairs = held.shape[0] // len(firsts), held.shape[2]
        self.copies = []
        self.ends = [0] + [min(end, pairs) for end in PARTS]
        for i in range(len(PARTS)):
            part = pl.ds(self.ends[i], self.ends[i + 1] - self.ends[i])
            self.copies.append([])
            for j, first in enumerate(firsts):
                self.copies[i].append(
                    pltpu.make_async_copy(
                        model.at[pl.ds(first, count), :, part],
                        held.at[pl.ds(j * count, count), :, part],
                        sems.at[i, j],
                    )
                )
        for copies in self.copies:
            for copy in copies:
                copy.start()

    def each(self, body):
        for i, copies in enumerate(self.copies):
            for copy in copies:
                copy.wait()
            lax.fori_loop(self.ends[i], self.ends[i + 1], body, 0)


def bring(pairs, sems):
    copies = [pltpu.make_async_copy(*pair, sems.at[i]) for i, pair in enumerate(pairs)]
    for copy in copies:
        copy.start()
    return copies


def power_kernel(
    n, dpc, model_hbm, mask_hbm, unused_in, out_ref, unused_out, mask_ref, side, model_ref, sems
):
    (mask_copy,) = bring([(mask_hbm, mask_ref)], side)
    fetch = Fetch(model_hbm, model_ref, sems)
    out_ref[...] = jnp.zeros_like(out_ref)

    def pair(b, carry):
        weight = mask_ref[b].astype(F32)
        for d in range(model_ref.shape[0]):
            mr = model_ref[d, 0, b].astype(F32)
            mi = model_ref[d, 1, b].astype(F32)
            row = pl.ds(b * dpc + d % dpc, 1)
            out_ref[d // dpc, row, :] = jnp.sum(weight * (mr * mr + mi * mi), axis=0, keepdims=True)
        return carry

    mask_copy.wait()
    fetch.each(pair)


def wide(ref, dpc):
    return jnp.concatenate([ref[pl.ds(dd, STATIONS, stride=dpc), :] for dd in range(dpc)], axis=1)


def put(ref, value, dpc):
    for dd in range(dpc):
        ref[pl.ds(dd, STATIONS, stride=dpc), :] = value[:, dd * 128 : (dd + 1) * 128]
    ref[STATIONS * dpc :, :] = jnp.zeros((TILE, 128), F32)


def first_own_kernel(n, dpc, *rest):
    ins, (g_ref, onehot_ref, split, lines) = rest[:n], rest[n:]
    me = lax.axis_index("bl")
    k, c = lax.div(me, 2), lax.rem(me, 2)
    per = STATIONS // n
    rows = per * SOURCE_COUNT
    for o in range(n):
        peer = jnp.bitwise_xor(me, o)
        lines[pl.ds(peer, 1), :] = ins[o][2 * rows : 2 * rows + 1, :]
        done = []
        for s in range(per):
            at = s * SOURCE_COUNT + k * dpc
            x0, x1 = cross(ins[o][pl.ds(at, TILE), :], ins[o][pl.ds(rows + at, TILE), :])
            done.append(jnp.where(c == 0, x0, x1))
        for s in range(per):
            to = pl.multiple_of((peer * per + s) * TILE, TILE)
            split[pl.ds(to, TILE), :] = done[s]
    g = jnp.concatenate([split[pl.ds(dd, STATIONS, stride=TILE), :] for dd in range(dpc)], axis=1)
    put(g_ref, g, dpc)
    across = 128 // (2 * ROWS)
    station = lax.broadcasted_iota(jnp.int32, (STATIONS, 128), 0)
    for group in range(n // across):
        marks = jnp.zeros((1, 128), F32)
        for i in range(across):
            row = lines[group * across + i : group * across + i + 1, :]
            marks = marks + (pltpu.roll(row, i * 2 * ROWS, axis=1) if i else row)
        hit = station + 1 == marks.astype(jnp.int32)
        onehot_ref[:, group * 128 : (group + 1) * 128] = jnp.where(hit, 1.0, 0.0).astype(BF16)


def fill_powers(n, dpc, sums, sel_ref, terms, base):
    lo = lower((TILE, 128))
    for o in range(n):
        r = o * 2 * ROWS
        for dd in range(dpc):
            cols = slice(dd * 128, (dd + 1) * 128)
            dcols = slice(base + dd * 128, base + (dd + 1) * 128)
            W = sums[o, pl.ds(ROWS * dpc + dd, TILE, stride=dpc), :]
            Wx = swap(W)
            W = jnp.concatenate([jnp.where(lo, W, Wx), jnp.where(lo, Wx, W)], 0)
            p = sel_ref[r : r + ROWS, cols]
            q = sel_ref[r + ROWS : r + 2 * ROWS, cols]
            p2, q2 = p * p, q * q
            terms[r : r + ROWS, dcols] = W * (q2 + swap(q2))
            terms[r + ROWS : r + 2 * ROWS, dcols] = W * (p2 + swap(p2))


def fill_sums(n, dpc, sums, sel_ref, terms):
    lo = lower((ROWS, 128))
    sign = jnp.where(lo, -1.0, 1.0)
    for o in range(n):
        r = o * 2 * ROWS
        for dd in range(dpc):
            cols = slice(dd * 128, (dd + 1) * 128)
            B = sums[o, pl.ds(dd, ROWS, stride=dpc), :]
            p = sel_ref[r : r + ROWS, cols]
            q = sel_ref[r + ROWS : r + 2 * ROWS, cols]
            Bx = swap(B)
            Brr, Bii = jnp.where(lo, B, Bx), sign * jnp.where(lo, Bx, B)
            terms[r : r + ROWS, cols] = Brr * q + Bii * swap(q)
            terms[r + ROWS : r + 2 * ROWS, cols] = Brr * p - Bii * swap(p)


def own_kernel(n, dpc, g_in, onehot_ref, sums, g_out, terms, sel_ref):
    width = dpc * 128
    sel_ref[...] = pick(onehot_ref[...], wide(g_in, dpc), ((0,), (0,)))
    fill_sums(n, dpc, sums, sel_ref, terms)
    fill_powers(n, dpc, sums, sel_ref, terms, width)
    total = pick(onehot_ref[...], terms[...], ((1,), (0,)))
    put(g_out, 0.5 * (wide(g_in, dpc) + total[:, :width] / (total[:, width:] + ridge)), dpc)


def prepare_kernel(n, dpc, g_ref, onehot_ref, sums, den_ref, terms, sel_ref):
    sel_ref[...] = pick(onehot_ref[...], wide(g_ref, dpc), ((0,), (0,)))
    fill_powers(n, dpc, sums, sel_ref, terms, 0)
    den_ref[...] = pick(onehot_ref[...], terms[...], ((1,), (0,))) + ridge


def later_own_kernel(n, dpc, g_in, onehot_ref, den_ref, sums, g_out, terms, sel_ref):
    sel_ref[...] = pick(onehot_ref[...], wide(g_in, dpc), ((0,), (0,)))
    fill_sums(n, dpc, sums, sel_ref, terms)
    total = pick(onehot_ref[...], terms[...], ((1,), (0,)))
    put(g_out, 0.5 * (wide(g_in, dpc) + total / den_ref[...]), dpc)


def clear(dpc, pairs, *refs):
    for ref in refs:
        chips, rows, _ = ref.shape
        for m in range(chips):
            ref[m, pairs * dpc :, :] = jnp.zeros((rows - pairs * dpc, 128), F32)


def products_first(n, dpc, me, first_ref, second_ref, ins, hre, him, stack):
    per = STATIONS // n
    rows = per * SOURCE_COUNT
    for o in range(n):
        stack[jnp.bitwise_xor(me, o)] = ins[o][...]

    def block(station, k, part):
        at = lax.rem(station, per) * SOURCE_COUNT + k * dpc + part * rows
        return stack[lax.div(station, per), pl.ds(at, TILE), :]

    def one(b, k):
        p, q = first_ref[b], second_ref[b]
        return block(p, k, 0), block(p, k, 1), block(q, k, 0), block(q, k, 1)

    assemble(dpc, first_ref.shape[0], range(n // 2), one, hre, him)


def assemble(dpc, pairs, chips, one, hre, him):
    size = 3 if pairs % 3 == 0 else 1

    def group(i, carry):
        done = []
        for u in range(size):
            for m in chips:
                pr, pi, qr, qi = one(i * size + u, m)
                done.append((u, m, pr * qr + pi * qi, pi * qr - pr * qi))
        for u, m, re, im in done:
            rows = pl.ds((i * size + u) * dpc, TILE)
            hre[m, rows, :] = re
            him[m, rows, :] = im
        return carry

    lax.fori_loop(0, pairs // size, group, 0)
    clear(dpc, pairs, hre, him)


def piece_pair(dpc, even, ins, m, station):
    a = ins[2 * m][pl.ds(station * dpc, TILE), :]
    b = ins[2 * m + 1][pl.ds(station * dpc, TILE), :]
    return cross(jnp.where(even, a, b), jnp.where(even, b, a))


def products(dpc, me, first_ref, second_ref, ins, hre, him):
    even = lax.rem(me, 2) == 0

    def one(b, m):
        return *piece_pair(dpc, even, ins, m, first_ref[b]), *piece_pair(dpc, even, ins, m, second_ref[b])

    assemble(dpc, first_ref.shape[0], range(len(ins) // 2), one, hre, him)


def predict(dpc, b, acc, chips, model_ref, hre, him):
    tiles = [slice(t, t + TILE) for t in range(0, acc[0].shape[0], TILE)]
    acc_re, acc_im = ([x[t] for t in tiles] for x in acc)
    for m, k in enumerate(chips):
        for dd in range(dpc):
            mr = model_ref[k * dpc + dd, 0, b].astype(F32)
            mi = model_ref[k * dpc + dd, 1, b].astype(F32)
            row = pl.ds(b * dpc + dd, TILE, stride=0)
            hr, hi = hre[m, row, :], him[m, row, :]
            for i, t in enumerate(tiles):
                acc_re[i] = acc_re[i] - (hr * mr[t] - hi * mi[t])
                acc_im[i] = acc_im[i] - (hr * mi[t] + hi * mr[t])
    return jnp.concatenate(acc_re, 0), jnp.concatenate(acc_im, 0)


def weighted(b, acc, mask_ref):
    weight = mask_ref[b].astype(F32)
    return weight * acc[0], weight * acc[1]


def fold(a, b, step):
    if a is None:
        return None
    if b is None:
        return a + pltpu.roll(a, step, axis=0)
    mine = (lax.broadcasted_iota(jnp.int32, a.shape, 0) & step) == 0
    return jnp.where(mine, a, b) + pltpu.roll(jnp.where(mine, b, a), step, axis=0)


def row_sums(values):
    values = list(values) + [None] * (TILE - len(values))
    step = 1
    while step < TILE:
        values = [fold(a, b, step) for a, b in zip(values[::2], values[1::2])]
        step *= 2
    return values[0]


def tile_sum(x):
    total = x[:TILE]
    for t in range(1, x.shape[0] // TILE):
        total = total + x[t * TILE : (t + 1) * TILE]
    return total


def correlate(dpc, b, res, chips, model_ref, cre, cim, weight=None, power_ref=None):
    res_re, res_im = res
    done = []
    for m, k in enumerate(chips):
        re, im, power = [], [], []
        for dd in range(dpc):
            mr = model_ref[k * dpc + dd, 0, b].astype(F32)
            mi = model_ref[k * dpc + dd, 1, b].astype(F32)
            re.append(tile_sum(mr * res_re + mi * res_im))
            im.append(tile_sum(mr * res_im - mi * res_re))
            if weight is not None and m >= len(chips) // 2:
                power.append(tile_sum(weight * (mr * mr + mi * mi)))
        done.append((m, row_sums(re), row_sums(im), row_sums(power) if power else None))
    for m, re, im, power in done:
        cre[m, pl.ds(b * dpc, TILE), :] = re
        cim[m, pl.ds(b * dpc, TILE), :] = im
        if power is not None:
            power_ref[m, pl.ds(b * dpc, TILE), :] = power


def write_sums(dpc, chips, cre, cim, tiles, power_ref, out_ref, start):
    for m, k in enumerate(chips):
        re, im, at = tiles(m)
        done = []
        for t in range(ROWS * dpc // TILE):
            rows = slice(t * TILE, (t + 1) * TILE)
            w = power_ref[k, rows, :]
            done.append(cross(cre[m, rows, :] + re[at, rows, :] * w, cim[m, rows, :] + im[at, rows, :] * w))
        if start:
            for t in range(dpc):
                low, high = (slice(u * TILE, (u + 1) * TILE) for u in (t, t + dpc))
                done.append(cross(power_ref[k, low, :], power_ref[k, high, :]))
        for t, (x0, x1) in enumerate(done):
            rows = slice(t * TILE, (t + 1) * TILE)
            out_ref[2 * k, rows, :] = x0
            out_ref[2 * k + 1, rows, :] = x1


def first_pass_kernel(n, dpc, first_ref, second_ref, model_hbm, vis_hbm, mask_hbm, power_in, *rest):
    ins, rest = rest[:n], rest[n:]
    out_ref, power_ref, vis_ref, mask_ref, side, model_ref, sems, hre, him, cre, cim, stack = rest
    copies = bring([(vis_hbm, vis_ref), (mask_hbm, mask_ref)], side)
    fetch = Fetch(model_hbm, model_ref, sems)
    products_first(n, dpc, lax.axis_index("bl"), first_ref, second_ref, ins, hre, him, stack)
    for copy in copies:
        copy.wait()
    chips = range(n // 2)
    power_ref[: n // 4] = power_in[...]

    def pair(b, carry):
        acc = predict(dpc, b, (vis_ref[0, b], vis_ref[1, b]), chips, model_ref, hre, him)
        weight = mask_ref[b].astype(F32)
        correlate(dpc, b, weighted(b, acc, mask_ref), chips, model_ref, cre, cim, weight, power_ref)
        return carry

    fetch.each(pair)
    clear(dpc, mask_ref.shape[0], cre, cim, power_ref)
    write_sums(dpc, chips, cre, cim, lambda m: (hre, him, m), power_ref, out_ref, True)


NEAR, FAR = (0, 1, 2, 6), (3, 4, 5, 7)


def chips_of(me, pairs):
    return [jnp.bitwise_xor(lax.div(me, 2), m) for m in pairs]


def early_kernel(n, dpc, first_ref, second_ref, model_hbm, vis_hbm, unused_in, *rest):
    ins, rest = rest[: 2 * len(NEAR)], rest[2 * len(NEAR) :]
    acc_ref, hre, him, unused_out, vis_ref, side, model_ref, sems = rest
    me = lax.axis_index("bl")
    (vis_copy,) = bring([(vis_hbm, vis_ref)], side)
    fetch = Fetch(model_hbm, model_ref, sems, [k * dpc for k in chips_of(me, NEAR)])
    products(dpc, me, first_ref, second_ref, ins, hre, him)

    vis_copy.wait()

    def pair(b, carry):
        acc = vis_ref[0, b], vis_ref[1, b]
        acc_ref[0, b], acc_ref[1, b] = predict(dpc, b, acc, range(len(NEAR)), model_ref, hre, him)
        return carry

    fetch.each(pair)


def later_pass_kernel(
    n,
    dpc,
    first_ref,
    second_ref,
    model_hbm,
    mask_hbm,
    power_ref,
    acc_ref,
    near_re,
    near_im,
    *rest,
):
    ins, rest = rest[: 2 * len(FAR)], rest[2 * len(FAR) :]
    out_ref, mask_ref, side, model_ref, sems, hre, him, cre, cim = rest
    (mask_copy,) = bring([(mask_hbm, mask_ref)], side)
    fetch = Fetch(model_hbm, model_ref, sems)
    me = lax.axis_index("bl")
    products(dpc, me, first_ref, second_ref, ins, hre, him)
    far = chips_of(me, FAR)
    chips = chips_of(me, NEAR) + far

    mask_copy.wait()

    def pair(b, carry):
        acc = predict(dpc, b, (acc_ref[0, b], acc_ref[1, b]), far, model_ref, hre, him)
        correlate(dpc, b, weighted(b, acc, mask_ref), chips, model_ref, cre, cim)
        return carry

    fetch.each(pair)

    def tiles(m):
        for re, im, pairs in ((near_re, near_im, NEAR), (hre, him, FAR)):
            if m < len(pairs):
                return re, im, m
            m -= len(pairs)

    clear(dpc, mask_ref.shape[0], cre, cim)
    write_sums(dpc, chips, cre, cim, tiles, power_ref, out_ref, False)


def last_kernel(n, dpc, first_ref, second_ref, model_hbm, mask_hbm, acc_ref, *rest):
    ins, (res_ref, gains_ref, mask_ref, side, model_ref, sems, hre, him) = rest[:n], rest[n:]
    (mask_copy,) = bring([(mask_hbm, mask_ref)], side)
    me = lax.axis_index("bl")
    fetch = Fetch(model_hbm, model_ref, sems, [k * dpc for k in chips_of(me, FAR)])
    products(dpc, me, first_ref, second_ref, ins[: 2 * len(FAR)], hre, him)
    per = STATIONS // n
    even = lax.rem(me, 2) == 0
    for m, k in enumerate(chips_of(me, FAR + NEAR)):
        done = [piece_pair(dpc, even, ins, m, me * per + s) for s in range(per)]
        for s, parts in enumerate(done):
            for dd in range(dpc):
                at = s * SOURCE_COUNT + k * dpc + dd
                gains_ref[0, pl.ds(at, 1), :] = parts[0][dd : dd + 1]
                gains_ref[1, pl.ds(at, 1), :] = parts[1][dd : dd + 1]

    mask_copy.wait()

    def pair(b, carry):
        acc = acc_ref[0, b], acc_ref[1, b]
        acc = predict(dpc, b, acc, range(len(FAR)), model_ref, hre, him)
        res_ref[0, b], res_ref[1, b] = weighted(b, acc, mask_ref)
        return carry

    fetch.each(pair)


SMEM = pl.BlockSpec(memory_space=pltpu.SMEM)
VMEM = pl.BlockSpec(memory_space=pltpu.VMEM)
HBM = pl.BlockSpec(memory_space=pltpu.HBM)


def shape(*dims, dtype=F32):
    return jax.ShapeDtypeStruct(dims, dtype)


def exchange(x):
    return lax.all_to_all(x, "bl", split_axis=0, concat_axis=0, tiled=True)


def gather(n, piece, beside):
    def send(x, o):
        return lax.ppermute(x, "bl", [(i, i ^ o) for i in range(n)])

    got = {0: piece}
    got[12], got[2], got[4], got[1] = (send(piece, o) for o in (12, 2, 4, 1))
    got[8] = send(got[12], 4)
    got[6], got[14], got[10] = send(got[4], 2), send(got[12], 2), send(got[8], 2)
    for o in (2, 4, 12, 6, 14, 8, 10):
        if o == 6:
            got[o] = beside(got[o], got)
        got[o + 1] = send(got[o], 1)
    return [got[o] for o in range(n)]


def fast_body(n, vis, model, mask, first, second, gre, gim):
    starts = (first.reshape(1, -1), second.reshape(1, -1), gre, gim)
    model, vis, mask, *starts = (
        pltpu.with_memory_space_constraint(x, pltpu.HBM) for x in (model, vis, mask, *starts)
    )
    dpc = SOURCE_COUNT // (n // 2)
    width = dpc * 128
    pairs, times, channels = mask.shape
    params = pltpu.CompilerParams(vmem_limit_bytes=VMEM_LIMIT)
    plane = (n // 2, ROWS * dpc + TILE, channels)
    half = (len(FAR), ROWS * dpc + TILE, channels)
    lots = n * 2 * ROWS
    mine = (STATIONS * dpc + TILE, channels)
    sems = pltpu.SemaphoreType.DMA((len(PARTS), n // 4))
    side = pltpu.SemaphoreType.DMA((2,))
    mask_held = [pltpu.VMEM(mask.shape, jnp.int32), side]
    held = [pltpu.VMEM(model.shape, BF16), sems]
    held_half = [pltpu.VMEM((SOURCE_COUNT // 2,) + model.shape[1:], BF16), sems]

    def call(kernel, args, outs, scratch=(), micros=1, aliases={}):
        def place(x):
            if any(x is y for y in (model, vis, mask, *starts)):
                return HBM
            return SMEM if x.ndim == 1 else VMEM

        return pl.pallas_call(
            functools.partial(kernel, n, dpc),
            in_specs=[place(x) for x in args],
            out_specs=[VMEM for o in outs],
            out_shape=outs,
            scratch_shapes=[pltpu.VMEM(x, F32) if isinstance(x, tuple) else x for x in scratch],
            compiler_params=params,
            input_output_aliases=aliases,
            cost_estimate=pl.CostEstimate(
                flops=0, bytes_accessed=int(micros * 3.69e6), transcendentals=0
            ),
        )(*args)

    (piece,) = call(
        pack_kernel,
        starts,
        [shape(2 * gre.shape[0] + TILE, channels)],
        [pltpu.VMEM((1, pairs), jnp.int32)] * 2 + [pltpu.SemaphoreType.DMA((4,))],
    )
    power = None

    def powers_beside(x, got):
        nonlocal power
        outs = [shape(*half), shape(*x.shape)]
        power, x = call(power_kernel, (model, mask, x), outs, mask_held + held_half, micros=20, aliases={2: 1})
        return x

    got = gather(n, piece, powers_beside)
    g, onehot = call(
        first_own_kernel,
        got,
        [shape(*mine), shape(STATIONS, lots, dtype=BF16)],
        [(STATIONS * TILE, channels), (n, channels)],
        micros=2,
    )
    sums, power = call(
        first_pass_kernel,
        (first, second, model, vis, mask, power, *got),
        [shape(n, (ROWS + TILE) * dpc, channels), pltpu.HBM(plane, F32)],
        [vis.shape] + mask_held + held + [plane] * 4 + [(n,) + piece.shape],
        micros=9,
    )
    powers = exchange(sums)
    (g,) = call(
        own_kernel,
        (g, onehot, powers),
        [shape(*mine)],
        [(lots, 2 * width), (lots, width)],
    )

    def slots(got, pairs):
        return [got[2 * m + c] for m in pairs for c in (0, 1)]

    def gather_near(g):
        near = None

        def beside(x, got):
            nonlocal near
            args = (first, second, model, vis, x, *slots(got, NEAR))
            outs = [shape(*vis.shape), shape(*half), shape(*half), shape(*x.shape)]
            *near, x = call(early_kernel, args, outs, [vis.shape, side] + held_half, aliases={4: 3})
            return x

        got = gather(n, g, beside)
        return near, slots(got, FAR + NEAR)

    for step in range(1, ITERS):
        near, got = gather_near(g)
        (den,) = call(
            prepare_kernel,
            (g, onehot, powers),
            [shape(STATIONS, width)],
            [(lots, width)] * 2,
            micros=2,
        )
        (sums,) = call(
            later_pass_kernel,
            (first, second, model, mask, power, *near, *got[: 2 * len(FAR)]),
            [shape(n, ROWS * dpc, channels)],
            mask_held + held + [half] * 2 + [plane] * 2,
            micros=7,
        )
        sums = exchange(sums)
        (g,) = call(
            later_own_kernel,
            (g, onehot, den, sums),
            [shape(*mine)],
            [(lots, width)] * 2,
        )
    near, got = gather_near(g)
    residual, gains = call(
        last_kernel,
        (first, second, model, mask, near[0], *got),
        [shape(*vis.shape), shape(2, *gre.shape)],
        mask_held + held_half + [half] * 2,
        micros=4,
    )
    return gains, residual


def block_pass(full_re, full_im, vis_blk, coh_blk, weight, first, second, want_sums):
    ar = jnp.transpose(full_re[first], (1, 0, 2))
    ai = jnp.transpose(full_im[first], (1, 0, 2))
    br = jnp.transpose(full_re[second], (1, 0, 2))
    bi = jnp.transpose(full_im[second], (1, 0, 2))
    mr = coh_blk[:, 0].astype(F32)
    mi = coh_blk[:, 1].astype(F32)
    hr = ar * br + ai * bi
    hi = ai * br - ar * bi
    hr_t, hi_t = hr[:, :, None], hi[:, :, None]
    res_re = weight * (vis_blk[0] - jnp.sum(hr_t * mr - hi_t * mi, 0))
    res_im = weight * (vis_blk[1] - jnp.sum(hr_t * mi + hi_t * mr, 0))
    residual = jnp.stack([res_re, res_im])
    if not want_sums:
        return (residual, None)
    power = jnp.sum(weight[None] * (mr * mr + mi * mi), 2)
    sum_re = jnp.sum(mr * res_re + mi * res_im, 2) + hr * power
    sum_im = jnp.sum(mr * res_im - mi * res_re, 2) + hi * power
    terms_first = jnp.stack([br * sum_re - bi * sum_im, br * sum_im + bi * sum_re, power * (br * br + bi * bi)])
    terms_second = jnp.stack([ar * sum_re + ai * sum_im, ai * sum_re - ar * sum_im, power * (ar * ar + ai * ai)])
    stations = jnp.arange(STATIONS, dtype=jnp.int32)
    onehot_first = (first[:, None] == stations[None, :]).astype(F32)
    onehot_second = (second[:, None] == stations[None, :]).astype(F32)
    exact = lax.Precision.HIGHEST
    sums = jnp.einsum("bs,cdbf->csdf", onehot_first, terms_first, precision=exact)
    sums = sums + jnp.einsum("bs,cdbf->csdf", onehot_second, terms_second, precision=exact)
    return (residual, sums)


def plain_body(vis, model, mask, first, second, gre, gim):
    weight = mask.astype(F32)
    rows, channels = gre.shape
    shaped = (STATIONS, SOURCE_COUNT, channels)
    full_re = lax.all_gather(gre, "bl", axis=0, tiled=True).reshape(shaped)
    full_im = lax.all_gather(gim, "bl", axis=0, tiled=True).reshape(shaped)
    for step in range(ITERS):
        unused, sums = block_pass(full_re, full_im, vis, model, weight, first, second, True)
        totals = lax.psum(sums, "bl")
        denom = totals[2] + ridge
        full_re = 0.5 * (full_re + totals[0] / denom)
        full_im = 0.5 * (full_im + totals[1] / denom)
    residual, unused = block_pass(full_re, full_im, vis, model, weight, first, second, False)
    both = jnp.stack([full_re, full_im]).reshape(2, STATIONS * SOURCE_COUNT, channels)
    return lax.dynamic_slice_in_dim(both, lax.axis_index("bl") * rows, rows, 1), residual


def solution(mesh):
    n = mesh.shape["bl"]
    split = n == 16

    def body(vis, model, mask, first, second, gre, gim):
        if split and mask.shape[0] <= ROWS:
            return fast_body(n, vis, model, mask, first, second, gre, gim)
        return plain_body(vis, model, mask, first, second, gre, gim)

    in_specs = (
        P(None, ("grp", "bl"), None, None),
        P(None, None, ("grp", "bl"), None, None),
        P(("grp", "bl"), None, None),
        P(("grp", "bl")),
        P(("grp", "bl")),
        P(("grp", "bl"), None),
        P(("grp", "bl"), None),
    )
    out_specs = (P(None, ("grp", "bl"), None), P(None, ("grp", "bl"), None, None))
    return jax.shard_map(body, mesh=mesh, in_specs=in_specs, out_specs=out_specs, check_vma=False)
```

```python
import functools

import jax
import jax.numpy as jnp
from jax import lax
from jax.experimental import pallas as pl
from jax.experimental.pallas import tpu as pltpu
from jax.sharding import PartitionSpec as P

STATIONS = 64
SOURCE_COUNT = 40
ITERS = 2
ROWS = 16

ridge = 1.0
F32 = jnp.float32
BF16 = jnp.bfloat16
VMEM_LIMIT = 24 * 1024 * 1024


def swap(x):
    return pltpu.roll(x, x.shape[-1] // 2, axis=x.ndim - 1)


def lower(shape):
    return lax.broadcasted_iota(jnp.int32, shape, len(shape) - 1) < shape[-1] // 2


def cross(a, b):
    lo = lower(a.shape)
    return jnp.where(lo, a, swap(b)), jnp.where(lo, swap(a), b)


def halves_of(x):
    hi = x.astype(BF16)
    return hi, (x - hi.astype(F32)).astype(BF16)


def pick(onehot, x, dims):
    return sum(
        lax.dot_general(onehot, part, (dims, ((), ())), preferred_element_type=F32)
        for part in halves_of(x)
    )


TILE = 8
PARTS = (1, 3, 7, ROWS)


def pack_kernel(n, dpc, first_hbm, second_hbm, re_hbm, im_hbm, out_ref, first_ref, second_ref, sems):
    rows = re_hbm.shape[0]
    copies = [
        pltpu.make_async_copy(first_hbm, first_ref, sems.at[0]),
        pltpu.make_async_copy(second_hbm, second_ref, sems.at[1]),
        pltpu.make_async_copy(re_hbm, out_ref.at[pl.ds(0, rows)], sems.at[2]),
        pltpu.make_async_copy(im_hbm, out_ref.at[pl.ds(rows, rows)], sems.at[3]),
    ]
    for copy in copies:
        copy.start()
    out_ref[2 * rows :] = jnp.zeros((TILE, 128), F32)
    for copy in copies:
        copy.wait()
    pairs = first_ref.shape[1]
    out_ref[2 * rows : 2 * rows + 1, :pairs] = (first_ref[...] + 1).astype(F32)
    out_ref[2 * rows : 2 * rows + 1, ROWS : ROWS + pairs] = (second_ref[...] + 1).astype(F32)


class Fetch:
    def __init__(self, model, held, sems, firsts=(0,)):
        count, pairs = held.shape[0] // len(firsts), held.shape[2]
        self.copies = []
        self.ends = [0] + [min(end, pairs) for end in PARTS]
        for i in range(len(PARTS)):
            part = pl.ds(self.ends[i], self.ends[i + 1] - self.ends[i])
            self.copies.append([])
            for j, first in enumerate(firsts):
                self.copies[i].append(
                    pltpu.make_async_copy(
                        model.at[pl.ds(first, count), :, part],
                        held.at[pl.ds(j * count, count), :, part],
                        sems.at[i, j],
                    )
                )
        for copies in self.copies:
            for copy in copies:
                copy.start()

    def each(self, body):
        for i, copies in enumerate(self.copies):
            for copy in copies:
                copy.wait()
            lax.fori_loop(self.ends[i], self.ends[i + 1], body, 0)


def bring(pairs, sems):
    copies = [pltpu.make_async_copy(*pair, sems.at[i]) for i, pair in enumerate(pairs)]
    for copy in copies:
        copy.start()
    return copies


def power_kernel(
    n, dpc, model_hbm, mask_hbm, unused_in, out_ref, unused_out, mask_ref, side, model_ref, sems
):
    (mask_copy,) = bring([(mask_hbm, mask_ref)], side)
    fetch = Fetch(model_hbm, model_ref, sems)
    out_ref[...] = jnp.zeros_like(out_ref)

    def pair(b, carry):
        weight = mask_ref[b].astype(F32)
        for d in range(model_ref.shape[0]):
            mr = model_ref[d, 0, b].astype(F32)
            mi = model_ref[d, 1, b].astype(F32)
            row = pl.ds(b * dpc + d % dpc, 1)
            out_ref[d // dpc, row, :] = jnp.sum(weight * (mr * mr + mi * mi), axis=0, keepdims=True)
        return carry

    mask_copy.wait()
    fetch.each(pair)


def wide(ref, dpc):
    return jnp.concatenate([ref[pl.ds(dd, STATIONS, stride=dpc), :] for dd in range(dpc)], axis=1)


def put(ref, value, dpc):
    for dd in range(dpc):
        ref[pl.ds(dd, STATIONS, stride=dpc), :] = value[:, dd * 128 : (dd + 1) * 128]
    ref[STATIONS * dpc :, :] = jnp.zeros((TILE, 128), F32)


def first_own_kernel(n, dpc, *rest):
    ins, (g_ref, onehot_ref, split, lines) = rest[:n], rest[n:]
    me = lax.axis_index("bl")
    k, c = lax.div(me, 2), lax.rem(me, 2)
    per = STATIONS // n
    rows = per * SOURCE_COUNT
    for o in range(n):
        peer = jnp.bitwise_xor(me, o)
        lines[pl.ds(peer, 1), :] = ins[o][2 * rows : 2 * rows + 1, :]
        done = []
        for s in range(per):
            at = s * SOURCE_COUNT + k * dpc
            x0, x1 = cross(ins[o][pl.ds(at, TILE), :], ins[o][pl.ds(rows + at, TILE), :])
            done.append(jnp.where(c == 0, x0, x1))
        for s in range(per):
            to = pl.multiple_of((peer * per + s) * TILE, TILE)
            split[pl.ds(to, TILE), :] = done[s]
    g = jnp.concatenate([split[pl.ds(dd, STATIONS, stride=TILE), :] for dd in range(dpc)], axis=1)
    put(g_ref, g, dpc)
    across = 128 // (2 * ROWS)
    station = lax.broadcasted_iota(jnp.int32, (STATIONS, 128), 0)
    for group in range(n // across):
        marks = jnp.zeros((1, 128), F32)
        for i in range(across):
            row = lines[group * across + i : group * across + i + 1, :]
            marks = marks + (pltpu.roll(row, i * 2 * ROWS, axis=1) if i else row)
        hit = station + 1 == marks.astype(jnp.int32)
        onehot_ref[:, group * 128 : (group + 1) * 128] = jnp.where(hit, 1.0, 0.0).astype(BF16)


def fill_powers(n, dpc, sums, sel_ref, terms, base):
    lo = lower((TILE, 128))
    for o in range(n):
        r = o * 2 * ROWS
        for dd in range(dpc):
            cols = slice(dd * 128, (dd + 1) * 128)
            dcols = slice(base + dd * 128, base + (dd + 1) * 128)
            W = sums[o, pl.ds(ROWS * dpc + dd, TILE, stride=dpc), :]
            Wx = swap(W)
            W = jnp.concatenate([jnp.where(lo, W, Wx), jnp.where(lo, Wx, W)], 0)
            p = sel_ref[r : r + ROWS, cols]
            q = sel_ref[r + ROWS : r + 2 * ROWS, cols]
            p2, q2 = p * p, q * q
            terms[r : r + ROWS, dcols] = W * (q2 + swap(q2))
            terms[r + ROWS : r + 2 * ROWS, dcols] = W * (p2 + swap(p2))


def fill_sums(n, dpc, sums, sel_ref, terms):
    lo = lower((ROWS, 128))
    sign = jnp.where(lo, -1.0, 1.0)
    for o in range(n):
        r = o * 2 * ROWS
        for dd in range(dpc):
            cols = slice(dd * 128, (dd + 1) * 128)
            B = sums[o, pl.ds(dd, ROWS, stride=dpc), :]
            p = sel_ref[r : r + ROWS, cols]
            q = sel_ref[r + ROWS : r + 2 * ROWS, cols]
            Bx = swap(B)
            Brr, Bii = jnp.where(lo, B, Bx), sign * jnp.where(lo, Bx, B)
            terms[r : r + ROWS, cols] = Brr * q + Bii * swap(q)
            terms[r + ROWS : r + 2 * ROWS, cols] = Brr * p - Bii * swap(p)


def own_kernel(n, dpc, g_in, onehot_ref, sums, g_out, terms, sel_ref):
    width = dpc * 128
    sel_ref[...] = pick(onehot_ref[...], wide(g_in, dpc), ((0,), (0,)))
    fill_sums(n, dpc, sums, sel_ref, terms)
    fill_powers(n, dpc, sums, sel_ref, terms, width)
    total = pick(onehot_ref[...], terms[...], ((1,), (0,)))
    put(g_out, 0.5 * (wide(g_in, dpc) + total[:, :width] / (total[:, width:] + ridge)), dpc)


def prepare_kernel(n, dpc, g_ref, onehot_ref, sums, den_ref, terms, sel_ref):
    sel_ref[...] = pick(onehot_ref[...], wide(g_ref, dpc), ((0,), (0,)))
    fill_powers(n, dpc, sums, sel_ref, terms, 0)
    den_ref[...] = pick(onehot_ref[...], terms[...], ((1,), (0,))) + ridge


def later_own_kernel(n, dpc, g_in, onehot_ref, den_ref, sums, g_out, terms, sel_ref):
    sel_ref[...] = pick(onehot_ref[...], wide(g_in, dpc), ((0,), (0,)))
    fill_sums(n, dpc, sums, sel_ref, terms)
    total = pick(onehot_ref[...], terms[...], ((1,), (0,)))
    put(g_out, 0.5 * (wide(g_in, dpc) + total / den_ref[...]), dpc)


def clear(dpc, pairs, *refs):
    for ref in refs:
        chips, rows, _ = ref.shape
        for m in range(chips):
            ref[m, pairs * dpc :, :] = jnp.zeros((rows - pairs * dpc, 128), F32)


def products_first(n, dpc, me, first_ref, second_ref, ins, hre, him, stack):
    per = STATIONS // n
    rows = per * SOURCE_COUNT
    for o in range(n):
        stack[jnp.bitwise_xor(me, o)] = ins[o][...]

    def block(station, k, part):
        at = lax.rem(station, per) * SOURCE_COUNT + k * dpc + part * rows
        return stack[lax.div(station, per), pl.ds(at, TILE), :]

    def one(b, k):
        p, q = first_ref[b], second_ref[b]
        return block(p, k, 0), block(p, k, 1), block(q, k, 0), block(q, k, 1)

    assemble(dpc, first_ref.shape[0], range(n // 2), one, hre, him)


def assemble(dpc, pairs, chips, one, hre, him):
    size = 3 if pairs % 3 == 0 else 1

    def group(i, carry):
        done = []
        for u in range(size):
            for m in chips:
                pr, pi, qr, qi = one(i * size + u, m)
                done.append((u, m, pr * qr + pi * qi, pi * qr - pr * qi))
        for u, m, re, im in done:
            rows = pl.ds((i * size + u) * dpc, TILE)
            hre[m, rows, :] = re
            him[m, rows, :] = im
        return carry

    lax.fori_loop(0, pairs // size, group, 0)
    clear(dpc, pairs, hre, him)


def piece_pair(dpc, even, ins, m, station):
    a = ins[2 * m][pl.ds(station * dpc, TILE), :]
    b = ins[2 * m + 1][pl.ds(station * dpc, TILE), :]
    return cross(jnp.where(even, a, b), jnp.where(even, b, a))


def products(dpc, me, first_ref, second_ref, ins, hre, him):
    even = lax.rem(me, 2) == 0

    def one(b, m):
        return *piece_pair(dpc, even, ins, m, first_ref[b]), *piece_pair(dpc, even, ins, m, second_ref[b])

    assemble(dpc, first_ref.shape[0], range(len(ins) // 2), one, hre, him)


def predict(dpc, b, acc, chips, model_ref, hre, him):
    tiles = [slice(t, t + TILE) for t in range(0, acc[0].shape[0], TILE)]
    acc_re, acc_im = ([x[t] for t in tiles] for x in acc)
    for m, k in enumerate(chips):
        for dd in range(dpc):
            mr = model_ref[k * dpc + dd, 0, b].astype(F32)
            mi = model_ref[k * dpc + dd, 1, b].astype(F32)
            row = pl.ds(b * dpc + dd, TILE, stride=0)
            hr, hi = hre[m, row, :], him[m, row, :]
            for i, t in enumerate(tiles):
                acc_re[i] = acc_re[i] - (hr * mr[t] - hi * mi[t])
                acc_im[i] = acc_im[i] - (hr * mi[t] + hi * mr[t])
    return jnp.concatenate(acc_re, 0), jnp.concatenate(acc_im, 0)


def weighted(b, acc, mask_ref):
    weight = mask_ref[b].astype(F32)
    return weight * acc[0], weight * acc[1]


def fold(a, b, step):
    if a is None:
        return None
    if b is None:
        return a + pltpu.roll(a, step, axis=0)
    mine = (lax.broadcasted_iota(jnp.int32, a.shape, 0) & step) == 0
    return jnp.where(mine, a, b) + pltpu.roll(jnp.where(mine, b, a), step, axis=0)


def row_sums(values):
    values = list(values) + [None] * (TILE - len(values))
    step = 1
    while step < TILE:
        values = [fold(a, b, step) for a, b in zip(values[::2], values[1::2])]
        step *= 2
    return values[0]


def tile_sum(x):
    total = x[:TILE]
    for t in range(1, x.shape[0] // TILE):
        total = total + x[t * TILE : (t + 1) * TILE]
    return total


def correlate(dpc, b, res, chips, model_ref, cre, cim, weight=None, power_ref=None):
    res_re, res_im = res
    done = []
    for m, k in enumerate(chips):
        re, im, power = [], [], []
        for dd in range(dpc):
            mr = model_ref[k * dpc + dd, 0, b].astype(F32)
            mi = model_ref[k * dpc + dd, 1, b].astype(F32)
            re.append(tile_sum(mr * res_re + mi * res_im))
            im.append(tile_sum(mr * res_im - mi * res_re))
            if weight is not None and m >= len(chips) // 2:
                power.append(tile_sum(weight * (mr * mr + mi * mi)))
        done.append((m, row_sums(re), row_sums(im), row_sums(power) if power else None))
    for m, re, im, power in done:
        cre[m, pl.ds(b * dpc, TILE), :] = re
        cim[m, pl.ds(b * dpc, TILE), :] = im
        if power is not None:
            power_ref[m, pl.ds(b * dpc, TILE), :] = power


def write_sums(dpc, chips, cre, cim, tiles, power_ref, out_ref, start):
    for m, k in enumerate(chips):
        re, im, at = tiles(m)
        done = []
        for t in range(ROWS * dpc // TILE):
            rows = slice(t * TILE, (t + 1) * TILE)
            w = power_ref[k, rows, :]
            done.append(cross(cre[m, rows, :] + re[at, rows, :] * w, cim[m, rows, :] + im[at, rows, :] * w))
        if start:
            for t in range(dpc):
                low, high = (slice(u * TILE, (u + 1) * TILE) for u in (t, t + dpc))
                done.append(cross(power_ref[k, low, :], power_ref[k, high, :]))
        for t, (x0, x1) in enumerate(done):
            rows = slice(t * TILE, (t + 1) * TILE)
            out_ref[2 * k, rows, :] = x0
            out_ref[2 * k + 1, rows, :] = x1


def first_pass_kernel(n, dpc, first_ref, second_ref, model_hbm, vis_hbm, mask_hbm, power_in, *rest):
    ins, rest = rest[:n], rest[n:]
    out_ref, power_ref, vis_ref, mask_ref, side, model_ref, sems, hre, him, cre, cim, stack = rest
    copies = bring([(vis_hbm, vis_ref), (mask_hbm, mask_ref)], side)
    fetch = Fetch(model_hbm, model_ref, sems)
    products_first(n, dpc, lax.axis_index("bl"), first_ref, second_ref, ins, hre, him, stack)
    for copy in copies:
        copy.wait()
    chips = range(n // 2)
    power_ref[: n // 4] = power_in[...]

    def pair(b, carry):
        acc = predict(dpc, b, (vis_ref[0, b], vis_ref[1, b]), chips, model_ref, hre, him)
        weight = mask_ref[b].astype(F32)
        correlate(dpc, b, weighted(b, acc, mask_ref), chips, model_ref, cre, cim, weight, power_ref)
        return carry

    fetch.each(pair)
    clear(dpc, mask_ref.shape[0], cre, cim, power_ref)
    write_sums(dpc, chips, cre, cim, lambda m: (hre, him, m), power_ref, out_ref, True)


NEAR, FAR = (0, 1, 2, 6), (3, 4, 5, 7)


def chips_of(me, pairs):
    return [jnp.bitwise_xor(lax.div(me, 2), m) for m in pairs]


def early_kernel(n, dpc, first_ref, second_ref, model_hbm, vis_ref, unused_in, *rest):
    ins, rest = rest[: 2 * len(NEAR)], rest[2 * len(NEAR) :]
    acc_ref, hre, him, unused_out, model_ref, sems = rest
    me = lax.axis_index("bl")
    fetch = Fetch(model_hbm, model_ref, sems, [k * dpc for k in chips_of(me, NEAR)])
    products(dpc, me, first_ref, second_ref, ins, hre, him)

    def pair(b, carry):
        acc = vis_ref[0, b], vis_ref[1, b]
        acc_ref[0, b], acc_ref[1, b] = predict(dpc, b, acc, range(len(NEAR)), model_ref, hre, him)
        return carry

    fetch.each(pair)


def later_pass_kernel(
    n,
    dpc,
    first_ref,
    second_ref,
    model_hbm,
    mask_ref,
    power_ref,
    acc_ref,
    near_re,
    near_im,
    *rest,
):
    ins, rest = rest[: 2 * len(FAR)], rest[2 * len(FAR) :]
    out_ref, model_ref, sems, hre, him, cre, cim = rest
    fetch = Fetch(model_hbm, model_ref, sems)
    me = lax.axis_index("bl")
    products(dpc, me, first_ref, second_ref, ins, hre, him)
    far = chips_of(me, FAR)
    chips = chips_of(me, NEAR) + far

    def pair(b, carry):
        acc = predict(dpc, b, (acc_ref[0, b], acc_ref[1, b]), far, model_ref, hre, him)
        correlate(dpc, b, weighted(b, acc, mask_ref), chips, model_ref, cre, cim)
        return carry

    fetch.each(pair)

    def tiles(m):
        for re, im, pairs in ((near_re, near_im, NEAR), (hre, him, FAR)):
            if m < len(pairs):
                return re, im, m
            m -= len(pairs)

    clear(dpc, mask_ref.shape[0], cre, cim)
    write_sums(dpc, chips, cre, cim, tiles, power_ref, out_ref, False)


def last_kernel(n, dpc, first_ref, second_ref, model_hbm, mask_ref, acc_ref, *rest):
    ins, (res_ref, gains_ref, model_ref, sems, hre, him) = rest[:n], rest[n:]
    me = lax.axis_index("bl")
    fetch = Fetch(model_hbm, model_ref, sems, [k * dpc for k in chips_of(me, FAR)])
    products(dpc, me, first_ref, second_ref, ins[: 2 * len(FAR)], hre, him)
    per = STATIONS // n
    even = lax.rem(me, 2) == 0
    for m, k in enumerate(chips_of(me, FAR + NEAR)):
        done = [piece_pair(dpc, even, ins, m, me * per + s) for s in range(per)]
        for s, parts in enumerate(done):
            for dd in range(dpc):
                at = s * SOURCE_COUNT + k * dpc + dd
                gains_ref[0, pl.ds(at, 1), :] = parts[0][dd : dd + 1]
                gains_ref[1, pl.ds(at, 1), :] = parts[1][dd : dd + 1]

    def pair(b, carry):
        acc = acc_ref[0, b], acc_ref[1, b]
        acc = predict(dpc, b, acc, range(len(FAR)), model_ref, hre, him)
        res_ref[0, b], res_ref[1, b] = weighted(b, acc, mask_ref)
        return carry

    fetch.each(pair)


SMEM = pl.BlockSpec(memory_space=pltpu.SMEM)
VMEM = pl.BlockSpec(memory_space=pltpu.VMEM)
HBM = pl.BlockSpec(memory_space=pltpu.HBM)


def shape(*dims, dtype=F32):
    return jax.ShapeDtypeStruct(dims, dtype)


def exchange(x):
    return lax.all_to_all(x, "bl", split_axis=0, concat_axis=0, tiled=True)


def gather(n, piece, beside):
    def send(x, o):
        return lax.ppermute(x, "bl", [(i, i ^ o) for i in range(n)])

    got = {0: piece}
    got[12], got[2], got[4], got[1] = (send(piece, o) for o in (12, 2, 4, 1))
    got[8] = send(got[12], 4)
    got[6], got[14], got[10] = send(got[4], 2), send(got[12], 2), send(got[8], 2)
    for o in (2, 4, 12, 6, 14, 8, 10):
        if o == 6:
            got[o] = beside(got[o], got)
        got[o + 1] = send(got[o], 1)
    return [got[o] for o in range(n)]


def fast_body(n, vis, model, mask, first, second, gre, gim):
    starts = (first.reshape(1, -1), second.reshape(1, -1), gre, gim)
    model, far_vis, far_mask, *starts = (
        pltpu.with_memory_space_constraint(x, pltpu.HBM) for x in (model, vis, mask, *starts)
    )
    dpc = SOURCE_COUNT // (n // 2)
    width = dpc * 128
    pairs, times, channels = mask.shape
    params = pltpu.CompilerParams(vmem_limit_bytes=VMEM_LIMIT)
    plane = (n // 2, ROWS * dpc + TILE, channels)
    half = (len(FAR), ROWS * dpc + TILE, channels)
    lots = n * 2 * ROWS
    mine = (STATIONS * dpc + TILE, channels)
    sems = pltpu.SemaphoreType.DMA((len(PARTS), n // 4))
    side = pltpu.SemaphoreType.DMA((2,))
    mask_held = [pltpu.VMEM(mask.shape, jnp.int32), side]
    held = [pltpu.VMEM(model.shape, BF16), sems]
    held_half = [pltpu.VMEM((SOURCE_COUNT // 2,) + model.shape[1:], BF16), sems]

    def call(kernel, args, outs, scratch=(), micros=1, aliases={}):
        def place(x):
            if any(x is y for y in (model, far_vis, far_mask, *starts)):
                return HBM
            return SMEM if x.ndim == 1 else VMEM

        return pl.pallas_call(
            functools.partial(kernel, n, dpc),
            in_specs=[place(x) for x in args],
            out_specs=[VMEM for o in outs],
            out_shape=outs,
            scratch_shapes=[pltpu.VMEM(x, F32) if isinstance(x, tuple) else x for x in scratch],
            compiler_params=params,
            input_output_aliases=aliases,
            cost_estimate=pl.CostEstimate(
                flops=0, bytes_accessed=int(micros * 3.69e6), transcendentals=0
            ),
        )(*args)

    (piece,) = call(
        pack_kernel,
        starts,
        [shape(2 * gre.shape[0] + TILE, channels)],
        [pltpu.VMEM((1, pairs), jnp.int32)] * 2 + [pltpu.SemaphoreType.DMA((4,))],
    )
    power = None

    def powers_beside(x, got):
        nonlocal power
        outs = [shape(*half), shape(*x.shape)]
        power, x = call(power_kernel, (model, far_mask, x), outs, mask_held + held_half, micros=20, aliases={2: 1})
        return x

    got = gather(n, piece, powers_beside)
    g, onehot = call(
        first_own_kernel,
        got,
        [shape(*mine), shape(STATIONS, lots, dtype=BF16)],
        [(STATIONS * TILE, channels), (n, channels)],
        micros=2,
    )
    sums, power = call(
        first_pass_kernel,
        (first, second, model, far_vis, far_mask, power, *got),
        [shape(n, (ROWS + TILE) * dpc, channels), pltpu.HBM(plane, F32)],
        [vis.shape] + mask_held + held + [plane] * 4 + [(n,) + piece.shape],
        micros=9,
    )
    powers = exchange(sums)
    (g,) = call(
        own_kernel,
        (g, onehot, powers),
        [shape(*mine)],
        [(lots, 2 * width), (lots, width)],
    )

    def slots(got, pairs):
        return [got[2 * m + c] for m in pairs for c in (0, 1)]

    def gather_near(g):
        near = None

        def beside(x, got):
            nonlocal near
            args = (first, second, model, vis, x, *slots(got, NEAR))
            outs = [shape(*vis.shape), shape(*half), shape(*half), shape(*x.shape)]
            *near, x = call(early_kernel, args, outs, held_half, aliases={4: 3})
            return x

        got = gather(n, g, beside)
        return near, slots(got, FAR + NEAR)

    for step in range(1, ITERS):
        near, got = gather_near(g)
        (den,) = call(
            prepare_kernel,
            (g, onehot, powers),
            [shape(STATIONS, width)],
            [(lots, width)] * 2,
            micros=2,
        )
        (sums,) = call(
            later_pass_kernel,
            (first, second, model, mask, power, *near, *got[: 2 * len(FAR)]),
            [shape(n, ROWS * dpc, channels)],
            held + [half] * 2 + [plane] * 2,
            micros=7,
        )
        sums = exchange(sums)
        (g,) = call(
            later_own_kernel,
            (g, onehot, den, sums),
            [shape(*mine)],
            [(lots, width)] * 2,
        )
    near, got = gather_near(g)
    residual, gains = call(
        last_kernel,
        (first, second, model, mask, near[0], *got),
        [shape(*vis.shape), shape(2, *gre.shape)],
        held_half + [half] * 2,
        micros=4,
    )
    return gains, residual


def block_pass(full_re, full_im, vis_blk, coh_blk, weight, first, second, want_sums):
    ar = jnp.transpose(full_re[first], (1, 0, 2))
    ai = jnp.transpose(full_im[first], (1, 0, 2))
    br = jnp.transpose(full_re[second], (1, 0, 2))
    bi = jnp.transpose(full_im[second], (1, 0, 2))
    mr = coh_blk[:, 0].astype(F32)
    mi = coh_blk[:, 1].astype(F32)
    hr = ar * br + ai * bi
    hi = ai * br - ar * bi
    hr_t, hi_t = hr[:, :, None], hi[:, :, None]
    res_re = weight * (vis_blk[0] - jnp.sum(hr_t * mr - hi_t * mi, 0))
    res_im = weight * (vis_blk[1] - jnp.sum(hr_t * mi + hi_t * mr, 0))
    residual = jnp.stack([res_re, res_im])
    if not want_sums:
        return (residual, None)
    power = jnp.sum(weight[None] * (mr * mr + mi * mi), 2)
    sum_re = jnp.sum(mr * res_re + mi * res_im, 2) + hr * power
    sum_im = jnp.sum(mr * res_im - mi * res_re, 2) + hi * power
    terms_first = jnp.stack([br * sum_re - bi * sum_im, br * sum_im + bi * sum_re, power * (br * br + bi * bi)])
    terms_second = jnp.stack([ar * sum_re + ai * sum_im, ai * sum_re - ar * sum_im, power * (ar * ar + ai * ai)])
    stations = jnp.arange(STATIONS, dtype=jnp.int32)
    onehot_first = (first[:, None] == stations[None, :]).astype(F32)
    onehot_second = (second[:, None] == stations[None, :]).astype(F32)
    exact = lax.Precision.HIGHEST
    sums = jnp.einsum("bs,cdbf->csdf", onehot_first, terms_first, precision=exact)
    sums = sums + jnp.einsum("bs,cdbf->csdf", onehot_second, terms_second, precision=exact)
    return (residual, sums)


def plain_body(vis, model, mask, first, second, gre, gim):
    weight = mask.astype(F32)
    rows, channels = gre.shape
    shaped = (STATIONS, SOURCE_COUNT, channels)
    full_re = lax.all_gather(gre, "bl", axis=0, tiled=True).reshape(shaped)
    full_im = lax.all_gather(gim, "bl", axis=0, tiled=True).reshape(shaped)
    for step in range(ITERS):
        unused, sums = block_pass(full_re, full_im, vis, model, weight, first, second, True)
        totals = lax.psum(sums, "bl")
        denom = totals[2] + ridge
        full_re = 0.5 * (full_re + totals[0] / denom)
        full_im = 0.5 * (full_im + totals[1] / denom)
    residual, unused = block_pass(full_re, full_im, vis, model, weight, first, second, False)
    both = jnp.stack([full_re, full_im]).reshape(2, STATIONS * SOURCE_COUNT, channels)
    return lax.dynamic_slice_in_dim(both, lax.axis_index("bl") * rows, rows, 1), residual


def solution(mesh):
    n = mesh.shape["bl"]
    split = n == 16

    def body(vis, model, mask, first, second, gre, gim):
        if split and mask.shape[0] <= ROWS:
            return fast_body(n, vis, model, mask, first, second, gre, gim)
        return plain_body(vis, model, mask, first, second, gre, gim)

    in_specs = (
        P(None, ("grp", "bl"), None, None),
        P(None, None, ("grp", "bl"), None, None),
        P(("grp", "bl"), None, None),
        P(("grp", "bl")),
        P(("grp", "bl")),
        P(("grp", "bl"), None),
        P(("grp", "bl"), None),
    )
    out_specs = (P(None, ("grp", "bl"), None), P(None, ("grp", "bl"), None, None))
    return jax.shard_map(body, mesh=mesh, in_specs=in_specs, out_specs=out_specs, check_vma=False)
```

```python
import functools

import jax
import jax.numpy as jnp
from jax import lax
from jax.experimental import pallas as pl
from jax.experimental.pallas import tpu as pltpu
from jax.sharding import PartitionSpec as P

STATIONS = 64
SOURCE_COUNT = 40
ITERS = 2
ROWS = 16

ridge = 1.0
F32 = jnp.float32
BF16 = jnp.bfloat16
VMEM_LIMIT = 24 * 1024 * 1024


def swap(x):
    return pltpu.roll(x, x.shape[-1] // 2, axis=x.ndim - 1)


def lower(shape):
    return lax.broadcasted_iota(jnp.int32, shape, len(shape) - 1) < shape[-1] // 2


def cross(a, b):
    lo = lower(a.shape)
    return jnp.where(lo, a, swap(b)), jnp.where(lo, swap(a), b)


def halves_of(x):
    hi = x.astype(BF16)
    return hi, (x - hi.astype(F32)).astype(BF16)


def pick(onehot, x, dims):
    return sum(
        lax.dot_general(onehot, part, (dims, ((), ())), preferred_element_type=F32)
        for part in halves_of(x)
    )


TILE = 8
PARTS = (1, 3, 7, ROWS)


def pack_kernel(n, dpc, first_hbm, second_hbm, re_hbm, im_hbm, out_ref, first_ref, second_ref, sems):
    rows = re_hbm.shape[0]
    copies = [
        pltpu.make_async_copy(first_hbm, first_ref, sems.at[0]),
        pltpu.make_async_copy(second_hbm, second_ref, sems.at[1]),
        pltpu.make_async_copy(re_hbm, out_ref.at[pl.ds(0, rows)], sems.at[2]),
        pltpu.make_async_copy(im_hbm, out_ref.at[pl.ds(rows, rows)], sems.at[3]),
    ]
    for copy in copies:
        copy.start()
    out_ref[2 * rows :] = jnp.zeros((TILE, 128), F32)
    for copy in copies:
        copy.wait()
    pairs = first_ref.shape[1]
    out_ref[2 * rows : 2 * rows + 1, :pairs] = (first_ref[...] + 1).astype(F32)
    out_ref[2 * rows : 2 * rows + 1, ROWS : ROWS + pairs] = (second_ref[...] + 1).astype(F32)


class Fetch:
    def __init__(self, model, held, sems, firsts=(0,)):
        count, pairs = held.shape[0] // len(firsts), held.shape[2]
        self.copies = []
        self.ends = [0] + [min(end, pairs) for end in PARTS]
        for i in range(len(PARTS)):
            part = pl.ds(self.ends[i], self.ends[i + 1] - self.ends[i])
            self.copies.append([])
            for j, first in enumerate(firsts):
                self.copies[i].append(
                    pltpu.make_async_copy(
                        model.at[pl.ds(first, count), :, part],
                        held.at[pl.ds(j * count, count), :, part],
                        sems.at[i, j],
                    )
                )
        for copies in self.copies:
            for copy in copies:
                copy.start()

    def each(self, body):
        for i, copies in enumerate(self.copies):
            for copy in copies:
                copy.wait()
            lax.fori_loop(self.ends[i], self.ends[i + 1], body, 0)


def bring(pairs, sems):
    copies = [pltpu.make_async_copy(*pair, sems.at[i]) for i, pair in enumerate(pairs)]
    for copy in copies:
        copy.start()
    return copies


def power_kernel(
    n, dpc, model_hbm, mask_hbm, unused_in, out_ref, unused_out, mask_ref, side, model_ref, sems
):
    (mask_copy,) = bring([(mask_hbm, mask_ref)], side)
    fetch = Fetch(model_hbm, model_ref, sems)
    out_ref[...] = jnp.zeros_like(out_ref)

    def pair(b, carry):
        weight = mask_ref[b].astype(F32)
        for d in range(model_ref.shape[0]):
            mr = model_ref[d, 0, b].astype(F32)
            mi = model_ref[d, 1, b].astype(F32)
            row = pl.ds(b * dpc + d % dpc, 1)
            out_ref[d // dpc, row, :] = jnp.sum(weight * (mr * mr + mi * mi), axis=0, keepdims=True)
        return carry

    mask_copy.wait()
    fetch.each(pair)


def wide(ref, dpc):
    return jnp.concatenate([ref[pl.ds(dd, STATIONS, stride=dpc), :] for dd in range(dpc)], axis=1)


def put(ref, value, dpc):
    for dd in range(dpc):
        ref[pl.ds(dd, STATIONS, stride=dpc), :] = value[:, dd * 128 : (dd + 1) * 128]
    ref[STATIONS * dpc :, :] = jnp.zeros((TILE, 128), F32)


def first_own_kernel(n, dpc, *rest):
    ins, (g_ref, onehot_ref, unused_out, split, lines) = rest[:n], rest[n:]
    me = lax.axis_index("bl")
    k, c = lax.div(me, 2), lax.rem(me, 2)
    per = STATIONS // n
    rows = per * SOURCE_COUNT
    for o in range(n):
        peer = jnp.bitwise_xor(me, o)
        lines[pl.ds(peer, 1), :] = ins[o][2 * rows : 2 * rows + 1, :]
        done = []
        for s in range(per):
            at = s * SOURCE_COUNT + k * dpc
            x0, x1 = cross(ins[o][pl.ds(at, TILE), :], ins[o][pl.ds(rows + at, TILE), :])
            done.append(jnp.where(c == 0, x0, x1))
        for s in range(per):
            to = pl.multiple_of((peer * per + s) * TILE, TILE)
            split[pl.ds(to, TILE), :] = done[s]
    g = jnp.concatenate([split[pl.ds(dd, STATIONS, stride=TILE), :] for dd in range(dpc)], axis=1)
    put(g_ref, g, dpc)
    across = 128 // (2 * ROWS)
    station = lax.broadcasted_iota(jnp.int32, (STATIONS, 128), 0)
    for group in range(n // across):
        marks = jnp.zeros((1, 128), F32)
        for i in range(across):
            row = lines[group * across + i : group * across + i + 1, :]
            marks = marks + (pltpu.roll(row, i * 2 * ROWS, axis=1) if i else row)
        hit = station + 1 == marks.astype(jnp.int32)
        onehot_ref[:, group * 128 : (group + 1) * 128] = jnp.where(hit, 1.0, 0.0).astype(BF16)


def fill_powers(n, dpc, sums, sel_ref, terms, base):
    lo = lower((TILE, 128))
    for o in range(n):
        r = o * 2 * ROWS
        for dd in range(dpc):
            cols = slice(dd * 128, (dd + 1) * 128)
            dcols = slice(base + dd * 128, base + (dd + 1) * 128)
            W = sums[o, pl.ds(ROWS * dpc + dd, TILE, stride=dpc), :]
            Wx = swap(W)
            W = jnp.concatenate([jnp.where(lo, W, Wx), jnp.where(lo, Wx, W)], 0)
            p = sel_ref[r : r + ROWS, cols]
            q = sel_ref[r + ROWS : r + 2 * ROWS, cols]
            p2, q2 = p * p, q * q
            terms[r : r + ROWS, dcols] = W * (q2 + swap(q2))
            terms[r + ROWS : r + 2 * ROWS, dcols] = W * (p2 + swap(p2))


def fill_sums(n, dpc, sums, sel_ref, terms):
    lo = lower((ROWS, 128))
    sign = jnp.where(lo, -1.0, 1.0)
    for o in range(n):
        r = o * 2 * ROWS
        for dd in range(dpc):
            cols = slice(dd * 128, (dd + 1) * 128)
            B = sums[o, pl.ds(dd, ROWS, stride=dpc), :]
            p = sel_ref[r : r + ROWS, cols]
            q = sel_ref[r + ROWS : r + 2 * ROWS, cols]
            Bx = swap(B)
            Brr, Bii = jnp.where(lo, B, Bx), sign * jnp.where(lo, Bx, B)
            terms[r : r + ROWS, cols] = Brr * q + Bii * swap(q)
            terms[r + ROWS : r + 2 * ROWS, cols] = Brr * p - Bii * swap(p)


def own_kernel(n, dpc, g_in, onehot_ref, sums, g_out, terms, sel_ref):
    width = dpc * 128
    sel_ref[...] = pick(onehot_ref[...], wide(g_in, dpc), ((0,), (0,)))
    fill_sums(n, dpc, sums, sel_ref, terms)
    fill_powers(n, dpc, sums, sel_ref, terms, width)
    total = pick(onehot_ref[...], terms[...], ((1,), (0,)))
    put(g_out, 0.5 * (wide(g_in, dpc) + total[:, :width] / (total[:, width:] + ridge)), dpc)


def prepare_kernel(n, dpc, g_ref, onehot_ref, sums, den_ref, terms, sel_ref):
    sel_ref[...] = pick(onehot_ref[...], wide(g_ref, dpc), ((0,), (0,)))
    fill_powers(n, dpc, sums, sel_ref, terms, 0)
    den_ref[...] = pick(onehot_ref[...], terms[...], ((1,), (0,))) + ridge


def later_own_kernel(n, dpc, g_in, onehot_ref, den_ref, sums, g_out, terms, sel_ref):
    sel_ref[...] = pick(onehot_ref[...], wide(g_in, dpc), ((0,), (0,)))
    fill_sums(n, dpc, sums, sel_ref, terms)
    total = pick(onehot_ref[...], terms[...], ((1,), (0,)))
    put(g_out, 0.5 * (wide(g_in, dpc) + total / den_ref[...]), dpc)


def clear(dpc, pairs, *refs):
    for ref in refs:
        chips, rows, _ = ref.shape
        for m in range(chips):
            ref[m, pairs * dpc :, :] = jnp.zeros((rows - pairs * dpc, 128), F32)


def products_first(n, dpc, me, first_ref, second_ref, ins, hre, him, stack):
    per = STATIONS // n
    rows = per * SOURCE_COUNT
    for o in range(n):
        stack[jnp.bitwise_xor(me, o)] = ins[o][...]

    def block(station, k, part):
        at = lax.rem(station, per) * SOURCE_COUNT + k * dpc + part * rows
        return stack[lax.div(station, per), pl.ds(at, TILE), :]

    def one(b, k):
        p, q = first_ref[b], second_ref[b]
        return block(p, k, 0), block(p, k, 1), block(q, k, 0), block(q, k, 1)

    assemble(dpc, first_ref.shape[0], range(n // 2), one, hre, him)


def assemble(dpc, pairs, chips, one, hre, him):
    size = 3 if pairs % 3 == 0 else 1

    def group(i, carry):
        done = []
        for u in range(size):
            for m in chips:
                pr, pi, qr, qi = one(i * size + u, m)
                done.append((u, m, pr * qr + pi * qi, pi * qr - pr * qi))
        for u, m, re, im in done:
            rows = pl.ds((i * size + u) * dpc, TILE)
            hre[m, rows, :] = re
            him[m, rows, :] = im
        return carry

    lax.fori_loop(0, pairs // size, group, 0)
    clear(dpc, pairs, hre, him)


def piece_pair(dpc, even, ins, m, station):
    a = ins[2 * m][pl.ds(station * dpc, TILE), :]
    b = ins[2 * m + 1][pl.ds(station * dpc, TILE), :]
    return cross(jnp.where(even, a, b), jnp.where(even, b, a))


def products(dpc, me, first_ref, second_ref, ins, hre, him):
    even = lax.rem(me, 2) == 0

    def one(b, m):
        return *piece_pair(dpc, even, ins, m, first_ref[b]), *piece_pair(dpc, even, ins, m, second_ref[b])

    assemble(dpc, first_ref.shape[0], range(len(ins) // 2), one, hre, him)


def predict(dpc, b, acc, chips, model_ref, hre, him):
    tiles = [slice(t, t + TILE) for t in range(0, acc[0].shape[0], TILE)]
    acc_re, acc_im = ([x[t] for t in tiles] for x in acc)
    for m, k in enumerate(chips):
        for dd in range(dpc):
            mr = model_ref[k * dpc + dd, 0, b].astype(F32)
            mi = model_ref[k * dpc + dd, 1, b].astype(F32)
            row = pl.ds(b * dpc + dd, TILE, stride=0)
            hr, hi = hre[m, row, :], him[m, row, :]
            for i, t in enumerate(tiles):
                acc_re[i] = acc_re[i] - (hr * mr[t] - hi * mi[t])
                acc_im[i] = acc_im[i] - (hr * mi[t] + hi * mr[t])
    return jnp.concatenate(acc_re, 0), jnp.concatenate(acc_im, 0)


def weighted(b, acc, mask_ref):
    weight = mask_ref[b].astype(F32)
    return weight * acc[0], weight * acc[1]


def fold(a, b, step):
    if a is None:
        return None
    if b is None:
        return a + pltpu.roll(a, step, axis=0)
    mine = (lax.broadcasted_iota(jnp.int32, a.shape, 0) & step) == 0
    return jnp.where(mine, a, b) + pltpu.roll(jnp.where(mine, b, a), step, axis=0)


def row_sums(values):
    values = list(values) + [None] * (TILE - len(values))
    step = 1
    while step < TILE:
        values = [fold(a, b, step) for a, b in zip(values[::2], values[1::2])]
        step *= 2
    return values[0]


def tile_sum(x):
    total = x[:TILE]
    for t in range(1, x.shape[0] // TILE):
        total = total + x[t * TILE : (t + 1) * TILE]
    return total


def correlate(dpc, b, res, chips, model_ref, cre, cim, weight=None, power_ref=None):
    res_re, res_im = res
    done = []
    for m, k in enumerate(chips):
        re, im, power = [], [], []
        for dd in range(dpc):
            mr = model_ref[k * dpc + dd, 0, b].astype(F32)
            mi = model_ref[k * dpc + dd, 1, b].astype(F32)
            re.append(tile_sum(mr * res_re + mi * res_im))
            im.append(tile_sum(mr * res_im - mi * res_re))
            if weight is not None and m >= len(chips) // 2:
                power.append(tile_sum(weight * (mr * mr + mi * mi)))
        done.append((m, row_sums(re), row_sums(im), row_sums(power) if power else None))
    for m, re, im, power in done:
        cre[m, pl.ds(b * dpc, TILE), :] = re
        cim[m, pl.ds(b * dpc, TILE), :] = im
        if power is not None:
            power_ref[m, pl.ds(b * dpc, TILE), :] = power


def write_sums(dpc, chips, cre, cim, tiles, power_ref, out_ref, start):
    for m, k in enumerate(chips):
        re, im, at = tiles(m)
        done = []
        for t in range(ROWS * dpc // TILE):
            rows = slice(t * TILE, (t + 1) * TILE)
            w = power_ref[k, rows, :]
            done.append(cross(cre[m, rows, :] + re[at, rows, :] * w, cim[m, rows, :] + im[at, rows, :] * w))
        if start:
            for t in range(dpc):
                low, high = (slice(u * TILE, (u + 1) * TILE) for u in (t, t + dpc))
                done.append(cross(power_ref[k, low, :], power_ref[k, high, :]))
        for t, (x0, x1) in enumerate(done):
            rows = slice(t * TILE, (t + 1) * TILE)
            out_ref[2 * k, rows, :] = x0
            out_ref[2 * k + 1, rows, :] = x1


def first_pass_kernel(n, dpc, first_ref, second_ref, model_hbm, vis_hbm, mask_hbm, power_in, *rest):
    ins, rest = rest[:n], rest[n:]
    out_ref, power_ref, vis_ref, mask_ref, side, model_ref, sems, hre, him, cre, cim, stack = rest
    copies = bring([(vis_hbm, vis_ref), (mask_hbm, mask_ref)], side)
    fetch = Fetch(model_hbm, model_ref, sems)
    products_first(n, dpc, lax.axis_index("bl"), first_ref, second_ref, ins, hre, him, stack)
    for copy in copies:
        copy.wait()
    chips = range(n // 2)
    power_ref[: n // 4] = power_in[...]

    def pair(b, carry):
        acc = predict(dpc, b, (vis_ref[0, b], vis_ref[1, b]), chips, model_ref, hre, him)
        weight = mask_ref[b].astype(F32)
        correlate(dpc, b, weighted(b, acc, mask_ref), chips, model_ref, cre, cim, weight, power_ref)
        return carry

    fetch.each(pair)
    clear(dpc, mask_ref.shape[0], cre, cim, power_ref)
    write_sums(dpc, chips, cre, cim, lambda m: (hre, him, m), power_ref, out_ref, True)


NEAR, FAR = (0, 1, 2, 6), (3, 4, 5, 7)


def chips_of(me, pairs):
    return [jnp.bitwise_xor(lax.div(me, 2), m) for m in pairs]


def early_kernel(n, dpc, first_ref, second_ref, model_hbm, vis_ref, unused_in, *rest):
    ins, rest = rest[: 2 * len(NEAR)], rest[2 * len(NEAR) :]
    acc_ref, hre, him, unused_out, model_ref, sems = rest
    me = lax.axis_index("bl")
    fetch = Fetch(model_hbm, model_ref, sems, [k * dpc for k in chips_of(me, NEAR)])
    products(dpc, me, first_ref, second_ref, ins, hre, him)

    def pair(b, carry):
        acc = vis_ref[0, b], vis_ref[1, b]
        acc_ref[0, b], acc_ref[1, b] = predict(dpc, b, acc, range(len(NEAR)), model_ref, hre, him)
        return carry

    fetch.each(pair)


def later_pass_kernel(
    n,
    dpc,
    first_ref,
    second_ref,
    model_hbm,
    mask_ref,
    power_ref,
    acc_ref,
    near_re,
    near_im,
    *rest,
):
    ins, rest = rest[: 2 * len(FAR)], rest[2 * len(FAR) :]
    out_ref, model_ref, sems, hre, him, cre, cim = rest
    fetch = Fetch(model_hbm, model_ref, sems)
    me = lax.axis_index("bl")
    products(dpc, me, first_ref, second_ref, ins, hre, him)
    far = chips_of(me, FAR)
    chips = chips_of(me, NEAR) + far

    def pair(b, carry):
        acc = predict(dpc, b, (acc_ref[0, b], acc_ref[1, b]), far, model_ref, hre, him)
        correlate(dpc, b, weighted(b, acc, mask_ref), chips, model_ref, cre, cim)
        return carry

    fetch.each(pair)

    def tiles(m):
        for re, im, pairs in ((near_re, near_im, NEAR), (hre, him, FAR)):
            if m < len(pairs):
                return re, im, m
            m -= len(pairs)

    clear(dpc, mask_ref.shape[0], cre, cim)
    write_sums(dpc, chips, cre, cim, tiles, power_ref, out_ref, False)


def last_kernel(n, dpc, first_ref, second_ref, model_hbm, mask_ref, acc_ref, *rest):
    ins, (res_ref, gains_ref, model_ref, sems, hre, him) = rest[:n], rest[n:]
    me = lax.axis_index("bl")
    fetch = Fetch(model_hbm, model_ref, sems, [k * dpc for k in chips_of(me, FAR)])
    products(dpc, me, first_ref, second_ref, ins[: 2 * len(FAR)], hre, him)
    per = STATIONS // n
    even = lax.rem(me, 2) == 0
    for m, k in enumerate(chips_of(me, FAR + NEAR)):
        done = [piece_pair(dpc, even, ins, m, me * per + s) for s in range(per)]
        for s, parts in enumerate(done):
            for dd in range(dpc):
                at = s * SOURCE_COUNT + k * dpc + dd
                gains_ref[0, pl.ds(at, 1), :] = parts[0][dd : dd + 1]
                gains_ref[1, pl.ds(at, 1), :] = parts[1][dd : dd + 1]

    def pair(b, carry):
        acc = acc_ref[0, b], acc_ref[1, b]
        acc = predict(dpc, b, acc, range(len(FAR)), model_ref, hre, him)
        res_ref[0, b], res_ref[1, b] = weighted(b, acc, mask_ref)
        return carry

    fetch.each(pair)


SMEM = pl.BlockSpec(memory_space=pltpu.SMEM)
VMEM = pl.BlockSpec(memory_space=pltpu.VMEM)
HBM = pl.BlockSpec(memory_space=pltpu.HBM)


def shape(*dims, dtype=F32):
    return jax.ShapeDtypeStruct(dims, dtype)


def exchange(x):
    return lax.all_to_all(x, "bl", split_axis=0, concat_axis=0, tiled=True)


def gather(n, piece, beside):
    def send(x, o):
        return lax.ppermute(x, "bl", [(i, i ^ o) for i in range(n)])

    got = {0: piece}
    got[12], got[2], got[4], got[1] = (send(piece, o) for o in (12, 2, 4, 1))
    got[8] = send(got[12], 4)
    got[6], got[14], got[10] = send(got[4], 2), send(got[12], 2), send(got[8], 2)
    for o in (2, 4, 12, 6, 14, 8, 10):
        if o == 6:
            got[o] = beside(got[o], got)
        got[o + 1] = send(got[o], 1)
    return [got[o] for o in range(n)]


def fast_body(n, vis, model, mask, first, second, gre, gim):
    starts = (first.reshape(1, -1), second.reshape(1, -1), gre, gim)
    model, far_vis, far_mask, *starts = (
        pltpu.with_memory_space_constraint(x, pltpu.HBM) for x in (model, vis, mask, *starts)
    )
    dpc = SOURCE_COUNT // (n // 2)
    width = dpc * 128
    pairs, times, channels = mask.shape
    params = pltpu.CompilerParams(vmem_limit_bytes=VMEM_LIMIT)
    plane = (n // 2, ROWS * dpc + TILE, channels)
    half = (len(FAR), ROWS * dpc + TILE, channels)
    lots = n * 2 * ROWS
    mine = (STATIONS * dpc + TILE, channels)
    sems = pltpu.SemaphoreType.DMA((len(PARTS), n // 4))
    side = pltpu.SemaphoreType.DMA((2,))
    mask_held = [pltpu.VMEM(mask.shape, jnp.int32), side]
    held = [pltpu.VMEM(model.shape, BF16), sems]
    held_half = [pltpu.VMEM((SOURCE_COUNT // 2,) + model.shape[1:], BF16), sems]

    def call(kernel, args, outs, scratch=(), micros=1, aliases={}):
        def place(x):
            if any(x is y for y in (model, far_vis, far_mask, *starts)):
                return HBM
            return SMEM if x.ndim == 1 else VMEM

        return pl.pallas_call(
            functools.partial(kernel, n, dpc),
            in_specs=[place(x) for x in args],
            out_specs=[VMEM for o in outs],
            out_shape=outs,
            scratch_shapes=[pltpu.VMEM(x, F32) if isinstance(x, tuple) else x for x in scratch],
            compiler_params=params,
            input_output_aliases=aliases,
            cost_estimate=pl.CostEstimate(
                flops=0, bytes_accessed=int(micros * 3.69e6), transcendentals=0
            ),
        )(*args)

    (piece,) = call(
        pack_kernel,
        starts,
        [shape(2 * gre.shape[0] + TILE, channels)],
        [pltpu.VMEM((1, pairs), jnp.int32)] * 2 + [pltpu.SemaphoreType.DMA((4,))],
    )
    power = None

    def powers_beside(x, got):
        nonlocal power
        outs = [shape(*half), shape(*x.shape)]
        power, x = call(power_kernel, (model, far_mask, x), outs, mask_held + held_half, micros=20, aliases={2: 1})
        return x

    got = gather(n, piece, powers_beside)
    g, onehot, got[0] = call(
        first_own_kernel,
        got,
        [shape(*mine), shape(STATIONS, lots, dtype=BF16), shape(*piece.shape)],
        [(STATIONS * TILE, channels), (n, channels)],
        micros=2,
        aliases={0: 2},
    )
    sums, power = call(
        first_pass_kernel,
        (first, second, model, far_vis, far_mask, power, *got),
        [shape(n, (ROWS + TILE) * dpc, channels), pltpu.HBM(plane, F32)],
        [vis.shape] + mask_held + held + [plane] * 4 + [(n,) + piece.shape],
        micros=9,
    )
    powers = exchange(sums)
    (g,) = call(
        own_kernel,
        (g, onehot, powers),
        [shape(*mine)],
        [(lots, 2 * width), (lots, width)],
    )

    def slots(got, pairs):
        return [got[2 * m + c] for m in pairs for c in (0, 1)]

    def gather_near(g):
        near = None

        def beside(x, got):
            nonlocal near
            args = (first, second, model, vis, x, *slots(got, NEAR))
            outs = [shape(*vis.shape), shape(*half), shape(*half), shape(*x.shape)]
            *near, x = call(early_kernel, args, outs, held_half, aliases={4: 3})
            return x

        got = gather(n, g, beside)
        return near, slots(got, FAR + NEAR)

    for step in range(1, ITERS):
        near, got = gather_near(g)
        (den,) = call(
            prepare_kernel,
            (g, onehot, powers),
            [shape(STATIONS, width)],
            [(lots, width)] * 2,
            micros=2,
        )
        (sums,) = call(
            later_pass_kernel,
            (first, second, model, mask, power, *near, *got[: 2 * len(FAR)]),
            [shape(n, ROWS * dpc, channels)],
            held + [half] * 2 + [plane] * 2,
            micros=7,
        )
        sums = exchange(sums)
        (g,) = call(
            later_own_kernel,
            (g, onehot, den, sums),
            [shape(*mine)],
            [(lots, width)] * 2,
        )
    near, got = gather_near(g)
    residual, gains = call(
        last_kernel,
        (first, second, model, mask, near[0], *got),
        [shape(*vis.shape), shape(2, *gre.shape)],
        held_half + [half] * 2,
        micros=4,
    )
    return gains, residual


def block_pass(full_re, full_im, vis_blk, coh_blk, weight, first, second, want_sums):
    ar = jnp.transpose(full_re[first], (1, 0, 2))
    ai = jnp.transpose(full_im[first], (1, 0, 2))
    br = jnp.transpose(full_re[second], (1, 0, 2))
    bi = jnp.transpose(full_im[second], (1, 0, 2))
    mr = coh_blk[:, 0].astype(F32)
    mi = coh_blk[:, 1].astype(F32)
    hr = ar * br + ai * bi
    hi = ai * br - ar * bi
    hr_t, hi_t = hr[:, :, None], hi[:, :, None]
    res_re = weight * (vis_blk[0] - jnp.sum(hr_t * mr - hi_t * mi, 0))
    res_im = weight * (vis_blk[1] - jnp.sum(hr_t * mi + hi_t * mr, 0))
    residual = jnp.stack([res_re, res_im])
    if not want_sums:
        return (residual, None)
    power = jnp.sum(weight[None] * (mr * mr + mi * mi), 2)
    sum_re = jnp.sum(mr * res_re + mi * res_im, 2) + hr * power
    sum_im = jnp.sum(mr * res_im - mi * res_re, 2) + hi * power
    terms_first = jnp.stack([br * sum_re - bi * sum_im, br * sum_im + bi * sum_re, power * (br * br + bi * bi)])
    terms_second = jnp.stack([ar * sum_re + ai * sum_im, ai * sum_re - ar * sum_im, power * (ar * ar + ai * ai)])
    stations = jnp.arange(STATIONS, dtype=jnp.int32)
    onehot_first = (first[:, None] == stations[None, :]).astype(F32)
    onehot_second = (second[:, None] == stations[None, :]).astype(F32)
    exact = lax.Precision.HIGHEST
    sums = jnp.einsum("bs,cdbf->csdf", onehot_first, terms_first, precision=exact)
    sums = sums + jnp.einsum("bs,cdbf->csdf", onehot_second, terms_second, precision=exact)
    return (residual, sums)


def plain_body(vis, model, mask, first, second, gre, gim):
    weight = mask.astype(F32)
    rows, channels = gre.shape
    shaped = (STATIONS, SOURCE_COUNT, channels)
    full_re = lax.all_gather(gre, "bl", axis=0, tiled=True).reshape(shaped)
    full_im = lax.all_gather(gim, "bl", axis=0, tiled=True).reshape(shaped)
    for step in range(ITERS):
        unused, sums = block_pass(full_re, full_im, vis, model, weight, first, second, True)
        totals = lax.psum(sums, "bl")
        denom = totals[2] + ridge
        full_re = 0.5 * (full_re + totals[0] / denom)
        full_im = 0.5 * (full_im + totals[1] / denom)
    residual, unused = block_pass(full_re, full_im, vis, model, weight, first, second, False)
    both = jnp.stack([full_re, full_im]).reshape(2, STATIONS * SOURCE_COUNT, channels)
    return lax.dynamic_slice_in_dim(both, lax.axis_index("bl") * rows, rows, 1), residual


def solution(mesh):
    n = mesh.shape["bl"]
    split = n == 16

    def body(vis, model, mask, first, second, gre, gim):
        if split and mask.shape[0] <= ROWS:
            return fast_body(n, vis, model, mask, first, second, gre, gim)
        return plain_body(vis, model, mask, first, second, gre, gim)

    in_specs = (
        P(None, ("grp", "bl"), None, None),
        P(None, None, ("grp", "bl"), None, None),
        P(("grp", "bl"), None, None),
        P(("grp", "bl")),
        P(("grp", "bl")),
        P(("grp", "bl"), None),
        P(("grp", "bl"), None),
    )
    out_specs = (P(None, ("grp", "bl"), None), P(None, ("grp", "bl"), None, None))
    return jax.shard_map(body, mesh=mesh, in_specs=in_specs, out_specs=out_specs, check_vma=False)
```

```python
import functools

import jax
import jax.numpy as jnp
from jax import lax
from jax.experimental import pallas as pl
from jax.experimental.pallas import tpu as pltpu
from jax.sharding import PartitionSpec as P

STATIONS = 64
SOURCE_COUNT = 40
ITERS = 2
ROWS = 16

ridge = 1.0
F32 = jnp.float32
BF16 = jnp.bfloat16
VMEM_LIMIT = 24 * 1024 * 1024


def swap(x):
    return pltpu.roll(x, x.shape[-1] // 2, axis=x.ndim - 1)


def lower(shape):
    return lax.broadcasted_iota(jnp.int32, shape, len(shape) - 1) < shape[-1] // 2


def cross(a, b):
    lo = lower(a.shape)
    return jnp.where(lo, a, swap(b)), jnp.where(lo, swap(a), b)


def halves_of(x):
    hi = x.astype(BF16)
    return hi, (x - hi.astype(F32)).astype(BF16)


def pick(onehot, x, dims):
    return sum(
        lax.dot_general(onehot, part, (dims, ((), ())), preferred_element_type=F32)
        for part in halves_of(x)
    )


TILE = 8
PARTS = (1, 3, 7, ROWS)


def pack_kernel(n, dpc, first_hbm, second_hbm, re_hbm, im_hbm, out_ref, first_ref, second_ref, sems):
    rows = re_hbm.shape[0]
    copies = [
        pltpu.make_async_copy(first_hbm, first_ref, sems.at[0]),
        pltpu.make_async_copy(second_hbm, second_ref, sems.at[1]),
        pltpu.make_async_copy(re_hbm, out_ref.at[pl.ds(0, rows)], sems.at[2]),
        pltpu.make_async_copy(im_hbm, out_ref.at[pl.ds(rows, rows)], sems.at[3]),
    ]
    for copy in copies:
        copy.start()
    out_ref[2 * rows :] = jnp.zeros((TILE, 128), F32)
    for copy in copies:
        copy.wait()
    pairs = first_ref.shape[1]
    out_ref[2 * rows : 2 * rows + 1, :pairs] = (first_ref[...] + 1).astype(F32)
    out_ref[2 * rows : 2 * rows + 1, ROWS : ROWS + pairs] = (second_ref[...] + 1).astype(F32)


class Fetch:
    def __init__(self, model, held, sems, firsts=(0,)):
        count, pairs = held.shape[0] // len(firsts), held.shape[2]
        self.copies = []
        self.ends = [0] + [min(end, pairs) for end in PARTS]
        for i in range(len(PARTS)):
            part = pl.ds(self.ends[i], self.ends[i + 1] - self.ends[i])
            self.copies.append([])
            for j, first in enumerate(firsts):
                self.copies[i].append(
                    pltpu.make_async_copy(
                        model.at[pl.ds(first, count), :, part],
                        held.at[pl.ds(j * count, count), :, part],
                        sems.at[i, j],
                    )
                )
        for copies in self.copies:
            for copy in copies:
                copy.start()

    def each(self, body):
        for i, copies in enumerate(self.copies):
            for copy in copies:
                copy.wait()
            lax.fori_loop(self.ends[i], self.ends[i + 1], body, 0)


def bring(pairs, sems):
    copies = [pltpu.make_async_copy(*pair, sems.at[i]) for i, pair in enumerate(pairs)]
    for copy in copies:
        copy.start()
    return copies


def power_kernel(
    n, dpc, model_hbm, mask_hbm, unused_in, out_ref, unused_out, mask_ref, side, model_ref, sems
):
    (mask_copy,) = bring([(mask_hbm, mask_ref)], side)
    fetch = Fetch(model_hbm, model_ref, sems)
    out_ref[...] = jnp.zeros_like(out_ref)

    def pair(b, carry):
        weight = mask_ref[b].astype(F32)
        for d in range(model_ref.shape[0]):
            mr = model_ref[d, 0, b].astype(F32)
            mi = model_ref[d, 1, b].astype(F32)
            row = pl.ds(b * dpc + d % dpc, 1)
            out_ref[d // dpc, row, :] = jnp.sum(weight * (mr * mr + mi * mi), axis=0, keepdims=True)
        return carry

    mask_copy.wait()
    fetch.each(pair)


def wide(ref, dpc):
    return jnp.concatenate([ref[pl.ds(dd, STATIONS, stride=dpc), :] for dd in range(dpc)], axis=1)


def put(ref, value, dpc):
    for dd in range(dpc):
        ref[pl.ds(dd, STATIONS, stride=dpc), :] = value[:, dd * 128 : (dd + 1) * 128]
    ref[STATIONS * dpc :, :] = jnp.zeros((TILE, 128), F32)


def first_own_kernel(n, dpc, *rest):
    ins, (g_ref, onehot_ref, unused_out, split, lines) = rest[:n], rest[n:]
    me = lax.axis_index("bl")
    k, c = lax.div(me, 2), lax.rem(me, 2)
    per = STATIONS // n
    rows = per * SOURCE_COUNT
    for o in range(n):
        peer = jnp.bitwise_xor(me, o)
        lines[pl.ds(peer, 1), :] = ins[o][2 * rows : 2 * rows + 1, :]
        done = []
        for s in range(per):
            at = s * SOURCE_COUNT + k * dpc
            x0, x1 = cross(ins[o][pl.ds(at, TILE), :], ins[o][pl.ds(rows + at, TILE), :])
            done.append(jnp.where(c == 0, x0, x1))
        for s in range(per):
            to = pl.multiple_of((peer * per + s) * TILE, TILE)
            split[pl.ds(to, TILE), :] = done[s]
    g = jnp.concatenate([split[pl.ds(dd, STATIONS, stride=TILE), :] for dd in range(dpc)], axis=1)
    put(g_ref, g, dpc)
    across = 128 // (2 * ROWS)
    station = lax.broadcasted_iota(jnp.int32, (STATIONS, 128), 0)
    for group in range(n // across):
        marks = jnp.zeros((1, 128), F32)
        for i in range(across):
            row = lines[group * across + i : group * across + i + 1, :]
            marks = marks + (pltpu.roll(row, i * 2 * ROWS, axis=1) if i else row)
        hit = station + 1 == marks.astype(jnp.int32)
        onehot_ref[:, group * 128 : (group + 1) * 128] = jnp.where(hit, 1.0, 0.0).astype(BF16)


def fill_powers(n, dpc, sums, sel_ref, terms, base):
    lo = lower((TILE, 128))
    for o in range(n):
        r = o * 2 * ROWS
        for dd in range(dpc):
            cols = slice(dd * 128, (dd + 1) * 128)
            dcols = slice(base + dd * 128, base + (dd + 1) * 128)
            W = sums[o, pl.ds(ROWS * dpc + dd, TILE, stride=dpc), :]
            Wx = swap(W)
            W = jnp.concatenate([jnp.where(lo, W, Wx), jnp.where(lo, Wx, W)], 0)
            p = sel_ref[r : r + ROWS, cols]
            q = sel_ref[r + ROWS : r + 2 * ROWS, cols]
            p2, q2 = p * p, q * q
            terms[r : r + ROWS, dcols] = W * (q2 + swap(q2))
            terms[r + ROWS : r + 2 * ROWS, dcols] = W * (p2 + swap(p2))


def fill_sums(n, dpc, sums, sel_ref, terms):
    lo = lower((ROWS, 128))
    sign = jnp.where(lo, -1.0, 1.0)
    for o in range(n):
        r = o * 2 * ROWS
        for dd in range(dpc):
            cols = slice(dd * 128, (dd + 1) * 128)
            B = sums[o, pl.ds(dd, ROWS, stride=dpc), :]
            p = sel_ref[r : r + ROWS, cols]
            q = sel_ref[r + ROWS : r + 2 * ROWS, cols]
            Bx = swap(B)
            Brr, Bii = jnp.where(lo, B, Bx), sign * jnp.where(lo, Bx, B)
            terms[r : r + ROWS, cols] = Brr * q + Bii * swap(q)
            terms[r + ROWS : r + 2 * ROWS, cols] = Brr * p - Bii * swap(p)


def own_kernel(n, dpc, g_in, onehot_ref, sums, g_out, terms, sel_ref):
    width = dpc * 128
    sel_ref[...] = pick(onehot_ref[...], wide(g_in, dpc), ((0,), (0,)))
    fill_sums(n, dpc, sums, sel_ref, terms)
    fill_powers(n, dpc, sums, sel_ref, terms, width)
    total = pick(onehot_ref[...], terms[...], ((1,), (0,)))
    put(g_out, 0.5 * (wide(g_in, dpc) + total[:, :width] / (total[:, width:] + ridge)), dpc)


def prepare_kernel(n, dpc, g_ref, onehot_ref, sums, den_ref, terms, sel_ref):
    sel_ref[...] = pick(onehot_ref[...], wide(g_ref, dpc), ((0,), (0,)))
    fill_powers(n, dpc, sums, sel_ref, terms, 0)
    den_ref[...] = pick(onehot_ref[...], terms[...], ((1,), (0,))) + ridge


def later_own_kernel(n, dpc, g_in, onehot_ref, den_ref, sums, g_out, terms, sel_ref):
    sel_ref[...] = pick(onehot_ref[...], wide(g_in, dpc), ((0,), (0,)))
    fill_sums(n, dpc, sums, sel_ref, terms)
    total = pick(onehot_ref[...], terms[...], ((1,), (0,)))
    put(g_out, 0.5 * (wide(g_in, dpc) + total / den_ref[...]), dpc)


def clear(dpc, pairs, *refs):
    for ref in refs:
        chips, rows, _ = ref.shape
        for m in range(chips):
            ref[m, pairs * dpc :, :] = jnp.zeros((rows - pairs * dpc, 128), F32)


def products_first(n, dpc, me, first_ref, second_ref, ins, hre, him, stack):
    per = STATIONS // n
    rows = per * SOURCE_COUNT
    for o in range(n):
        stack[jnp.bitwise_xor(me, o)] = ins[o][...]

    def block(station, k, part):
        at = lax.rem(station, per) * SOURCE_COUNT + k * dpc + part * rows
        return stack[lax.div(station, per), pl.ds(at, TILE), :]

    def one(b, k):
        p, q = first_ref[b], second_ref[b]
        return block(p, k, 0), block(p, k, 1), block(q, k, 0), block(q, k, 1)

    assemble(dpc, first_ref.shape[0], range(n // 2), one, hre, him)


def assemble(dpc, pairs, chips, one, hre, him):
    size = 3 if pairs % 3 == 0 else 1

    def group(i, carry):
        done = []
        for u in range(size):
            for m in chips:
                pr, pi, qr, qi = one(i * size + u, m)
                done.append((u, m, pr * qr + pi * qi, pi * qr - pr * qi))
        for u, m, re, im in done:
            rows = pl.ds((i * size + u) * dpc, TILE)
            hre[m, rows, :] = re
            him[m, rows, :] = im
        return carry

    lax.fori_loop(0, pairs // size, group, 0)
    clear(dpc, pairs, hre, him)


def piece_pair(dpc, even, ins, m, station):
    a = ins[2 * m][pl.ds(station * dpc, TILE), :]
    b = ins[2 * m + 1][pl.ds(station * dpc, TILE), :]
    return cross(jnp.where(even, a, b), jnp.where(even, b, a))


def products(dpc, me, first_ref, second_ref, ins, hre, him):
    even = lax.rem(me, 2) == 0

    def one(b, m):
        return *piece_pair(dpc, even, ins, m, first_ref[b]), *piece_pair(dpc, even, ins, m, second_ref[b])

    assemble(dpc, first_ref.shape[0], range(len(ins) // 2), one, hre, him)


def predict(dpc, b, acc, chips, model_ref, hre, him):
    tiles = [slice(t, t + TILE) for t in range(0, acc[0].shape[0], TILE)]
    acc_re, acc_im = ([x[t] for t in tiles] for x in acc)
    for m, k in enumerate(chips):
        for dd in range(dpc):
            mr = model_ref[k * dpc + dd, 0, b].astype(F32)
            mi = model_ref[k * dpc + dd, 1, b].astype(F32)
            row = pl.ds(b * dpc + dd, TILE, stride=0)
            hr, hi = hre[m, row, :], him[m, row, :]
            for i, t in enumerate(tiles):
                acc_re[i] = acc_re[i] - (hr * mr[t] - hi * mi[t])
                acc_im[i] = acc_im[i] - (hr * mi[t] + hi * mr[t])
    return jnp.concatenate(acc_re, 0), jnp.concatenate(acc_im, 0)


def weighted(b, acc, mask_ref):
    weight = mask_ref[b].astype(F32)
    return weight * acc[0], weight * acc[1]


def fold(a, b, step):
    if a is None:
        return None
    if b is None:
        return a + pltpu.roll(a, step, axis=0)
    mine = (lax.broadcasted_iota(jnp.int32, a.shape, 0) & step) == 0
    return jnp.where(mine, a, b) + pltpu.roll(jnp.where(mine, b, a), step, axis=0)


def row_sums(values):
    values = list(values) + [None] * (TILE - len(values))
    step = 1
    while step < TILE:
        values = [fold(a, b, step) for a, b in zip(values[::2], values[1::2])]
        step *= 2
    return values[0]


def tile_sum(x):
    total = x[:TILE]
    for t in range(1, x.shape[0] // TILE):
        total = total + x[t * TILE : (t + 1) * TILE]
    return total


def correlate(dpc, b, res, chips, model_ref, cre, cim, weight=None, power_ref=None):
    res_re, res_im = res
    done = []
    for m, k in enumerate(chips):
        re, im, power = [], [], []
        for dd in range(dpc):
            mr = model_ref[k * dpc + dd, 0, b].astype(F32)
            mi = model_ref[k * dpc + dd, 1, b].astype(F32)
            re.append(tile_sum(mr * res_re + mi * res_im))
            im.append(tile_sum(mr * res_im - mi * res_re))
            if weight is not None and m >= len(chips) // 2:
                power.append(tile_sum(weight * (mr * mr + mi * mi)))
        done.append((m, row_sums(re), row_sums(im), row_sums(power) if power else None))
    for m, re, im, power in done:
        cre[m, pl.ds(b * dpc, TILE), :] = re
        cim[m, pl.ds(b * dpc, TILE), :] = im
        if power is not None:
            power_ref[m, pl.ds(b * dpc, TILE), :] = power


def write_sums(dpc, chips, cre, cim, tiles, power_ref, out_ref, start):
    for m, k in enumerate(chips):
        re, im, at = tiles(m)
        done = []
        for t in range(ROWS * dpc // TILE):
            rows = slice(t * TILE, (t + 1) * TILE)
            w = power_ref[k, rows, :]
            done.append(cross(cre[m, rows, :] + re[at, rows, :] * w, cim[m, rows, :] + im[at, rows, :] * w))
        if start:
            for t in range(dpc):
                low, high = (slice(u * TILE, (u + 1) * TILE) for u in (t, t + dpc))
                done.append(cross(power_ref[k, low, :], power_ref[k, high, :]))
        for t, (x0, x1) in enumerate(done):
            rows = slice(t * TILE, (t + 1) * TILE)
            out_ref[2 * k, rows, :] = x0
            out_ref[2 * k + 1, rows, :] = x1


def first_pass_kernel(n, dpc, first_ref, second_ref, model_hbm, vis_hbm, mask_hbm, power_in, *rest):
    ins, rest = rest[:n], rest[n:]
    out_ref, power_ref, vis_ref, mask_ref, side, model_ref, sems, hre, him, cre, cim, stack = rest
    copies = bring([(vis_hbm, vis_ref), (mask_hbm, mask_ref)], side)
    fetch = Fetch(model_hbm, model_ref, sems)
    products_first(n, dpc, lax.axis_index("bl"), first_ref, second_ref, ins, hre, him, stack)
    for copy in copies:
        copy.wait()
    chips = range(n // 2)
    power_ref[: n // 4] = power_in[...]

    def pair(b, carry):
        acc = predict(dpc, b, (vis_ref[0, b], vis_ref[1, b]), chips, model_ref, hre, him)
        weight = mask_ref[b].astype(F32)
        correlate(dpc, b, weighted(b, acc, mask_ref), chips, model_ref, cre, cim, weight, power_ref)
        return carry

    fetch.each(pair)
    clear(dpc, mask_ref.shape[0], cre, cim, power_ref)
    write_sums(dpc, chips, cre, cim, lambda m: (hre, him, m), power_ref, out_ref, True)


NEAR, FAR = (0, 1, 2, 6), (3, 4, 5, 7)


def chips_of(me, pairs):
    return [jnp.bitwise_xor(lax.div(me, 2), m) for m in pairs]


def early_kernel(n, dpc, first_ref, second_ref, model_hbm, vis_ref, unused_in, *rest):
    ins, rest = rest[: 2 * len(NEAR)], rest[2 * len(NEAR) :]
    acc_ref, unused_out, hre, him, model_ref, sems = rest
    me = lax.axis_index("bl")
    fetch = Fetch(model_hbm, model_ref, sems, [k * dpc for k in chips_of(me, NEAR)])
    products(dpc, me, first_ref, second_ref, ins, hre, him)

    def pair(b, carry):
        acc = vis_ref[0, b], vis_ref[1, b]
        acc_ref[0, b], acc_ref[1, b] = predict(dpc, b, acc, range(len(NEAR)), model_ref, hre, him)
        return carry

    fetch.each(pair)


def later_pass_kernel(
    n,
    dpc,
    first_ref,
    second_ref,
    model_hbm,
    mask_ref,
    power_ref,
    acc_ref,
    near_re,
    near_im,
    *rest,
):
    ins, rest = rest[: 2 * len(FAR)], rest[2 * len(FAR) :]
    out_ref, model_ref, sems, hre, him, cre, cim = rest
    fetch = Fetch(model_hbm, model_ref, sems)
    me = lax.axis_index("bl")
    products(dpc, me, first_ref, second_ref, ins, hre, him)
    far = chips_of(me, FAR)
    chips = chips_of(me, NEAR) + far

    def pair(b, carry):
        acc = predict(dpc, b, (acc_ref[0, b], acc_ref[1, b]), far, model_ref, hre, him)
        correlate(dpc, b, weighted(b, acc, mask_ref), chips, model_ref, cre, cim)
        return carry

    fetch.each(pair)

    def tiles(m):
        for re, im, pairs in ((near_re, near_im, NEAR), (hre, him, FAR)):
            if m < len(pairs):
                return re, im, m
            m -= len(pairs)

    clear(dpc, mask_ref.shape[0], cre, cim)
    write_sums(dpc, chips, cre, cim, tiles, power_ref, out_ref, False)


def last_kernel(n, dpc, first_ref, second_ref, model_hbm, mask_ref, acc_ref, *rest):
    ins, (res_ref, gains_ref, model_ref, sems, hre, him) = rest[:n], rest[n:]
    me = lax.axis_index("bl")
    fetch = Fetch(model_hbm, model_ref, sems, [k * dpc for k in chips_of(me, FAR)])
    products(dpc, me, first_ref, second_ref, ins[: 2 * len(FAR)], hre, him)
    per = STATIONS // n
    even = lax.rem(me, 2) == 0
    for m, k in enumerate(chips_of(me, FAR + NEAR)):
        done = [piece_pair(dpc, even, ins, m, me * per + s) for s in range(per)]
        for s, parts in enumerate(done):
            for dd in range(dpc):
                at = s * SOURCE_COUNT + k * dpc + dd
                gains_ref[0, pl.ds(at, 1), :] = parts[0][dd : dd + 1]
                gains_ref[1, pl.ds(at, 1), :] = parts[1][dd : dd + 1]

    def pair(b, carry):
        acc = acc_ref[0, b], acc_ref[1, b]
        acc = predict(dpc, b, acc, range(len(FAR)), model_ref, hre, him)
        res_ref[0, b], res_ref[1, b] = weighted(b, acc, mask_ref)
        return carry

    fetch.each(pair)


SMEM = pl.BlockSpec(memory_space=pltpu.SMEM)
VMEM = pl.BlockSpec(memory_space=pltpu.VMEM)
HBM = pl.BlockSpec(memory_space=pltpu.HBM)


def shape(*dims, dtype=F32):
    return jax.ShapeDtypeStruct(dims, dtype)


def exchange(x):
    return lax.all_to_all(x, "bl", split_axis=0, concat_axis=0, tiled=True)


def gather(n, piece, beside):
    def send(x, o):
        return lax.ppermute(x, "bl", [(i, i ^ o) for i in range(n)])

    got = {0: piece}
    got[12], got[2], got[4], got[1] = (send(piece, o) for o in (12, 2, 4, 1))
    got[8] = send(got[12], 4)
    got[6], got[14], got[10] = send(got[4], 2), send(got[12], 2), send(got[8], 2)
    for o in (2, 4, 12, 6, 14, 8, 10):
        if o == 6:
            got[o] = beside(got[o], got)
        got[o + 1] = send(got[o], 1)
    return [got[o] for o in range(n)]


def fast_body(n, vis, model, mask, first, second, gre, gim):
    starts = (first.reshape(1, -1), second.reshape(1, -1), gre, gim)
    model, far_vis, far_mask, *starts = (
        pltpu.with_memory_space_constraint(x, pltpu.HBM) for x in (model, vis, mask, *starts)
    )
    dpc = SOURCE_COUNT // (n // 2)
    width = dpc * 128
    pairs, times, channels = mask.shape
    params = pltpu.CompilerParams(vmem_limit_bytes=VMEM_LIMIT)
    plane = (n // 2, ROWS * dpc + TILE, channels)
    half = (len(FAR), ROWS * dpc + TILE, channels)
    lots = n * 2 * ROWS
    mine = (STATIONS * dpc + TILE, channels)
    sems = pltpu.SemaphoreType.DMA((len(PARTS), n // 4))
    side = pltpu.SemaphoreType.DMA((2,))
    mask_held = [pltpu.VMEM(mask.shape, jnp.int32), side]
    held = [pltpu.VMEM(model.shape, BF16), sems]
    held_half = [pltpu.VMEM((SOURCE_COUNT // 2,) + model.shape[1:], BF16), sems]

    def call(kernel, args, outs, scratch=(), micros=1, aliases={}):
        def place(x):
            if any(x is y for y in (model, far_vis, far_mask, *starts)):
                return HBM
            return SMEM if x.ndim == 1 else VMEM

        return pl.pallas_call(
            functools.partial(kernel, n, dpc),
            in_specs=[place(x) for x in args],
            out_specs=[VMEM for o in outs],
            out_shape=outs,
            scratch_shapes=[pltpu.VMEM(x, F32) if isinstance(x, tuple) else x for x in scratch],
            compiler_params=params,
            input_output_aliases=aliases,
            cost_estimate=pl.CostEstimate(
                flops=0, bytes_accessed=int(micros * 3.69e6), transcendentals=0
            ),
        )(*args)

    (piece,) = call(
        pack_kernel,
        starts,
        [shape(2 * gre.shape[0] + TILE, channels)],
        [pltpu.VMEM((1, pairs), jnp.int32)] * 2 + [pltpu.SemaphoreType.DMA((4,))],
    )
    power = None

    def powers_beside(x, got):
        nonlocal power
        outs = [shape(*half), shape(*x.shape)]
        power, x = call(power_kernel, (model, far_mask, x), outs, mask_held + held_half, micros=20, aliases={2: 1})
        return x

    got = gather(n, piece, powers_beside)
    g, onehot, got[0] = call(
        first_own_kernel,
        got,
        [shape(*mine), shape(STATIONS, lots, dtype=BF16), shape(*piece.shape)],
        [(STATIONS * TILE, channels), (n, channels)],
        micros=2,
        aliases={0: 2},
    )
    sums, power = call(
        first_pass_kernel,
        (first, second, model, far_vis, far_mask, power, *got),
        [shape(n, (ROWS + TILE) * dpc, channels), pltpu.HBM(plane, F32)],
        [vis.shape] + mask_held + held + [plane] * 4 + [(n,) + piece.shape],
        micros=9,
    )
    powers = exchange(sums)
    (g,) = call(
        own_kernel,
        (g, onehot, powers),
        [shape(*mine)],
        [(lots, 2 * width), (lots, width)],
    )

    def slots(got, pairs):
        return [got[2 * m + c] for m in pairs for c in (0, 1)]

    def gather_near(g, last):
        near = None

        def beside(x, got):
            nonlocal near
            args = (first, second, model, vis, x, *slots(got, NEAR))
            outs = [shape(*vis.shape), shape(*x.shape)]
            if last:
                near, x = call(early_kernel, args, outs, [half, half] + held_half, aliases={4: 1})
            else:
                outs += [shape(*half), shape(*half)]
                acc, x, *tiles = call(early_kernel, args, outs, held_half, aliases={4: 1})
                near = (acc, *tiles)
            return x

        got = gather(n, g, beside)
        return near, slots(got, FAR + NEAR)

    for step in range(1, ITERS):
        near, got = gather_near(g, False)
        (den,) = call(
            prepare_kernel,
            (g, onehot, powers),
            [shape(STATIONS, width)],
            [(lots, width)] * 2,
            micros=2,
        )
        (sums,) = call(
            later_pass_kernel,
            (first, second, model, mask, power, *near, *got[: 2 * len(FAR)]),
            [shape(n, ROWS * dpc, channels)],
            held + [half] * 2 + [plane] * 2,
            micros=7,
        )
        sums = exchange(sums)
        (g,) = call(
            later_own_kernel,
            (g, onehot, den, sums),
            [shape(*mine)],
            [(lots, width)] * 2,
        )
    near, got = gather_near(g, True)
    residual, gains = call(
        last_kernel,
        (first, second, model, mask, near, *got),
        [shape(*vis.shape), shape(2, *gre.shape)],
        held_half + [half] * 2,
        micros=4,
    )
    return gains, residual


def block_pass(full_re, full_im, vis_blk, coh_blk, weight, first, second, want_sums):
    ar = jnp.transpose(full_re[first], (1, 0, 2))
    ai = jnp.transpose(full_im[first], (1, 0, 2))
    br = jnp.transpose(full_re[second], (1, 0, 2))
    bi = jnp.transpose(full_im[second], (1, 0, 2))
    mr = coh_blk[:, 0].astype(F32)
    mi = coh_blk[:, 1].astype(F32)
    hr = ar * br + ai * bi
    hi = ai * br - ar * bi
    hr_t, hi_t = hr[:, :, None], hi[:, :, None]
    res_re = weight * (vis_blk[0] - jnp.sum(hr_t * mr - hi_t * mi, 0))
    res_im = weight * (vis_blk[1] - jnp.sum(hr_t * mi + hi_t * mr, 0))
    residual = jnp.stack([res_re, res_im])
    if not want_sums:
        return (residual, None)
    power = jnp.sum(weight[None] * (mr * mr + mi * mi), 2)
    sum_re = jnp.sum(mr * res_re + mi * res_im, 2) + hr * power
    sum_im = jnp.sum(mr * res_im - mi * res_re, 2) + hi * power
    terms_first = jnp.stack([br * sum_re - bi * sum_im, br * sum_im + bi * sum_re, power * (br * br + bi * bi)])
    terms_second = jnp.stack([ar * sum_re + ai * sum_im, ai * sum_re - ar * sum_im, power * (ar * ar + ai * ai)])
    stations = jnp.arange(STATIONS, dtype=jnp.int32)
    onehot_first = (first[:, None] == stations[None, :]).astype(F32)
    onehot_second = (second[:, None] == stations[None, :]).astype(F32)
    exact = lax.Precision.HIGHEST
    sums = jnp.einsum("bs,cdbf->csdf", onehot_first, terms_first, precision=exact)
    sums = sums + jnp.einsum("bs,cdbf->csdf", onehot_second, terms_second, precision=exact)
    return (residual, sums)


def plain_body(vis, model, mask, first, second, gre, gim):
    weight = mask.astype(F32)
    rows, channels = gre.shape
    shaped = (STATIONS, SOURCE_COUNT, channels)
    full_re = lax.all_gather(gre, "bl", axis=0, tiled=True).reshape(shaped)
    full_im = lax.all_gather(gim, "bl", axis=0, tiled=True).reshape(shaped)
    for step in range(ITERS):
        unused, sums = block_pass(full_re, full_im, vis, model, weight, first, second, True)
        totals = lax.psum(sums, "bl")
        denom = totals[2] + ridge
        full_re = 0.5 * (full_re + totals[0] / denom)
        full_im = 0.5 * (full_im + totals[1] / denom)
    residual, unused = block_pass(full_re, full_im, vis, model, weight, first, second, False)
    both = jnp.stack([full_re, full_im]).reshape(2, STATIONS * SOURCE_COUNT, channels)
    return lax.dynamic_slice_in_dim(both, lax.axis_index("bl") * rows, rows, 1), residual


def solution(mesh):
    n = mesh.shape["bl"]
    split = n == 16

    def body(vis, model, mask, first, second, gre, gim):
        if split and mask.shape[0] <= ROWS:
            return fast_body(n, vis, model, mask, first, second, gre, gim)
        return plain_body(vis, model, mask, first, second, gre, gim)

    in_specs = (
        P(None, ("grp", "bl"), None, None),
        P(None, None, ("grp", "bl"), None, None),
        P(("grp", "bl"), None, None),
        P(("grp", "bl")),
        P(("grp", "bl")),
        P(("grp", "bl"), None),
        P(("grp", "bl"), None),
    )
    out_specs = (P(None, ("grp", "bl"), None), P(None, ("grp", "bl"), None, None))
    return jax.shard_map(body, mesh=mesh, in_specs=in_specs, out_specs=out_specs, check_vma=False)
```

```python
import functools

import jax
import jax.numpy as jnp
from jax import lax
from jax.experimental import pallas as pl
from jax.experimental.pallas import tpu as pltpu
from jax.sharding import PartitionSpec as P

STATIONS = 64
SOURCE_COUNT = 40
ITERS = 2
ROWS = 16

ridge = 1.0
F32 = jnp.float32
BF16 = jnp.bfloat16
VMEM_LIMIT = 24 * 1024 * 1024


def swap(x):
    return pltpu.roll(x, x.shape[-1] // 2, axis=x.ndim - 1)


def lower(shape):
    return lax.broadcasted_iota(jnp.int32, shape, len(shape) - 1) < shape[-1] // 2


def cross(a, b):
    lo = lower(a.shape)
    return jnp.where(lo, a, swap(b)), jnp.where(lo, swap(a), b)


def halves_of(x):
    hi = x.astype(BF16)
    return hi, (x - hi.astype(F32)).astype(BF16)


def pick(onehot, x, dims):
    return sum(
        lax.dot_general(onehot, part, (dims, ((), ())), preferred_element_type=F32)
        for part in halves_of(x)
    )


TILE = 8
PARTS = (1, 3, 6, 9, 12, ROWS)


def pack_kernel(n, dpc, first_hbm, second_hbm, re_hbm, im_hbm, out_ref, first_ref, second_ref, sems):
    rows = re_hbm.shape[0]
    copies = [
        pltpu.make_async_copy(first_hbm, first_ref, sems.at[0]),
        pltpu.make_async_copy(second_hbm, second_ref, sems.at[1]),
        pltpu.make_async_copy(re_hbm, out_ref.at[pl.ds(0, rows)], sems.at[2]),
        pltpu.make_async_copy(im_hbm, out_ref.at[pl.ds(rows, rows)], sems.at[3]),
    ]
    for copy in copies:
        copy.start()
    out_ref[2 * rows :] = jnp.zeros((TILE, 128), F32)
    for copy in copies:
        copy.wait()
    pairs = first_ref.shape[1]
    out_ref[2 * rows : 2 * rows + 1, :pairs] = (first_ref[...] + 1).astype(F32)
    out_ref[2 * rows : 2 * rows + 1, ROWS : ROWS + pairs] = (second_ref[...] + 1).astype(F32)


class Fetch:
    def __init__(self, model, held, sems, firsts=(0,)):
        count, pairs = held.shape[0] // len(firsts), held.shape[2]
        self.copies = []
        self.ends = [0] + [min(end, pairs) for end in PARTS]
        for i in range(len(PARTS)):
            part = pl.ds(self.ends[i], self.ends[i + 1] - self.ends[i])
            self.copies.append([])
            for j, first in enumerate(firsts):
                self.copies[i].append(
                    pltpu.make_async_copy(
                        model.at[pl.ds(first, count), :, part],
                        held.at[pl.ds(j * count, count), :, part],
                        sems.at[i, j],
                    )
                )
        for copies in self.copies:
            for copy in copies:
                copy.start()

    def each(self, body):
        for i, copies in enumerate(self.copies):
            for copy in copies:
                copy.wait()
            lax.fori_loop(self.ends[i], self.ends[i + 1], body, 0)


def bring(pairs, sems):
    copies = [pltpu.make_async_copy(*pair, sems.at[i]) for i, pair in enumerate(pairs)]
    for copy in copies:
        copy.start()
    return copies


def power_kernel(
    n, dpc, model_hbm, mask_hbm, unused_in, out_ref, unused_out, mask_ref, side, model_ref, sems
):
    (mask_copy,) = bring([(mask_hbm, mask_ref)], side)
    fetch = Fetch(model_hbm, model_ref, sems)
    out_ref[...] = jnp.zeros_like(out_ref)

    def pair(b, carry):
        weight = mask_ref[b].astype(F32)
        for d in range(model_ref.shape[0]):
            mr = model_ref[d, 0, b].astype(F32)
            mi = model_ref[d, 1, b].astype(F32)
            row = pl.ds(b * dpc + d % dpc, 1)
            out_ref[d // dpc, row, :] = jnp.sum(weight * (mr * mr + mi * mi), axis=0, keepdims=True)
        return carry

    mask_copy.wait()
    fetch.each(pair)


def wide(ref, dpc):
    return jnp.concatenate([ref[pl.ds(dd, STATIONS, stride=dpc), :] for dd in range(dpc)], axis=1)


def put(ref, value, dpc):
    for dd in range(dpc):
        ref[pl.ds(dd, STATIONS, stride=dpc), :] = value[:, dd * 128 : (dd + 1) * 128]
    ref[STATIONS * dpc :, :] = jnp.zeros((TILE, 128), F32)


def first_own_kernel(n, dpc, *rest):
    ins, (g_ref, onehot_ref, unused_out, split, lines) = rest[:n], rest[n:]
    me = lax.axis_index("bl")
    k, c = lax.div(me, 2), lax.rem(me, 2)
    per = STATIONS // n
    rows = per * SOURCE_COUNT
    for o in range(n):
        peer = jnp.bitwise_xor(me, o)
        lines[pl.ds(peer, 1), :] = ins[o][2 * rows : 2 * rows + 1, :]
        done = []
        for s in range(per):
            at = s * SOURCE_COUNT + k * dpc
            x0, x1 = cross(ins[o][pl.ds(at, TILE), :], ins[o][pl.ds(rows + at, TILE), :])
            done.append(jnp.where(c == 0, x0, x1))
        for s in range(per):
            to = pl.multiple_of((peer * per + s) * TILE, TILE)
            split[pl.ds(to, TILE), :] = done[s]
    g = jnp.concatenate([split[pl.ds(dd, STATIONS, stride=TILE), :] for dd in range(dpc)], axis=1)
    put(g_ref, g, dpc)
    across = 128 // (2 * ROWS)
    station = lax.broadcasted_iota(jnp.int32, (STATIONS, 128), 0)
    for group in range(n // across):
        marks = jnp.zeros((1, 128), F32)
        for i in range(across):
            row = lines[group * across + i : group * across + i + 1, :]
            marks = marks + (pltpu.roll(row, i * 2 * ROWS, axis=1) if i else row)
        hit = station + 1 == marks.astype(jnp.int32)
        onehot_ref[:, group * 128 : (group + 1) * 128] = jnp.where(hit, 1.0, 0.0).astype(BF16)


def fill_powers(n, dpc, sums, sel_ref, terms, base):
    lo = lower((TILE, 128))
    for o in range(n):
        r = o * 2 * ROWS
        for dd in range(dpc):
            cols = slice(dd * 128, (dd + 1) * 128)
            dcols = slice(base + dd * 128, base + (dd + 1) * 128)
            W = sums[o, pl.ds(ROWS * dpc + dd, TILE, stride=dpc), :]
            Wx = swap(W)
            W = jnp.concatenate([jnp.where(lo, W, Wx), jnp.where(lo, Wx, W)], 0)
            p = sel_ref[r : r + ROWS, cols]
            q = sel_ref[r + ROWS : r + 2 * ROWS, cols]
            p2, q2 = p * p, q * q
            terms[r : r + ROWS, dcols] = W * (q2 + swap(q2))
            terms[r + ROWS : r + 2 * ROWS, dcols] = W * (p2 + swap(p2))


def fill_sums(n, dpc, sums, sel_ref, terms):
    lo = lower((ROWS, 128))
    sign = jnp.where(lo, -1.0, 1.0)
    for o in range(n):
        r = o * 2 * ROWS
        for dd in range(dpc):
            cols = slice(dd * 128, (dd + 1) * 128)
            B = sums[o, pl.ds(dd, ROWS, stride=dpc), :]
            p = sel_ref[r : r + ROWS, cols]
            q = sel_ref[r + ROWS : r + 2 * ROWS, cols]
            Bx = swap(B)
            Brr, Bii = jnp.where(lo, B, Bx), sign * jnp.where(lo, Bx, B)
            terms[r : r + ROWS, cols] = Brr * q + Bii * swap(q)
            terms[r + ROWS : r + 2 * ROWS, cols] = Brr * p - Bii * swap(p)


def own_kernel(n, dpc, g_in, onehot_ref, sums, g_out, terms, sel_ref):
    width = dpc * 128
    sel_ref[...] = pick(onehot_ref[...], wide(g_in, dpc), ((0,), (0,)))
    fill_sums(n, dpc, sums, sel_ref, terms)
    fill_powers(n, dpc, sums, sel_ref, terms, width)
    total = pick(onehot_ref[...], terms[...], ((1,), (0,)))
    put(g_out, 0.5 * (wide(g_in, dpc) + total[:, :width] / (total[:, width:] + ridge)), dpc)


def prepare_kernel(n, dpc, g_ref, onehot_ref, sums, den_ref, terms, sel_ref):
    sel_ref[...] = pick(onehot_ref[...], wide(g_ref, dpc), ((0,), (0,)))
    fill_powers(n, dpc, sums, sel_ref, terms, 0)
    den_ref[...] = pick(onehot_ref[...], terms[...], ((1,), (0,))) + ridge


def later_own_kernel(n, dpc, g_in, onehot_ref, den_ref, sums, g_out, terms, sel_ref):
    sel_ref[...] = pick(onehot_ref[...], wide(g_in, dpc), ((0,), (0,)))
    fill_sums(n, dpc, sums, sel_ref, terms)
    total = pick(onehot_ref[...], terms[...], ((1,), (0,)))
    put(g_out, 0.5 * (wide(g_in, dpc) + total / den_ref[...]), dpc)


def clear(dpc, pairs, *refs):
    for ref in refs:
        chips, rows, _ = ref.shape
        for m in range(chips):
            ref[m, pairs * dpc :, :] = jnp.zeros((rows - pairs * dpc, 128), F32)


def products_first(n, dpc, me, first_ref, second_ref, ins, hre, him, stack):
    per = STATIONS // n
    rows = per * SOURCE_COUNT
    for o in range(n):
        stack[jnp.bitwise_xor(me, o)] = ins[o][...]

    def block(station, k, part):
        at = lax.rem(station, per) * SOURCE_COUNT + k * dpc + part * rows
        return stack[lax.div(station, per), pl.ds(at, TILE), :]

    def one(b, k):
        p, q = first_ref[b], second_ref[b]
        return block(p, k, 0), block(p, k, 1), block(q, k, 0), block(q, k, 1)

    assemble(dpc, first_ref.shape[0], range(n // 2), one, hre, him)


def assemble(dpc, pairs, chips, one, hre, him):
    size = 3 if pairs % 3 == 0 else 1

    def group(i, carry):
        done = []
        for u in range(size):
            for m in chips:
                pr, pi, qr, qi = one(i * size + u, m)
                done.append((u, m, pr * qr + pi * qi, pi * qr - pr * qi))
        for u, m, re, im in done:
            rows = pl.ds((i * size + u) * dpc, TILE)
            hre[m, rows, :] = re
            him[m, rows, :] = im
        return carry

    lax.fori_loop(0, pairs // size, group, 0)
    clear(dpc, pairs, hre, him)


def piece_pair(dpc, even, ins, m, station):
    a = ins[2 * m][pl.ds(station * dpc, TILE), :]
    b = ins[2 * m + 1][pl.ds(station * dpc, TILE), :]
    return cross(jnp.where(even, a, b), jnp.where(even, b, a))


def products(dpc, me, first_ref, second_ref, ins, hre, him):
    even = lax.rem(me, 2) == 0

    def one(b, m):
        return *piece_pair(dpc, even, ins, m, first_ref[b]), *piece_pair(dpc, even, ins, m, second_ref[b])

    assemble(dpc, first_ref.shape[0], range(len(ins) // 2), one, hre, him)


def predict(dpc, b, acc, chips, model_ref, hre, him):
    tiles = [slice(t, t + TILE) for t in range(0, acc[0].shape[0], TILE)]
    acc_re, acc_im = ([x[t] for t in tiles] for x in acc)
    for m, k in enumerate(chips):
        for dd in range(dpc):
            mr = model_ref[k * dpc + dd, 0, b].astype(F32)
            mi = model_ref[k * dpc + dd, 1, b].astype(F32)
            row = pl.ds(b * dpc + dd, TILE, stride=0)
            hr, hi = hre[m, row, :], him[m, row, :]
            for i, t in enumerate(tiles):
                acc_re[i] = acc_re[i] - (hr * mr[t] - hi * mi[t])
                acc_im[i] = acc_im[i] - (hr * mi[t] + hi * mr[t])
    return jnp.concatenate(acc_re, 0), jnp.concatenate(acc_im, 0)


def weighted(b, acc, mask_ref):
    weight = mask_ref[b].astype(F32)
    return weight * acc[0], weight * acc[1]


def fold(a, b, step):
    if a is None:
        return None
    if b is None:
        return a + pltpu.roll(a, step, axis=0)
    mine = (lax.broadcasted_iota(jnp.int32, a.shape, 0) & step) == 0
    return jnp.where(mine, a, b) + pltpu.roll(jnp.where(mine, b, a), step, axis=0)


def row_sums(values):
    values = list(values) + [None] * (TILE - len(values))
    step = 1
    while step < TILE:
        values = [fold(a, b, step) for a, b in zip(values[::2], values[1::2])]
        step *= 2
    return values[0]


def tile_sum(x):
    total = x[:TILE]
    for t in range(1, x.shape[0] // TILE):
        total = total + x[t * TILE : (t + 1) * TILE]
    return total


def correlate(dpc, b, res, chips, model_ref, cre, cim, weight=None, power_ref=None):
    res_re, res_im = res
    done = []
    for m, k in enumerate(chips):
        re, im, power = [], [], []
        for dd in range(dpc):
            mr = model_ref[k * dpc + dd, 0, b].astype(F32)
            mi = model_ref[k * dpc + dd, 1, b].astype(F32)
            re.append(tile_sum(mr * res_re + mi * res_im))
            im.append(tile_sum(mr * res_im - mi * res_re))
            if weight is not None and m >= len(chips) // 2:
                power.append(tile_sum(weight * (mr * mr + mi * mi)))
        done.append((m, row_sums(re), row_sums(im), row_sums(power) if power else None))
    for m, re, im, power in done:
        cre[m, pl.ds(b * dpc, TILE), :] = re
        cim[m, pl.ds(b * dpc, TILE), :] = im
        if power is not None:
            power_ref[m, pl.ds(b * dpc, TILE), :] = power


def write_sums(dpc, chips, cre, cim, tiles, power_ref, out_ref, start):
    for m, k in enumerate(chips):
        re, im, at = tiles(m)
        done = []
        for t in range(ROWS * dpc // TILE):
            rows = slice(t * TILE, (t + 1) * TILE)
            w = power_ref[k, rows, :]
            done.append(cross(cre[m, rows, :] + re[at, rows, :] * w, cim[m, rows, :] + im[at, rows, :] * w))
        if start:
            for t in range(dpc):
                low, high = (slice(u * TILE, (u + 1) * TILE) for u in (t, t + dpc))
                done.append(cross(power_ref[k, low, :], power_ref[k, high, :]))
        for t, (x0, x1) in enumerate(done):
            rows = slice(t * TILE, (t + 1) * TILE)
            out_ref[2 * k, rows, :] = x0
            out_ref[2 * k + 1, rows, :] = x1


def first_pass_kernel(n, dpc, first_ref, second_ref, model_hbm, vis_hbm, mask_hbm, power_in, *rest):
    ins, rest = rest[:n], rest[n:]
    out_ref, power_ref, vis_ref, mask_ref, side, model_ref, sems, hre, him, cre, cim, stack = rest
    copies = bring([(vis_hbm, vis_ref), (mask_hbm, mask_ref)], side)
    fetch = Fetch(model_hbm, model_ref, sems)
    products_first(n, dpc, lax.axis_index("bl"), first_ref, second_ref, ins, hre, him, stack)
    for copy in copies:
        copy.wait()
    chips = range(n // 2)
    power_ref[: n // 4] = power_in[...]

    def pair(b, carry):
        acc = predict(dpc, b, (vis_ref[0, b], vis_ref[1, b]), chips, model_ref, hre, him)
        weight = mask_ref[b].astype(F32)
        correlate(dpc, b, weighted(b, acc, mask_ref), chips, model_ref, cre, cim, weight, power_ref)
        return carry

    fetch.each(pair)
    clear(dpc, mask_ref.shape[0], cre, cim, power_ref)
    write_sums(dpc, chips, cre, cim, lambda m: (hre, him, m), power_ref, out_ref, True)


NEAR, FAR = (0, 1, 2, 6), (3, 4, 5, 7)


def chips_of(me, pairs):
    return [jnp.bitwise_xor(lax.div(me, 2), m) for m in pairs]


def early_kernel(n, dpc, first_ref, second_ref, model_hbm, vis_ref, unused_in, *rest):
    ins, rest = rest[: 2 * len(NEAR)], rest[2 * len(NEAR) :]
    acc_ref, unused_out, hre, him, model_ref, sems = rest
    me = lax.axis_index("bl")
    fetch = Fetch(model_hbm, model_ref, sems, [k * dpc for k in chips_of(me, NEAR)])
    products(dpc, me, first_ref, second_ref, ins, hre, him)

    def pair(b, carry):
        acc = vis_ref[0, b], vis_ref[1, b]
        acc_ref[0, b], acc_ref[1, b] = predict(dpc, b, acc, range(len(NEAR)), model_ref, hre, him)
        return carry

    fetch.each(pair)


def later_pass_kernel(
    n,
    dpc,
    first_ref,
    second_ref,
    model_hbm,
    mask_ref,
    power_ref,
    acc_ref,
    near_re,
    near_im,
    *rest,
):
    ins, rest = rest[: 2 * len(FAR)], rest[2 * len(FAR) :]
    out_ref, model_ref, sems, hre, him, cre, cim = rest
    fetch = Fetch(model_hbm, model_ref, sems)
    me = lax.axis_index("bl")
    products(dpc, me, first_ref, second_ref, ins, hre, him)
    far = chips_of(me, FAR)
    chips = chips_of(me, NEAR) + far

    def pair(b, carry):
        acc = predict(dpc, b, (acc_ref[0, b], acc_ref[1, b]), far, model_ref, hre, him)
        correlate(dpc, b, weighted(b, acc, mask_ref), chips, model_ref, cre, cim)
        return carry

    fetch.each(pair)

    def tiles(m):
        for re, im, pairs in ((near_re, near_im, NEAR), (hre, him, FAR)):
            if m < len(pairs):
                return re, im, m
            m -= len(pairs)

    clear(dpc, mask_ref.shape[0], cre, cim)
    write_sums(dpc, chips, cre, cim, tiles, power_ref, out_ref, False)


def last_kernel(n, dpc, first_ref, second_ref, model_hbm, mask_ref, acc_ref, *rest):
    ins, (res_ref, gains_ref, model_ref, sems, hre, him) = rest[:n], rest[n:]
    me = lax.axis_index("bl")
    fetch = Fetch(model_hbm, model_ref, sems, [k * dpc for k in chips_of(me, FAR)])
    products(dpc, me, first_ref, second_ref, ins[: 2 * len(FAR)], hre, him)
    per = STATIONS // n
    even = lax.rem(me, 2) == 0
    for m, k in enumerate(chips_of(me, FAR + NEAR)):
        done = [piece_pair(dpc, even, ins, m, me * per + s) for s in range(per)]
        for s, parts in enumerate(done):
            for dd in range(dpc):
                at = s * SOURCE_COUNT + k * dpc + dd
                gains_ref[0, pl.ds(at, 1), :] = parts[0][dd : dd + 1]
                gains_ref[1, pl.ds(at, 1), :] = parts[1][dd : dd + 1]

    def pair(b, carry):
        acc = acc_ref[0, b], acc_ref[1, b]
        acc = predict(dpc, b, acc, range(len(FAR)), model_ref, hre, him)
        res_ref[0, b], res_ref[1, b] = weighted(b, acc, mask_ref)
        return carry

    fetch.each(pair)


SMEM = pl.BlockSpec(memory_space=pltpu.SMEM)
VMEM = pl.BlockSpec(memory_space=pltpu.VMEM)
HBM = pl.BlockSpec(memory_space=pltpu.HBM)


def shape(*dims, dtype=F32):
    return jax.ShapeDtypeStruct(dims, dtype)


def exchange(x):
    return lax.all_to_all(x, "bl", split_axis=0, concat_axis=0, tiled=True)


def gather(n, piece, beside):
    def send(x, o):
        return lax.ppermute(x, "bl", [(i, i ^ o) for i in range(n)])

    got = {0: piece}
    got[12], got[2], got[4], got[1] = (send(piece, o) for o in (12, 2, 4, 1))
    got[8] = send(got[12], 4)
    got[6], got[14], got[10] = send(got[4], 2), send(got[12], 2), send(got[8], 2)
    for o in (2, 4, 12, 6, 14, 8, 10):
        if o == 6:
            got[o] = beside(got[o], got)
        got[o + 1] = send(got[o], 1)
    return [got[o] for o in range(n)]


def fast_body(n, vis, model, mask, first, second, gre, gim):
    starts = (first.reshape(1, -1), second.reshape(1, -1), gre, gim)
    model, far_vis, far_mask, *starts = (
        pltpu.with_memory_space_constraint(x, pltpu.HBM) for x in (model, vis, mask, *starts)
    )
    dpc = SOURCE_COUNT // (n // 2)
    width = dpc * 128
    pairs, times, channels = mask.shape
    params = pltpu.CompilerParams(vmem_limit_bytes=VMEM_LIMIT)
    plane = (n // 2, ROWS * dpc + TILE, channels)
    half = (len(FAR), ROWS * dpc + TILE, channels)
    lots = n * 2 * ROWS
    mine = (STATIONS * dpc + TILE, channels)
    sems = pltpu.SemaphoreType.DMA((len(PARTS), n // 4))
    side = pltpu.SemaphoreType.DMA((2,))
    mask_held = [pltpu.VMEM(mask.shape, jnp.int32), side]
    held = [pltpu.VMEM(model.shape, BF16), sems]
    held_half = [pltpu.VMEM((SOURCE_COUNT // 2,) + model.shape[1:], BF16), sems]

    def call(kernel, args, outs, scratch=(), micros=1, aliases={}):
        def place(x):
            if any(x is y for y in (model, far_vis, far_mask, *starts)):
                return HBM
            return SMEM if x.ndim == 1 else VMEM

        return pl.pallas_call(
            functools.partial(kernel, n, dpc),
            in_specs=[place(x) for x in args],
            out_specs=[VMEM for o in outs],
            out_shape=outs,
            scratch_shapes=[pltpu.VMEM(x, F32) if isinstance(x, tuple) else x for x in scratch],
            compiler_params=params,
            input_output_aliases=aliases,
            cost_estimate=pl.CostEstimate(
                flops=0, bytes_accessed=int(micros * 3.69e6), transcendentals=0
            ),
        )(*args)

    (piece,) = call(
        pack_kernel,
        starts,
        [shape(2 * gre.shape[0] + TILE, channels)],
        [pltpu.VMEM((1, pairs), jnp.int32)] * 2 + [pltpu.SemaphoreType.DMA((4,))],
    )
    power = None

    def powers_beside(x, got):
        nonlocal power
        outs = [shape(*half), shape(*x.shape)]
        power, x = call(power_kernel, (model, far_mask, x), outs, mask_held + held_half, micros=20, aliases={2: 1})
        return x

    got = gather(n, piece, powers_beside)
    g, onehot, got[0] = call(
        first_own_kernel,
        got,
        [shape(*mine), shape(STATIONS, lots, dtype=BF16), shape(*piece.shape)],
        [(STATIONS * TILE, channels), (n, channels)],
        micros=2,
        aliases={0: 2},
    )
    sums, power = call(
        first_pass_kernel,
        (first, second, model, far_vis, far_mask, power, *got),
        [shape(n, (ROWS + TILE) * dpc, channels), pltpu.HBM(plane, F32)],
        [vis.shape] + mask_held + held + [plane] * 4 + [(n,) + piece.shape],
        micros=9,
    )
    powers = exchange(sums)
    (g,) = call(
        own_kernel,
        (g, onehot, powers),
        [shape(*mine)],
        [(lots, 2 * width), (lots, width)],
    )

    def slots(got, pairs):
        return [got[2 * m + c] for m in pairs for c in (0, 1)]

    def gather_near(g, last):
        near = None

        def beside(x, got):
            nonlocal near
            args = (first, second, model, vis, x, *slots(got, NEAR))
            outs = [shape(*vis.shape), shape(*x.shape)]
            if last:
                near, x = call(early_kernel, args, outs, [half, half] + held_half, aliases={4: 1})
            else:
                outs += [shape(*half), shape(*half)]
                acc, x, *tiles = call(early_kernel, args, outs, held_half, aliases={4: 1})
                near = (acc, *tiles)
            return x

        got = gather(n, g, beside)
        return near, slots(got, FAR + NEAR)

    for step in range(1, ITERS):
        near, got = gather_near(g, False)
        (den,) = call(
            prepare_kernel,
            (g, onehot, powers),
            [shape(STATIONS, width)],
            [(lots, width)] * 2,
            micros=2,
        )
        (sums,) = call(
            later_pass_kernel,
            (first, second, model, mask, power, *near, *got[: 2 * len(FAR)]),
            [shape(n, ROWS * dpc, channels)],
            held + [half] * 2 + [plane] * 2,
            micros=7,
        )
        sums = exchange(sums)
        (g,) = call(
            later_own_kernel,
            (g, onehot, den, sums),
            [shape(*mine)],
            [(lots, width)] * 2,
        )
    near, got = gather_near(g, True)
    residual, gains = call(
        last_kernel,
        (first, second, model, mask, near, *got),
        [shape(*vis.shape), shape(2, *gre.shape)],
        held_half + [half] * 2,
        micros=4,
    )
    return gains, residual


def block_pass(full_re, full_im, vis_blk, coh_blk, weight, first, second, want_sums):
    ar = jnp.transpose(full_re[first], (1, 0, 2))
    ai = jnp.transpose(full_im[first], (1, 0, 2))
    br = jnp.transpose(full_re[second], (1, 0, 2))
    bi = jnp.transpose(full_im[second], (1, 0, 2))
    mr = coh_blk[:, 0].astype(F32)
    mi = coh_blk[:, 1].astype(F32)
    hr = ar * br + ai * bi
    hi = ai * br - ar * bi
    hr_t, hi_t = hr[:, :, None], hi[:, :, None]
    res_re = weight * (vis_blk[0] - jnp.sum(hr_t * mr - hi_t * mi, 0))
    res_im = weight * (vis_blk[1] - jnp.sum(hr_t * mi + hi_t * mr, 0))
    residual = jnp.stack([res_re, res_im])
    if not want_sums:
        return (residual, None)
    power = jnp.sum(weight[None] * (mr * mr + mi * mi), 2)
    sum_re = jnp.sum(mr * res_re + mi * res_im, 2) + hr * power
    sum_im = jnp.sum(mr * res_im - mi * res_re, 2) + hi * power
    terms_first = jnp.stack([br * sum_re - bi * sum_im, br * sum_im + bi * sum_re, power * (br * br + bi * bi)])
    terms_second = jnp.stack([ar * sum_re + ai * sum_im, ai * sum_re - ar * sum_im, power * (ar * ar + ai * ai)])
    stations = jnp.arange(STATIONS, dtype=jnp.int32)
    onehot_first = (first[:, None] == stations[None, :]).astype(F32)
    onehot_second = (second[:, None] == stations[None, :]).astype(F32)
    exact = lax.Precision.HIGHEST
    sums = jnp.einsum("bs,cdbf->csdf", onehot_first, terms_first, precision=exact)
    sums = sums + jnp.einsum("bs,cdbf->csdf", onehot_second, terms_second, precision=exact)
    return (residual, sums)


def plain_body(vis, model, mask, first, second, gre, gim):
    weight = mask.astype(F32)
    rows, channels = gre.shape
    shaped = (STATIONS, SOURCE_COUNT, channels)
    full_re = lax.all_gather(gre, "bl", axis=0, tiled=True).reshape(shaped)
    full_im = lax.all_gather(gim, "bl", axis=0, tiled=True).reshape(shaped)
    for step in range(ITERS):
        unused, sums = block_pass(full_re, full_im, vis, model, weight, first, second, True)
        totals = lax.psum(sums, "bl")
        denom = totals[2] + ridge
        full_re = 0.5 * (full_re + totals[0] / denom)
        full_im = 0.5 * (full_im + totals[1] / denom)
    residual, unused = block_pass(full_re, full_im, vis, model, weight, first, second, False)
    both = jnp.stack([full_re, full_im]).reshape(2, STATIONS * SOURCE_COUNT, channels)
    return lax.dynamic_slice_in_dim(both, lax.axis_index("bl") * rows, rows, 1), residual


def solution(mesh):
    n = mesh.shape["bl"]
    split = n == 16

    def body(vis, model, mask, first, second, gre, gim):
        if split and mask.shape[0] <= ROWS:
            return fast_body(n, vis, model, mask, first, second, gre, gim)
        return plain_body(vis, model, mask, first, second, gre, gim)

    in_specs = (
        P(None, ("grp", "bl"), None, None),
        P(None, None, ("grp", "bl"), None, None),
        P(("grp", "bl"), None, None),
        P(("grp", "bl")),
        P(("grp", "bl")),
        P(("grp", "bl"), None),
        P(("grp", "bl"), None),
    )
    out_specs = (P(None, ("grp", "bl"), None), P(None, ("grp", "bl"), None, None))
    return jax.shard_map(body, mesh=mesh, in_specs=in_specs, out_specs=out_specs, check_vma=False)
```
